32 devices in a mesh: section: 2 (over x), dp: 4 (over z), ctx: 4 (over y, core).
Axes of the slice: x: 2, y: 2, z: 4, core: 2. Of those that a mesh axis runs over, the one named last changes fastest.
Arguments:
- inputs: bfloat16 [2, 4, 1024, 768], P(None, 'dp', 'ctx'), may hold values from -6 to 6
- slot_order: int32 [2, 4, 8], P(None, 'dp'), may hold values from 0 to 7, as said below
- cotangent: bfloat16 [2, 4, 1024, 768], P(None, 'dp', 'ctx'), may hold values from -6 to 6
- gains: float32 [2, 2, 768], P('section'), may hold values from 0.25 to 1.75
- biases: float32 [2, 7680], P('section'), may hold values from -2 to 2
- w_qkv: bfloat16 [2, 768, 2304], P('section'), may hold values from -0.21875 to 0.21875
- w_out: bfloat16 [2, 768, 768], P('section'), may hold values from -3 to 3
- w_up: bfloat16 [2, 768, 3072], P('section'), may hold values from -0.21875 to 0.21875
- w_down: bfloat16 [2, 3072, 768], P('section'), may hold values from -0.109375 to 0.109375
Outputs:
- acts: bfloat16 [2, 2, 4, 1024, 768], P('section', None, 'dp', 'ctx')
- grads: float32 [2, 2, 4, 1024, 768], P('section', None, 'dp', 'ctx')
- grad_gains: float32 [2, 2, 768], P('section', None, ('dp', 'ctx'))
- grad_biases: float32 [2, 7680], P('section', ('dp', 'ctx'))
- grad_qkv: float32 [2, 768, 2304], P('section', ('dp', 'ctx'))
- grad_out: float32 [2, 768, 768], P('section', ('dp', 'ctx'))
- grad_up: float32 [2, 768, 3072], P('section', ('dp', 'ctx'))
- grad_down: float32 [2, 3072, 768], P('section', ('dp', 'ctx'))
The draws below stay inside these ranges and needn't reach their ends.
Inputs may be any that keep to these rules, and one draw needn't show every extreme that they name: `slot_order`: for each micro-batch and replica the 8 entries are a permutation of 0 to 7, and slots 2 m and 2 m + 1 add up to 7.
All inputs are finite; a program needn't handle non-finite values.
Results may differ from the reference program's by a relative error of at most 0.03.
Values may be sent and summed in bfloat16 or wider, within the bound.
No kernel may reach another device: no remote copies, remote signals or barrier semaphores. Data moves between devices by JAX's collectives and lax.ppermute only.
A program may use at most 320 MiB of HBM per device.

```python
import jax
import jax.numpy as jnp
from jax import lax

D = 768
HEADS = 12
HDIM = 64
FF = 3072
MB = 2
SPAN = 128
SLOTS = 8
SEQ = 1024
KEY_BLOCK = 512
N_DP = 4
N_CTX = 4


def draw_slot_order(key, part):
    key = jax.random.fold_in(key, 11)
    seq_keys = jax.random.split(key, MB * N_DP)

    def one_sequence(seq_key):
        first_key, second_key = jax.random.split(seq_key)
        lower = jax.random.permutation(first_key, N_CTX).astype(jnp.int32)
        flipped = jax.random.randint(second_key, (N_CTX,), 0, 2)
        upper = SLOTS - 1 - lower
        leading = jnp.where(flipped == 1, upper, lower)
        trailing = jnp.where(flipped == 1, lower, upper)
        return jnp.stack([leading, trailing], axis=1).reshape(SLOTS)
    return jax.vmap(one_sequence)(seq_keys).reshape(MB, N_DP, SLOTS).astype(jnp.int32)


def raised(values, stream_key, source, target, blocks, factor):
    owner, partner = [(jnp.arange(values.shape[dim]) // (values.shape[dim] // blocks)).reshape([-1 if axis == dim else 1 for axis in range(values.ndim)]) for dim in (source, target)]
    chosen = jax.random.permutation(stream_key, blocks)[partner]
    strong = (owner == chosen) | (owner == (partner + blocks // 2) % blocks)
    return jnp.where(strong, factor * values, values)


def shard_levels(own_key, dims, pieces, smallest, largest):
    gain, own = 1.0, jax.random.fold_in(own_key, 6)
    for axis_at, blocks in pieces:
        heights = jnp.exp(jax.random.uniform(jax.random.fold_in(own, axis_at), (blocks,), jnp.float32, smallest / len(pieces), largest / len(pieces)))
        gain = gain * jnp.repeat(heights, dims[axis_at] // blocks).reshape([-1 if axis == axis_at else 1 for axis in range(len(dims))])
    return gain


def bell_draw(key, extent, width, limit, cuts=(), kind=jnp.bfloat16):
    drawn = jax.random.normal(key, extent, jnp.float32) * width
    if len(cuts) > 0:
        drawn = shard_levels(key, extent, cuts, -0.22, 0.18) * drawn
    return jnp.clip(drawn, min=-limit, max=limit).astype(kind)


def noise_with(stream_key, extent, width, most, cuts, heavy, kind=jnp.bfloat16):
    drawn = width * jax.random.normal(stream_key, extent, jnp.float32)
    if cuts:
        drawn = drawn * shard_levels(stream_key, extent, cuts, -0.22, 0.18)
    return jnp.clip(raised(drawn, jax.random.fold_in(stream_key, 3), *heavy), -most, most).astype(kind)


def setup_inputs(seed: int = 0) -> dict:
    streams_of = jax.random.split(jax.random.key(seed), 10)
    return {
        "inputs": noise_with(streams_of[0], (MB, N_DP, SEQ, D), 1.0, 6.0, ((1, 4), (2, 4)), (2, 3, 4, 2.0)),
        "slot_order": draw_slot_order(jax.random.fold_in(streams_of[9], 71), 0),
        "cotangent": noise_with(streams_of[2], (MB, N_DP, SEQ, D), 1.0, 6.0, ((1, 4), (2, 4)), (2, 3, 4, 2.0)),
        "gains": jnp.clip(1.0 + 0.15 * jax.random.normal(streams_of[3], (2, 2, D), jnp.float32), 0.25, 1.75),
        "biases": bell_draw(streams_of[4], (2, 6 * D + FF), 0.3, 2.0, ((0, 2),), jnp.float32),
        "w_qkv": bell_draw(streams_of[5], (2, D, 3 * D), D ** -0.5, 0.21875, ((0, 2),)),
        "w_out": bell_draw(streams_of[6], (2, D, D), (max(D // 192, 1)) ** -0.5, 3.0, ((0, 2),)),
        "w_up": bell_draw(streams_of[7], (2, D, FF), D ** -0.5, 0.21875, ((0, 2),)),
        "w_down": bell_draw(streams_of[8], (2, FF, D), FF ** -0.5, 0.109375, ((0, 2),)),
    }


@jax.custom_vjp
def low(v):
    return lax.optimization_barrier(v.astype(jnp.bfloat16)).astype(jnp.float32)

@jax.custom_vjp
def low_back(v):
    return v

def low_keep(v):
    return (low(v), None)

def low_pass(kept, grad):
    return (grad,)

def back_keep(v):
    return (v, None)

def back_low(kept, grad):
    return (low(grad),)
low.defvjp(low_keep, low_pass)
low_back.defvjp(back_keep, back_low)
highest = lax.Precision.HIGHEST

def layer_norm(inputs_row, gain_row, offset):
    center = inputs_row - lax.optimization_barrier(jnp.mean(inputs_row, axis=-1, keepdims=True))
    spread = lax.optimization_barrier(jnp.mean(center * center, axis=-1, keepdims=True))
    return center * lax.rsqrt(spread + 1e-05) * gain_row + offset

def matmul(left, right):
    return jnp.dot(left, right, precision=highest)

def attend_block(queries, query_pos, key_rows, value_rows, key_pos, signed):
    scores = low_back(jnp.einsum('bhe,she->hbs', queries, key_rows, precision=highest) * 0.125)
    permitted_mask = key_pos[None, None, :] <= query_pos[None, :, None]
    if signed:
        argument = jnp.sqrt(scores * scores + 1.0)
        sign_pattern = scores / argument
    else:
        argument = scores
        sign_pattern = jnp.ones_like(scores)
    masked_scores = jnp.where(permitted_mask, argument, -1e+30)
    log_total = jax.nn.logsumexp(masked_scores, axis=-1, keepdims=True)
    attention_weights = low(jnp.where(permitted_mask, sign_pattern * jnp.exp(masked_scores - log_total), 0.0))
    return jnp.einsum('hbs,she->bhe', attention_weights, value_rows, precision=highest)

def attention(queries, key_rows, value_rows, positions, signed):
    blocks = SEQ // KEY_BLOCK
    query_blocks = queries.reshape(blocks, KEY_BLOCK, HEADS, HDIM)
    pos_blocks = positions.reshape(blocks, KEY_BLOCK)

    def one_block(block_pair):
        return attend_block(block_pair[0], block_pair[1], key_rows, value_rows, positions, signed)
    outputs = lax.map(jax.checkpoint(one_block), (query_blocks, pos_blocks))
    return outputs.reshape(SEQ, D)

def layer_apply(inputs_row, gain_pair, bias_row, w_qkv, w_out, w_up, w_down, positions, signed):
    normed = low(layer_norm(inputs_row, gain_pair[0], bias_row[0:D]))
    qkv_bias = jnp.concatenate([bias_row[2 * D:3 * D], jnp.zeros((D,), bias_row.dtype), bias_row[3 * D:4 * D]])
    projected = low(low_back(matmul(normed, w_qkv)) + qkv_bias)
    queries = projected[:, 0:D].reshape(SEQ, HEADS, HDIM)
    key_rows = projected[:, D:2 * D].reshape(SEQ, HEADS, HDIM)
    value_rows = projected[:, 2 * D:3 * D].reshape(SEQ, HEADS, HDIM)
    attended = low(low_back(attention(queries, key_rows, value_rows, positions, signed)))
    middle = inputs_row + low_back(matmul(attended, w_out)) + bias_row[4 * D:5 * D]
    normed_two = low(layer_norm(middle, gain_pair[1], bias_row[D:2 * D]))
    hidden = low_back(matmul(normed_two, w_up)) + bias_row[6 * D:]
    active = low(jax.nn.gelu(hidden, approximate=True))
    return middle + low_back(matmul(active, w_down)) + bias_row[5 * D:6 * D]

def reference(inputs, slot_order, cotangent, gains, biases, w_qkv, w_out, w_up, w_down):
    params = (gains.astype(jnp.float32), biases.astype(jnp.float32), w_qkv.astype(jnp.float32), w_out.astype(jnp.float32), w_up.astype(jnp.float32), w_down.astype(jnp.float32))
    seq_count = MB * N_DP
    flat_in = inputs.reshape(seq_count, SEQ, D)
    flat_order = slot_order.reshape(seq_count, SLOTS)
    flat_cot = cotangent.reshape(seq_count, SEQ, D)
    offsets = jnp.arange(SPAN, dtype=jnp.int32)

    def one_sequence(running_total, element):
        seq_in, order_row, seq_cot = element
        positions = (order_row[:, None].astype(jnp.int32) * SPAN + offsets[None, :]).reshape(SEQ).astype(jnp.int32)

        def forward(seq_x, offset_in, weights_all):
            gain_set, bias_set, qkv_set, out_set, up_set, down_set = weights_all
            first = layer_apply(seq_x, gain_set[0], bias_set[0], qkv_set[0], out_set[0], up_set[0], down_set[0], positions, True)
            handed = low_back(low(first + offset_in))
            second = layer_apply(handed, gain_set[1], bias_set[1], qkv_set[1], out_set[1], up_set[1], down_set[1], positions, False)
            return (second, handed)
        seq_x = seq_in.astype(jnp.float32)
        second, pullback, handed = jax.vjp(forward, seq_x, jnp.zeros_like(seq_x), params, has_aux=True)
        grad_x, grad_handed, grad_params = pullback(seq_cot.astype(jnp.float32))
        running_total = jax.tree.map(jnp.add, running_total, grad_params)
        return (running_total, (handed, second, grad_x, grad_handed))
    start = jax.tree.map(jnp.zeros_like, params)
    totals, (handed, second, grad_x, grad_handed) = lax.scan(one_sequence, start, (flat_in, flat_order, flat_cot))
    acts = jnp.stack([handed, second]).reshape(2, MB, N_DP, SEQ, D).astype(jnp.bfloat16)
    grads = jnp.stack([grad_x, grad_handed]).reshape(2, MB, N_DP, SEQ, D).astype(jnp.float32)
    return (acts, grads, totals[0], totals[1], totals[2], totals[3], totals[4], totals[5])
```

```python
import functools
import jax
import jax.numpy as jnp
from jax import lax
from jax.experimental import pallas as pl
from jax.experimental.pallas import tpu as pltpu
from jax.sharding import PartitionSpec as P

D = 768
HEADS = 12
HDIM = 64
PAIR = 2 * HDIM
PAIRS = HEADS // 2
OWN = 4
NT = (((1,), (1,)), ((), ()))
TN = (((0,), (0,)), ((), ()))
NN = (((1,), (0,)), ((), ()))


def dot(left, right, dims):
    return lax.dot_general(left, right, dims, preferred_element_type=jnp.float32)


def slot_meta(own_pos, other_pos, signed):
    ranked = jnp.argsort(own_pos).astype(jnp.int32)
    return jnp.concatenate(
        [own_pos, other_pos, ranked, own_pos[ranked], signed.astype(jnp.int32)[None]]
    )


def sort_rows(meta, own, other, target, span):
    for slot in range(OWN):
        for base, source in ((0, own), (OWN, other)):
            start = pl.multiple_of(meta[base + slot] * span, span)
            target[pl.ds(start, span), :] = source[slot * span : (slot + 1) * span, :]


def reach(rank, slots):
    return ((0, slots // 2 - 2), (1, slots // 2 - 1), (slots // 2, slots - 2), (slots // 2 + 1, slots - 1))[rank]


def lane_is_second(shape):
    return lax.broadcasted_iota(jnp.int32, shape, 1) >= HDIM


def stacked_heads(rows):
    second = lane_is_second(rows.shape)
    zero = jnp.zeros_like(rows)
    return jnp.concatenate([jnp.where(second, zero, rows), jnp.where(second, rows, zero)], axis=0)


def masked_part(values, least, span, position, fill):
    if least * span >= values.shape[0]:
        return values
    tail = values[least * span :]
    key_at = lax.broadcasted_iota(jnp.int32, tail.shape, 0) + least * span
    lane = lax.broadcasted_iota(jnp.int32, tail.shape, 1)
    query_at = position * span + jnp.where(lane >= span, lane - span, lane)
    tail = jnp.where(key_at <= query_at, tail, fill)
    if least == 0:
        return tail
    return jnp.concatenate([values[: least * span], tail], axis=0)


def unstack(pair, span):
    row = lax.broadcasted_iota(jnp.int32, (PAIR, span), 0)
    return jnp.where(row < HDIM, pair[:, :span], pair[:, span:]).T


def forward_kernel(meta, q_ref, k_ref, v_ref, k2_ref, v2_ref, o_ref, lse_ref, keys, values, *, span):
    slots = keys.shape[0] // span
    sort_rows(meta, k_ref, k2_ref, keys, span)
    sort_rows(meta, v_ref, v2_ref, values, span)

    def run(signed):
        for rank in reversed(range(OWN)):
            least, most = reach(rank, slots)
            count = (most + 1) * span
            row_at = pl.multiple_of(meta[2 * OWN + rank] * span, span)
            position = meta[3 * OWN + rank]
            queries = stacked_heads(q_ref[pl.ds(row_at, span), :] * 0.125)
            scores = dot(keys[:count, :], queries, NT)
            if signed:
                square = scores * scores + 1.0
                inverse = lax.rsqrt(square)
                argument = square * inverse
                sign_pattern = scores * inverse
            else:
                argument = scores
            argument = masked_part(argument, least, span, position, -1e30)
            largest = jnp.max(argument, axis=0, keepdims=True)
            weights = jnp.exp(argument - largest)
            total = jnp.sum(weights, axis=0, keepdims=True)
            lse_ref[0, rank : rank + 1, :] = largest + jnp.log(total)
            if signed:
                weights = weights * sign_pattern
            gathered = dot(values[:count, :], weights.astype(jnp.bfloat16), TN)
            gathered = gathered * (1.0 / total)
            o_ref[pl.ds(row_at, span), :] = unstack(gathered, span).astype(jnp.bfloat16)

    @pl.when(meta[4 * OWN] == 1)
    def _():
        run(True)

    @pl.when(meta[4 * OWN] == 0)
    def _():
        run(False)


def sorted_attend(meta, qkv, kv_other):
    rows = qkv.shape[0]
    span = rows // OWN
    def spec(first):
        return pl.BlockSpec((rows, PAIR), lambda h, _: (0, first + h))
    return pl.pallas_call(
        functools.partial(forward_kernel, span=span),
        grid_spec=pltpu.PrefetchScalarGridSpec(
            num_scalar_prefetch=1,
            grid=(PAIRS,),
            in_specs=[spec(0), spec(PAIRS), spec(2 * PAIRS), spec(0), spec(PAIRS)],
            out_specs=[spec(0), pl.BlockSpec((1, OWN, 2 * span), lambda h, _: (h, 0, 0))],
            scratch_shapes=[pltpu.VMEM((2 * rows, PAIR), jnp.bfloat16)] * 2,
        ),
        out_shape=[
            jax.ShapeDtypeStruct((rows, D), jnp.bfloat16),
            jax.ShapeDtypeStruct((PAIRS, OWN, 2 * span), jnp.float32),
        ],
        compiler_params=pltpu.CompilerParams(vmem_limit_bytes=40 * 1024 * 1024),
        name="attend",
    )(meta, qkv, qkv, qkv, kv_other, kv_other)


def backward_kernel(
    meta, q_ref, k_ref, v_ref, k2_ref, v2_ref, o_ref, do_ref, lse_ref,
    dq_ref, own_ref, other_ref, keys, values, grad_k, grad_v, *, span,
):
    slots = keys.shape[0] // span
    sort_rows(meta, k_ref, k2_ref, keys, span)
    sort_rows(meta, v_ref, v2_ref, values, span)

    def run(signed):
        for rank in reversed(range(OWN)):
            least, most = reach(rank, slots)
            count = (most + 1) * span
            row_at = pl.multiple_of(meta[2 * OWN + rank] * span, span)
            position = meta[3 * OWN + rank]
            queries = stacked_heads(q_ref[pl.ds(row_at, span), :] * 0.125)
            grad_rows = do_ref[pl.ds(row_at, span), :]
            grads = stacked_heads(grad_rows)
            product = grad_rows.astype(jnp.float32) * o_ref[pl.ds(row_at, span), :].astype(jnp.float32)
            product = stacked_heads(product)
            delta = jnp.sum(product.T, axis=0, keepdims=True)
            lse = lse_ref[0, rank : rank + 1, :]
            scores = dot(keys[:count, :], queries, NT)
            along = dot(values[:count, :], grads, NT)
            if signed:
                square = scores * scores + 1.0
                inverse = lax.rsqrt(square)
                argument = masked_part(square * inverse, least, span, position, -1e30)
                prob = jnp.exp(argument - lse)
                sign_pattern = scores * inverse
                weights = prob * sign_pattern
                dscore = prob * ((sign_pattern * along - delta) * sign_pattern + along * (inverse * inverse * inverse))
            else:
                argument = masked_part(scores, least, span, position, -1e30)
                weights = jnp.exp(argument - lse)
                dscore = weights * (along - delta)
            weights = weights.astype(jnp.bfloat16)
            dscore = dscore.astype(jnp.bfloat16)
            added_v = dot(weights, grads, NN)
            added_k = dot(dscore, queries, NN)
            if rank == OWN - 1:
                grad_v[...] = added_v
                grad_k[...] = added_k
            else:
                grad_v[:count, :] += added_v
                grad_k[:count, :] += added_k
            gathered = dot(keys[:count, :], dscore, TN)
            dq_ref[pl.ds(row_at, span), :] = (unstack(gathered, span) * 0.125).astype(jnp.bfloat16)

    @pl.when(meta[4 * OWN] == 1)
    def _():
        run(True)

    @pl.when(meta[4 * OWN] == 0)
    def _():
        run(False)

    for slot in range(OWN):
        there = slice(slot * span, (slot + 1) * span)
        own_at = pl.multiple_of(meta[slot] * span, span)
        other_at = pl.multiple_of(meta[OWN + slot] * span, span)
        for part, total in enumerate((grad_k, grad_v)):
            own_ref[part, there, :] = total[pl.ds(own_at, span), :]
            other_ref[part, there, :] = total[pl.ds(other_at, span), :].astype(jnp.bfloat16)


def sorted_attend_back(meta, qkv, kv_other, attended, grad_att, lse):
    rows = qkv.shape[0]
    span = rows // OWN
    def spec(first):
        return pl.BlockSpec((rows, PAIR), lambda h, _: (0, first + h))
    two = pl.BlockSpec((2, rows, PAIR), lambda h, _: (0, 0, h))
    return pl.pallas_call(
        functools.partial(backward_kernel, span=span),
        grid_spec=pltpu.PrefetchScalarGridSpec(
            num_scalar_prefetch=1,
            grid=(PAIRS,),
            in_specs=[
                spec(0), spec(PAIRS), spec(2 * PAIRS), spec(0), spec(PAIRS), spec(0), spec(0),
                pl.BlockSpec((1, OWN, 2 * span), lambda h, _: (h, 0, 0)),
            ],
            out_specs=[spec(0), two, two],
            scratch_shapes=[pltpu.VMEM((2 * rows, PAIR), jnp.bfloat16)] * 2
            + [pltpu.VMEM((2 * rows, PAIR), jnp.float32)] * 2,
        ),
        out_shape=[
            jax.ShapeDtypeStruct((rows, D), jnp.bfloat16),
            jax.ShapeDtypeStruct((2, rows, D), jnp.float32),
            jax.ShapeDtypeStruct((2, rows, D), jnp.bfloat16),
        ],
        compiler_params=pltpu.CompilerParams(vmem_limit_bytes=48 * 1024 * 1024),
        name="attend_back",
    )(meta, qkv, qkv, qkv, kv_other, kv_other, attended, grad_att, lse)


def shifted(value, axis, steps):
    count = lax.axis_size(axis)
    initial, last = (max(0, -steps), min(count, count - steps))
    return lax.ppermute(value, axis, [(source, source + steps) for source in range(initial, last)])


def layer_norm(inputs_row, gain_row, offset):
    center = inputs_row - jnp.mean(inputs_row, axis=-1, keepdims=True)
    spread = jnp.mean(center * center, axis=-1, keepdims=True)
    return center * lax.rsqrt(spread + 1e-05) * gain_row + offset


def gelu_tanh(hidden):
    return jax.nn.gelu(hidden, approximate=True)


def score_terms(queries, key_rows, query_pos, key_pos, signed):
    key_count = key_rows.shape[0]
    scores = (
        jnp.einsum(
            "rhe,khe->hrk",
            queries,
            key_rows.reshape(key_count, HEADS, HDIM),
            preferred_element_type=jnp.float32,
        )
        * 0.125
    )
    curved = jnp.sqrt(scores * scores + 1.0)
    argument = jnp.where(signed, curved, scores)
    sign_pattern = jnp.where(signed, scores / curved, 1.0)
    slope = jnp.where(signed, sign_pattern, 1.0)
    bend = jnp.where(signed, 1.0 / (curved * curved * curved), 0.0)
    permitted_mask = key_pos[None, None, :] <= query_pos[None, :, None]
    return (argument, sign_pattern, slope, bend, permitted_mask)


def score_grads(
    queries, key_rows, value_rows, query_pos, key_pos, log_total, delta, grad_att, signed
):
    argument, sign_pattern, slope, bend, permitted_mask = score_terms(
        queries, key_rows, query_pos, key_pos, signed
    )
    prob = jnp.where(permitted_mask, jnp.exp(argument - log_total[..., None]), 0.0)
    along = jnp.einsum("rhe,khe->hrk", grad_att, value_rows, preferred_element_type=jnp.float32)
    dscore = (prob * ((sign_pattern * along - delta[..., None]) * slope + along * bend)).astype(
        jnp.bfloat16
    )
    return ((sign_pattern * prob).astype(jnp.bfloat16), dscore)


def key_blocks_of(key_all, value_all, key_pos, key_block):
    blocks = key_all.shape[0] // key_block
    return (
        key_all.reshape(blocks, key_block, D),
        value_all.reshape(blocks, key_block, HEADS, HDIM),
        key_pos.reshape(blocks, key_block),
    )


def attend(queries, query_pos, key_all, value_all, key_pos, signed, key_block):
    row_count = queries.shape[0]
    key_split, value_split, pos_split = key_blocks_of(key_all, value_all, key_pos, key_block)

    def running_total(state_in, element):
        largest, row_total_sum, gathered = state_in
        key_rows, value_rows, block_pos = element
        argument, sign_pattern, _, _, permitted_mask = score_terms(
            queries, key_rows, query_pos, block_pos, signed
        )
        masked_scores = jnp.where(permitted_mask, argument, -1e30)
        exponent_values = jnp.maximum(largest, jnp.max(masked_scores, axis=-1))
        multiplier = jnp.exp(largest - exponent_values)
        added_terms = jnp.where(
            permitted_mask, jnp.exp(masked_scores - exponent_values[..., None]), 0.0
        )
        row_total_sum = row_total_sum * multiplier + jnp.sum(added_terms, axis=-1)
        attention_weights = (sign_pattern * added_terms).astype(jnp.bfloat16)
        added = jnp.einsum(
            "hrk,khe->rhe", attention_weights, value_rows, preferred_element_type=jnp.float32
        )
        gathered = gathered * multiplier.T[:, :, None] + added
        return ((exponent_values, row_total_sum, gathered), None)

    start_max = jnp.full((HEADS, row_count), -1e30, jnp.float32)
    start_sum = jnp.zeros((HEADS, row_count), jnp.float32)
    start_out = jnp.zeros((row_count, HEADS, HDIM), jnp.float32)
    (largest, row_total_sum, gathered), _ = lax.scan(
        running_total, (start_max, start_sum, start_out), (key_split, value_split, pos_split)
    )
    log_total = largest + jnp.log(row_total_sum)
    attended = gathered / row_total_sum.T[:, :, None]
    return (attended, log_total)


def backward_summed(
    queries, query_pos, key_all, value_all, key_pos, log_total, delta, grad_att, signed, key_block
):
    key_split, value_split, pos_split = key_blocks_of(key_all, value_all, key_pos, key_block)

    def step_back(grad_q, element):
        key_rows, value_rows, block_pos = element
        attention_weights, dscore = score_grads(
            queries, key_rows, value_rows, query_pos, block_pos, log_total, delta, grad_att, signed
        )
        grad_q = (
            grad_q
            + jnp.einsum(
                "hrk,khe->rhe",
                dscore,
                key_rows.reshape(-1, HEADS, HDIM),
                preferred_element_type=jnp.float32,
            )
            * 0.125
        )
        grad_k = (
            jnp.einsum("hrk,rhe->khe", dscore, queries, preferred_element_type=jnp.float32) * 0.125
        )
        grad_v = jnp.einsum(
            "hrk,rhe->khe", attention_weights, grad_att, preferred_element_type=jnp.float32
        )
        return (grad_q, (grad_k.reshape(key_block, D), grad_v.reshape(key_block, D)))

    start_q = jnp.zeros(queries.shape, jnp.float32)
    grad_q, (grad_k, grad_v) = lax.scan(step_back, start_q, (key_split, value_split, pos_split))
    grad_k, grad_v = (
        lax.psum_scatter(
            grad_k.reshape(-1, D).astype(jnp.bfloat16), "ctx", scatter_dimension=0, tiled=True
        ).astype(jnp.float32),
        lax.psum_scatter(
            grad_v.reshape(-1, D).astype(jnp.bfloat16), "ctx", scatter_dimension=0, tiled=True
        ).astype(jnp.float32),
    )
    return (grad_q.reshape(-1, D), grad_k, grad_v)


def layer_front(inputs_row, gain_pair, bias_row, qkv_w):
    normed = layer_norm(inputs_row, gain_pair[0], bias_row[0:D]).astype(jnp.bfloat16)
    qkv_bias = jnp.concatenate(
        [bias_row[2 * D : 3 * D], jnp.zeros((D,), jnp.float32), bias_row[3 * D : 4 * D]]
    )
    projected = (jnp.dot(normed, qkv_w, preferred_element_type=jnp.float32) + qkv_bias).astype(
        jnp.bfloat16
    )
    return (normed, projected)


def layer_rest(inputs_row, attended_b, gain_pair, bias_row, out_w, up_w, down_w):
    middle = (
        inputs_row
        + jnp.dot(attended_b, out_w, preferred_element_type=jnp.float32)
        + bias_row[4 * D : 5 * D]
    )
    normed_two = layer_norm(middle, gain_pair[1], bias_row[D : 2 * D]).astype(jnp.bfloat16)
    hidden = jnp.dot(normed_two, up_w, preferred_element_type=jnp.float32) + bias_row[6 * D :]
    active = gelu_tanh(hidden).astype(jnp.bfloat16)
    result = (
        middle
        + jnp.dot(active, down_w, preferred_element_type=jnp.float32)
        + bias_row[5 * D : 6 * D]
    )
    return (middle, normed_two, hidden, active, result)


def general_body(inputs, slot_order, cotangent, gains, biases, w_qkv, w_out, w_up, w_down):
    micro_count = inputs.shape[0]
    row_count = inputs.shape[2]
    section_at = lax.axis_index("section")
    ctx_at = lax.axis_index("ctx")
    signed = section_at == 0
    gain_pair = gains[0]
    bias_row = biases[0]
    qkv_w = w_qkv[0]
    out_w = w_out[0]
    up_w = w_up[0]
    down_w = w_down[0]
    span_len = row_count // 2
    seq_pos = (
        slot_order[:, 0, :, None] * span_len + jnp.arange(span_len, dtype=jnp.int32)
    ).reshape(micro_count, -1)
    key_block = min(seq_pos.shape[1], 512)
    first_inputs = inputs[:, 0]
    cot_rows = cotangent[:, 0]

    def sequence_pos(index):
        whole_pos = lax.dynamic_index_in_dim(seq_pos, index, 0, keepdims=False)
        own_pos = lax.dynamic_slice_in_dim(whole_pos, ctx_at * row_count, row_count, 0)
        return (whole_pos, own_pos)

    def layer_forward(entry, index):
        whole_pos, own_pos = sequence_pos(index)
        inputs_row = entry.astype(jnp.float32)
        normed, projected = layer_front(inputs_row, gain_pair, bias_row, qkv_w)
        key_all, value_all = (
            lax.all_gather(projected[:, D : 2 * D], "ctx", axis=0, tiled=True),
            lax.all_gather(projected[:, 2 * D :], "ctx", axis=0, tiled=True),
        )
        queries = projected[:, :D].reshape(row_count, HEADS, HDIM)
        attended, _ = attend(queries, own_pos, key_all, value_all, whole_pos, signed, key_block)
        attended_b = attended.reshape(row_count, D).astype(jnp.bfloat16)
        result = layer_rest(inputs_row, attended_b, gain_pair, bias_row, out_w, up_w, down_w)[4]
        return result.astype(jnp.bfloat16)

    def layer_reverse_pass(entry, result_gradient, index):
        whole_pos, own_pos = sequence_pos(index)
        inputs_row = entry.astype(jnp.float32)
        normed, projected = layer_front(inputs_row, gain_pair, bias_row, qkv_w)
        queries = projected[:, :D].reshape(row_count, HEADS, HDIM)
        key_all, value_all = (
            lax.all_gather(projected[:, D : 2 * D], "ctx", axis=0, tiled=True),
            lax.all_gather(projected[:, 2 * D :], "ctx", axis=0, tiled=True),
        )
        attended, log_total = attend(
            queries, own_pos, key_all, value_all, whole_pos, signed, key_block
        )
        attended_b = attended.reshape(row_count, D).astype(jnp.bfloat16)
        middle, normed_two, hidden, active, _ = layer_rest(
            inputs_row, attended_b, gain_pair, bias_row, out_w, up_w, down_w
        )
        grad_down_b = result_gradient.astype(jnp.bfloat16)
        grad_wdown = jnp.dot(active.T, grad_down_b, preferred_element_type=jnp.float32)
        grad_active = jnp.dot(grad_down_b, down_w.T, preferred_element_type=jnp.float32)
        _, gelu_back = jax.vjp(gelu_tanh, hidden)
        grad_hidden = gelu_back(grad_active)[0]
        grad_hidden_b = grad_hidden.astype(jnp.bfloat16)
        grad_wup = jnp.dot(normed_two.T, grad_hidden_b, preferred_element_type=jnp.float32)
        grad_normed_two = jnp.dot(grad_hidden_b, up_w.T, preferred_element_type=jnp.float32)
        _, norm_back_two = jax.vjp(layer_norm, middle, gain_pair[1], bias_row[D : 2 * D])
        grad_middle_part, grad_gain_two, grad_offset_two = norm_back_two(grad_normed_two)
        grad_middle = result_gradient + grad_middle_part
        grad_proj_b = grad_middle.astype(jnp.bfloat16)
        grad_wout = jnp.dot(attended_b.T, grad_proj_b, preferred_element_type=jnp.float32)
        grad_att_flat = jnp.dot(grad_proj_b, out_w.T, preferred_element_type=jnp.float32).astype(
            jnp.bfloat16
        )
        grad_att = grad_att_flat.reshape(row_count, HEADS, HDIM)
        delta = jnp.einsum("rhe,rhe->hr", grad_att.astype(jnp.float32), attended)
        grad_q, grad_k, grad_v = backward_summed(
            queries,
            own_pos,
            key_all,
            value_all,
            whole_pos,
            log_total,
            delta,
            grad_att,
            signed,
            key_block,
        )
        grad_qkv_b = jnp.concatenate([grad_q, grad_k, grad_v], axis=1).astype(jnp.bfloat16)
        grad_wqkv = jnp.dot(normed.T, grad_qkv_b, preferred_element_type=jnp.float32)
        grad_normed = jnp.dot(grad_qkv_b, qkv_w.T, preferred_element_type=jnp.float32)
        _, norm_back_one = jax.vjp(layer_norm, inputs_row, gain_pair[0], bias_row[0:D])
        grad_in_part, grad_gain_one, grad_offset_one = norm_back_one(grad_normed)
        input_gradient = grad_middle + grad_in_part
        grad_gain_rows = jnp.stack([grad_gain_one, grad_gain_two])
        grad_bias_row = jnp.concatenate(
            [
                grad_offset_one,
                grad_offset_two,
                jnp.sum(grad_q, axis=0),
                jnp.sum(grad_v, axis=0),
                jnp.sum(grad_middle, axis=0),
                jnp.sum(result_gradient, axis=0),
                jnp.sum(grad_hidden, axis=0),
            ]
        )
        return (
            input_gradient,
            (grad_gain_rows, grad_bias_row, grad_wqkv, grad_wout, grad_wup, grad_wdown),
        )

    def tick(tick_at, state_in):
        arrived, returned, stored, acts_rows, grad_rows, partial_sums = state_in
        ahead = tick_at - section_at
        ahead_ok = (ahead >= 0) & (ahead < micro_count)
        ahead_at = jnp.clip(ahead, 0, micro_count - 1)
        fresh = jnp.where(
            signed, lax.dynamic_index_in_dim(first_inputs, ahead_at, 0, keepdims=False), arrived
        )
        previous = lax.dynamic_index_in_dim(stored, ahead_at, 0, keepdims=False)
        entry = jnp.where(ahead_ok, fresh, previous)
        stored = lax.dynamic_update_index_in_dim(stored, entry, ahead_at, 0)
        sent = layer_forward(entry, ahead_at)
        old_acts = lax.dynamic_index_in_dim(acts_rows, ahead_at, 0, keepdims=False)
        acts_rows = lax.dynamic_update_index_in_dim(
            acts_rows, jnp.where(ahead_ok, sent, old_acts), ahead_at, 0
        )
        behind = tick_at - 2 + section_at
        trailing_valid = (behind >= 0) & (behind < micro_count)
        trailing_position = jnp.clip(behind, 0, micro_count - 1)
        entry_gradient = lax.dynamic_index_in_dim(stored, trailing_position, 0, keepdims=False)
        given_cot = lax.dynamic_index_in_dim(cot_rows, trailing_position, 0, keepdims=False).astype(
            jnp.float32
        )
        result_gradient = jnp.where(signed, returned.astype(jnp.float32), given_cot)
        input_gradient, added_terms = layer_reverse_pass(
            entry_gradient, result_gradient, trailing_position
        )
        partial_sums = jax.tree.map(
            lambda running_total, added_term: running_total
            + jnp.where(trailing_valid, added_term, 0.0),
            partial_sums,
            added_terms,
        )
        handed = input_gradient.astype(jnp.bfloat16)
        kept_grad = jnp.where(signed, input_gradient, handed.astype(jnp.float32))
        old_grads = lax.dynamic_index_in_dim(grad_rows, trailing_position, 0, keepdims=False)
        grad_rows = lax.dynamic_update_index_in_dim(
            grad_rows, jnp.where(trailing_valid, kept_grad, old_grads), trailing_position, 0
        )
        arrived = shifted(sent, "section", 1)
        returned = shifted(handed, "section", -1)
        return (arrived, returned, stored, acts_rows, grad_rows, partial_sums)

    zero_rows = jnp.zeros((row_count, D), jnp.bfloat16)
    start_sums = (
        jnp.zeros((2, D), jnp.float32),
        jnp.zeros((bias_row.shape[0],), jnp.float32),
        jnp.zeros(qkv_w.shape, jnp.float32),
        jnp.zeros(out_w.shape, jnp.float32),
        jnp.zeros(up_w.shape, jnp.float32),
        jnp.zeros(down_w.shape, jnp.float32),
    )
    start_state = (
        zero_rows,
        zero_rows,
        jnp.zeros((micro_count, row_count, D), jnp.bfloat16),
        jnp.zeros((micro_count, row_count, D), jnp.bfloat16),
        jnp.zeros((micro_count, row_count, D), jnp.float32),
        start_sums,
    )
    final_state = lax.fori_loop(0, micro_count + 2, tick, start_state)
    acts_rows = final_state[3]
    grad_rows = final_state[4]
    partial_sums = final_state[5]
    totals = (
        lax.psum_scatter(partial_sums[0], ("dp", "ctx"), scatter_dimension=1, tiled=True),
        lax.psum_scatter(partial_sums[1], ("dp", "ctx"), scatter_dimension=0, tiled=True),
        lax.psum_scatter(partial_sums[2], ("dp", "ctx"), scatter_dimension=0, tiled=True),
        lax.psum_scatter(partial_sums[3], ("dp", "ctx"), scatter_dimension=0, tiled=True),
        lax.psum_scatter(partial_sums[4], ("dp", "ctx"), scatter_dimension=0, tiled=True),
        lax.psum_scatter(partial_sums[5], ("dp", "ctx"), scatter_dimension=0, tiled=True),
    )
    return (
        acts_rows[None, :, None],
        grad_rows[None, :, None],
        totals[0][None],
        totals[1][None],
        totals[2][None],
        totals[3][None],
        totals[4][None],
        totals[5][None],
    )


def norm_parts(rows):
    center = rows - jnp.mean(rows, axis=-1, keepdims=True)
    spread = jnp.mean(center * center, axis=-1, keepdims=True)
    inverse = lax.rsqrt(spread + 1e-05)
    return center * inverse, inverse


def norm_back(unit, inverse, gain_row, grad):
    scaled = grad * gain_row
    along = jnp.mean(scaled * unit, axis=-1, keepdims=True)
    grad_rows = inverse * (scaled - jnp.mean(scaled, axis=-1, keepdims=True) - unit * along)
    return grad_rows, jnp.sum(grad * unit, axis=0), jnp.sum(grad, axis=0)


def product(left, right):
    return jnp.dot(left, right, preferred_element_type=jnp.float32)


def product_nt(left, right):
    return dot(left, right, NT)


def product_tn(left, right):
    return dot(left, right, TN)


def swap_halves(value):
    count = lax.axis_size("ctx")
    return lax.ppermute(value, "ctx", [(at, (at + count // 2) % count) for at in range(count)])


def swap_cores(value):
    return lax.ppermute(value, "ctx", [(at, at ^ 1) for at in range(lax.axis_size("ctx"))])


def scattered_sum(partial):
    z_count = lax.axis_size("dp")
    z_at = lax.axis_index("dp")
    ctx_at = lax.axis_index("ctx")
    y_at, core_at = ctx_at // 2, ctx_at % 2
    width = partial.shape[1]
    block = partial.shape[0] // (4 * z_count)
    parts = partial.reshape(z_count, 2, 2, block, width)

    def halves(values, at, axis, exchange):
        sent = lax.dynamic_index_in_dim(values, 1 - at, axis, keepdims=False)
        kept = lax.dynamic_index_in_dim(values, at, axis, keepdims=False)
        arrived = exchange(sent)
        return kept.astype(jnp.float32) + arrived.astype(jnp.float32)

    parts = halves(parts, core_at, 2, swap_cores).astype(jnp.bfloat16)
    parts = halves(parts, y_at, 1, swap_halves).astype(jnp.bfloat16)
    total = lax.dynamic_index_in_dim(parts, z_at, 0, keepdims=False).astype(jnp.float32)
    for step in range(1, z_count):
        for way in (step, -step):
            target = jnp.clip(z_at + way, 0, z_count - 1)
            sent = lax.dynamic_index_in_dim(parts, target, 0, keepdims=False)
            moves = [(at, at + way) for at in range(z_count) if 0 <= at + way < z_count]
            total = total + lax.ppermute(sent, "dp", moves).astype(jnp.float32)
    return total


def split_rows(vector, blocks):
    return vector.reshape(*vector.shape[:-1], blocks, vector.shape[-1] // blocks)


def fast_body(inputs, slot_order, cotangent, gains, biases, w_qkv, w_out, w_up, w_down):
    rows = inputs.shape[2]
    count = lax.axis_size("ctx")
    half = count // 2
    section_at = lax.axis_index("section")
    ctx_at = lax.axis_index("ctx")
    mine = ctx_at // half
    signed = section_at == 0
    gain_pair, bias_row = gains[0], biases[0]
    qkv_w, out_w, up_w, down_w = w_qkv[0], w_out[0], w_up[0], w_down[0]
    shift_one, shift_two = bias_row[:D], bias_row[D : 2 * D]
    qkv_bias = jnp.concatenate(
        [bias_row[2 * D : 3 * D], jnp.zeros((D,), jnp.float32), bias_row[3 * D : 4 * D]]
    )
    out_bias, down_bias, up_bias = bias_row[4 * D : 5 * D], bias_row[5 * D : 6 * D], bias_row[6 * D :]

    def gathered(value):
        kept = lax.dynamic_index_in_dim(value, mine, 0, keepdims=False)
        sent = lax.dynamic_index_in_dim(value, 1 - mine, 0, keepdims=False)
        return jnp.concatenate([kept, swap_halves(sent)], axis=0)

    def returned(value):
        kept, sent = value[:rows], value[rows:]
        arrived = swap_halves(sent.astype(jnp.bfloat16)).astype(value.dtype)
        first = jnp.where(mine == 0, kept, arrived)
        second = jnp.where(mine == 0, arrived, kept)
        return jnp.stack([first, second])

    order = lax.dynamic_index_in_dim(slot_order[:, 0], mine, 0, keepdims=False)
    pairs = order.reshape(count, 2)

    def slots_of(device):
        partner = (device + half) % count
        return jnp.concatenate([pairs[device], pairs[partner]])

    meta = slot_meta(slots_of(ctx_at), slots_of(ctx_at ^ 1), signed)

    def forward(entry):
        rows_in = entry.astype(jnp.float32)
        unit_one, inverse_one = norm_parts(rows_in)
        normed = (unit_one * gain_pair[0] + shift_one).astype(jnp.bfloat16)
        qkv = (product(normed, qkv_w) + qkv_bias).astype(jnp.bfloat16)
        kv_other = swap_cores(qkv[:, D:])
        attended, lse = sorted_attend(meta, qkv, kv_other)
        middle = rows_in + product(attended, out_w) + out_bias
        unit_two, inverse_two = norm_parts(middle)
        normed_two = (unit_two * gain_pair[1] + shift_two).astype(jnp.bfloat16)
        hidden = product(normed_two, up_w) + up_bias
        active, gelu_back = jax.vjp(gelu_tanh, hidden)
        active = active.astype(jnp.bfloat16)
        slope = gelu_back(jnp.ones_like(hidden))[0].astype(jnp.bfloat16)
        result = (middle + product(active, down_w) + down_bias).astype(jnp.bfloat16)
        return result, (rows_in, normed, qkv, kv_other, attended, lse, middle, normed_two, active, slope)

    def backward(kept, result_gradient, whole):
        rows_in, normed, qkv, kv_other, attended, lse, middle, normed_two, active, slope = kept
        grad_hidden = product_nt(result_gradient, down_w) * slope.astype(jnp.float32)
        grad_hidden_b = grad_hidden.astype(jnp.bfloat16)
        unit_two, inverse_two = norm_parts(middle)
        through_two, gain_two, offset_two = norm_back(
            unit_two, inverse_two, gain_pair[1], product_nt(grad_hidden_b, up_w)
        )
        grad_middle = result_gradient.astype(jnp.float32) + through_two
        grad_middle_b = grad_middle.astype(jnp.bfloat16)
        grad_att = product_nt(grad_middle_b, out_w).astype(jnp.bfloat16)
        grad_q, grad_own, grad_other = sorted_attend_back(meta, qkv, kv_other, attended, grad_att, lse)
        grad_kv = (grad_own + swap_cores(grad_other).astype(jnp.float32)).astype(jnp.bfloat16)
        grad_qkv = jnp.concatenate([grad_q, grad_kv[0], grad_kv[1]], axis=1)
        unit_one, inverse_one = norm_parts(rows_in)
        through_one, gain_one, offset_one = norm_back(
            unit_one, inverse_one, gain_pair[0], product_nt(grad_qkv, qkv_w)
        )
        input_gradient = grad_middle + through_one
        if not whole:
            return input_gradient
        narrow = jnp.bfloat16
        grad_wdown = product_tn(active, result_gradient).astype(narrow)
        grad_wup = product_tn(normed_two, grad_hidden_b).astype(narrow)
        grad_wout = product_tn(attended, grad_middle_b).astype(narrow)
        grad_wqkv = product_tn(normed, grad_qkv).astype(narrow)
        bias_terms = [
            offset_one, offset_two,
            jnp.sum(grad_q.astype(jnp.float32), axis=0),
            jnp.sum(grad_kv[1].astype(jnp.float32), axis=0),
            jnp.sum(grad_middle, axis=0),
            jnp.sum(result_gradient.astype(jnp.float32), axis=0),
            jnp.sum(grad_hidden, axis=0),
        ]
        return input_gradient, (grad_wdown, grad_wup, grad_wout, grad_wqkv), (jnp.stack([gain_one, gain_two]), jnp.concatenate(bias_terms))

    first = gathered(inputs[:, 0])
    given = gathered(cotangent[:, 0])
    sent, _ = forward(first)
    entry = jnp.where(signed, first, shifted(sent, "section", 1))
    result, kept = forward(entry)
    acts_rows = returned(result)
    handed = backward(kept, given, False).astype(jnp.bfloat16)
    result_gradient = jnp.where(signed, shifted(handed, "section", -1), given)
    input_gradient, weights, small = backward(kept, result_gradient, True)
    input_gradient = jnp.where(signed, input_gradient, input_gradient.astype(jnp.bfloat16).astype(jnp.float32))
    grad_rows = returned(input_gradient)
    wdown, wup, wout, wqkv = [scattered_sum(part) for part in weights]
    blocks = count * lax.axis_size("dp")
    gain_terms, bias_terms = small
    packed = jnp.concatenate([split_rows(gain_terms[0], blocks), split_rows(gain_terms[1], blocks), split_rows(bias_terms, blocks)], axis=1)
    coarse = packed.astype(jnp.bfloat16)
    fine = (packed - coarse.astype(jnp.float32)).astype(jnp.bfloat16)
    packed = scattered_sum(jnp.concatenate([coarse, fine], axis=1))
    width = packed.shape[1] // 2
    packed = packed[0, :width] + packed[0, width:]
    piece = D // blocks
    return (
        acts_rows[None, :, None],
        grad_rows[None, :, None],
        jnp.stack([packed[:piece], packed[piece : 2 * piece]])[None],
        packed[2 * piece :][None],
        wqkv[None],
        wout[None],
        wup[None],
        wdown[None],
    )


def body_for(mesh):
    shape = dict(mesh.shape)
    return fast_body if shape["ctx"] == 4 else general_body


def solution(mesh):
    in_specs = (
        P(None, "dp", "ctx", None),
        P(None, "dp", None),
        P(None, "dp", "ctx", None),
        P("section", None, None),
        P("section", None),
        P("section", None, None),
        P("section", None, None),
        P("section", None, None),
        P("section", None, None),
    )
    out_specs = (
        P("section", None, "dp", "ctx", None),
        P("section", None, "dp", "ctx", None),
        P("section", None, ("dp", "ctx")),
        P("section", ("dp", "ctx")),
        P("section", ("dp", "ctx"), None),
        P("section", ("dp", "ctx"), None),
        P("section", ("dp", "ctx"), None),
        P("section", ("dp", "ctx"), None),
    )
    return jax.shard_map(
        body_for(mesh), mesh=mesh, in_specs=in_specs, out_specs=out_specs, check_vma=False
    )
```

```python
import functools
import math
import jax
import jax.numpy as jnp
from jax import lax
from jax.experimental import pallas as pl
from jax.experimental.pallas import tpu as pltpu
from jax.sharding import PartitionSpec as P

D = 768
HEADS = 12
HDIM = 64
PAIR = 2 * HDIM
PAIRS = HEADS // 2
OWN = 4
CHUNK = 128
BACK_CHUNK = 1024
SAFE = 60.0
NT = (((1,), (1,)), ((), ()))
TN = (((0,), (0,)), ((), ()))
NN = (((1,), (0,)), ((), ()))


def dot(left, right, dims):
    return lax.dot_general(left, right, dims, preferred_element_type=jnp.float32)


def slot_meta(own_pos, other_pos, signed):
    rank = jnp.sum((own_pos[None, :] < own_pos[:, None]).astype(jnp.int32), axis=1)
    chosen = rank[None, :] == jnp.arange(OWN, dtype=jnp.int32)[:, None]
    ranked = jnp.sum(jnp.where(chosen, jnp.arange(OWN, dtype=jnp.int32)[None, :], 0), axis=1)
    ranked_pos = jnp.sum(jnp.where(chosen, own_pos[None, :], 0), axis=1)
    return jnp.concatenate([own_pos, other_pos, ranked, ranked_pos, signed.astype(jnp.int32)[None]])


def sort_rows(meta, own, other, target, span, first):
    columns = slice(first, first + D)
    for slot in range(OWN):
        for base, source in ((0, own), (OWN, other)):
            start = pl.multiple_of(meta[base + slot] * span, span)
            target[pl.ds(start, span), :] = source[slot * span : (slot + 1) * span, columns]


def reach(rank, slots):
    return ((0, slots // 2 - 2), (1, slots // 2 - 1), (slots // 2, slots - 2), (slots // 2 + 1, slots - 1))[rank]


def stacked_heads(rows):
    second = lax.broadcasted_iota(jnp.int32, rows.shape, 1) >= HDIM
    zero = jnp.zeros_like(rows)
    return jnp.concatenate([jnp.where(second, zero, rows), jnp.where(second, rows, zero)], axis=0)


def visible(values, start, least, span, position, fill):
    if start + values.shape[0] <= least * span:
        return values
    key_at = lax.broadcasted_iota(jnp.int32, values.shape, 0) + start
    lane = lax.broadcasted_iota(jnp.int32, values.shape, 1)
    query_at = position * span + jnp.where(lane >= span, lane - span, lane)
    return jnp.where(key_at <= query_at, values, fill)


def unstack(pair, span):
    row = lax.broadcasted_iota(jnp.int32, (PAIR, span), 0)
    return jnp.where(row < HDIM, pair[:, :span], pair[:, span:]).T


def chunks_of(count, chunk):
    return [slice(start, min(start + chunk, count)) for start in range(0, count, chunk)]


def eight(values):
    return values.reshape(-1, 8, values.shape[-1])


def pair_columns(at):
    return pl.ds(pl.multiple_of(at * PAIR, PAIR), PAIR)


def largest_norm(rows_ref):
    feature = lax.broadcasted_iota(jnp.int32, (D, PAIR), 0) // HDIM
    head = lax.broadcasted_iota(jnp.int32, (D, PAIR), 1)
    chosen = jnp.where(feature == head, 1.0, 0.0).astype(jnp.bfloat16)
    rows = rows_ref[...]
    return jnp.max(dot(rows * rows, chosen, NN))


def forward_kernel(meta, q_ref, kv_ref, kv2_ref, o_ref, lse_ref, keys, values, *, span):
    slots = keys.shape[0] // span
    sort_rows(meta, kv_ref, kv2_ref, keys, span, 0)
    sort_rows(meta, kv_ref, kv2_ref, values, span, D)
    bound = largest_norm(q_ref) * largest_norm(keys) * (1.1 / HDIM)
    near = bound < SAFE * SAFE

    def run(signed, safe):
        def one_pair(pair, _):
            columns = pair_columns(pair)
            values_t = values[:, columns].T
            for rank in reversed(range(OWN)):
                least, most = reach(rank, slots)
                count = (most + 1) * span
                row_at = pl.multiple_of(meta[2 * OWN + rank] * span, span)
                position = meta[3 * OWN + rank]
                queries = stacked_heads(q_ref[pl.ds(row_at, span), columns] * 0.125)
                largest = None
                if not safe:
                    most_seen = jnp.full((8, 2 * span), -1e30, jnp.float32)
                    for part in chunks_of(count, CHUNK):
                        scores = dot(keys[part, columns], queries, NT)
                        scores = jnp.abs(scores) if signed else scores
                        scores = visible(scores, part.start, least, span, position, -1e30)
                        most_seen = jnp.maximum(most_seen, jnp.max(eight(scores), axis=0))
                    largest = jnp.max(most_seen, axis=0, keepdims=True)
                    if signed:
                        square = largest * largest + 1.0
                        largest = square * lax.rsqrt(square)
                total = jnp.zeros((8, 2 * span), jnp.float32)
                gathered = jnp.zeros((PAIR, 2 * span), jnp.float32)
                for part in chunks_of(count, CHUNK):
                    scores = dot(keys[part, columns], queries, NT)
                    argument = scores
                    if signed:
                        square = scores * scores + 1.0
                        inverse = lax.rsqrt(square)
                        argument = square * inverse
                    if not safe:
                        argument = argument - largest
                    weights = jnp.exp(visible(argument, part.start, least, span, position, -1e30))
                    total += jnp.sum(eight(weights), axis=0)
                    if signed:
                        weights = weights * (scores * inverse)
                    gathered += dot(values_t[:, part], weights.astype(jnp.bfloat16), NN)
                total = jnp.sum(total, axis=0, keepdims=True)
                lse = jnp.log(total)
                lse_ref[pair, rank : rank + 1, :] = lse if safe else lse + largest
                gathered = gathered * (1.0 / total)
                o_ref[pl.ds(row_at, span), columns] = unstack(gathered, span).astype(jnp.bfloat16)
            return 0

        lax.fori_loop(0, PAIRS, one_pair, 0)

    for signed in (True, False):
        for safe in (True, False):
            chosen = (meta[4 * OWN] == int(signed)) & (near == safe)
            pl.when(chosen)(functools.partial(run, signed, safe))


SMEM_SPEC = pl.BlockSpec(memory_space=pltpu.SMEM)
VMEM_SPEC = pl.BlockSpec(memory_space=pltpu.VMEM)


def sorted_attend(meta, queries, kv, kv_other):
    rows = kv.shape[0]
    span = rows // OWN
    return pl.pallas_call(
        functools.partial(forward_kernel, span=span),
        in_specs=[SMEM_SPEC] + [VMEM_SPEC] * 3,
        out_specs=[VMEM_SPEC] * 2,
        scratch_shapes=[pltpu.VMEM((2 * rows, D), jnp.bfloat16)] * 2,
        out_shape=[
            jax.ShapeDtypeStruct((rows, D), jnp.bfloat16),
            jax.ShapeDtypeStruct((PAIRS, OWN, 2 * span), jnp.float32),
        ],
        compiler_params=pltpu.CompilerParams(vmem_limit_bytes=12 * 1024 * 1024),
        cost_estimate=pl.CostEstimate(flops=4_000_000_000, bytes_accessed=0, transcendentals=0),
        name="attend",
    )(meta, queries, kv, kv_other)


def backward_kernel(
    meta, q_ref, kv_ref, kv2_ref, o_ref, do_ref, lse_ref,
    dq_ref, own_ref, other_ref, keys, values, grad_k, grad_v, *, span,
):
    slots = keys.shape[0] // span
    sort_rows(meta, kv_ref, kv2_ref, keys, span, 0)
    sort_rows(meta, kv_ref, kv2_ref, values, span, D)

    def run(signed):
        def one_pair(pair, _):
            columns = pair_columns(pair)
            keys_t = keys[:, columns].T
            for rank in reversed(range(OWN)):
                least, most = reach(rank, slots)
                count = (most + 1) * span
                row_at = pl.multiple_of(meta[2 * OWN + rank] * span, span)
                position = meta[3 * OWN + rank]
                queries = stacked_heads(q_ref[pl.ds(row_at, span), columns] * 0.125)
                grad_rows = do_ref[pl.ds(row_at, span), columns]
                grads = stacked_heads(grad_rows)
                product = grad_rows.astype(jnp.float32) * o_ref[pl.ds(row_at, span), columns].astype(jnp.float32)
                delta = jnp.sum(stacked_heads(product).T, axis=0, keepdims=True)
                lse = lse_ref[pair, rank : rank + 1, :]
                gathered = jnp.zeros((PAIR, 2 * span), jnp.float32)
                for part in chunks_of(count, BACK_CHUNK):
                    scores = dot(keys[part, columns], queries, NT)
                    along = dot(values[part, columns], grads, NT)
                    argument = scores
                    if signed:
                        square = scores * scores + 1.0
                        inverse = lax.rsqrt(square)
                        argument = square * inverse
                    prob = jnp.exp(visible(argument - lse, part.start, least, span, position, -1e30))
                    if signed:
                        sign_pattern = scores * inverse
                        weights = prob * sign_pattern
                        bend = inverse * inverse * inverse
                        dscore = prob * ((sign_pattern * along - delta) * sign_pattern + along * bend)
                    else:
                        weights = prob
                        dscore = prob * (along - delta)
                    weights = weights.astype(jnp.bfloat16)
                    dscore = dscore.astype(jnp.bfloat16)
                    added_v = dot(weights, grads, NN)
                    added_k = dot(dscore, queries, NN)
                    if rank == OWN - 1:
                        grad_v[part, :] = added_v
                        grad_k[part, :] = added_k
                    else:
                        grad_v[part, :] += added_v
                        grad_k[part, :] += added_k
                    gathered += dot(keys_t[:, part], dscore, NN)
                dq_ref[pl.ds(row_at, span), columns] = (unstack(gathered, span) * 0.125).astype(jnp.bfloat16)
            for slot in range(OWN):
                there = slice(slot * span, (slot + 1) * span)
                own_at = pl.multiple_of(meta[slot] * span, span)
                other_at = pl.multiple_of(meta[OWN + slot] * span, span)
                for part, total in enumerate((grad_k, grad_v)):
                    own_ref[part, there, columns] = total[pl.ds(own_at, span), :].astype(jnp.bfloat16)
                    other_ref[part, there, columns] = total[pl.ds(other_at, span), :].astype(jnp.bfloat16)
            return 0

        lax.fori_loop(0, PAIRS, one_pair, 0)

    for signed in (True, False):
        pl.when(meta[4 * OWN] == int(signed))(functools.partial(run, signed))


def sorted_attend_back(meta, queries, kv, kv_other, attended, grad_att, lse):
    rows = kv.shape[0]
    span = rows // OWN
    return pl.pallas_call(
        functools.partial(backward_kernel, span=span),
        in_specs=[SMEM_SPEC] + [VMEM_SPEC] * 6,
        out_specs=[VMEM_SPEC] * 3,
        scratch_shapes=[pltpu.VMEM((2 * rows, D), jnp.bfloat16)] * 2
        + [pltpu.VMEM((2 * rows, PAIR), jnp.float32)] * 2,
        out_shape=[
            jax.ShapeDtypeStruct((rows, D), jnp.bfloat16),
            jax.ShapeDtypeStruct((2, rows, D), jnp.bfloat16),
            jax.ShapeDtypeStruct((2, rows, D), jnp.bfloat16),
        ],
        compiler_params=pltpu.CompilerParams(vmem_limit_bytes=18 * 1024 * 1024),
        cost_estimate=pl.CostEstimate(flops=8_000_000_000, bytes_accessed=0, transcendentals=0),
        name="attend_back",
    )(meta, queries, kv, kv_other, attended, grad_att, lse)


TURN_TANH = 0.7978845608028654
CUBE = 0.044715
CHUNKS = 1


def normalised(rows):
    center = rows - jnp.mean(rows, axis=-1, keepdims=True)
    inverse = lax.rsqrt(jnp.mean(center * center, axis=-1, keepdims=True) + 1e-05)
    return center * inverse, inverse


def norm_back(unit, inverse, gain_row, grad):
    scaled = grad * gain_row
    along = jnp.mean(scaled * unit, axis=-1, keepdims=True)
    return inverse * (scaled - jnp.mean(scaled, axis=-1, keepdims=True) - unit * along)


def row_chunks(rows, chunks=CHUNKS):
    return [slice(at * rows // chunks, (at + 1) * rows // chunks) for at in range(chunks)]


def column_sum(values):
    return jnp.sum(values, axis=0, keepdims=True)


def gelu_parts(hidden):
    square = hidden * hidden
    curve = jnp.tanh(hidden * (TURN_TANH + TURN_TANH * CUBE * square))
    half = 0.5 + 0.5 * curve
    inner = hidden * (TURN_TANH + 3.0 * TURN_TANH * CUBE * square)
    return hidden * half, half + 0.5 * (1.0 - curve * curve) * inner


def gelu_only(hidden):
    square = hidden * hidden
    curve = jnp.tanh(hidden * (TURN_TANH + TURN_TANH * CUBE * square))
    return hidden * (0.5 + 0.5 * curve)


def cost(flops, nbytes):
    return pl.CostEstimate(flops=int(flops) // 8, bytes_accessed=0, transcendentals=0)


def call(kernel, name, megabytes, flops, outs, scratch, *operands, smem=0):
    shapes = [jax.ShapeDtypeStruct(shape, dtype) for shape, dtype in outs]
    nbytes = sum(value.size * value.dtype.itemsize for value in (*operands, *shapes))
    return pl.pallas_call(
        kernel,
        in_specs=[SMEM_SPEC] * smem + [VMEM_SPEC] * (len(operands) - smem),
        out_specs=[VMEM_SPEC] * len(shapes),
        out_shape=shapes,
        scratch_shapes=scratch,
        compiler_params=pltpu.CompilerParams(vmem_limit_bytes=megabytes * 1024 * 1024),
        cost_estimate=cost(flops, nbytes),
        name=name,
    )(*operands)


def bias_part(biases, at):
    return biases[0:1, at * D : (at + 1) * D]


def tile(at):
    return slice(at * D, (at + 1) * D)


def whole(*shape):
    return pl.BlockSpec(shape, lambda *_: (0,) * len(shape))


def front_kernel(x_ref, gains, biases, w_ref, normed_ref, q_ref, kv_ref):
    for part in row_chunks(x_ref.shape[0]):
        unit, _ = normalised(x_ref[part, :].astype(jnp.float32))
        normed = (unit * gains[0:1, :] + bias_part(biases, 0)).astype(jnp.bfloat16)
        normed_ref[part, :] = normed
        kv_ref[part, :D] = dot(normed, w_ref[0, :, tile(1)], NN).astype(jnp.bfloat16)
        kv_ref[part, D:] = (dot(normed, w_ref[0, :, tile(2)], NN) + bias_part(biases, 3)).astype(jnp.bfloat16)
        q_ref[part, :] = (dot(normed, w_ref[0, :, tile(0)], NN) + bias_part(biases, 2)).astype(jnp.bfloat16)


def front(entry, gains, biases, w_qkv):
    rows = entry.shape[0]
    narrow = jnp.bfloat16
    outs = [((rows, D), narrow), ((rows, D), narrow), ((rows, 2 * D), narrow)]
    return call(front_kernel, "front", 8, 6 * rows * D * D, outs, [], entry, gains, biases, w_qkv)


def middle_rows(x_ref, o_ref, w_out, biases, part):
    return x_ref[part, :].astype(jnp.float32) + dot(o_ref[part, :], w_out[0], NN) + bias_part(biases, 4)


def rest_kernel(x_ref, o_ref, gains, biases, w_out, w_up, w_down, result_ref):
    for part in row_chunks(x_ref.shape[0]):
        middle = middle_rows(x_ref, o_ref, w_out, biases, part)
        unit, _ = normalised(middle)
        normed = (unit * gains[1:2, :] + bias_part(biases, 1)).astype(jnp.bfloat16)
        total = middle + bias_part(biases, 5)
        for at in range(w_up.shape[2] // D):
            hidden = dot(normed, w_up[0, :, tile(at)], NN) + bias_part(biases, 6 + at)
            total += dot(gelu_only(hidden).astype(jnp.bfloat16), w_down[0, tile(at), :], NN)
        result_ref[part, :] = total.astype(jnp.bfloat16)


def rest(entry, attended, gains, biases, w_out, w_up, w_down):
    rows = entry.shape[0]
    flops = 2 * rows * (D * D + 2 * w_up.size)
    return call(
        rest_kernel, "rest", 8, flops, [((rows, D), jnp.bfloat16)], [],
        entry, attended, gains, biases, w_out, w_up, w_down,
    )[0]


def turn_kernel(
    x_ref, o_ref, d_ref, gains, biases, w_out, w_up, out_t, up_t, down_t,
    middle_ref, normed_ref, active_ref, slope_ref, grad_ref, grad_att_ref,
):
    for part in row_chunks(x_ref.shape[0]):
        middle = middle_rows(x_ref, o_ref, w_out, biases, part)
        middle_ref[part, :] = middle
        unit, inverse = normalised(middle)
        normed = (unit * gains[1:2, :] + bias_part(biases, 1)).astype(jnp.bfloat16)
        normed_ref[part, :] = normed
        total = jnp.zeros_like(middle)
        for at in range(w_up.shape[2] // D):
            hidden = dot(normed, w_up[0, :, tile(at)], NN) + bias_part(biases, 6 + at)
            active, slope = gelu_parts(hidden)
            active_ref[part, tile(at)] = active.astype(jnp.bfloat16)
            slope_ref[part, tile(at)] = slope.astype(jnp.bfloat16)
            grad_hidden = dot(d_ref[part, :], down_t[:, tile(at)], NN) * slope
            total += dot(grad_hidden.astype(jnp.bfloat16), up_t[tile(at), :], NN)
        unit, inverse = normalised(middle_ref[part, :])
        grad = d_ref[part, :].astype(jnp.float32) + norm_back(unit, inverse, gains[1:2, :], total)
        grad_ref[part, :] = grad
        grad_att_ref[part, :] = dot(grad.astype(jnp.bfloat16), out_t[...], NN).astype(jnp.bfloat16)


def turn(entry, attended, result_gradient, gains, biases, w_out, w_up, out_t, up_t, down_t):
    rows = entry.shape[0]
    wide, narrow = jnp.float32, jnp.bfloat16
    inner = w_up.shape[2]
    outs = [
        ((rows, D), wide), ((rows, D), narrow), ((rows, inner), narrow),
        ((rows, inner), narrow), ((rows, D), wide), ((rows, D), narrow),
    ]
    return call(
        turn_kernel, "turn", 12, 2 * rows * (2 * D * D + 3 * w_up.size), outs, [],
        entry, attended, result_gradient, gains, biases, w_out, w_up, out_t, up_t, down_t,
    )


def down_back_kernel(
    d_ref, slope_ref, middle_ref, gains, out_t, up_t, down_t,
    hidden_ref, grad_ref, grad_b_ref, grad_att_ref, sums_ref, up_ref,
):
    sums = [jnp.zeros((1, D), jnp.float32)] * 4
    steps = up_t.shape[0] // D
    up_sums = [jnp.zeros((1, D), jnp.float32)] * steps
    for part in row_chunks(d_ref.shape[0]):
        given = d_ref[part, :]
        through = jnp.zeros(given.shape, jnp.float32)
        for at in range(steps):
            grad_hidden = dot(given, down_t[:, tile(at)], NN) * slope_ref[part, tile(at)].astype(jnp.float32)
            up_sums[at] = up_sums[at] + column_sum(grad_hidden)
            grad_hidden = grad_hidden.astype(jnp.bfloat16)
            hidden_ref[part, tile(at)] = grad_hidden
            through += dot(grad_hidden, up_t[tile(at), :], NN)
        unit, inverse = normalised(middle_ref[part, :])
        given = given.astype(jnp.float32)
        grad = given + norm_back(unit, inverse, gains[1:2, :], through)
        grad_ref[part, :] = grad
        grad_b = grad.astype(jnp.bfloat16)
        grad_b_ref[part, :] = grad_b
        grad_att_ref[part, :] = dot(grad_b, out_t[...], NN).astype(jnp.bfloat16)
        for at, term in enumerate((through * unit, through, grad, given)):
            sums[at] = sums[at] + column_sum(term)
    sums_ref[...] = jnp.concatenate(sums, axis=0)
    up_ref[...] = jnp.concatenate(up_sums, axis=0)


def down_back(result_gradient, slope, middle, gains, out_t, up_t, down_t):
    rows = result_gradient.shape[0]
    wide, narrow = jnp.float32, jnp.bfloat16
    inner = up_t.shape[0]
    outs = [
        ((rows, inner), narrow), ((rows, D), wide), ((rows, D), narrow),
        ((rows, D), narrow), ((4, D), wide), ((inner // D, D), wide),
    ]
    return call(
        down_back_kernel, "down_back", 10, 2 * rows * (D * D + 2 * up_t.size), outs, [],
        result_gradient, slope, middle, gains, out_t, up_t, down_t,
    )


def qkv_tiles(part, q_ref, own_ref, there_ref):
    tiles = [q_ref[part, :]]
    for at in range(2):
        total = own_ref[at, part, :].astype(jnp.float32) + there_ref[at, part, :].astype(jnp.float32)
        tiles.append(total.astype(jnp.bfloat16))
    return tiles


def front_back_kernel(q_ref, own_ref, there_ref, x_ref, grad_ref, gains, qkv_t, out_ref, sums_ref):
    sums = [jnp.zeros((1, D), jnp.float32)] * 4
    for part in row_chunks(x_ref.shape[0]):
        tiles = qkv_tiles(part, q_ref, own_ref, there_ref)
        through = sum(dot(value, qkv_t[tile(at), :], NN) for at, value in enumerate(tiles))
        unit, inverse = normalised(x_ref[part, :].astype(jnp.float32))
        out = grad_ref[part, :] + norm_back(unit, inverse, gains[0:1, :], through)
        out_ref[part, :] = out.astype(out_ref.dtype)
        terms = (through * unit, through, tiles[0].astype(jnp.float32), tiles[2].astype(jnp.float32))
        for at, term in enumerate(terms):
            sums[at] = sums[at] + column_sum(term)
    sums_ref[...] = jnp.concatenate(sums, axis=0)


def front_back(grad_q, own, there, entry, grad_middle, gains, qkv_t, dtype):
    rows = entry.shape[0]
    outs = [((rows, D), dtype), ((4, D), jnp.float32)]
    return call(
        front_back_kernel, "front_back", 8, 6 * rows * D * D, outs, [],
        grad_q, own, there, entry, grad_middle, gains, qkv_t,
    )


def write_blocks(place, tile, order, kept_ref, sent_ref):
    rows = kept_ref.shape[2]

    def write(core):
        for at, (z_at, y_at, core_at) in enumerate(order):
            target = kept_ref if core_at == core else sent_ref
            target[y_at, z_at] = tile[at * rows : (at + 1) * rows]

    for core in range(2):
        pl.when(place[0] == core)(functools.partial(write, core))


def weight_grad_kernel(place, left_ref, right_ref, kept_ref, sent_ref, *, order):
    tile = dot(left_ref[...], right_ref[...], NN).astype(jnp.bfloat16)
    write_blocks(place, tile, order, kept_ref, sent_ref)


def qkv_weight_grad_kernel(place, left_ref, q_ref, own_ref, there_ref, kept_ref, sent_ref, right, *, order):
    step = pl.program_id(0)

    @pl.when(step == 0)
    def _():
        right[...] = q_ref[...]

    @pl.when(step > 0)
    def _():
        total = own_ref[0].astype(jnp.float32) + there_ref[0].astype(jnp.float32)
        right[...] = total.astype(jnp.bfloat16)

    weight_grad_kernel(place, left_ref, right, kept_ref, sent_ref, order=order)


def all_blocks(z_count):
    return [(z_at, y_at, core) for z_at in range(z_count) for y_at in range(2) for core in range(2)]


def qkv_weight_grad(place, left, grad_q, own, there, z_count):
    rows = left.shape[1]
    block = D // (4 * z_count)
    part = pl.BlockSpec((1, rows, D), lambda i, _: (jnp.maximum(i - 1, 0), 0, 0))
    out_spec = pl.BlockSpec((2, z_count, block, D), lambda i, _: (0, 0, 0, i))
    shape = jax.ShapeDtypeStruct((2, z_count, block, 3 * D), jnp.bfloat16)
    return pl.pallas_call(
        functools.partial(qkv_weight_grad_kernel, order=all_blocks(z_count)),
        grid_spec=pltpu.PrefetchScalarGridSpec(
            num_scalar_prefetch=1,
            grid=(3,),
            in_specs=[whole(D, rows), whole(rows, D), part, part],
            out_specs=[out_spec, out_spec],
            scratch_shapes=[pltpu.VMEM((rows, D), jnp.bfloat16)],
        ),
        out_shape=[shape, shape],
        compiler_params=pltpu.CompilerParams(vmem_limit_bytes=14 * 1024 * 1024),
        cost_estimate=cost(6 * rows * D * D, 20 * rows * D + 6 * D * D),
        name="qkv_weight_grad",
    )(place, left, grad_q, own, there)


def weight_grad(place, left, right, z_count):
    height, rows = left.shape
    width = right.shape[1]
    block = height // (4 * z_count)
    if height > D:
        grid = z_count
        order = [(0, y_at, core) for y_at in range(2) for core in range(2)]
        left_spec = pl.BlockSpec((height // grid, rows), lambda i, _: (i, 0))
        right_spec = whole(rows, width)
        out_spec = pl.BlockSpec((2, 1, block, width), lambda i, _: (0, i, 0, 0))
    else:
        grid = width // D
        order = all_blocks(z_count)
        left_spec = whole(height, rows)
        right_spec = pl.BlockSpec((rows, D), lambda i, _: (0, i))
        out_spec = pl.BlockSpec((2, z_count, block, D), lambda i, _: (0, 0, 0, i))
    shape = jax.ShapeDtypeStruct((2, z_count, block, width), jnp.bfloat16)
    return pl.pallas_call(
        functools.partial(weight_grad_kernel, order=order),
        grid_spec=pltpu.PrefetchScalarGridSpec(
            num_scalar_prefetch=1,
            grid=(grid,),
            in_specs=[left_spec, right_spec],
            out_specs=[out_spec, out_spec],
        ),
        out_shape=[shape, shape],
        compiler_params=pltpu.CompilerParams(vmem_limit_bytes=14 * 1024 * 1024),
        cost_estimate=cost(2 * rows * height * width, 2 * (rows * height + rows * width + height * width)),
        name="weight_grad",
    )(place, left, right)


def shifted(value, axis, steps):
    count = lax.axis_size(axis)
    initial, last = (max(0, -steps), min(count, count - steps))
    return lax.ppermute(value, axis, [(source, source + steps) for source in range(initial, last)])


def layer_norm(inputs_row, gain_row, offset):
    center = inputs_row - jnp.mean(inputs_row, axis=-1, keepdims=True)
    spread = jnp.mean(center * center, axis=-1, keepdims=True)
    return center * lax.rsqrt(spread + 1e-05) * gain_row + offset


def gelu_tanh(hidden):
    return jax.nn.gelu(hidden, approximate=True)


def score_terms(queries, key_rows, query_pos, key_pos, signed):
    key_count = key_rows.shape[0]
    scores = (
        jnp.einsum(
            "rhe,khe->hrk",
            queries,
            key_rows.reshape(key_count, HEADS, HDIM),
            preferred_element_type=jnp.float32,
        )
        * 0.125
    )
    curved = jnp.sqrt(scores * scores + 1.0)
    argument = jnp.where(signed, curved, scores)
    sign_pattern = jnp.where(signed, scores / curved, 1.0)
    slope = jnp.where(signed, sign_pattern, 1.0)
    bend = jnp.where(signed, 1.0 / (curved * curved * curved), 0.0)
    permitted_mask = key_pos[None, None, :] <= query_pos[None, :, None]
    return (argument, sign_pattern, slope, bend, permitted_mask)


def score_grads(
    queries, key_rows, value_rows, query_pos, key_pos, log_total, delta, grad_att, signed
):
    argument, sign_pattern, slope, bend, permitted_mask = score_terms(
        queries, key_rows, query_pos, key_pos, signed
    )
    prob = jnp.where(permitted_mask, jnp.exp(argument - log_total[..., None]), 0.0)
    along = jnp.einsum("rhe,khe->hrk", grad_att, value_rows, preferred_element_type=jnp.float32)
    dscore = (prob * ((sign_pattern * along - delta[..., None]) * slope + along * bend)).astype(
        jnp.bfloat16
    )
    return ((sign_pattern * prob).astype(jnp.bfloat16), dscore)


def key_blocks_of(key_all, value_all, key_pos, key_block):
    blocks = key_all.shape[0] // key_block
    return (
        key_all.reshape(blocks, key_block, D),
        value_all.reshape(blocks, key_block, HEADS, HDIM),
        key_pos.reshape(blocks, key_block),
    )


def attend(queries, query_pos, key_all, value_all, key_pos, signed, key_block):
    row_count = queries.shape[0]
    key_split, value_split, pos_split = key_blocks_of(key_all, value_all, key_pos, key_block)

    def running_total(state_in, element):
        largest, row_total_sum, gathered = state_in
        key_rows, value_rows, block_pos = element
        argument, sign_pattern, _, _, permitted_mask = score_terms(
            queries, key_rows, query_pos, block_pos, signed
        )
        masked_scores = jnp.where(permitted_mask, argument, -1e30)
        exponent_values = jnp.maximum(largest, jnp.max(masked_scores, axis=-1))
        multiplier = jnp.exp(largest - exponent_values)
        added_terms = jnp.where(
            permitted_mask, jnp.exp(masked_scores - exponent_values[..., None]), 0.0
        )
        row_total_sum = row_total_sum * multiplier + jnp.sum(added_terms, axis=-1)
        attention_weights = (sign_pattern * added_terms).astype(jnp.bfloat16)
        added = jnp.einsum(
            "hrk,khe->rhe", attention_weights, value_rows, preferred_element_type=jnp.float32
        )
        gathered = gathered * multiplier.T[:, :, None] + added
        return ((exponent_values, row_total_sum, gathered), None)

    start_max = jnp.full((HEADS, row_count), -1e30, jnp.float32)
    start_sum = jnp.zeros((HEADS, row_count), jnp.float32)
    start_out = jnp.zeros((row_count, HEADS, HDIM), jnp.float32)
    (largest, row_total_sum, gathered), _ = lax.scan(
        running_total, (start_max, start_sum, start_out), (key_split, value_split, pos_split)
    )
    log_total = largest + jnp.log(row_total_sum)
    attended = gathered / row_total_sum.T[:, :, None]
    return (attended, log_total)


def backward_summed(
    queries, query_pos, key_all, value_all, key_pos, log_total, delta, grad_att, signed, key_block
):
    key_split, value_split, pos_split = key_blocks_of(key_all, value_all, key_pos, key_block)

    def step_back(grad_q, element):
        key_rows, value_rows, block_pos = element
        attention_weights, dscore = score_grads(
            queries, key_rows, value_rows, query_pos, block_pos, log_total, delta, grad_att, signed
        )
        grad_q = (
            grad_q
            + jnp.einsum(
                "hrk,khe->rhe",
                dscore,
                key_rows.reshape(-1, HEADS, HDIM),
                preferred_element_type=jnp.float32,
            )
            * 0.125
        )
        grad_k = (
            jnp.einsum("hrk,rhe->khe", dscore, queries, preferred_element_type=jnp.float32) * 0.125
        )
        grad_v = jnp.einsum(
            "hrk,rhe->khe", attention_weights, grad_att, preferred_element_type=jnp.float32
        )
        return (grad_q, (grad_k.reshape(key_block, D), grad_v.reshape(key_block, D)))

    start_q = jnp.zeros(queries.shape, jnp.float32)
    grad_q, (grad_k, grad_v) = lax.scan(step_back, start_q, (key_split, value_split, pos_split))
    grad_k, grad_v = (
        lax.psum_scatter(
            grad_k.reshape(-1, D).astype(jnp.bfloat16), "ctx", scatter_dimension=0, tiled=True
        ).astype(jnp.float32),
        lax.psum_scatter(
            grad_v.reshape(-1, D).astype(jnp.bfloat16), "ctx", scatter_dimension=0, tiled=True
        ).astype(jnp.float32),
    )
    return (grad_q.reshape(-1, D), grad_k, grad_v)


def layer_front(inputs_row, gain_pair, bias_row, qkv_w):
    normed = layer_norm(inputs_row, gain_pair[0], bias_row[0:D]).astype(jnp.bfloat16)
    qkv_bias = jnp.concatenate(
        [bias_row[2 * D : 3 * D], jnp.zeros((D,), jnp.float32), bias_row[3 * D : 4 * D]]
    )
    projected = (jnp.dot(normed, qkv_w, preferred_element_type=jnp.float32) + qkv_bias).astype(
        jnp.bfloat16
    )
    return (normed, projected)


def layer_rest(inputs_row, attended_b, gain_pair, bias_row, out_w, up_w, down_w):
    middle = (
        inputs_row
        + jnp.dot(attended_b, out_w, preferred_element_type=jnp.float32)
        + bias_row[4 * D : 5 * D]
    )
    normed_two = layer_norm(middle, gain_pair[1], bias_row[D : 2 * D]).astype(jnp.bfloat16)
    hidden = jnp.dot(normed_two, up_w, preferred_element_type=jnp.float32) + bias_row[6 * D :]
    active = gelu_tanh(hidden).astype(jnp.bfloat16)
    result = (
        middle
        + jnp.dot(active, down_w, preferred_element_type=jnp.float32)
        + bias_row[5 * D : 6 * D]
    )
    return (middle, normed_two, hidden, active, result)


def general_body(inputs, slot_order, cotangent, gains, biases, w_qkv, w_out, w_up, w_down):
    micro_count = inputs.shape[0]
    row_count = inputs.shape[2]
    section_at = lax.axis_index("section")
    ctx_at = lax.axis_index("ctx")
    signed = section_at == 0
    gain_pair = gains[0]
    bias_row = biases[0]
    qkv_w = w_qkv[0]
    out_w = w_out[0]
    up_w = w_up[0]
    down_w = w_down[0]
    span_len = row_count // 2
    seq_pos = (
        slot_order[:, 0, :, None] * span_len + jnp.arange(span_len, dtype=jnp.int32)
    ).reshape(micro_count, -1)
    key_block = min(seq_pos.shape[1], 512)
    first_inputs = inputs[:, 0]
    cot_rows = cotangent[:, 0]

    def sequence_pos(index):
        whole_pos = lax.dynamic_index_in_dim(seq_pos, index, 0, keepdims=False)
        own_pos = lax.dynamic_slice_in_dim(whole_pos, ctx_at * row_count, row_count, 0)
        return (whole_pos, own_pos)

    def layer_forward(entry, index):
        whole_pos, own_pos = sequence_pos(index)
        inputs_row = entry.astype(jnp.float32)
        normed, projected = layer_front(inputs_row, gain_pair, bias_row, qkv_w)
        key_all, value_all = (
            lax.all_gather(projected[:, D : 2 * D], "ctx", axis=0, tiled=True),
            lax.all_gather(projected[:, 2 * D :], "ctx", axis=0, tiled=True),
        )
        queries = projected[:, :D].reshape(row_count, HEADS, HDIM)
        attended, _ = attend(queries, own_pos, key_all, value_all, whole_pos, signed, key_block)
        attended_b = attended.reshape(row_count, D).astype(jnp.bfloat16)
        result = layer_rest(inputs_row, attended_b, gain_pair, bias_row, out_w, up_w, down_w)[4]
        return result.astype(jnp.bfloat16)

    def layer_reverse_pass(entry, result_gradient, index):
        whole_pos, own_pos = sequence_pos(index)
        inputs_row = entry.astype(jnp.float32)
        normed, projected = layer_front(inputs_row, gain_pair, bias_row, qkv_w)
        queries = projected[:, :D].reshape(row_count, HEADS, HDIM)
        key_all, value_all = (
            lax.all_gather(projected[:, D : 2 * D], "ctx", axis=0, tiled=True),
            lax.all_gather(projected[:, 2 * D :], "ctx", axis=0, tiled=True),
        )
        attended, log_total = attend(
            queries, own_pos, key_all, value_all, whole_pos, signed, key_block
        )
        attended_b = attended.reshape(row_count, D).astype(jnp.bfloat16)
        middle, normed_two, hidden, active, _ = layer_rest(
            inputs_row, attended_b, gain_pair, bias_row, out_w, up_w, down_w
        )
        grad_down_b = result_gradient.astype(jnp.bfloat16)
        grad_wdown = jnp.dot(active.T, grad_down_b, preferred_element_type=jnp.float32)
        grad_active = jnp.dot(grad_down_b, down_w.T, preferred_element_type=jnp.float32)
        _, gelu_back = jax.vjp(gelu_tanh, hidden)
        grad_hidden = gelu_back(grad_active)[0]
        grad_hidden_b = grad_hidden.astype(jnp.bfloat16)
        grad_wup = jnp.dot(normed_two.T, grad_hidden_b, preferred_element_type=jnp.float32)
        grad_normed_two = jnp.dot(grad_hidden_b, up_w.T, preferred_element_type=jnp.float32)
        _, norm_back_two = jax.vjp(layer_norm, middle, gain_pair[1], bias_row[D : 2 * D])
        grad_middle_part, grad_gain_two, grad_offset_two = norm_back_two(grad_normed_two)
        grad_middle = result_gradient + grad_middle_part
        grad_proj_b = grad_middle.astype(jnp.bfloat16)
        grad_wout = jnp.dot(attended_b.T, grad_proj_b, preferred_element_type=jnp.float32)
        grad_att_flat = jnp.dot(grad_proj_b, out_w.T, preferred_element_type=jnp.float32).astype(
            jnp.bfloat16
        )
        grad_att = grad_att_flat.reshape(row_count, HEADS, HDIM)
        delta = jnp.einsum("rhe,rhe->hr", grad_att.astype(jnp.float32), attended)
        grad_q, grad_k, grad_v = backward_summed(
            queries,
            own_pos,
            key_all,
            value_all,
            whole_pos,
            log_total,
            delta,
            grad_att,
            signed,
            key_block,
        )
        grad_qkv_b = jnp.concatenate([grad_q, grad_k, grad_v], axis=1).astype(jnp.bfloat16)
        grad_wqkv = jnp.dot(normed.T, grad_qkv_b, preferred_element_type=jnp.float32)
        grad_normed = jnp.dot(grad_qkv_b, qkv_w.T, preferred_element_type=jnp.float32)
        _, norm_back_one = jax.vjp(layer_norm, inputs_row, gain_pair[0], bias_row[0:D])
        grad_in_part, grad_gain_one, grad_offset_one = norm_back_one(grad_normed)
        input_gradient = grad_middle + grad_in_part
        grad_gain_rows = jnp.stack([grad_gain_one, grad_gain_two])
        grad_bias_row = jnp.concatenate(
            [
                grad_offset_one,
                grad_offset_two,
                jnp.sum(grad_q, axis=0),
                jnp.sum(grad_v, axis=0),
                jnp.sum(grad_middle, axis=0),
                jnp.sum(result_gradient, axis=0),
                jnp.sum(grad_hidden, axis=0),
            ]
        )
        return (
            input_gradient,
            (grad_gain_rows, grad_bias_row, grad_wqkv, grad_wout, grad_wup, grad_wdown),
        )

    def tick(tick_at, state_in):
        arrived, returned, stored, acts_rows, grad_rows, partial_sums = state_in
        ahead = tick_at - section_at
        ahead_ok = (ahead >= 0) & (ahead < micro_count)
        ahead_at = jnp.clip(ahead, 0, micro_count - 1)
        fresh = jnp.where(
            signed, lax.dynamic_index_in_dim(first_inputs, ahead_at, 0, keepdims=False), arrived
        )
        previous = lax.dynamic_index_in_dim(stored, ahead_at, 0, keepdims=False)
        entry = jnp.where(ahead_ok, fresh, previous)
        stored = lax.dynamic_update_index_in_dim(stored, entry, ahead_at, 0)
        sent = layer_forward(entry, ahead_at)
        old_acts = lax.dynamic_index_in_dim(acts_rows, ahead_at, 0, keepdims=False)
        acts_rows = lax.dynamic_update_index_in_dim(
            acts_rows, jnp.where(ahead_ok, sent, old_acts), ahead_at, 0
        )
        behind = tick_at - 2 + section_at
        trailing_valid = (behind >= 0) & (behind < micro_count)
        trailing_position = jnp.clip(behind, 0, micro_count - 1)
        entry_gradient = lax.dynamic_index_in_dim(stored, trailing_position, 0, keepdims=False)
        given_cot = lax.dynamic_index_in_dim(cot_rows, trailing_position, 0, keepdims=False).astype(
            jnp.float32
        )
        result_gradient = jnp.where(signed, returned.astype(jnp.float32), given_cot)
        input_gradient, added_terms = layer_reverse_pass(
            entry_gradient, result_gradient, trailing_position
        )
        partial_sums = jax.tree.map(
            lambda running_total, added_term: running_total
            + jnp.where(trailing_valid, added_term, 0.0),
            partial_sums,
            added_terms,
        )
        handed = input_gradient.astype(jnp.bfloat16)
        kept_grad = jnp.where(signed, input_gradient, handed.astype(jnp.float32))
        old_grads = lax.dynamic_index_in_dim(grad_rows, trailing_position, 0, keepdims=False)
        grad_rows = lax.dynamic_update_index_in_dim(
            grad_rows, jnp.where(trailing_valid, kept_grad, old_grads), trailing_position, 0
        )
        arrived = shifted(sent, "section", 1)
        returned = shifted(handed, "section", -1)
        return (arrived, returned, stored, acts_rows, grad_rows, partial_sums)

    zero_rows = jnp.zeros((row_count, D), jnp.bfloat16)
    start_sums = (
        jnp.zeros((2, D), jnp.float32),
        jnp.zeros((bias_row.shape[0],), jnp.float32),
        jnp.zeros(qkv_w.shape, jnp.float32),
        jnp.zeros(out_w.shape, jnp.float32),
        jnp.zeros(up_w.shape, jnp.float32),
        jnp.zeros(down_w.shape, jnp.float32),
    )
    start_state = (
        zero_rows,
        zero_rows,
        jnp.zeros((micro_count, row_count, D), jnp.bfloat16),
        jnp.zeros((micro_count, row_count, D), jnp.bfloat16),
        jnp.zeros((micro_count, row_count, D), jnp.float32),
        start_sums,
    )
    final_state = lax.fori_loop(0, micro_count + 2, tick, start_state)
    acts_rows = final_state[3]
    grad_rows = final_state[4]
    partial_sums = final_state[5]
    totals = (
        lax.psum_scatter(partial_sums[0], ("dp", "ctx"), scatter_dimension=1, tiled=True),
        lax.psum_scatter(partial_sums[1], ("dp", "ctx"), scatter_dimension=0, tiled=True),
        lax.psum_scatter(partial_sums[2], ("dp", "ctx"), scatter_dimension=0, tiled=True),
        lax.psum_scatter(partial_sums[3], ("dp", "ctx"), scatter_dimension=0, tiled=True),
        lax.psum_scatter(partial_sums[4], ("dp", "ctx"), scatter_dimension=0, tiled=True),
        lax.psum_scatter(partial_sums[5], ("dp", "ctx"), scatter_dimension=0, tiled=True),
    )
    return (
        acts_rows[None, :, None],
        grad_rows[None, :, None],
        totals[0][None],
        totals[1][None],
        totals[2][None],
        totals[3][None],
        totals[4][None],
        totals[5][None],
    )


def swap_halves(value):
    count = lax.axis_size("ctx")
    return lax.ppermute(value, "ctx", [(at, (at + count // 2) % count) for at in range(count)])


def swap_cores(value):
    return lax.ppermute(value, "ctx", [(at, at ^ 1) for at in range(lax.axis_size("ctx"))])


def swap_z(value, step):
    return lax.ppermute(value, "dp", [(at, at ^ step) for at in range(lax.axis_size("dp"))])


def fold_kernel(place, kept_ref, arrived_ref, keep_ref, send_ref):
    for target, chosen in ((send_ref, 1 - place[0]), (keep_ref, place[0])):
        for at in range(target.shape[0]):
            total = kept_ref[at, chosen].astype(jnp.float32) + arrived_ref[at, chosen].astype(jnp.float32)
            target[at] = total.astype(target.dtype)


def fold(kept, arrived, place, outer):
    rows, width = kept.shape[-2:]
    lead = math.prod(kept.shape[:outer])
    inner = math.prod(kept.shape[outer + 1 : -1])
    shape = (lead, 2, inner, width)
    outs = [((lead, inner, width), kept.dtype)] * 2
    keep, send = call(
        fold_kernel, "fold", 4, 0, outs, [], place, kept.reshape(shape), arrived.reshape(shape), smem=1
    )
    left = kept.shape[:outer] + kept.shape[outer + 1 :]
    return keep.reshape(left), send.reshape(left)


def wide_sum(kept, arrived):
    return kept.astype(jnp.float32) + arrived.astype(jnp.float32)


def fast_body(inputs, slot_order, cotangent, gains, biases, w_qkv, w_out, w_up, w_down):
    rows = inputs.shape[2]
    count = lax.axis_size("ctx")
    z_count = lax.axis_size("dp")
    half = count // 2
    ctx_at = lax.axis_index("ctx")
    mine = ctx_at // half
    y_at, core_at = ctx_at // 2, ctx_at % 2
    signed = lax.axis_index("section") == 0
    place = core_at[None].astype(jnp.int32)
    y_place = y_at[None].astype(jnp.int32)
    z_at = lax.axis_index("dp")
    gain_pair = gains[0]
    wide, narrow, barrier = jnp.float32, jnp.bfloat16, lax.optimization_barrier

    def gathered(value):
        kept = lax.dynamic_index_in_dim(value, mine, 0, keepdims=False)
        sent = lax.dynamic_index_in_dim(value, 1 - mine, 0, keepdims=False)
        return jnp.concatenate([kept, swap_halves(sent)], axis=0)

    def returned(kept, arrived):
        arrived = arrived.astype(kept.dtype)
        first = jnp.where(mine == 0, kept, arrived)
        second = jnp.where(mine == 0, arrived, kept)
        return jnp.stack([first, second])

    order = lax.dynamic_index_in_dim(slot_order[:, 0], mine, 0, keepdims=False)
    pairs = order.reshape(count, 2)

    def slots_of(device):
        return jnp.concatenate([pairs[device], pairs[(device + half) % count]])

    meta = slot_meta(slots_of(ctx_at), slots_of(ctx_at ^ 1), signed)

    def through_attention(entry):
        normed, queries, kv = front(entry, gain_pair, biases, w_qkv)
        there = swap_cores(kv)
        attended, lse = sorted_attend(meta, queries, kv, there)
        return normed, queries, kv, there, attended, lse

    inputs, meta = barrier((inputs, meta))
    first = gathered(inputs[:, 0])
    qkv_t, out_t = w_qkv[0].T, w_out[0].T
    first, qkv_t, out_t = barrier((first, qkv_t, out_t))
    attended = through_attention(first)[4]
    sent = rest(first, attended, gain_pair, biases, w_out, w_up, w_down)
    sent, later = barrier((sent, (cotangent, w_up, w_down)))
    arrived = shifted(sent, "section", 1)
    given = gathered(later[0][:, 0])
    up_t, down_t = [weight[0].T for weight in later[1:]]
    arrived, given, up_t, down_t = barrier((arrived, given, up_t, down_t))
    entry = jnp.where(signed, first, arrived)

    normed, queries, kv, kv_there, attended, lse = through_attention(entry)
    middle, normed_two, active, slope, grad_middle, grad_att = turn(
        entry, attended, given, gain_pair, biases, w_out, w_up, out_t, up_t, down_t
    )

    def attention_back(grad_att):
        grad_q, own, sent = sorted_attend_back(meta, queries, kv, kv_there, attended, grad_att, lse)
        return grad_q, own, swap_cores(sent)

    grad_qkv = attention_back(grad_att)
    handed, _ = front_back(*grad_qkv, entry, grad_middle, gain_pair, qkv_t, narrow)
    lefts = (active, normed, attended, normed_two)
    handed, lefts = barrier((handed, lefts))
    back = shifted(handed, "section", -1)
    active = lefts[0]
    lefts = [value.T for value in lefts]
    result = middle + dot(active, w_down[0], NN) + biases[0, 5 * D : 6 * D]
    result = result.astype(narrow)
    acts_there = swap_halves(result[rows:])
    back, acts_there, lefts = barrier((back, acts_there, lefts))
    active_t, normed_t, attended_t, normed_two_t = lefts
    back = jnp.where(signed, back, given)

    z_steps = [1 << at for at in range(z_count.bit_length() - 1)]
    split = [2] * len(z_steps)
    by_z = [((z_at >> at) & 1)[None].astype(jnp.int32) for at in range(len(z_steps))]

    def bits(value, before):
        return value.reshape(value.shape[:before] + tuple(split) + value.shape[before + 1 :])

    grad_hidden, grad_middle, grad_middle_b, grad_att, sums_two, up_sum = down_back(
        back, slope, middle, gain_pair, out_t, up_t, down_t
    )
    back, grad_hidden = barrier((back, grad_hidden))
    down_kept, down_sent = weight_grad(place, active_t, back, z_count)
    grad_hidden, down_sent = barrier((grad_hidden, down_sent))
    down_there = swap_cores(down_sent)
    up_kept, up_sent = weight_grad(place, normed_two_t, grad_hidden, z_count)
    grad_middle_b, up_sent = barrier((grad_middle_b, up_sent))
    up_there = swap_cores(up_sent)
    down_kept, down_sent = fold(down_kept, down_there, y_place, 0)
    grad_middle_b, down_sent = barrier((grad_middle_b, down_sent))
    down_there = swap_halves(down_sent)
    out_kept, out_sent = weight_grad(place, attended_t, grad_middle_b, z_count)
    out_there = swap_cores(out_sent)
    up_kept, up_sent = fold(bits(up_kept, 1), bits(up_there, 1), by_z[0], len(split))
    grad_att, up_sent, out_there = barrier((grad_att, up_sent, out_there))
    up_there = swap_z(up_sent, z_steps[0])
    grad_q, own, sent = sorted_attend_back(meta, queries, kv, kv_there, attended, grad_att, lse)
    sent, own, down_there, up_there = barrier((sent, own, down_there, up_there))
    there = swap_cores(sent)
    down_kept, down_sent = fold(bits(down_kept, 0), bits(down_there, 0), by_z[0], len(split) - 1)
    up_kept, up_sent = fold(up_kept, up_there, y_place, 0)
    there, down_sent, up_sent = barrier((there, down_sent, up_sent))
    down_there, up_there = swap_z(down_sent, z_steps[0]), swap_halves(up_sent)
    qkv_kept, qkv_sent = qkv_weight_grad(place, normed_t, grad_q, own, there, z_count)
    qkv_sent, grad_q, own, there = barrier((qkv_sent, grad_q, own, there))
    qkv_there = swap_cores(qkv_sent)
    input_gradient, sums_one = front_back(grad_q, own, there, entry, grad_middle, gain_pair, qkv_t, wide)
    out_kept, out_sent = fold(out_kept, out_there, y_place, 0)
    small = jnp.concatenate([sums_one, sums_two, up_sum], axis=0)
    small = small + swap_cores(small)
    qkv_kept, qkv_sent = fold(qkv_kept, qkv_there, y_place, 0)
    qkv_sent, out_sent, small = barrier((qkv_sent, out_sent, small))
    small_there, qkv_there, out_there = swap_halves(small), swap_halves(qkv_sent), swap_halves(out_sent)
    down_kept, down_sent = fold(down_kept, down_there, by_z[1], 0)
    down_there = swap_z(down_sent, z_steps[1])
    up_kept, up_sent = fold(up_kept, up_there, by_z[1], 0)
    up_there = swap_z(up_sent, z_steps[1])
    qkv_kept, qkv_sent = fold(bits(qkv_kept, 0), bits(qkv_there, 0), by_z[0], len(split) - 1)
    out_kept, out_sent = fold(bits(out_kept, 0), bits(out_there, 0), by_z[0], len(split) - 1)
    small = small + small_there
    rounded = input_gradient.astype(narrow)
    qkv_sent, out_sent, small, rounded = barrier((qkv_sent, out_sent, small, rounded))
    small_there, qkv_there, out_there = [swap_z(value, z_steps[0]) for value in (small, qkv_sent, out_sent)]
    grads_there = swap_halves(rounded[rows:])
    qkv_kept, qkv_sent = fold(qkv_kept, qkv_there, by_z[1], 0)
    out_kept, out_sent = fold(out_kept, out_there, by_z[1], 0)
    small = small + small_there
    qkv_sent, out_sent, small = barrier((qkv_sent, out_sent, small))
    small_there, qkv_there, out_there = [swap_z(value, z_steps[1]) for value in (small, qkv_sent, out_sent)]
    wdown = wide_sum(down_kept, down_there)
    wup = wide_sum(up_kept, up_there)
    wqkv = wide_sum(qkv_kept, qkv_there)
    wout = wide_sum(out_kept, out_there)
    small = small + small_there
    grads_kept = jnp.where(signed, input_gradient[:rows], rounded[:rows].astype(wide))
    blocks = count * z_count
    block_at = lax.axis_index("dp") * count + ctx_at
    gain_piece = lax.dynamic_slice_in_dim(small[0:5:4], block_at * (D // blocks), D // blocks, 1)
    bias_rows = [small[1], small[5], small[2], small[3], small[6], small[7], small[8:].reshape(-1)]
    bias_row = jnp.concatenate(bias_rows)
    width = bias_row.shape[0] // blocks
    bias_piece = lax.dynamic_slice_in_dim(bias_row, block_at * width, width, 0)
    return (
        returned(result[:rows], acts_there)[None, :, None],
        returned(grads_kept, grads_there)[None, :, None],
        gain_piece[None],
        bias_piece[None],
        wqkv[None],
        wout[None],
        wup[None],
        wdown[None],
    )


def body_for(mesh):
    sizes = dict(mesh.shape)
    return fast_body if (sizes["ctx"], sizes["dp"]) == (4, 4) else general_body


def solution(mesh):
    in_specs = (
        P(None, "dp", "ctx", None),
        P(None, "dp", None),
        P(None, "dp", "ctx", None),
        P("section", None, None),
        P("section", None),
        P("section", None, None),
        P("section", None, None),
        P("section", None, None),
        P("section", None, None),
    )
    out_specs = (
        P("section", None, "dp", "ctx", None),
        P("section", None, "dp", "ctx", None),
        P("section", None, ("dp", "ctx")),
        P("section", ("dp", "ctx")),
        P("section", ("dp", "ctx"), None),
        P("section", ("dp", "ctx"), None),
        P("section", ("dp", "ctx"), None),
        P("section", ("dp", "ctx"), None),
    )
    return jax.shard_map(
        body_for(mesh), mesh=mesh, in_specs=in_specs, out_specs=out_specs, check_vma=False
    )
```

```python
import functools
import math
import jax
import jax.numpy as jnp
from jax import lax
from jax.experimental import pallas as pl
from jax.experimental.pallas import tpu as pltpu
from jax.sharding import PartitionSpec as P

D = 768
HEADS = 12
HDIM = 64
PAIR = 2 * HDIM
PAIRS = HEADS // 2
OWN = 4
CHUNK = 128
BACK_CHUNK = 1024
SAFE = 60.0
IDLE = 2
NT = (((1,), (1,)), ((), ()))
TN = (((0,), (0,)), ((), ()))
NN = (((1,), (0,)), ((), ()))


def dot(left, right, dims):
    return lax.dot_general(left, right, dims, preferred_element_type=jnp.float32)


def slot_meta(own_pos, other_pos, signed):
    rank = jnp.sum((own_pos[None, :] < own_pos[:, None]).astype(jnp.int32), axis=1)
    chosen = rank[None, :] == jnp.arange(OWN, dtype=jnp.int32)[:, None]
    ranked = jnp.sum(jnp.where(chosen, jnp.arange(OWN, dtype=jnp.int32)[None, :], 0), axis=1)
    ranked_pos = jnp.sum(jnp.where(chosen, own_pos[None, :], 0), axis=1)
    return jnp.concatenate([own_pos, other_pos, ranked, ranked_pos, signed.astype(jnp.int32)[None]])


def sort_rows(meta, own, other, target, span, first):
    columns = slice(first, first + D)
    for slot in range(OWN):
        for base, source in ((0, own), (OWN, other)):
            start = pl.multiple_of(meta[base + slot] * span, span)
            target[pl.ds(start, span), :] = source[slot * span : (slot + 1) * span, columns]


def reach(rank, slots):
    return ((0, slots // 2 - 2), (1, slots // 2 - 1), (slots // 2, slots - 2), (slots // 2 + 1, slots - 1))[rank]


def stacked_heads(rows):
    second = lax.broadcasted_iota(jnp.int32, rows.shape, 1) >= HDIM
    zero = jnp.zeros_like(rows)
    return jnp.concatenate([jnp.where(second, zero, rows), jnp.where(second, rows, zero)], axis=0)


def visible(values, start, least, span, position, fill):
    if start + values.shape[0] <= least * span:
        return values
    key_at = lax.broadcasted_iota(jnp.int32, values.shape, 0) + start
    lane = lax.broadcasted_iota(jnp.int32, values.shape, 1)
    query_at = position * span + jnp.where(lane >= span, lane - span, lane)
    return jnp.where(key_at <= query_at, values, fill)


def unstack(pair, span):
    row = lax.broadcasted_iota(jnp.int32, (PAIR, span), 0)
    return jnp.where(row < HDIM, pair[:, :span], pair[:, span:]).T


def chunks_of(count, chunk):
    return [slice(start, min(start + chunk, count)) for start in range(0, count, chunk)]


def eight(values):
    return values.reshape(-1, 8, values.shape[-1])


def pair_columns(at):
    return pl.ds(pl.multiple_of(at * PAIR, PAIR), PAIR)


def largest_norm(rows_ref):
    feature = lax.broadcasted_iota(jnp.int32, (D, PAIR), 0) // HDIM
    head = lax.broadcasted_iota(jnp.int32, (D, PAIR), 1)
    chosen = jnp.where(feature == head, 1.0, 0.0).astype(jnp.bfloat16)
    rows = rows_ref[...]
    return jnp.max(dot(rows * rows, chosen, NN))


def forward_kernel(meta, q_ref, kv_ref, kv2_ref, o_ref, lse_ref, keys, values, *, span):
    slots = keys.shape[0] // span
    sort_rows(meta, kv_ref, kv2_ref, keys, span, 0)
    sort_rows(meta, kv_ref, kv2_ref, values, span, D)
    bound = largest_norm(q_ref) * largest_norm(keys) * (1.1 / HDIM)
    near = bound < SAFE * SAFE

    def run(signed, safe):
        def one_pair(pair, _):
            columns = pair_columns(pair)
            values_t = values[:, columns].T
            for rank in reversed(range(OWN)):
                least, most = reach(rank, slots)
                count = (most + 1) * span
                row_at = pl.multiple_of(meta[2 * OWN + rank] * span, span)
                position = meta[3 * OWN + rank]
                queries = stacked_heads(q_ref[pl.ds(row_at, span), columns] * 0.125)
                largest = None
                if not safe:
                    most_seen = jnp.full((8, 2 * span), -1e30, jnp.float32)
                    for part in chunks_of(count, CHUNK):
                        scores = dot(keys[part, columns], queries, NT)
                        scores = jnp.abs(scores) if signed else scores
                        scores = visible(scores, part.start, least, span, position, -1e30)
                        most_seen = jnp.maximum(most_seen, jnp.max(eight(scores), axis=0))
                    largest = jnp.max(most_seen, axis=0, keepdims=True)
                    if signed:
                        square = largest * largest + 1.0
                        largest = square * lax.rsqrt(square)
                total = jnp.zeros((8, 2 * span), jnp.float32)
                gathered = jnp.zeros((PAIR, 2 * span), jnp.float32)
                for part in chunks_of(count, CHUNK):
                    scores = dot(keys[part, columns], queries, NT)
                    argument = scores
                    if signed:
                        square = scores * scores + 1.0
                        inverse = lax.rsqrt(square)
                        argument = square * inverse
                    if not safe:
                        argument = argument - largest
                    weights = jnp.exp(visible(argument, part.start, least, span, position, -1e30))
                    total += jnp.sum(eight(weights), axis=0)
                    if signed:
                        weights = weights * (scores * inverse)
                    gathered += dot(values_t[:, part], weights.astype(jnp.bfloat16), NN)
                total = jnp.sum(total, axis=0, keepdims=True)
                lse = jnp.log(total)
                lse_ref[pair, rank : rank + 1, :] = lse if safe else lse + largest
                gathered = gathered * (1.0 / total)
                o_ref[pl.ds(row_at, span), columns] = unstack(gathered, span).astype(jnp.bfloat16)
            return 0

        lax.fori_loop(0, PAIRS, one_pair, 0)

    for signed in (True, False):
        for safe in (True, False):
            chosen = (meta[4 * OWN] == int(signed)) & (near == safe)
            pl.when(chosen)(functools.partial(run, signed, safe))


def in_vmem(*values):
    return [pltpu.with_memory_space_constraint(value, pltpu.VMEM) for value in values]


SMEM_SPEC = pl.BlockSpec(memory_space=pltpu.SMEM)
VMEM_SPEC = pl.BlockSpec(memory_space=pltpu.VMEM)


def sorted_attend(meta, queries, kv, kv_other):
    rows = kv.shape[0]
    span = rows // OWN
    return pl.pallas_call(
        functools.partial(forward_kernel, span=span),
        in_specs=[SMEM_SPEC] + [VMEM_SPEC] * 3,
        out_specs=[VMEM_SPEC] * 2,
        scratch_shapes=[pltpu.VMEM((2 * rows, D), jnp.bfloat16)] * 2,
        out_shape=[
            jax.ShapeDtypeStruct((rows, D), jnp.bfloat16),
            jax.ShapeDtypeStruct((PAIRS, OWN, 2 * span), jnp.float32),
        ],
        compiler_params=pltpu.CompilerParams(vmem_limit_bytes=10 * 1024 * 1024),
        cost_estimate=pl.CostEstimate(flops=4_000_000_000, bytes_accessed=0, transcendentals=0),
        name="attend",
    )(meta, *in_vmem(queries, kv, kv_other))


def backward_kernel(
    meta, q_ref, kv_ref, kv2_ref, o_ref, do_ref, lse_ref,
    dq_ref, own_ref, other_ref, keys, values, grad_k, grad_v, *, span,
):
    slots = keys.shape[0] // span
    sort_rows(meta, kv_ref, kv2_ref, keys, span, 0)
    sort_rows(meta, kv_ref, kv2_ref, values, span, D)

    def run(signed):
        def one_pair(pair, _):
            columns = pair_columns(pair)
            keys_t = keys[:, columns].T
            for rank in reversed(range(OWN)):
                least, most = reach(rank, slots)
                count = (most + 1) * span
                row_at = pl.multiple_of(meta[2 * OWN + rank] * span, span)
                position = meta[3 * OWN + rank]
                queries = stacked_heads(q_ref[pl.ds(row_at, span), columns] * 0.125)
                grad_rows = do_ref[pl.ds(row_at, span), columns]
                grads = stacked_heads(grad_rows)
                product = grad_rows.astype(jnp.float32) * o_ref[pl.ds(row_at, span), columns].astype(jnp.float32)
                delta = jnp.sum(stacked_heads(product).T, axis=0, keepdims=True)
                lse = lse_ref[pair, rank : rank + 1, :]
                gathered = jnp.zeros((PAIR, 2 * span), jnp.float32)
                for part in chunks_of(count, BACK_CHUNK):
                    scores = dot(keys[part, columns], queries, NT)
                    along = dot(values[part, columns], grads, NT)
                    argument = scores
                    if signed:
                        square = scores * scores + 1.0
                        inverse = lax.rsqrt(square)
                        argument = square * inverse
                    prob = jnp.exp(visible(argument - lse, part.start, least, span, position, -1e30))
                    if signed:
                        sign_pattern = scores * inverse
                        weights = prob * sign_pattern
                        bend = inverse * inverse * inverse
                        dscore = prob * ((sign_pattern * along - delta) * sign_pattern + along * bend)
                    else:
                        weights = prob
                        dscore = prob * (along - delta)
                    weights = weights.astype(jnp.bfloat16)
                    dscore = dscore.astype(jnp.bfloat16)
                    added_v = dot(weights, grads, NN)
                    added_k = dot(dscore, queries, NN)
                    if rank == OWN - 1:
                        grad_v[part, :] = added_v
                        grad_k[part, :] = added_k
                    else:
                        grad_v[part, :] += added_v
                        grad_k[part, :] += added_k
                    gathered += dot(keys_t[:, part], dscore, NN)
                dq_ref[pl.ds(row_at, span), columns] = (unstack(gathered, span) * 0.125).astype(jnp.bfloat16)
            for slot in range(OWN):
                there = slice(slot * span, (slot + 1) * span)
                own_at = pl.multiple_of(meta[slot] * span, span)
                other_at = pl.multiple_of(meta[OWN + slot] * span, span)
                for part, total in enumerate((grad_k, grad_v)):
                    own_ref[part, there, columns] = total[pl.ds(own_at, span), :].astype(jnp.bfloat16)
                    other_ref[part, there, columns] = total[pl.ds(other_at, span), :].astype(jnp.bfloat16)
            return 0

        lax.fori_loop(0, PAIRS, one_pair, 0)

    for signed in (True, False):
        pl.when(meta[4 * OWN] == int(signed))(functools.partial(run, signed))

    @pl.when(meta[4 * OWN] == IDLE)
    def _():
        for out_ref in (dq_ref, own_ref, other_ref):
            out_ref[...] = jnp.zeros_like(out_ref)


def sorted_attend_back(meta, queries, kv, kv_other, attended, grad_att, lse):
    rows = kv.shape[0]
    span = rows // OWN
    return pl.pallas_call(
        functools.partial(backward_kernel, span=span),
        in_specs=[SMEM_SPEC] + [VMEM_SPEC] * 6,
        out_specs=[VMEM_SPEC] * 3,
        scratch_shapes=[pltpu.VMEM((2 * rows, D), jnp.bfloat16)] * 2
        + [pltpu.VMEM((2 * rows, PAIR), jnp.float32)] * 2,
        out_shape=[
            jax.ShapeDtypeStruct((rows, D), jnp.bfloat16),
            jax.ShapeDtypeStruct((2, rows, D), jnp.bfloat16),
            jax.ShapeDtypeStruct((2, rows, D), jnp.bfloat16),
        ],
        compiler_params=pltpu.CompilerParams(vmem_limit_bytes=10 * 1024 * 1024),
        cost_estimate=pl.CostEstimate(flops=8_000_000_000, bytes_accessed=0, transcendentals=0),
        name="attend_back",
    )(meta, *in_vmem(queries, kv, kv_other, attended, grad_att), lse)


TURN_TANH = 0.7978845608028654
CUBE = 0.044715
CHUNKS = 1


def normalised(rows):
    center = rows - jnp.mean(rows, axis=-1, keepdims=True)
    inverse = lax.rsqrt(jnp.mean(center * center, axis=-1, keepdims=True) + 1e-05)
    return center * inverse, inverse


def norm_back(unit, inverse, gain_row, grad):
    scaled = grad * gain_row
    along = jnp.mean(scaled * unit, axis=-1, keepdims=True)
    return inverse * (scaled - jnp.mean(scaled, axis=-1, keepdims=True) - unit * along)


def row_chunks(rows, chunks=CHUNKS):
    return [slice(at * rows // chunks, (at + 1) * rows // chunks) for at in range(chunks)]


def column_sum(values):
    return jnp.sum(values, axis=0, keepdims=True)


def gelu_parts(hidden):
    square = hidden * hidden
    curve = jnp.tanh(hidden * (TURN_TANH + TURN_TANH * CUBE * square))
    half = 0.5 + 0.5 * curve
    inner = hidden * (TURN_TANH + 3.0 * TURN_TANH * CUBE * square)
    return hidden * half, half + 0.5 * (1.0 - curve * curve) * inner


def gelu_only(hidden):
    square = hidden * hidden
    curve = jnp.tanh(hidden * (TURN_TANH + TURN_TANH * CUBE * square))
    return hidden * (0.5 + 0.5 * curve)


def cost(flops):
    return pl.CostEstimate(flops=int(flops) // 8, bytes_accessed=0, transcendentals=0)


def in_hbm(value):
    return pltpu.with_memory_space_constraint(value, pltpu.HBM)


def placed(shape, dtype, space=None):
    return jax.ShapeDtypeStruct(shape, dtype) if space is None else space(shape, dtype)


def call(kernel, name, megabytes, flops, outs, scratch, *operands, smem=0):
    return pl.pallas_call(
        kernel,
        in_specs=[SMEM_SPEC] * smem + [VMEM_SPEC] * (len(operands) - smem),
        out_specs=[VMEM_SPEC] * len(outs),
        out_shape=[placed(*out) for out in outs],
        scratch_shapes=scratch,
        compiler_params=pltpu.CompilerParams(vmem_limit_bytes=megabytes * 1024 * 1024),
        cost_estimate=cost(flops),
        name=name,
    )(*operands)


def bias_part(biases, at):
    return biases[0:1, at * D : (at + 1) * D]


def tile(at):
    return slice(at * D, (at + 1) * D)


def whole(*shape):
    return pl.BlockSpec(shape, lambda *_: (0,) * len(shape))


def flip_kernel(in_ref, out_ref):
    out_ref[...] = in_ref[...].T


def copy_kernel(in_ref, out_ref):
    out_ref[...] = in_ref[...]


def fetched(value):
    height, width = value.shape
    block = pl.BlockSpec((height // 4, width), lambda i: (i, 0))
    return pl.pallas_call(
        copy_kernel,
        grid=(4,),
        in_specs=[block],
        out_specs=block,
        out_shape=placed(value.shape, value.dtype, pltpu.VMEM),
        compiler_params=pltpu.CompilerParams(vmem_limit_bytes=7 * 1024 * 1024),
        cost_estimate=cost(0),
        name="fetched",
    )(in_hbm(value))


def flip(value, space=None):
    height, width = value.shape[-2:]
    lead = (None,) * (value.ndim - 2)
    zeros = (0,) * (value.ndim - 2)
    if height > D:
        grid = height // D
        in_spec = pl.BlockSpec(lead + (D, width), lambda i: zeros + (i, 0))
        out_spec = pl.BlockSpec((width, D), lambda i: (0, i))
    else:
        step = min(width, D)
        grid = width // step
        in_spec = pl.BlockSpec(lead + (height, step), lambda i: zeros + (0, i))
        out_spec = pl.BlockSpec((step, height), lambda i: (i, 0))
    return pl.pallas_call(
        flip_kernel,
        grid=(grid,),
        in_specs=[in_spec],
        out_specs=out_spec,
        out_shape=placed((width, height), value.dtype, space),
        compiler_params=pltpu.CompilerParams(vmem_limit_bytes=7 * 1024 * 1024),
        cost_estimate=cost(0),
        name="flip",
    )(value)


def front_kernel(x_ref, gains, biases, w_ref, normed_ref, q_ref, kv_ref):
    for part in row_chunks(x_ref.shape[0]):
        unit, _ = normalised(x_ref[part, :].astype(jnp.float32))
        normed = (unit * gains[0:1, :] + bias_part(biases, 0)).astype(jnp.bfloat16)
        normed_ref[part, :] = normed
        kv_ref[part, :D] = dot(normed, w_ref[0, :, tile(1)], NN).astype(jnp.bfloat16)
        kv_ref[part, D:] = (dot(normed, w_ref[0, :, tile(2)], NN) + bias_part(biases, 3)).astype(jnp.bfloat16)
        q_ref[part, :] = (dot(normed, w_ref[0, :, tile(0)], NN) + bias_part(biases, 2)).astype(jnp.bfloat16)


def front(entry, gains, biases, w_qkv):
    rows = entry.shape[0]
    narrow = jnp.bfloat16
    outs = [((rows, D), narrow), ((rows, D), narrow), ((rows, 2 * D), narrow)]
    return call(front_kernel, "front", 8, 6 * rows * D * D, outs, [], entry, gains, biases, w_qkv)


def middle_rows(x_ref, o_ref, w_out, biases, part):
    return x_ref[part, :].astype(jnp.float32) + dot(o_ref[part, :], w_out[0], NN) + bias_part(biases, 4)


def rest_kernel(x_ref, o_ref, gains, biases, w_out, w_up, w_down, result_ref):
    for part in row_chunks(x_ref.shape[0]):
        middle = middle_rows(x_ref, o_ref, w_out, biases, part)
        unit, _ = normalised(middle)
        normed = (unit * gains[1:2, :] + bias_part(biases, 1)).astype(jnp.bfloat16)
        total = middle + bias_part(biases, 5)
        for at in range(w_up.shape[2] // D):
            hidden = dot(normed, w_up[0, :, tile(at)], NN) + bias_part(biases, 6 + at)
            total += dot(gelu_only(hidden).astype(jnp.bfloat16), w_down[0, tile(at), :], NN)
        result_ref[part, :] = total.astype(jnp.bfloat16)


def rest(entry, attended, gains, biases, w_out, w_up, w_down):
    rows = entry.shape[0]
    flops = 2 * rows * (D * D + 2 * w_up.size)
    return call(
        rest_kernel, "rest", 7, flops, [((rows, D), jnp.bfloat16)], [],
        entry, attended, gains, biases, w_out, w_up, w_down,
    )[0]


def turn_kernel(
    x_ref, o_ref, d_ref, gains, biases, w_out, w_up, out_t, up_t, down_t,
    middle_ref, normed_ref, active_ref, slope_ref, grad_ref, grad_att_ref,
    middle, normed, actives, slopes, done,
):
    copies = []

    def leave(source, target):
        copies.append(pltpu.make_async_copy(source, target, done.at[len(copies)]))
        copies[-1].start()

    rows = x_ref[...].astype(jnp.float32) + dot(o_ref[...], w_out[0], NN) + bias_part(biases, 4)
    middle[...] = rows
    leave(middle, middle_ref)
    unit, _ = normalised(rows)
    normed[...] = (unit * gains[1:2, :] + bias_part(biases, 1)).astype(jnp.bfloat16)
    leave(normed, normed_ref)
    total = jnp.zeros_like(rows)
    for at in range(w_up.shape[2] // D):
        hidden = dot(normed[...], w_up[0, :, tile(at)], NN) + bias_part(biases, 6 + at)
        active, slope = gelu_parts(hidden)
        actives[at] = active.astype(jnp.bfloat16)
        slopes[at] = slope.astype(jnp.bfloat16)
        leave(actives.at[at], active_ref.at[:, tile(at)])
        leave(slopes.at[at], slope_ref.at[:, tile(at)])
        grad_hidden = dot(d_ref[...], down_t[:, tile(at)], NN) * slope
        total += dot(grad_hidden.astype(jnp.bfloat16), up_t[tile(at), :], NN)
    unit, inverse = normalised(middle[...])
    grad = d_ref[...].astype(jnp.float32) + norm_back(unit, inverse, gains[1:2, :], total)
    grad = grad.astype(jnp.bfloat16)
    grad_ref[...] = grad
    grad_att_ref[...] = dot(grad, out_t[...], NN).astype(jnp.bfloat16)
    for copy in copies:
        copy.wait()


def turn(entry, attended, result_gradient, gains, biases, w_out, w_up, out_t, up_t, down_t):
    rows = entry.shape[0]
    wide, narrow = jnp.float32, jnp.bfloat16
    inner = w_up.shape[2]
    steps = inner // D
    far = [((rows, D), wide), ((rows, D), narrow), ((rows, inner), narrow), ((rows, inner), narrow)]
    return pl.pallas_call(
        turn_kernel,
        in_specs=[VMEM_SPEC] * 10,
        out_specs=[pl.BlockSpec(memory_space=pltpu.HBM)] * len(far) + [VMEM_SPEC] * 2,
        out_shape=[placed(*out, pltpu.HBM) for out in far] + [placed((rows, D), narrow)] * 2,
        scratch_shapes=[
            pltpu.VMEM((rows, D), wide),
            pltpu.VMEM((rows, D), narrow),
            pltpu.VMEM((steps, rows, D), narrow),
            pltpu.VMEM((steps, rows, D), narrow),
            pltpu.SemaphoreType.DMA((2 + 2 * steps,)),
        ],
        compiler_params=pltpu.CompilerParams(vmem_limit_bytes=18 * 1024 * 1024),
        cost_estimate=cost(2 * rows * (2 * D * D + 3 * w_up.size)),
        name="turn",
    )(entry, attended, result_gradient, gains, biases, w_out, w_up, out_t, up_t, down_t)


def down_back_kernel(
    d_ref, slope_ref, middle_ref, gains, out_t, up_t, down_t,
    hidden_ref, grad_ref, grad_att_ref, sums_ref, up_ref,
):
    sums = [jnp.zeros((1, D), jnp.float32)] * 4
    steps = up_t.shape[0] // D
    up_sums = [jnp.zeros((1, D), jnp.float32)] * steps
    for part in row_chunks(d_ref.shape[0]):
        given = d_ref[part, :]
        through = jnp.zeros(given.shape, jnp.float32)
        for at in range(steps):
            grad_hidden = dot(given, down_t[:, tile(at)], NN) * slope_ref[part, tile(at)].astype(jnp.float32)
            up_sums[at] = up_sums[at] + column_sum(grad_hidden)
            grad_hidden = grad_hidden.astype(jnp.bfloat16)
            hidden_ref[part, tile(at)] = grad_hidden
            through += dot(grad_hidden, up_t[tile(at), :], NN)
        unit, inverse = normalised(middle_ref[part, :])
        given = given.astype(jnp.float32)
        grad = given + norm_back(unit, inverse, gains[1:2, :], through)
        grad_b = grad.astype(jnp.bfloat16)
        grad_ref[part, :] = grad_b
        grad_att_ref[part, :] = dot(grad_b, out_t[...], NN).astype(jnp.bfloat16)
        for at, term in enumerate((through * unit, through, grad, given)):
            sums[at] = sums[at] + column_sum(term)
    sums_ref[...] = jnp.concatenate(sums, axis=0)
    up_ref[...] = jnp.concatenate(up_sums, axis=0)


def down_back(result_gradient, slope, middle, gains, out_t, up_t, down_t):
    rows = result_gradient.shape[0]
    wide, narrow = jnp.float32, jnp.bfloat16
    inner = up_t.shape[0]
    outs = [
        ((rows, inner), narrow), ((rows, D), narrow), ((rows, D), narrow),
        ((4, D), wide), ((inner // D, D), wide),
    ]
    return call(
        down_back_kernel, "down_back", 8, 2 * rows * (D * D + 2 * up_t.size), outs, [],
        result_gradient, slope, middle, gains, out_t, up_t, down_t,
    )


def qkv_tiles(part, q_ref, own_ref, there_ref):
    tiles = [q_ref[part, :]]
    for at in range(2):
        total = own_ref[at, part, :].astype(jnp.float32) + there_ref[at, part, :].astype(jnp.float32)
        tiles.append(total.astype(jnp.bfloat16))
    return tiles


def front_back_kernel(q_ref, own_ref, there_ref, x_ref, grad_ref, gains, qkv_t, out_ref, sums_ref):
    sums = [jnp.zeros((1, D), jnp.float32)] * 4
    for part in row_chunks(x_ref.shape[0]):
        tiles = qkv_tiles(part, q_ref, own_ref, there_ref)
        through = sum(dot(value, qkv_t[tile(at), :], NN) for at, value in enumerate(tiles))
        unit, inverse = normalised(x_ref[part, :].astype(jnp.float32))
        out = grad_ref[part, :].astype(jnp.float32) + norm_back(unit, inverse, gains[0:1, :], through)
        out_ref[part, :] = out.astype(out_ref.dtype)
        terms = (through * unit, through, tiles[0].astype(jnp.float32), tiles[2].astype(jnp.float32))
        for at, term in enumerate(terms):
            sums[at] = sums[at] + column_sum(term)
    sums_ref[...] = jnp.concatenate(sums, axis=0)


def front_back(grad_q, own, there, entry, grad_middle, gains, qkv_t, dtype):
    rows = entry.shape[0]
    outs = [((rows, D), dtype, pltpu.VMEM), ((4, D), jnp.float32)]
    return call(
        front_back_kernel, "front_back", 8, 6 * rows * D * D, outs, [],
        grad_q, own, there, entry, grad_middle, gains, qkv_t,
    )


def write_blocks(place, tile, order, kept_ref, sent_ref):
    rows = kept_ref.shape[2]

    def write(core):
        for at, (z_at, y_at, core_at) in enumerate(order):
            target = kept_ref if core_at == core else sent_ref
            target[y_at, z_at] = tile[at * rows : (at + 1) * rows]

    for core in range(2):
        pl.when(place[0] == core)(functools.partial(write, core))


def weight_grad_kernel(place, left_ref, right_ref, kept_ref, sent_ref, *, order):
    tile = dot(left_ref[...], right_ref[...], NN).astype(jnp.bfloat16)
    write_blocks(place, tile, order, kept_ref, sent_ref)


def outer_grad_kernel(place, o_ref, normed_ref, d_ref, q_ref, kept_ref, sent_ref, *, order):
    for step, (left, right) in enumerate(((o_ref, d_ref), (normed_ref, q_ref))):
        pl.when(pl.program_id(0) == step)(
            functools.partial(weight_grad_kernel, place, left, right, kept_ref, sent_ref, order=order)
        )


def inner_grad_kernel(place, normed_ref, own_ref, there_ref, kept_ref, sent_ref, *, order):
    right = (own_ref[0].astype(jnp.float32) + there_ref[0].astype(jnp.float32)).astype(jnp.bfloat16)
    tile = dot(normed_ref[...], right, NN).astype(jnp.bfloat16)
    write_blocks(place, tile, order, kept_ref, sent_ref)


def all_blocks(z_count):
    return [(z_at, y_at, core) for z_at in range(z_count) for y_at in range(2) for core in range(2)]


def blocks_call(
    kernel, name, grid, order, in_specs, out_spec, block, width, z_count, flops, place, *operands, space=None
):
    shape = placed((2, z_count, block, width), jnp.bfloat16, space)
    return pl.pallas_call(
        functools.partial(kernel, order=order),
        grid_spec=pltpu.PrefetchScalarGridSpec(
            num_scalar_prefetch=1, grid=(grid,), in_specs=in_specs, out_specs=[out_spec, out_spec]
        ),
        out_shape=[shape, shape],
        compiler_params=pltpu.CompilerParams(vmem_limit_bytes=9 * 1024 * 1024),
        cost_estimate=cost(flops),
        name=name,
    )(place, *operands)


def column_blocks(block, z_count):
    return pl.BlockSpec((2, z_count, block, D), lambda i, _: (0, 0, 0, i))


def down_grad(place, active_t, back, z_count):
    height, rows = active_t.shape
    block = height // (4 * z_count)
    specs = [pl.BlockSpec((height // z_count, rows), lambda i, _: (i, 0)), whole(rows, D)]
    out_spec = pl.BlockSpec((2, 1, block, D), lambda i, _: (0, i, 0, 0))
    order = [(0, y_at, core) for y_at in range(2) for core in range(2)]
    return blocks_call(
        weight_grad_kernel, "down_grad", z_count, order, specs, out_spec, block, D, z_count,
        2 * rows * height * D, place, active_t, back, space=pltpu.HBM,
    )


def up_grad(place, normed_t, grad_hidden, z_count):
    rows, width = grad_hidden.shape
    block = D // (4 * z_count)
    specs = [whole(D, rows), pl.BlockSpec((rows, D), lambda i, _: (0, i))]
    return blocks_call(
        weight_grad_kernel, "up_grad", width // D, all_blocks(z_count), specs, column_blocks(block, z_count),
        block, width, z_count, 2 * rows * width * D, place, normed_t, grad_hidden, space=pltpu.HBM,
    )


def outer_grad(place, attended_t, normed_t, grad_middle, grad_q, z_count):
    rows = grad_q.shape[0]
    block = D // (4 * z_count)
    specs = [whole(D, rows)] * 2 + [whole(rows, D)] * 2
    return blocks_call(
        outer_grad_kernel, "outer_grad", 2, all_blocks(z_count), specs, column_blocks(block, z_count),
        block, 2 * D, z_count, 4 * rows * D * D, place, attended_t, normed_t, grad_middle, grad_q,
    )


def inner_grad(place, normed_t, own, there, z_count):
    rows = own.shape[1]
    block = D // (4 * z_count)
    part = pl.BlockSpec((1, rows, D), lambda i, _: (i, 0, 0))
    return blocks_call(
        inner_grad_kernel, "inner_grad", 2, all_blocks(z_count), [whole(D, rows), part, part],
        column_blocks(block, z_count), block, 2 * D, z_count, 4 * rows * D * D, place, normed_t, own, there,
    )


def added(kept, arrived, dtype=jnp.bfloat16):
    return (kept.astype(jnp.float32) + arrived.astype(jnp.float32)).astype(dtype)


def fold_kernel(place, kept_ref, arrived_ref, keep_ref, send_ref):
    for target, chosen in ((send_ref, 1 - place[0]), (keep_ref, place[0])):
        for at in range(target.shape[0]):
            target[at] = added(kept_ref[at, chosen], arrived_ref[at, chosen])


def fold(kept, arrived, place, outer):
    width = kept.shape[-1]
    lead = math.prod(kept.shape[:outer])
    inner = math.prod(kept.shape[outer + 1 : -1])
    shape = (lead, 2, inner, width)
    outs = [((lead, inner, width), kept.dtype)] * 2
    keep, send = call(
        fold_kernel, "fold", 4, 0, outs, [], place, kept.reshape(shape), arrived.reshape(shape), smem=1
    )
    left = kept.shape[:outer] + kept.shape[outer + 1 :]
    return keep.reshape(left), send.reshape(left)


def fold_halves_kernel(place, kept_ref, arrived_ref, y_keep, y_send, z_keep, z_send):
    y_at, z_at = place[0], place[1]
    half = y_keep.shape[1]
    first, second = slice(0, half), slice(half, 2 * half)
    for target, chosen in ((y_send, 1 - y_at), (y_keep, y_at)):
        for z_block in range(target.shape[0]):
            target[z_block] = added(kept_ref[chosen, z_block, first], arrived_ref[chosen, z_block, first])
    for target, chosen in ((z_send, 1 - z_at), (z_keep, z_at)):
        for y_block in range(2):
            for high in range(target.shape[1]):
                at = 2 * high + chosen
                target[y_block, high] = added(kept_ref[y_block, at, second], arrived_ref[y_block, at, second])


def fold_halves(kept, arrived, place):
    _, z_count, block, width = kept.shape
    y_shape, z_shape = (z_count, block // 2, width), (2, z_count // 2, block // 2, width)
    outs = [(shape, kept.dtype) for shape in (y_shape, y_shape, z_shape, z_shape)]
    return call(fold_halves_kernel, "fold_halves", 6, 0, outs, [], place, kept, arrived, smem=1)


def fold_columns_kernel(place, kept_a, arrived_a, kept_b, arrived_b, keep_ref, send_ref):
    width = kept_a.shape[-1]
    for target, chosen in ((send_ref, 1 - place[0]), (keep_ref, place[0])):
        for at in range(target.shape[0]):
            target[at, :, :width] = added(kept_a[chosen, at], arrived_a[chosen, at])
            target[at, :, width:] = added(kept_b[chosen, at], arrived_b[chosen, at])


def fold_columns(first, second, place):
    _, z_count, block, width = first[0].shape
    outs = [((z_count, block, 2 * width), jnp.bfloat16)] * 2
    return call(fold_columns_kernel, "fold_columns", 6, 0, outs, [], place, *first, *second, smem=1)


def fold_rows_kernel(place, kept_a, arrived_a, kept_b, arrived_b, keep_ref, send_ref):
    rows = kept_a.shape[1]
    for target, chosen in ((send_ref, 1 - place[0]), (keep_ref, place[0])):
        target[:rows] = added(kept_a[chosen], arrived_a[chosen])
        target[rows:] = added(kept_b[chosen], arrived_b[chosen])


def fold_rows(first, second, place):
    _, block, width = first[0].shape
    outs = [((2 * block, width), jnp.bfloat16)] * 2
    return call(fold_rows_kernel, "fold_rows", 4, 0, outs, [], place, *first, *second, smem=1)


def stream_fold_kernel(place, kept_keep, kept_send, arrived_keep, arrived_send, keep_ref, send_ref):
    send_ref[...] = added(kept_send[...], arrived_send[...])
    keep_ref[...] = added(kept_keep[...], arrived_keep[...])


def stream_fold(kept, arrived, place, outer):
    width = kept.shape[-1]
    lead = math.prod(kept.shape[:outer])
    inner = math.prod(kept.shape[outer + 1 : -1])
    parts = 1 if lead > 1 else 4
    shape = (lead, 2, inner, width)
    block = (None, None, inner // parts, width)
    keep_spec = pl.BlockSpec(block, lambda i, place: (i // parts, place[0], i % parts, 0))
    send_spec = pl.BlockSpec(block, lambda i, place: (i // parts, 1 - place[0], i % parts, 0))
    out_spec = pl.BlockSpec(block[1:], lambda i, place: (i // parts, i % parts, 0))
    left = kept.shape[:outer] + kept.shape[outer + 1 :]
    kept, arrived = [in_hbm(value.reshape(shape)) for value in (kept, arrived)]
    keep, send = pl.pallas_call(
        stream_fold_kernel,
        grid_spec=pltpu.PrefetchScalarGridSpec(
            num_scalar_prefetch=1,
            grid=(lead * parts,),
            in_specs=[keep_spec, send_spec] * 2,
            out_specs=[out_spec, out_spec],
        ),
        out_shape=[jax.ShapeDtypeStruct((lead, inner, width), jnp.bfloat16)] * 2,
        compiler_params=pltpu.CompilerParams(vmem_limit_bytes=6 * 1024 * 1024),
        cost_estimate=cost(0),
        name="stream_fold",
    )(place, kept, kept, arrived, arrived)
    return keep.reshape(left), send.reshape(left)


def shifted(value, axis, steps):
    count = lax.axis_size(axis)
    initial, last = (max(0, -steps), min(count, count - steps))
    return lax.ppermute(value, axis, [(source, source + steps) for source in range(initial, last)])


def layer_norm(inputs_row, gain_row, offset):
    center = inputs_row - jnp.mean(inputs_row, axis=-1, keepdims=True)
    spread = jnp.mean(center * center, axis=-1, keepdims=True)
    return center * lax.rsqrt(spread + 1e-05) * gain_row + offset


def gelu_tanh(hidden):
    return jax.nn.gelu(hidden, approximate=True)


def score_terms(queries, key_rows, query_pos, key_pos, signed):
    key_count = key_rows.shape[0]
    scores = (
        jnp.einsum(
            "rhe,khe->hrk",
            queries,
            key_rows.reshape(key_count, HEADS, HDIM),
            preferred_element_type=jnp.float32,
        )
        * 0.125
    )
    curved = jnp.sqrt(scores * scores + 1.0)
    argument = jnp.where(signed, curved, scores)
    sign_pattern = jnp.where(signed, scores / curved, 1.0)
    slope = jnp.where(signed, sign_pattern, 1.0)
    bend = jnp.where(signed, 1.0 / (curved * curved * curved), 0.0)
    permitted_mask = key_pos[None, None, :] <= query_pos[None, :, None]
    return (argument, sign_pattern, slope, bend, permitted_mask)


def score_grads(
    queries, key_rows, value_rows, query_pos, key_pos, log_total, delta, grad_att, signed
):
    argument, sign_pattern, slope, bend, permitted_mask = score_terms(
        queries, key_rows, query_pos, key_pos, signed
    )
    prob = jnp.where(permitted_mask, jnp.exp(argument - log_total[..., None]), 0.0)
    along = jnp.einsum("rhe,khe->hrk", grad_att, value_rows, preferred_element_type=jnp.float32)
    dscore = (prob * ((sign_pattern * along - delta[..., None]) * slope + along * bend)).astype(
        jnp.bfloat16
    )
    return ((sign_pattern * prob).astype(jnp.bfloat16), dscore)


def key_blocks_of(key_all, value_all, key_pos, key_block):
    blocks = key_all.shape[0] // key_block
    return (
        key_all.reshape(blocks, key_block, D),
        value_all.reshape(blocks, key_block, HEADS, HDIM),
        key_pos.reshape(blocks, key_block),
    )


def attend(queries, query_pos, key_all, value_all, key_pos, signed, key_block):
    row_count = queries.shape[0]
    key_split, value_split, pos_split = key_blocks_of(key_all, value_all, key_pos, key_block)

    def running_total(state_in, element):
        largest, row_total_sum, gathered = state_in
        key_rows, value_rows, block_pos = element
        argument, sign_pattern, _, _, permitted_mask = score_terms(
            queries, key_rows, query_pos, block_pos, signed
        )
        masked_scores = jnp.where(permitted_mask, argument, -1e30)
        exponent_values = jnp.maximum(largest, jnp.max(masked_scores, axis=-1))
        multiplier = jnp.exp(largest - exponent_values)
        added_terms = jnp.where(
            permitted_mask, jnp.exp(masked_scores - exponent_values[..., None]), 0.0
        )
        row_total_sum = row_total_sum * multiplier + jnp.sum(added_terms, axis=-1)
        attention_weights = (sign_pattern * added_terms).astype(jnp.bfloat16)
        added = jnp.einsum(
            "hrk,khe->rhe", attention_weights, value_rows, preferred_element_type=jnp.float32
        )
        gathered = gathered * multiplier.T[:, :, None] + added
        return ((exponent_values, row_total_sum, gathered), None)

    start_max = jnp.full((HEADS, row_count), -1e30, jnp.float32)
    start_sum = jnp.zeros((HEADS, row_count), jnp.float32)
    start_out = jnp.zeros((row_count, HEADS, HDIM), jnp.float32)
    (largest, row_total_sum, gathered), _ = lax.scan(
        running_total, (start_max, start_sum, start_out), (key_split, value_split, pos_split)
    )
    log_total = largest + jnp.log(row_total_sum)
    attended = gathered / row_total_sum.T[:, :, None]
    return (attended, log_total)


def backward_summed(
    queries, query_pos, key_all, value_all, key_pos, log_total, delta, grad_att, signed, key_block
):
    key_split, value_split, pos_split = key_blocks_of(key_all, value_all, key_pos, key_block)

    def step_back(grad_q, element):
        key_rows, value_rows, block_pos = element
        attention_weights, dscore = score_grads(
            queries, key_rows, value_rows, query_pos, block_pos, log_total, delta, grad_att, signed
        )
        grad_q = (
            grad_q
            + jnp.einsum(
                "hrk,khe->rhe",
                dscore,
                key_rows.reshape(-1, HEADS, HDIM),
                preferred_element_type=jnp.float32,
            )
            * 0.125
        )
        grad_k = (
            jnp.einsum("hrk,rhe->khe", dscore, queries, preferred_element_type=jnp.float32) * 0.125
        )
        grad_v = jnp.einsum(
            "hrk,rhe->khe", attention_weights, grad_att, preferred_element_type=jnp.float32
        )
        return (grad_q, (grad_k.reshape(key_block, D), grad_v.reshape(key_block, D)))

    start_q = jnp.zeros(queries.shape, jnp.float32)
    grad_q, (grad_k, grad_v) = lax.scan(step_back, start_q, (key_split, value_split, pos_split))
    grad_k, grad_v = (
        lax.psum_scatter(
            grad_k.reshape(-1, D).astype(jnp.bfloat16), "ctx", scatter_dimension=0, tiled=True
        ).astype(jnp.float32),
        lax.psum_scatter(
            grad_v.reshape(-1, D).astype(jnp.bfloat16), "ctx", scatter_dimension=0, tiled=True
        ).astype(jnp.float32),
    )
    return (grad_q.reshape(-1, D), grad_k, grad_v)


def layer_front(inputs_row, gain_pair, bias_row, qkv_w):
    normed = layer_norm(inputs_row, gain_pair[0], bias_row[0:D]).astype(jnp.bfloat16)
    qkv_bias = jnp.concatenate(
        [bias_row[2 * D : 3 * D], jnp.zeros((D,), jnp.float32), bias_row[3 * D : 4 * D]]
    )
    projected = (jnp.dot(normed, qkv_w, preferred_element_type=jnp.float32) + qkv_bias).astype(
        jnp.bfloat16
    )
    return (normed, projected)


def layer_rest(inputs_row, attended_b, gain_pair, bias_row, out_w, up_w, down_w):
    middle = (
        inputs_row
        + jnp.dot(attended_b, out_w, preferred_element_type=jnp.float32)
        + bias_row[4 * D : 5 * D]
    )
    normed_two = layer_norm(middle, gain_pair[1], bias_row[D : 2 * D]).astype(jnp.bfloat16)
    hidden = jnp.dot(normed_two, up_w, preferred_element_type=jnp.float32) + bias_row[6 * D :]
    active = gelu_tanh(hidden).astype(jnp.bfloat16)
    result = (
        middle
        + jnp.dot(active, down_w, preferred_element_type=jnp.float32)
        + bias_row[5 * D : 6 * D]
    )
    return (middle, normed_two, hidden, active, result)


def general_body(inputs, slot_order, cotangent, gains, biases, w_qkv, w_out, w_up, w_down):
    micro_count = inputs.shape[0]
    row_count = inputs.shape[2]
    section_at = lax.axis_index("section")
    ctx_at = lax.axis_index("ctx")
    signed = section_at == 0
    gain_pair = gains[0]
    bias_row = biases[0]
    qkv_w = w_qkv[0]
    out_w = w_out[0]
    up_w = w_up[0]
    down_w = w_down[0]
    span_len = row_count // 2
    seq_pos = (
        slot_order[:, 0, :, None] * span_len + jnp.arange(span_len, dtype=jnp.int32)
    ).reshape(micro_count, -1)
    key_block = min(seq_pos.shape[1], 512)
    first_inputs = inputs[:, 0]
    cot_rows = cotangent[:, 0]

    def sequence_pos(index):
        whole_pos = lax.dynamic_index_in_dim(seq_pos, index, 0, keepdims=False)
        own_pos = lax.dynamic_slice_in_dim(whole_pos, ctx_at * row_count, row_count, 0)
        return (whole_pos, own_pos)

    def layer_forward(entry, index):
        whole_pos, own_pos = sequence_pos(index)
        inputs_row = entry.astype(jnp.float32)
        normed, projected = layer_front(inputs_row, gain_pair, bias_row, qkv_w)
        key_all, value_all = (
            lax.all_gather(projected[:, D : 2 * D], "ctx", axis=0, tiled=True),
            lax.all_gather(projected[:, 2 * D :], "ctx", axis=0, tiled=True),
        )
        queries = projected[:, :D].reshape(row_count, HEADS, HDIM)
        attended, _ = attend(queries, own_pos, key_all, value_all, whole_pos, signed, key_block)
        attended_b = attended.reshape(row_count, D).astype(jnp.bfloat16)
        result = layer_rest(inputs_row, attended_b, gain_pair, bias_row, out_w, up_w, down_w)[4]
        return result.astype(jnp.bfloat16)

    def layer_reverse_pass(entry, result_gradient, index):
        whole_pos, own_pos = sequence_pos(index)
        inputs_row = entry.astype(jnp.float32)
        normed, projected = layer_front(inputs_row, gain_pair, bias_row, qkv_w)
        queries = projected[:, :D].reshape(row_count, HEADS, HDIM)
        key_all, value_all = (
            lax.all_gather(projected[:, D : 2 * D], "ctx", axis=0, tiled=True),
            lax.all_gather(projected[:, 2 * D :], "ctx", axis=0, tiled=True),
        )
        attended, log_total = attend(
            queries, own_pos, key_all, value_all, whole_pos, signed, key_block
        )
        attended_b = attended.reshape(row_count, D).astype(jnp.bfloat16)
        middle, normed_two, hidden, active, _ = layer_rest(
            inputs_row, attended_b, gain_pair, bias_row, out_w, up_w, down_w
        )
        grad_down_b = result_gradient.astype(jnp.bfloat16)
        grad_wdown = jnp.dot(active.T, grad_down_b, preferred_element_type=jnp.float32)
        grad_active = jnp.dot(grad_down_b, down_w.T, preferred_element_type=jnp.float32)
        _, gelu_back = jax.vjp(gelu_tanh, hidden)
        grad_hidden = gelu_back(grad_active)[0]
        grad_hidden_b = grad_hidden.astype(jnp.bfloat16)
        grad_wup = jnp.dot(normed_two.T, grad_hidden_b, preferred_element_type=jnp.float32)
        grad_normed_two = jnp.dot(grad_hidden_b, up_w.T, preferred_element_type=jnp.float32)
        _, norm_back_two = jax.vjp(layer_norm, middle, gain_pair[1], bias_row[D : 2 * D])
        grad_middle_part, grad_gain_two, grad_offset_two = norm_back_two(grad_normed_two)
        grad_middle = result_gradient + grad_middle_part
        grad_proj_b = grad_middle.astype(jnp.bfloat16)
        grad_wout = jnp.dot(attended_b.T, grad_proj_b, preferred_element_type=jnp.float32)
        grad_att_flat = jnp.dot(grad_proj_b, out_w.T, preferred_element_type=jnp.float32).astype(
            jnp.bfloat16
        )
        grad_att = grad_att_flat.reshape(row_count, HEADS, HDIM)
        delta = jnp.einsum("rhe,rhe->hr", grad_att.astype(jnp.float32), attended)
        grad_q, grad_k, grad_v = backward_summed(
            queries,
            own_pos,
            key_all,
            value_all,
            whole_pos,
            log_total,
            delta,
            grad_att,
            signed,
            key_block,
        )
        grad_qkv_b = jnp.concatenate([grad_q, grad_k, grad_v], axis=1).astype(jnp.bfloat16)
        grad_wqkv = jnp.dot(normed.T, grad_qkv_b, preferred_element_type=jnp.float32)
        grad_normed = jnp.dot(grad_qkv_b, qkv_w.T, preferred_element_type=jnp.float32)
        _, norm_back_one = jax.vjp(layer_norm, inputs_row, gain_pair[0], bias_row[0:D])
        grad_in_part, grad_gain_one, grad_offset_one = norm_back_one(grad_normed)
        input_gradient = grad_middle + grad_in_part
        grad_gain_rows = jnp.stack([grad_gain_one, grad_gain_two])
        grad_bias_row = jnp.concatenate(
            [
                grad_offset_one,
                grad_offset_two,
                jnp.sum(grad_q, axis=0),
                jnp.sum(grad_v, axis=0),
                jnp.sum(grad_middle, axis=0),
                jnp.sum(result_gradient, axis=0),
                jnp.sum(grad_hidden, axis=0),
            ]
        )
        return (
            input_gradient,
            (grad_gain_rows, grad_bias_row, grad_wqkv, grad_wout, grad_wup, grad_wdown),
        )

    def tick(tick_at, state_in):
        arrived, returned, stored, acts_rows, grad_rows, partial_sums = state_in
        ahead = tick_at - section_at
        ahead_ok = (ahead >= 0) & (ahead < micro_count)
        ahead_at = jnp.clip(ahead, 0, micro_count - 1)
        fresh = jnp.where(
            signed, lax.dynamic_index_in_dim(first_inputs, ahead_at, 0, keepdims=False), arrived
        )
        previous = lax.dynamic_index_in_dim(stored, ahead_at, 0, keepdims=False)
        entry = jnp.where(ahead_ok, fresh, previous)
        stored = lax.dynamic_update_index_in_dim(stored, entry, ahead_at, 0)
        sent = layer_forward(entry, ahead_at)
        old_acts = lax.dynamic_index_in_dim(acts_rows, ahead_at, 0, keepdims=False)
        acts_rows = lax.dynamic_update_index_in_dim(
            acts_rows, jnp.where(ahead_ok, sent, old_acts), ahead_at, 0
        )
        behind = tick_at - 2 + section_at
        trailing_valid = (behind >= 0) & (behind < micro_count)
        trailing_position = jnp.clip(behind, 0, micro_count - 1)
        entry_gradient = lax.dynamic_index_in_dim(stored, trailing_position, 0, keepdims=False)
        given_cot = lax.dynamic_index_in_dim(cot_rows, trailing_position, 0, keepdims=False).astype(
            jnp.float32
        )
        result_gradient = jnp.where(signed, returned.astype(jnp.float32), given_cot)
        input_gradient, added_terms = layer_reverse_pass(
            entry_gradient, result_gradient, trailing_position
        )
        partial_sums = jax.tree.map(
            lambda running_total, added_term: running_total
            + jnp.where(trailing_valid, added_term, 0.0),
            partial_sums,
            added_terms,
        )
        handed = input_gradient.astype(jnp.bfloat16)
        kept_grad = jnp.where(signed, input_gradient, handed.astype(jnp.float32))
        old_grads = lax.dynamic_index_in_dim(grad_rows, trailing_position, 0, keepdims=False)
        grad_rows = lax.dynamic_update_index_in_dim(
            grad_rows, jnp.where(trailing_valid, kept_grad, old_grads), trailing_position, 0
        )
        arrived = shifted(sent, "section", 1)
        returned = shifted(handed, "section", -1)
        return (arrived, returned, stored, acts_rows, grad_rows, partial_sums)

    zero_rows = jnp.zeros((row_count, D), jnp.bfloat16)
    start_sums = (
        jnp.zeros((2, D), jnp.float32),
        jnp.zeros((bias_row.shape[0],), jnp.float32),
        jnp.zeros(qkv_w.shape, jnp.float32),
        jnp.zeros(out_w.shape, jnp.float32),
        jnp.zeros(up_w.shape, jnp.float32),
        jnp.zeros(down_w.shape, jnp.float32),
    )
    start_state = (
        zero_rows,
        zero_rows,
        jnp.zeros((micro_count, row_count, D), jnp.bfloat16),
        jnp.zeros((micro_count, row_count, D), jnp.bfloat16),
        jnp.zeros((micro_count, row_count, D), jnp.float32),
        start_sums,
    )
    final_state = lax.fori_loop(0, micro_count + 2, tick, start_state)
    acts_rows = final_state[3]
    grad_rows = final_state[4]
    partial_sums = final_state[5]
    totals = (
        lax.psum_scatter(partial_sums[0], ("dp", "ctx"), scatter_dimension=1, tiled=True),
        lax.psum_scatter(partial_sums[1], ("dp", "ctx"), scatter_dimension=0, tiled=True),
        lax.psum_scatter(partial_sums[2], ("dp", "ctx"), scatter_dimension=0, tiled=True),
        lax.psum_scatter(partial_sums[3], ("dp", "ctx"), scatter_dimension=0, tiled=True),
        lax.psum_scatter(partial_sums[4], ("dp", "ctx"), scatter_dimension=0, tiled=True),
        lax.psum_scatter(partial_sums[5], ("dp", "ctx"), scatter_dimension=0, tiled=True),
    )
    return (
        acts_rows[None, :, None],
        grad_rows[None, :, None],
        totals[0][None],
        totals[1][None],
        totals[2][None],
        totals[3][None],
        totals[4][None],
        totals[5][None],
    )


def swap_halves(value):
    count = lax.axis_size("ctx")
    return lax.ppermute(value, "ctx", [(at, (at + count // 2) % count) for at in range(count)])


def swap_cores(value):
    return lax.ppermute(value, "ctx", [(at, at ^ 1) for at in range(lax.axis_size("ctx"))])


def swap_z(value, step):
    return lax.ppermute(value, "dp", [(at, at ^ step) for at in range(lax.axis_size("dp"))])


def wide_sum(kept, arrived):
    return kept.astype(jnp.float32) + arrived.astype(jnp.float32)


def fast_body(inputs, slot_order, cotangent, gains, biases, w_qkv, w_out, w_up, w_down):
    rows = inputs.shape[2]
    count = lax.axis_size("ctx")
    z_count = lax.axis_size("dp")
    half = count // 2
    ctx_at = lax.axis_index("ctx")
    mine = ctx_at // half
    y_at, core_at = ctx_at // 2, ctx_at % 2
    signed = lax.axis_index("section") == 0
    place = core_at[None].astype(jnp.int32)
    y_place = y_at[None].astype(jnp.int32)
    z_at = lax.axis_index("dp")
    gain_pair = gains[0]
    wide, narrow, barrier = jnp.float32, jnp.bfloat16, lax.optimization_barrier

    def gathered(value):
        kept = lax.dynamic_index_in_dim(value, mine, 0, keepdims=False)
        sent = lax.dynamic_index_in_dim(value, 1 - mine, 0, keepdims=False)
        return jnp.concatenate([kept, swap_halves(sent)], axis=0)

    def returned(kept, arrived):
        arrived = arrived.astype(kept.dtype)
        first = jnp.where(mine == 0, kept, arrived)
        second = jnp.where(mine == 0, arrived, kept)
        return jnp.stack([first, second])

    order = lax.dynamic_index_in_dim(slot_order[:, 0], mine, 0, keepdims=False)
    pairs = order.reshape(count, 2)

    def slots_of(device):
        return jnp.concatenate([pairs[device], pairs[(device + half) % count]])

    meta = slot_meta(slots_of(ctx_at), slots_of(ctx_at ^ 1), signed)

    def through_attention(entry, keep):
        normed, queries, kv = front(entry, gain_pair, biases, w_qkv)
        there = swap_cores(kv)
        normed_t = None
        if keep:
            normed_t = flip(normed, pltpu.HBM)
            there, normed_t = barrier((there, normed_t))
        attended, lse = sorted_attend(meta, queries, kv, there)
        return normed_t, queries, kv, there, attended, lse

    inputs, meta = barrier((inputs, meta))
    first = gathered(inputs[:, 0])
    qkv_t, out_t = flip(w_qkv, pltpu.HBM), flip(w_out, pltpu.HBM)
    first, qkv_t, out_t = barrier((first, qkv_t, out_t))
    attended = through_attention(first, False)[4]
    sent = rest(first, attended, gain_pair, biases, w_out, w_up, w_down)
    sent, later = barrier((sent, (cotangent, w_up, w_down)))
    arrived = shifted(sent, "section", 1)
    given = gathered(later[0][:, 0])
    up_t, down_t = [flip(weight, pltpu.HBM) for weight in later[1:]]
    arrived, given, up_t, down_t = barrier((arrived, given, up_t, down_t))
    entry = jnp.where(signed, first, arrived)

    normed_t, queries, kv, kv_there, attended, lse = through_attention(entry, True)
    middle, normed_two, active, slope, grad_middle, grad_att = turn(
        entry, attended, given, gain_pair, biases, w_out, w_up, out_t, up_t, down_t
    )

    waiting = meta.at[-1].set(jnp.where(signed, IDLE, 0))
    grad_q, own, sent = sorted_attend_back(waiting, queries, kv, kv_there, attended, grad_att, lse)
    own, sent, attended, normed_two = barrier((own, sent, attended, normed_two))
    there = swap_cores(sent)
    attended_t, normed_two_t = flip(attended, pltpu.HBM), flip(normed_two, pltpu.HBM)
    there, attended_t, normed_two_t = barrier((there, attended_t, normed_two_t))
    handed, _ = front_back(grad_q, own, there, entry, grad_middle, gain_pair, qkv_t, narrow)
    handed, active, middle, weights = barrier((handed, active, middle, (w_up, w_down)))
    back = shifted(handed, "section", -1)
    result = middle + dot(active, w_down[0], NN) + biases[0, 5 * D : 6 * D]
    result = result.astype(narrow)
    acts_there = swap_halves(result[rows:])
    middle, acts_there, active = barrier((middle, acts_there, active))
    up_t, down_t = [flip(in_hbm(weight), pltpu.VMEM) for weight in weights]
    active_t = flip(active, pltpu.VMEM)
    back, up_t, down_t, active_t = barrier((back, up_t, down_t, active_t))
    back = jnp.where(signed, back, given)

    z_steps = [1 << at for at in range(z_count.bit_length() - 1)]
    split = [2] * len(z_steps)
    by_z = [((z_at >> at) & 1)[None].astype(jnp.int32) for at in range(len(z_steps))]

    def bits(value, before):
        return value.reshape(value.shape[:before] + tuple(split) + value.shape[before + 1 :])

    grad_hidden, grad_middle, grad_att, sums_two, up_sum = down_back(
        back, slope, middle, gain_pair, out_t, up_t, down_t
    )
    back, grad_hidden = barrier((back, grad_hidden))
    down_kept, down_sent = down_grad(place, active_t, back, z_count)
    grad_hidden, down_sent = barrier((grad_hidden, down_sent))
    down_there = swap_cores(down_sent)
    up_kept, up_sent = up_grad(place, normed_two_t, grad_hidden, z_count)
    down_there, up_sent = barrier((down_there, up_sent))
    up_there = swap_cores(up_sent)
    down_kept, down_sent = stream_fold(down_kept, down_there, y_place, 0)
    up_there, down_sent = barrier((up_there, down_sent))
    up_kept, up_sent = stream_fold(bits(up_kept, 1), bits(up_there, 1), by_z[0], len(split))
    grad_att, down_sent, up_sent = barrier((grad_att, down_sent, up_sent))
    down_there, up_there = swap_halves(down_sent), swap_z(up_sent, z_steps[0])
    grad_q, own, sent = sorted_attend_back(meta, queries, kv, kv_there, attended, grad_att, lse)

    grad_q, own, sent, down_there, up_there = barrier((grad_q, own, sent, down_there, up_there))
    there = swap_cores(sent)
    outer_kept, outer_sent = outer_grad(place, attended_t, normed_t, grad_middle, grad_q, z_count)
    there, outer_sent = barrier((there, outer_sent))
    outer_there = swap_cores(outer_sent)
    inner_kept, inner_sent = inner_grad(place, normed_t, own, there, z_count)
    inner_sent, down_there, up_there = barrier((inner_sent, down_there, up_there))
    inner_there = swap_cores(inner_sent)
    down_kept, down_sent = fold(bits(down_kept, 0), bits(down_there, 0), by_z[0], len(split) - 1)
    up_kept, up_sent = fold(up_kept, up_there, by_z[1], 1)
    outer_there, inner_there, down_sent, up_sent = barrier((outer_there, inner_there, down_sent, up_sent))
    rest_kept, rest_sent = fold_columns((outer_kept, outer_there), (inner_kept, inner_there), y_place)
    rest_sent, down_sent, up_sent, grad_q, own, there = barrier((rest_sent, down_sent, up_sent, grad_q, own, there))
    rest_there, down_there, up_there = swap_halves(rest_sent), swap_z(down_sent, z_steps[0]), swap_z(up_sent, z_steps[1])
    input_gradient, sums_one = front_back(grad_q, own, there, entry, grad_middle, gain_pair, qkv_t, wide)
    small = jnp.concatenate([sums_one, sums_two, up_sum], axis=0)
    small = small + swap_cores(small)
    rounded = input_gradient.astype(narrow)
    small, rounded = barrier((small, rounded))
    small = small + swap_z(small, z_steps[0])
    rest_there, down_there, up_there, small = barrier((rest_there, down_there, up_there, small))

    rest_kept, rest_sent = fold(bits(rest_kept, 0), bits(rest_there, 0), by_z[0], len(split) - 1)
    rest_there = swap_z(rest_sent, z_steps[0])
    down_kept, down_sent = fold(down_kept, down_there, by_z[1], 0)
    up_kept, up_sent = fold(up_kept, up_there, y_place, 0)
    down_there, up_there = swap_z(down_sent, z_steps[1]), swap_halves(up_sent)
    small_there = swap_z(small, z_steps[1])
    rest_there, up_there, small_there, rounded = barrier((rest_there, up_there, small_there, rounded))
    rest_kept, rest_sent = fold(rest_kept, rest_there, by_z[1], 0)
    small = small + small_there
    rest_sent, small, rounded, result, acts_there = barrier((rest_sent, small, rounded, result, acts_there))
    rest_there = swap_z(rest_sent, z_steps[1])
    small = small + swap_halves(small)
    grads_there = swap_halves(rounded[rows:])
    wdown = wide_sum(down_kept, down_there)
    wup = wide_sum(up_kept, up_there)
    grads_kept = jnp.where(signed, input_gradient[:rows], rounded[:rows].astype(wide))
    wout = wide_sum(rest_kept[:, :D], rest_there[:, :D])
    wqkv = wide_sum(rest_kept[:, D:], rest_there[:, D:])
    blocks = count * z_count
    block_at = lax.axis_index("dp") * count + ctx_at
    gain_piece = lax.dynamic_slice_in_dim(small[0:5:4], block_at * (D // blocks), D // blocks, 1)
    bias_row = jnp.concatenate([small[1:2], small[5:6], small[2:4], small[6:]], axis=0).reshape(-1)
    width = bias_row.shape[0] // blocks
    bias_piece = lax.dynamic_slice_in_dim(bias_row, block_at * width, width, 0)
    return (
        returned(result[:rows], acts_there)[None, :, None],
        returned(grads_kept, grads_there)[None, :, None],
        gain_piece[None],
        bias_piece[None],
        wqkv[None],
        wout[None],
        wup[None],
        wdown[None],
    )


def body_for(mesh):
    sizes = dict(mesh.shape)
    return fast_body if (sizes["ctx"], sizes["dp"]) == (4, 4) else general_body


def solution(mesh):
    in_specs = (
        P(None, "dp", "ctx", None),
        P(None, "dp", None),
        P(None, "dp", "ctx", None),
        P("section", None, None),
        P("section", None),
        P("section", None, None),
        P("section", None, None),
        P("section", None, None),
        P("section", None, None),
    )
    out_specs = (
        P("section", None, "dp", "ctx", None),
        P("section", None, "dp", "ctx", None),
        P("section", None, ("dp", "ctx")),
        P("section", ("dp", "ctx")),
        P("section", ("dp", "ctx"), None),
        P("section", ("dp", "ctx"), None),
        P("section", ("dp", "ctx"), None),
        P("section", ("dp", "ctx"), None),
    )
    return jax.shard_map(
        body_for(mesh), mesh=mesh, in_specs=in_specs, out_specs=out_specs, check_vma=False
    )
```

```python
import functools
import math
import jax
import jax.numpy as jnp
from jax import lax
from jax.experimental import pallas as pl
from jax.experimental.pallas import tpu as pltpu
from jax.sharding import PartitionSpec as P

D = 768
HEADS = 12
HDIM = 64
PAIR = 2 * HDIM
PAIRS = HEADS // 2
OWN = 4
CHUNK = 128
BACK_CHUNK = 1024
SAFE = 60.0
IDLE = 2
NT = (((1,), (1,)), ((), ()))
TN = (((0,), (0,)), ((), ()))
NN = (((1,), (0,)), ((), ()))


def dot(left, right, dims):
    return lax.dot_general(left, right, dims, preferred_element_type=jnp.float32)


def slot_meta(own_pos, other_pos, signed):
    rank = jnp.sum((own_pos[None, :] < own_pos[:, None]).astype(jnp.int32), axis=1)
    chosen = rank[None, :] == jnp.arange(OWN, dtype=jnp.int32)[:, None]
    ranked = jnp.sum(jnp.where(chosen, jnp.arange(OWN, dtype=jnp.int32)[None, :], 0), axis=1)
    ranked_pos = jnp.sum(jnp.where(chosen, own_pos[None, :], 0), axis=1)
    return jnp.concatenate([own_pos, other_pos, ranked, ranked_pos, signed.astype(jnp.int32)[None]])


def sort_rows(meta, own, other, target, span, first):
    columns = slice(first, first + D)
    for slot in range(OWN):
        for base, source in ((0, own), (OWN, other)):
            start = pl.multiple_of(meta[base + slot] * span, span)
            target[pl.ds(start, span), :] = source[slot * span : (slot + 1) * span, columns]


def reach(rank, slots):
    return ((0, slots // 2 - 2), (1, slots // 2 - 1), (slots // 2, slots - 2), (slots // 2 + 1, slots - 1))[rank]


def stacked_heads(rows):
    second = lax.broadcasted_iota(jnp.int32, rows.shape, 1) >= HDIM
    zero = jnp.zeros_like(rows)
    return jnp.concatenate([jnp.where(second, zero, rows), jnp.where(second, rows, zero)], axis=0)


def visible(values, start, least, span, position, fill):
    if start + values.shape[0] <= least * span:
        return values
    key_at = lax.broadcasted_iota(jnp.int32, values.shape, 0) + start
    lane = lax.broadcasted_iota(jnp.int32, values.shape, 1)
    query_at = position * span + jnp.where(lane >= span, lane - span, lane)
    return jnp.where(key_at <= query_at, values, fill)


def unstack(pair, span):
    row = lax.broadcasted_iota(jnp.int32, (PAIR, span), 0)
    return jnp.where(row < HDIM, pair[:, :span], pair[:, span:]).T


def chunks_of(count, chunk):
    return [slice(start, min(start + chunk, count)) for start in range(0, count, chunk)]


def eight(values):
    return values.reshape(-1, 8, values.shape[-1])


def pair_columns(at):
    return pl.ds(pl.multiple_of(at * PAIR, PAIR), PAIR)


def largest_norm(rows_ref):
    feature = lax.broadcasted_iota(jnp.int32, (D, PAIR), 0) // HDIM
    head = lax.broadcasted_iota(jnp.int32, (D, PAIR), 1)
    chosen = jnp.where(feature == head, 1.0, 0.0).astype(jnp.bfloat16)
    rows = rows_ref[...]
    return jnp.max(dot(rows * rows, chosen, NN))


def forward_kernel(meta, q_ref, kv_ref, kv2_ref, o_ref, lse_ref, keys, values, *, span):
    slots = keys.shape[0] // span
    sort_rows(meta, kv_ref, kv2_ref, keys, span, 0)
    sort_rows(meta, kv_ref, kv2_ref, values, span, D)
    bound = largest_norm(q_ref) * largest_norm(keys) * (1.1 / HDIM)
    near = bound < SAFE * SAFE

    def run(signed, safe):
        def one_pair(pair, _):
            columns = pair_columns(pair)
            values_t = values[:, columns].T
            for rank in reversed(range(OWN)):
                least, most = reach(rank, slots)
                count = (most + 1) * span
                row_at = pl.multiple_of(meta[2 * OWN + rank] * span, span)
                position = meta[3 * OWN + rank]
                queries = stacked_heads(q_ref[pl.ds(row_at, span), columns] * 0.125)
                largest = None
                if not safe:
                    most_seen = jnp.full((8, 2 * span), -1e30, jnp.float32)
                    for part in chunks_of(count, CHUNK):
                        scores = dot(keys[part, columns], queries, NT)
                        scores = jnp.abs(scores) if signed else scores
                        scores = visible(scores, part.start, least, span, position, -1e30)
                        most_seen = jnp.maximum(most_seen, jnp.max(eight(scores), axis=0))
                    largest = jnp.max(most_seen, axis=0, keepdims=True)
                    if signed:
                        square = largest * largest + 1.0
                        largest = square * lax.rsqrt(square)
                total = jnp.zeros((8, 2 * span), jnp.float32)
                gathered = jnp.zeros((PAIR, 2 * span), jnp.float32)
                for part in chunks_of(count, CHUNK):
                    scores = dot(keys[part, columns], queries, NT)
                    argument = scores
                    if signed:
                        square = scores * scores + 1.0
                        inverse = lax.rsqrt(square)
                        argument = square * inverse
                    if not safe:
                        argument = argument - largest
                    weights = jnp.exp(visible(argument, part.start, least, span, position, -1e30))
                    total += jnp.sum(eight(weights), axis=0)
                    if signed:
                        weights = weights * (scores * inverse)
                    gathered += dot(values_t[:, part], weights.astype(jnp.bfloat16), NN)
                total = jnp.sum(total, axis=0, keepdims=True)
                lse = jnp.log(total)
                lse_ref[pair, rank : rank + 1, :] = lse if safe else lse + largest
                gathered = gathered * (1.0 / total)
                o_ref[pl.ds(row_at, span), columns] = unstack(gathered, span).astype(jnp.bfloat16)
            return 0

        lax.fori_loop(0, PAIRS, one_pair, 0)

    for signed in (True, False):
        for safe in (True, False):
            chosen = (meta[4 * OWN] == int(signed)) & (near == safe)
            pl.when(chosen)(functools.partial(run, signed, safe))


def in_vmem(*values):
    return [pltpu.with_memory_space_constraint(value, pltpu.VMEM) for value in values]


SMEM_SPEC = pl.BlockSpec(memory_space=pltpu.SMEM)
VMEM_SPEC = pl.BlockSpec(memory_space=pltpu.VMEM)


def sorted_attend(meta, queries, kv, kv_other):
    rows = kv.shape[0]
    span = rows // OWN
    return pl.pallas_call(
        functools.partial(forward_kernel, span=span),
        in_specs=[SMEM_SPEC] + [VMEM_SPEC] * 3,
        out_specs=[VMEM_SPEC] * 2,
        scratch_shapes=[pltpu.VMEM((2 * rows, D), jnp.bfloat16)] * 2,
        out_shape=[
            jax.ShapeDtypeStruct((rows, D), jnp.bfloat16),
            jax.ShapeDtypeStruct((PAIRS, OWN, 2 * span), jnp.float32),
        ],
        compiler_params=pltpu.CompilerParams(vmem_limit_bytes=10 * 1024 * 1024),
        cost_estimate=pl.CostEstimate(flops=4_000_000_000, bytes_accessed=0, transcendentals=0),
        name="attend",
    )(meta, *in_vmem(queries, kv, kv_other))


def backward_kernel(
    meta, q_ref, kv_ref, kv2_ref, o_ref, do_ref, lse_ref,
    dq_ref, own_ref, other_ref, keys, values, grad_k, grad_v, *, span,
):
    slots = keys.shape[0] // span
    sort_rows(meta, kv_ref, kv2_ref, keys, span, 0)
    sort_rows(meta, kv_ref, kv2_ref, values, span, D)

    def run(signed):
        def one_pair(pair, _):
            columns = pair_columns(pair)
            keys_t = keys[:, columns].T
            for rank in reversed(range(OWN)):
                least, most = reach(rank, slots)
                count = (most + 1) * span
                row_at = pl.multiple_of(meta[2 * OWN + rank] * span, span)
                position = meta[3 * OWN + rank]
                queries = stacked_heads(q_ref[pl.ds(row_at, span), columns] * 0.125)
                grad_rows = do_ref[pl.ds(row_at, span), columns]
                grads = stacked_heads(grad_rows)
                product = grad_rows.astype(jnp.float32) * o_ref[pl.ds(row_at, span), columns].astype(jnp.float32)
                delta = jnp.sum(stacked_heads(product).T, axis=0, keepdims=True)
                lse = lse_ref[pair, rank : rank + 1, :]
                gathered = jnp.zeros((PAIR, 2 * span), jnp.float32)
                for part in chunks_of(count, BACK_CHUNK):
                    scores = dot(keys[part, columns], queries, NT)
                    along = dot(values[part, columns], grads, NT)
                    argument = scores
                    if signed:
                        square = scores * scores + 1.0
                        inverse = lax.rsqrt(square)
                        argument = square * inverse
                    prob = jnp.exp(visible(argument - lse, part.start, least, span, position, -1e30))
                    if signed:
                        sign_pattern = scores * inverse
                        weights = prob * sign_pattern
                        bend = inverse * inverse * inverse
                        dscore = prob * ((sign_pattern * along - delta) * sign_pattern + along * bend)
                    else:
                        weights = prob
                        dscore = prob * (along - delta)
                    weights = weights.astype(jnp.bfloat16)
                    dscore = dscore.astype(jnp.bfloat16)
                    added_v = dot(weights, grads, NN)
                    added_k = dot(dscore, queries, NN)
                    if rank == OWN - 1:
                        grad_v[part, :] = added_v
                        grad_k[part, :] = added_k
                    else:
                        grad_v[part, :] += added_v
                        grad_k[part, :] += added_k
                    gathered += dot(keys_t[:, part], dscore, NN)
                dq_ref[pl.ds(row_at, span), columns] = (unstack(gathered, span) * 0.125).astype(jnp.bfloat16)
            for slot in range(OWN):
                there = slice(slot * span, (slot + 1) * span)
                own_at = pl.multiple_of(meta[slot] * span, span)
                other_at = pl.multiple_of(meta[OWN + slot] * span, span)
                for part, total in enumerate((grad_k, grad_v)):
                    own_ref[part, there, columns] = total[pl.ds(own_at, span), :].astype(jnp.bfloat16)
                    other_ref[part, there, columns] = total[pl.ds(other_at, span), :].astype(jnp.bfloat16)
            return 0

        lax.fori_loop(0, PAIRS, one_pair, 0)

    for signed in (True, False):
        pl.when(meta[4 * OWN] == int(signed))(functools.partial(run, signed))

    @pl.when(meta[4 * OWN] == IDLE)
    def _():
        for out_ref in (dq_ref, own_ref, other_ref):
            out_ref[...] = jnp.zeros_like(out_ref)


def sorted_attend_back(meta, queries, kv, kv_other, attended, grad_att, lse):
    rows = kv.shape[0]
    span = rows // OWN
    return pl.pallas_call(
        functools.partial(backward_kernel, span=span),
        in_specs=[SMEM_SPEC] + [VMEM_SPEC] * 6,
        out_specs=[VMEM_SPEC] * 3,
        scratch_shapes=[pltpu.VMEM((2 * rows, D), jnp.bfloat16)] * 2
        + [pltpu.VMEM((2 * rows, PAIR), jnp.float32)] * 2,
        out_shape=[
            jax.ShapeDtypeStruct((rows, D), jnp.bfloat16),
            jax.ShapeDtypeStruct((2, rows, D), jnp.bfloat16),
            jax.ShapeDtypeStruct((2, rows, D), jnp.bfloat16),
        ],
        compiler_params=pltpu.CompilerParams(vmem_limit_bytes=10 * 1024 * 1024),
        cost_estimate=pl.CostEstimate(flops=8_000_000_000, bytes_accessed=0, transcendentals=0),
        name="attend_back",
    )(meta, *in_vmem(queries, kv, kv_other, attended, grad_att), lse)


TURN_TANH = 0.7978845608028654
CUBE = 0.044715
CHUNKS = 1


def normalised(rows):
    center = rows - jnp.mean(rows, axis=-1, keepdims=True)
    inverse = lax.rsqrt(jnp.mean(center * center, axis=-1, keepdims=True) + 1e-05)
    return center * inverse, inverse


def norm_back(unit, inverse, gain_row, grad):
    scaled = grad * gain_row
    along = jnp.mean(scaled * unit, axis=-1, keepdims=True)
    return inverse * (scaled - jnp.mean(scaled, axis=-1, keepdims=True) - unit * along)


def row_chunks(rows, chunks=CHUNKS):
    return [slice(at * rows // chunks, (at + 1) * rows // chunks) for at in range(chunks)]


def column_sum(values):
    return jnp.sum(values, axis=0, keepdims=True)


def gelu_parts(hidden):
    square = hidden * hidden
    curve = jnp.tanh(hidden * (TURN_TANH + TURN_TANH * CUBE * square))
    half = 0.5 + 0.5 * curve
    inner = hidden * (TURN_TANH + 3.0 * TURN_TANH * CUBE * square)
    return hidden * half, half + 0.5 * (1.0 - curve * curve) * inner


def gelu_only(hidden):
    square = hidden * hidden
    curve = jnp.tanh(hidden * (TURN_TANH + TURN_TANH * CUBE * square))
    return hidden * (0.5 + 0.5 * curve)


def cost(flops):
    return pl.CostEstimate(flops=int(flops) // 8, bytes_accessed=0, transcendentals=0)


def in_hbm(value):
    return pltpu.with_memory_space_constraint(value, pltpu.HBM)


def placed(shape, dtype, space=None):
    return jax.ShapeDtypeStruct(shape, dtype) if space is None else space(shape, dtype)


def call(kernel, name, megabytes, flops, outs, scratch, *operands, smem=0):
    return pl.pallas_call(
        kernel,
        in_specs=[SMEM_SPEC] * smem + [VMEM_SPEC] * (len(operands) - smem),
        out_specs=[VMEM_SPEC] * len(outs),
        out_shape=[placed(*out) for out in outs],
        scratch_shapes=scratch,
        compiler_params=pltpu.CompilerParams(vmem_limit_bytes=megabytes * 1024 * 1024),
        cost_estimate=cost(flops),
        name=name,
    )(*operands)


def bias_part(biases, at):
    return biases[0:1, at * D : (at + 1) * D]


def tile(at):
    return slice(at * D, (at + 1) * D)


def whole(*shape):
    return pl.BlockSpec(shape, lambda *_: (0,) * len(shape))


def flip_kernel(in_ref, out_ref):
    out_ref[...] = in_ref[...].T


def copy_kernel(in_ref, out_ref):
    out_ref[...] = in_ref[...]


def fetched(value):
    height, width = value.shape
    block = pl.BlockSpec((height // 4, width), lambda i: (i, 0))
    return pl.pallas_call(
        copy_kernel,
        grid=(4,),
        in_specs=[block],
        out_specs=block,
        out_shape=placed(value.shape, value.dtype, pltpu.VMEM),
        compiler_params=pltpu.CompilerParams(vmem_limit_bytes=7 * 1024 * 1024),
        cost_estimate=cost(0),
        name="fetched",
    )(in_hbm(value))


def flip(value, space=None):
    height, width = value.shape[-2:]
    lead = (None,) * (value.ndim - 2)
    zeros = (0,) * (value.ndim - 2)
    if height > D:
        grid = height // D
        in_spec = pl.BlockSpec(lead + (D, width), lambda i: zeros + (i, 0))
        out_spec = pl.BlockSpec((width, D), lambda i: (0, i))
    else:
        step = min(width, D)
        grid = width // step
        in_spec = pl.BlockSpec(lead + (height, step), lambda i: zeros + (0, i))
        out_spec = pl.BlockSpec((step, height), lambda i: (i, 0))
    return pl.pallas_call(
        flip_kernel,
        grid=(grid,),
        in_specs=[in_spec],
        out_specs=out_spec,
        out_shape=placed((width, height), value.dtype, space),
        compiler_params=pltpu.CompilerParams(vmem_limit_bytes=7 * 1024 * 1024),
        cost_estimate=cost(0),
        name="flip",
    )(value)


def front_rows(x_ref, gains, biases, w_ref, normed_ref, q_ref, kv_ref):
    for part in row_chunks(x_ref.shape[0]):
        unit, _ = normalised(x_ref[part, :].astype(jnp.float32))
        normed = (unit * gains[0:1, :] + bias_part(biases, 0)).astype(jnp.bfloat16)
        normed_ref[part, :] = normed
        kv_ref[part, :D] = dot(normed, w_ref[0, :, tile(1)], NN).astype(jnp.bfloat16)
        kv_ref[part, D:] = (dot(normed, w_ref[0, :, tile(2)], NN) + bias_part(biases, 3)).astype(jnp.bfloat16)
        q_ref[part, :] = (dot(normed, w_ref[0, :, tile(0)], NN) + bias_part(biases, 2)).astype(jnp.bfloat16)


def choose(which, first_ref, second_ref, chosen_ref):
    for index, source in ((1, first_ref), (0, second_ref)):

        @pl.when(which[0] == index)
        def _():
            chosen_ref[...] = source[...]


def chosen_front_kernel(which, first_ref, second_ref, gains, biases, w_ref, chosen_ref, normed_ref, q_ref, kv_ref):
    choose(which, first_ref, second_ref, chosen_ref)
    front_rows(chosen_ref, gains, biases, w_ref, normed_ref, q_ref, kv_ref)


def front_outs(rows):
    narrow = jnp.bfloat16
    return [((rows, D), narrow), ((rows, D), narrow), ((rows, 2 * D), narrow)]


def front(entry, gains, biases, w_qkv):
    rows = entry.shape[0]
    return call(front_rows, "front", 8, 6 * rows * D * D, front_outs(rows), [], entry, gains, biases, w_qkv)


def chosen_front(which, first, second, gains, biases, w_qkv):
    rows = first.shape[0]
    outs = [((rows, D), jnp.bfloat16)] + front_outs(rows)
    return call(
        chosen_front_kernel, "chosen_front", 8, 6 * rows * D * D, outs, [],
        which, first, second, gains, biases, w_qkv, smem=1,
    )


def middle_rows(x_ref, o_ref, w_out, biases, part):
    return x_ref[part, :].astype(jnp.float32) + dot(o_ref[part, :], w_out[0], NN) + bias_part(biases, 4)


def rest_kernel(x_ref, o_ref, gains, biases, w_out, w_up, w_down, result_ref):
    for part in row_chunks(x_ref.shape[0]):
        middle = middle_rows(x_ref, o_ref, w_out, biases, part)
        unit, _ = normalised(middle)
        normed = (unit * gains[1:2, :] + bias_part(biases, 1)).astype(jnp.bfloat16)
        total = middle + bias_part(biases, 5)
        for at in range(w_up.shape[2] // D):
            hidden = dot(normed, w_up[0, :, tile(at)], NN) + bias_part(biases, 6 + at)
            total += dot(gelu_only(hidden).astype(jnp.bfloat16), w_down[0, tile(at), :], NN)
        result_ref[part, :] = total.astype(jnp.bfloat16)


def rest(entry, attended, gains, biases, w_out, w_up, w_down):
    rows = entry.shape[0]
    flops = 2 * rows * (D * D + 2 * w_up.size)
    return call(
        rest_kernel, "rest", 7, flops, [((rows, D), jnp.bfloat16)], [],
        entry, attended, gains, biases, w_out, w_up, w_down,
    )[0]


def turn_kernel(
    x_ref, o_ref, d_ref, gains, biases, w_out, w_up, out_t, up_t, down_t,
    middle_ref, normed_ref, active_ref, slope_ref, grad_ref, grad_att_ref,
    middle, normed, actives, slopes, done,
):
    copies = []

    def leave(source, target):
        copies.append(pltpu.make_async_copy(source, target, done.at[len(copies)]))
        copies[-1].start()

    rows = x_ref[...].astype(jnp.float32) + dot(o_ref[...], w_out[0], NN) + bias_part(biases, 4)
    middle[...] = rows
    leave(middle, middle_ref)
    unit, _ = normalised(rows)
    normed[...] = (unit * gains[1:2, :] + bias_part(biases, 1)).astype(jnp.bfloat16)
    leave(normed, normed_ref)
    total = jnp.zeros_like(rows)
    for at in range(w_up.shape[2] // D):
        hidden = dot(normed[...], w_up[0, :, tile(at)], NN) + bias_part(biases, 6 + at)
        active, slope = gelu_parts(hidden)
        actives[at] = active.astype(jnp.bfloat16)
        slopes[at] = slope.astype(jnp.bfloat16)
        leave(actives.at[at], active_ref.at[:, tile(at)])
        leave(slopes.at[at], slope_ref.at[:, tile(at)])
        grad_hidden = dot(d_ref[...], down_t[:, tile(at)], NN) * slope
        total += dot(grad_hidden.astype(jnp.bfloat16), up_t[tile(at), :], NN)
    unit, inverse = normalised(middle[...])
    grad = d_ref[...].astype(jnp.float32) + norm_back(unit, inverse, gains[1:2, :], total)
    grad = grad.astype(jnp.bfloat16)
    grad_ref[...] = grad
    grad_att_ref[...] = dot(grad, out_t[...], NN).astype(jnp.bfloat16)
    for copy in copies:
        copy.wait()


def turn(entry, attended, result_gradient, gains, biases, w_out, w_up, out_t, up_t, down_t):
    rows = entry.shape[0]
    wide, narrow = jnp.float32, jnp.bfloat16
    inner = w_up.shape[2]
    steps = inner // D
    far = [((rows, D), wide), ((rows, D), narrow), ((rows, inner), narrow), ((rows, inner), narrow)]
    return pl.pallas_call(
        turn_kernel,
        in_specs=[VMEM_SPEC] * 10,
        out_specs=[pl.BlockSpec(memory_space=pltpu.HBM)] * len(far) + [VMEM_SPEC] * 2,
        out_shape=[placed(*out, pltpu.HBM) for out in far] + [placed((rows, D), narrow)] * 2,
        scratch_shapes=[
            pltpu.VMEM((rows, D), wide),
            pltpu.VMEM((rows, D), narrow),
            pltpu.VMEM((steps, rows, D), narrow),
            pltpu.VMEM((steps, rows, D), narrow),
            pltpu.SemaphoreType.DMA((2 + 2 * steps,)),
        ],
        compiler_params=pltpu.CompilerParams(vmem_limit_bytes=18 * 1024 * 1024),
        cost_estimate=cost(2 * rows * (2 * D * D + 3 * w_up.size)),
        name="turn",
    )(entry, attended, result_gradient, gains, biases, w_out, w_up, out_t, up_t, down_t)


def down_back_kernel(
    which, first_ref, second_ref, slope_ref, middle_ref, gains, out_t, up_t, down_t,
    d_ref, hidden_ref, grad_ref, grad_att_ref, sums_ref, up_ref,
):
    choose(which, first_ref, second_ref, d_ref)
    sums = [jnp.zeros((1, D), jnp.float32)] * 4
    steps = up_t.shape[0] // D
    up_sums = [jnp.zeros((1, D), jnp.float32)] * steps
    for part in row_chunks(d_ref.shape[0]):
        given = d_ref[part, :]
        through = jnp.zeros(given.shape, jnp.float32)
        for at in range(steps):
            grad_hidden = dot(given, down_t[:, tile(at)], NN) * slope_ref[part, tile(at)].astype(jnp.float32)
            up_sums[at] = up_sums[at] + column_sum(grad_hidden)
            grad_hidden = grad_hidden.astype(jnp.bfloat16)
            hidden_ref[part, tile(at)] = grad_hidden
            through += dot(grad_hidden, up_t[tile(at), :], NN)
        unit, inverse = normalised(middle_ref[part, :])
        given = given.astype(jnp.float32)
        grad = given + norm_back(unit, inverse, gains[1:2, :], through)
        grad_b = grad.astype(jnp.bfloat16)
        grad_ref[part, :] = grad_b
        grad_att_ref[part, :] = dot(grad_b, out_t[...], NN).astype(jnp.bfloat16)
        for at, term in enumerate((through * unit, through, grad, given)):
            sums[at] = sums[at] + column_sum(term)
    sums_ref[...] = jnp.concatenate(sums, axis=0)
    up_ref[...] = jnp.concatenate(up_sums, axis=0)


def down_back(which, first, second, slope, middle, gains, out_t, up_t, down_t):
    rows = first.shape[0]
    wide, narrow = jnp.float32, jnp.bfloat16
    inner = up_t.shape[0]
    outs = [
        ((rows, D), narrow), ((rows, inner), narrow), ((rows, D), narrow), ((rows, D), narrow),
        ((4, D), wide), ((inner // D, D), wide),
    ]
    return call(
        down_back_kernel, "down_back", 8, 2 * rows * (D * D + 2 * up_t.size), outs, [],
        which, first, second, slope, middle, gains, out_t, up_t, down_t, smem=1,
    )


def qkv_tiles(part, q_ref, own_ref, there_ref):
    tiles = [q_ref[part, :]]
    for at in range(2):
        total = own_ref[at, part, :].astype(jnp.float32) + there_ref[at, part, :].astype(jnp.float32)
        tiles.append(total.astype(jnp.bfloat16))
    return tiles


def front_back_kernel(q_ref, own_ref, there_ref, x_ref, grad_ref, gains, qkv_t, out_ref, sums_ref):
    sums = [jnp.zeros((1, D), jnp.float32)] * 4
    for part in row_chunks(x_ref.shape[0]):
        tiles = qkv_tiles(part, q_ref, own_ref, there_ref)
        through = sum(dot(value, qkv_t[tile(at), :], NN) for at, value in enumerate(tiles))
        unit, inverse = normalised(x_ref[part, :].astype(jnp.float32))
        out = grad_ref[part, :].astype(jnp.float32) + norm_back(unit, inverse, gains[0:1, :], through)
        out_ref[part, :] = out.astype(out_ref.dtype)
        terms = (through * unit, through, tiles[0].astype(jnp.float32), tiles[2].astype(jnp.float32))
        for at, term in enumerate(terms):
            sums[at] = sums[at] + column_sum(term)
    sums_ref[...] = jnp.concatenate(sums, axis=0)


def front_back(grad_q, own, there, entry, grad_middle, gains, qkv_t, dtype):
    rows = entry.shape[0]
    outs = [((rows, D), dtype, pltpu.VMEM), ((4, D), jnp.float32)]
    return call(
        front_back_kernel, "front_back", 8, 6 * rows * D * D, outs, [],
        grad_q, own, there, entry, grad_middle, gains, qkv_t,
    )


def added(kept, arrived, dtype=jnp.bfloat16):
    return (kept.astype(jnp.float32) + arrived.astype(jnp.float32)).astype(dtype)


def core_rows(left_ref, core, order):
    block = left_ref.shape[0] // (2 * len(order))
    picked = [
        left_ref[pl.ds(pl.multiple_of((2 * (2 * z_at + y_at) + core) * block, block), block), :] for z_at, y_at in order
    ]
    return jnp.concatenate(picked, axis=0)


def by_y_then_z(z_count):
    return [(z_at, y_at) for y_at in range(2) for z_at in range(z_count)]


def down_sent_kernel(place, left_ref, right_ref, sent_ref):
    block = sent_ref.shape[2]
    rows = core_rows(left_ref, 1 - place[0], by_y_then_z(1))
    total = dot(rows, right_ref[...], NN).astype(jnp.bfloat16)
    for y_at in range(2):
        sent_ref[y_at, 0] = total[y_at * block : (y_at + 1) * block]


def down_kept_kernel(place, left_ref, right_ref, there_ref, keep_ref, send_ref):
    block = keep_ref.shape[1]
    total = dot(core_rows(left_ref, place[0], by_y_then_z(1)), right_ref[...], NN)
    parts = [added(total[y_at * block : (y_at + 1) * block], there_ref[y_at, 0]) for y_at in range(2)]

    def store(mine):
        keep_ref[0] = parts[mine]
        send_ref[0] = parts[1 - mine]

    for mine in range(2):
        pl.when(place[1] == mine)(functools.partial(store, mine))


def grid_call(kernel, name, grid, in_specs, out_specs, shapes, scratch, flops, place, *operands, far=0):
    return pl.pallas_call(
        kernel,
        grid_spec=pltpu.PrefetchScalarGridSpec(
            num_scalar_prefetch=1, grid=(grid,), in_specs=in_specs, out_specs=out_specs, scratch_shapes=scratch
        ),
        out_shape=[
            placed(shape, jnp.bfloat16, pltpu.HBM if at < far else None) for at, shape in enumerate(shapes)
        ],
        compiler_params=pltpu.CompilerParams(vmem_limit_bytes=9 * 1024 * 1024),
        cost_estimate=cost(flops),
        name=name,
    )(place, *operands)


def down_specs(active_t, z_count):
    height, rows = active_t.shape
    block = height // (4 * z_count)
    in_specs = [pl.BlockSpec((height // z_count, rows), lambda i, _: (i, 0)), whole(rows, D)]
    return block, in_specs, pl.BlockSpec((2, 1, block, D), lambda i, _: (0, i, 0, 0))


def down_sent(place, active_t, back, z_count):
    block, in_specs, sent_spec = down_specs(active_t, z_count)
    return grid_call(
        down_sent_kernel, "down_sent", z_count, in_specs, [sent_spec], [(2, z_count, block, D)], [],
        active_t.size * D, place, active_t, back,
    )[0]


def down_kept(place, active_t, back, there, z_count):
    block, in_specs, sent_spec = down_specs(active_t, z_count)
    out_spec = pl.BlockSpec((1, block, D), lambda i, _: (i, 0, 0))
    return grid_call(
        down_kept_kernel, "down_kept", z_count, in_specs + [sent_spec], [out_spec] * 2, [(z_count, block, D)] * 2, [],
        active_t.size * D, place, active_t, back, there, far=1,
    )


def up_sent_kernel(place, left_ref, right_ref, sent_ref, rows):
    z_count, block = sent_ref.shape[1:3]
    order = by_y_then_z(z_count)

    @pl.when(pl.program_id(0) == 0)
    def _():
        rows[...] = core_rows(left_ref, 1 - place[0], order)

    total = dot(rows[...], right_ref[...], NN).astype(jnp.bfloat16)
    for at, (z_at, y_at) in enumerate(order):
        sent_ref[y_at, z_at] = total[at * block : (at + 1) * block]


def up_kept_kernel(place, left_ref, right_ref, there_ref, keep_ref, send_ref, rows):
    z_count, block = there_ref.shape[1:3]
    order = by_y_then_z(z_count)

    @pl.when(pl.program_id(0) == 0)
    def _():
        rows[...] = core_rows(left_ref, place[0], order)

    total = dot(rows[...], right_ref[...], NN)
    parts = [added(total[at * block : (at + 1) * block], there_ref[y_at, z_at]) for at, (z_at, y_at) in enumerate(order)]

    def store(mine):
        for part, (z_at, y_at) in zip(parts, order):
            target = keep_ref if z_at % 2 == mine else send_ref
            target[y_at, z_at // 2] = part

    for mine in range(2):
        pl.when(place[2] == mine)(functools.partial(store, mine))


def half_rows(rows):
    return pltpu.VMEM((D // 2, rows), jnp.bfloat16)


def column_spec(z_count):
    return pl.BlockSpec((2, z_count, D // (4 * z_count), D), lambda i, _: (0, 0, 0, i))


def up_sent(place, normed_t, grad_hidden, z_count):
    rows, width = grad_hidden.shape
    in_specs = [whole(D, rows), pl.BlockSpec((rows, D), lambda i, _: (0, i))]
    return grid_call(
        up_sent_kernel, "up_sent", width // D, in_specs, [column_spec(z_count)],
        [(2, z_count, D // (4 * z_count), width)], [half_rows(rows)], grad_hidden.size * D, place, normed_t, grad_hidden,
    )[0]


def up_kept(place, normed_t, grad_hidden, there, z_count):
    rows, width = grad_hidden.shape
    in_specs = [whole(D, rows), pl.BlockSpec((rows, D), lambda i, _: (0, i)), column_spec(z_count)]
    shape = (2, z_count // 2, D // (4 * z_count), width)
    out_spec = pl.BlockSpec(shape[:3] + (D,), lambda i, _: (0, 0, 0, i))
    return grid_call(
        up_kept_kernel, "up_kept", width // D, in_specs, [out_spec] * 2, [shape] * 2, [half_rows(rows)],
        grad_hidden.size * D, place, normed_t, grad_hidden, there, far=1,
    )


def store_sent(sent_ref, at, total):
    z_count, block = sent_ref.shape[1:3]
    for row, (z_at, y_at) in enumerate(by_y_then_z(z_count)):
        sent_ref[y_at, z_at, :, tile(at)] = total[row * block : (row + 1) * block].astype(jnp.bfloat16)


def outer_sent_kernel(place, o_ref, normed_ref, d_ref, q_ref, sent_ref):
    order = by_y_then_z(sent_ref.shape[1])
    for at, (left, right) in enumerate(((o_ref, d_ref), (normed_ref, q_ref))):
        store_sent(sent_ref, at, dot(core_rows(left, 1 - place[0], order), right[...], NN))


def outer_sent(place, attended_t, normed_t, grad_middle, grad_q, z_count):
    outs = [((2, z_count, D // (4 * z_count), 2 * D), jnp.bfloat16)]
    return call(
        outer_sent_kernel, "outer_sent", 6, 2 * D * grad_q.size, outs, [],
        place, attended_t, normed_t, grad_middle, grad_q, smem=1,
    )[0]


def inner_sent_kernel(place, normed_ref, own_ref, there_ref, sent_ref):
    rows = core_rows(normed_ref, 1 - place[0], by_y_then_z(sent_ref.shape[1]))
    for at in range(2):
        store_sent(sent_ref, at, dot(rows, added(own_ref[at], there_ref[at]), NN))


def inner_sent(place, normed_t, own, there, z_count):
    outs = [((2, z_count, D // (4 * z_count), 2 * D), jnp.bfloat16)]
    return call(
        inner_sent_kernel, "inner_sent", 6, D * own.size, outs, [], place, normed_t, own, there, smem=1
    )[0]


def rest_kept_kernel(
    place, o_ref, normed_ref, d_ref, q_ref, own_ref, there_ref, outer_ref, inner_ref, keep_ref, send_ref
):
    z_count, block = keep_ref.shape[:2]
    order = by_y_then_z(z_count)
    attended, normed = [core_rows(left, place[0], order) for left in (o_ref, normed_ref)]

    def run(mine):
        for at in range(4):
            left = normed if at else attended
            right = (d_ref[...], q_ref[...])[at] if at < 2 else added(own_ref[at - 2], there_ref[at - 2])
            total = dot(left, right, NN)
            arrived = inner_ref if at > 1 else outer_ref
            for row, (z_at, y_at) in enumerate(order):
                target = keep_ref if y_at == mine else send_ref
                part = total[row * block : (row + 1) * block]
                target[z_at, :, tile(at)] = added(part, arrived[y_at, z_at, :, tile(at % 2)])

    for mine in range(2):
        pl.when(place[1] == mine)(functools.partial(run, mine))


def rest_kept(place, attended_t, normed_t, grad_middle, grad_q, own, there, outer_there, inner_there, z_count):
    outs = [((z_count, D // (4 * z_count), 4 * D), jnp.bfloat16)] * 2
    return call(
        rest_kept_kernel, "rest_kept", 10, 4 * D * grad_q.size, outs, [],
        place, attended_t, normed_t, grad_middle, grad_q, own, there, outer_there, inner_there, smem=1,
    )


def fold_kernel(place, kept_ref, arrived_ref, keep_ref, send_ref):
    for target, chosen in ((send_ref, 1 - place[0]), (keep_ref, place[0])):
        for at in range(target.shape[0]):
            target[at] = added(kept_ref[at, chosen], arrived_ref[at, chosen])


def fold(kept, arrived, place, outer):
    width = kept.shape[-1]
    lead = math.prod(kept.shape[:outer])
    inner = math.prod(kept.shape[outer + 1 : -1])
    shape = (lead, 2, inner, width)
    outs = [((lead, inner, width), kept.dtype)] * 2
    keep, send = call(
        fold_kernel, "fold", 4, 0, outs, [], place, kept.reshape(shape), arrived.reshape(shape), smem=1
    )
    left = kept.shape[:outer] + kept.shape[outer + 1 :]
    return keep.reshape(left), send.reshape(left)


def stream_fold_kernel(place, kept_keep, kept_send, arrived_keep, arrived_send, keep_ref, send_ref):
    send_ref[...] = added(kept_send[...], arrived_send[...])
    keep_ref[...] = added(kept_keep[...], arrived_keep[...])


def stream_fold(kept, arrived, place, outer):
    width = kept.shape[-1]
    lead = math.prod(kept.shape[:outer])
    inner = math.prod(kept.shape[outer + 1 : -1])
    parts = 1 if lead > 1 else 4
    shape = (lead, 2, inner, width)
    block = (None, None, inner // parts, width)
    keep_spec = pl.BlockSpec(block, lambda i, place: (i // parts, place[0], i % parts, 0))
    send_spec = pl.BlockSpec(block, lambda i, place: (i // parts, 1 - place[0], i % parts, 0))
    out_spec = pl.BlockSpec(block[1:], lambda i, place: (i // parts, i % parts, 0))
    left = kept.shape[:outer] + kept.shape[outer + 1 :]
    kept, arrived = [in_hbm(value.reshape(shape)) for value in (kept, arrived)]
    keep, send = pl.pallas_call(
        stream_fold_kernel,
        grid_spec=pltpu.PrefetchScalarGridSpec(
            num_scalar_prefetch=1,
            grid=(lead * parts,),
            in_specs=[keep_spec, send_spec] * 2,
            out_specs=[out_spec, out_spec],
        ),
        out_shape=[jax.ShapeDtypeStruct((lead, inner, width), jnp.bfloat16)] * 2,
        compiler_params=pltpu.CompilerParams(vmem_limit_bytes=6 * 1024 * 1024),
        cost_estimate=cost(0),
        name="stream_fold",
    )(place, kept, kept, arrived, arrived)
    return keep.reshape(left), send.reshape(left)


def shifted(value, axis, steps):
    count = lax.axis_size(axis)
    initial, last = (max(0, -steps), min(count, count - steps))
    return lax.ppermute(value, axis, [(source, source + steps) for source in range(initial, last)])


def layer_norm(inputs_row, gain_row, offset):
    center = inputs_row - jnp.mean(inputs_row, axis=-1, keepdims=True)
    spread = jnp.mean(center * center, axis=-1, keepdims=True)
    return center * lax.rsqrt(spread + 1e-05) * gain_row + offset


def gelu_tanh(hidden):
    return jax.nn.gelu(hidden, approximate=True)


def score_terms(queries, key_rows, query_pos, key_pos, signed):
    key_count = key_rows.shape[0]
    scores = (
        jnp.einsum(
            "rhe,khe->hrk",
            queries,
            key_rows.reshape(key_count, HEADS, HDIM),
            preferred_element_type=jnp.float32,
        )
        * 0.125
    )
    curved = jnp.sqrt(scores * scores + 1.0)
    argument = jnp.where(signed, curved, scores)
    sign_pattern = jnp.where(signed, scores / curved, 1.0)
    slope = jnp.where(signed, sign_pattern, 1.0)
    bend = jnp.where(signed, 1.0 / (curved * curved * curved), 0.0)
    permitted_mask = key_pos[None, None, :] <= query_pos[None, :, None]
    return (argument, sign_pattern, slope, bend, permitted_mask)


def score_grads(
    queries, key_rows, value_rows, query_pos, key_pos, log_total, delta, grad_att, signed
):
    argument, sign_pattern, slope, bend, permitted_mask = score_terms(
        queries, key_rows, query_pos, key_pos, signed
    )
    prob = jnp.where(permitted_mask, jnp.exp(argument - log_total[..., None]), 0.0)
    along = jnp.einsum("rhe,khe->hrk", grad_att, value_rows, preferred_element_type=jnp.float32)
    dscore = (prob * ((sign_pattern * along - delta[..., None]) * slope + along * bend)).astype(
        jnp.bfloat16
    )
    return ((sign_pattern * prob).astype(jnp.bfloat16), dscore)


def key_blocks_of(key_all, value_all, key_pos, key_block):
    blocks = key_all.shape[0] // key_block
    return (
        key_all.reshape(blocks, key_block, D),
        value_all.reshape(blocks, key_block, HEADS, HDIM),
        key_pos.reshape(blocks, key_block),
    )


def attend(queries, query_pos, key_all, value_all, key_pos, signed, key_block):
    row_count = queries.shape[0]
    key_split, value_split, pos_split = key_blocks_of(key_all, value_all, key_pos, key_block)

    def running_total(state_in, element):
        largest, row_total_sum, gathered = state_in
        key_rows, value_rows, block_pos = element
        argument, sign_pattern, _, _, permitted_mask = score_terms(
            queries, key_rows, query_pos, block_pos, signed
        )
        masked_scores = jnp.where(permitted_mask, argument, -1e30)
        exponent_values = jnp.maximum(largest, jnp.max(masked_scores, axis=-1))
        multiplier = jnp.exp(largest - exponent_values)
        added_terms = jnp.where(
            permitted_mask, jnp.exp(masked_scores - exponent_values[..., None]), 0.0
        )
        row_total_sum = row_total_sum * multiplier + jnp.sum(added_terms, axis=-1)
        attention_weights = (sign_pattern * added_terms).astype(jnp.bfloat16)
        added = jnp.einsum(
            "hrk,khe->rhe", attention_weights, value_rows, preferred_element_type=jnp.float32
        )
        gathered = gathered * multiplier.T[:, :, None] + added
        return ((exponent_values, row_total_sum, gathered), None)

    start_max = jnp.full((HEADS, row_count), -1e30, jnp.float32)
    start_sum = jnp.zeros((HEADS, row_count), jnp.float32)
    start_out = jnp.zeros((row_count, HEADS, HDIM), jnp.float32)
    (largest, row_total_sum, gathered), _ = lax.scan(
        running_total, (start_max, start_sum, start_out), (key_split, value_split, pos_split)
    )
    log_total = largest + jnp.log(row_total_sum)
    attended = gathered / row_total_sum.T[:, :, None]
    return (attended, log_total)


def backward_summed(
    queries, query_pos, key_all, value_all, key_pos, log_total, delta, grad_att, signed, key_block
):
    key_split, value_split, pos_split = key_blocks_of(key_all, value_all, key_pos, key_block)

    def step_back(grad_q, element):
        key_rows, value_rows, block_pos = element
        attention_weights, dscore = score_grads(
            queries, key_rows, value_rows, query_pos, block_pos, log_total, delta, grad_att, signed
        )
        grad_q = (
            grad_q
            + jnp.einsum(
                "hrk,khe->rhe",
                dscore,
                key_rows.reshape(-1, HEADS, HDIM),
                preferred_element_type=jnp.float32,
            )
            * 0.125
        )
        grad_k = (
            jnp.einsum("hrk,rhe->khe", dscore, queries, preferred_element_type=jnp.float32) * 0.125
        )
        grad_v = jnp.einsum(
            "hrk,rhe->khe", attention_weights, grad_att, preferred_element_type=jnp.float32
        )
        return (grad_q, (grad_k.reshape(key_block, D), grad_v.reshape(key_block, D)))

    start_q = jnp.zeros(queries.shape, jnp.float32)
    grad_q, (grad_k, grad_v) = lax.scan(step_back, start_q, (key_split, value_split, pos_split))
    grad_k, grad_v = (
        lax.psum_scatter(
            grad_k.reshape(-1, D).astype(jnp.bfloat16), "ctx", scatter_dimension=0, tiled=True
        ).astype(jnp.float32),
        lax.psum_scatter(
            grad_v.reshape(-1, D).astype(jnp.bfloat16), "ctx", scatter_dimension=0, tiled=True
        ).astype(jnp.float32),
    )
    return (grad_q.reshape(-1, D), grad_k, grad_v)


def layer_front(inputs_row, gain_pair, bias_row, qkv_w):
    normed = layer_norm(inputs_row, gain_pair[0], bias_row[0:D]).astype(jnp.bfloat16)
    qkv_bias = jnp.concatenate(
        [bias_row[2 * D : 3 * D], jnp.zeros((D,), jnp.float32), bias_row[3 * D : 4 * D]]
    )
    projected = (jnp.dot(normed, qkv_w, preferred_element_type=jnp.float32) + qkv_bias).astype(
        jnp.bfloat16
    )
    return (normed, projected)


def layer_rest(inputs_row, attended_b, gain_pair, bias_row, out_w, up_w, down_w):
    middle = (
        inputs_row
        + jnp.dot(attended_b, out_w, preferred_element_type=jnp.float32)
        + bias_row[4 * D : 5 * D]
    )
    normed_two = layer_norm(middle, gain_pair[1], bias_row[D : 2 * D]).astype(jnp.bfloat16)
    hidden = jnp.dot(normed_two, up_w, preferred_element_type=jnp.float32) + bias_row[6 * D :]
    active = gelu_tanh(hidden).astype(jnp.bfloat16)
    result = (
        middle
        + jnp.dot(active, down_w, preferred_element_type=jnp.float32)
        + bias_row[5 * D : 6 * D]
    )
    return (middle, normed_two, hidden, active, result)


def general_body(inputs, slot_order, cotangent, gains, biases, w_qkv, w_out, w_up, w_down):
    micro_count = inputs.shape[0]
    row_count = inputs.shape[2]
    section_at = lax.axis_index("section")
    ctx_at = lax.axis_index("ctx")
    signed = section_at == 0
    gain_pair = gains[0]
    bias_row = biases[0]
    qkv_w = w_qkv[0]
    out_w = w_out[0]
    up_w = w_up[0]
    down_w = w_down[0]
    span_len = row_count // 2
    seq_pos = (
        slot_order[:, 0, :, None] * span_len + jnp.arange(span_len, dtype=jnp.int32)
    ).reshape(micro_count, -1)
    key_block = min(seq_pos.shape[1], 512)
    first_inputs = inputs[:, 0]
    cot_rows = cotangent[:, 0]

    def sequence_pos(index):
        whole_pos = lax.dynamic_index_in_dim(seq_pos, index, 0, keepdims=False)
        own_pos = lax.dynamic_slice_in_dim(whole_pos, ctx_at * row_count, row_count, 0)
        return (whole_pos, own_pos)

    def layer_forward(entry, index):
        whole_pos, own_pos = sequence_pos(index)
        inputs_row = entry.astype(jnp.float32)
        normed, projected = layer_front(inputs_row, gain_pair, bias_row, qkv_w)
        key_all, value_all = (
            lax.all_gather(projected[:, D : 2 * D], "ctx", axis=0, tiled=True),
            lax.all_gather(projected[:, 2 * D :], "ctx", axis=0, tiled=True),
        )
        queries = projected[:, :D].reshape(row_count, HEADS, HDIM)
        attended, _ = attend(queries, own_pos, key_all, value_all, whole_pos, signed, key_block)
        attended_b = attended.reshape(row_count, D).astype(jnp.bfloat16)
        result = layer_rest(inputs_row, attended_b, gain_pair, bias_row, out_w, up_w, down_w)[4]
        return result.astype(jnp.bfloat16)

    def layer_reverse_pass(entry, result_gradient, index):
        whole_pos, own_pos = sequence_pos(index)
        inputs_row = entry.astype(jnp.float32)
        normed, projected = layer_front(inputs_row, gain_pair, bias_row, qkv_w)
        queries = projected[:, :D].reshape(row_count, HEADS, HDIM)
        key_all, value_all = (
            lax.all_gather(projected[:, D : 2 * D], "ctx", axis=0, tiled=True),
            lax.all_gather(projected[:, 2 * D :], "ctx", axis=0, tiled=True),
        )
        attended, log_total = attend(
            queries, own_pos, key_all, value_all, whole_pos, signed, key_block
        )
        attended_b = attended.reshape(row_count, D).astype(jnp.bfloat16)
        middle, normed_two, hidden, active, _ = layer_rest(
            inputs_row, attended_b, gain_pair, bias_row, out_w, up_w, down_w
        )
        grad_down_b = result_gradient.astype(jnp.bfloat16)
        grad_wdown = jnp.dot(active.T, grad_down_b, preferred_element_type=jnp.float32)
        grad_active = jnp.dot(grad_down_b, down_w.T, preferred_element_type=jnp.float32)
        _, gelu_back = jax.vjp(gelu_tanh, hidden)
        grad_hidden = gelu_back(grad_active)[0]
        grad_hidden_b = grad_hidden.astype(jnp.bfloat16)
        grad_wup = jnp.dot(normed_two.T, grad_hidden_b, preferred_element_type=jnp.float32)
        grad_normed_two = jnp.dot(grad_hidden_b, up_w.T, preferred_element_type=jnp.float32)
        _, norm_back_two = jax.vjp(layer_norm, middle, gain_pair[1], bias_row[D : 2 * D])
        grad_middle_part, grad_gain_two, grad_offset_two = norm_back_two(grad_normed_two)
        grad_middle = result_gradient + grad_middle_part
        grad_proj_b = grad_middle.astype(jnp.bfloat16)
        grad_wout = jnp.dot(attended_b.T, grad_proj_b, preferred_element_type=jnp.float32)
        grad_att_flat = jnp.dot(grad_proj_b, out_w.T, preferred_element_type=jnp.float32).astype(
            jnp.bfloat16
        )
        grad_att = grad_att_flat.reshape(row_count, HEADS, HDIM)
        delta = jnp.einsum("rhe,rhe->hr", grad_att.astype(jnp.float32), attended)
        grad_q, grad_k, grad_v = backward_summed(
            queries,
            own_pos,
            key_all,
            value_all,
            whole_pos,
            log_total,
            delta,
            grad_att,
            signed,
            key_block,
        )
        grad_qkv_b = jnp.concatenate([grad_q, grad_k, grad_v], axis=1).astype(jnp.bfloat16)
        grad_wqkv = jnp.dot(normed.T, grad_qkv_b, preferred_element_type=jnp.float32)
        grad_normed = jnp.dot(grad_qkv_b, qkv_w.T, preferred_element_type=jnp.float32)
        _, norm_back_one = jax.vjp(layer_norm, inputs_row, gain_pair[0], bias_row[0:D])
        grad_in_part, grad_gain_one, grad_offset_one = norm_back_one(grad_normed)
        input_gradient = grad_middle + grad_in_part
        grad_gain_rows = jnp.stack([grad_gain_one, grad_gain_two])
        grad_bias_row = jnp.concatenate(
            [
                grad_offset_one,
                grad_offset_two,
                jnp.sum(grad_q, axis=0),
                jnp.sum(grad_v, axis=0),
                jnp.sum(grad_middle, axis=0),
                jnp.sum(result_gradient, axis=0),
                jnp.sum(grad_hidden, axis=0),
            ]
        )
        return (
            input_gradient,
            (grad_gain_rows, grad_bias_row, grad_wqkv, grad_wout, grad_wup, grad_wdown),
        )

    def tick(tick_at, state_in):
        arrived, returned, stored, acts_rows, grad_rows, partial_sums = state_in
        ahead = tick_at - section_at
        ahead_ok = (ahead >= 0) & (ahead < micro_count)
        ahead_at = jnp.clip(ahead, 0, micro_count - 1)
        fresh = jnp.where(
            signed, lax.dynamic_index_in_dim(first_inputs, ahead_at, 0, keepdims=False), arrived
        )
        previous = lax.dynamic_index_in_dim(stored, ahead_at, 0, keepdims=False)
        entry = jnp.where(ahead_ok, fresh, previous)
        stored = lax.dynamic_update_index_in_dim(stored, entry, ahead_at, 0)
        sent = layer_forward(entry, ahead_at)
        old_acts = lax.dynamic_index_in_dim(acts_rows, ahead_at, 0, keepdims=False)
        acts_rows = lax.dynamic_update_index_in_dim(
            acts_rows, jnp.where(ahead_ok, sent, old_acts), ahead_at, 0
        )
        behind = tick_at - 2 + section_at
        trailing_valid = (behind >= 0) & (behind < micro_count)
        trailing_position = jnp.clip(behind, 0, micro_count - 1)
        entry_gradient = lax.dynamic_index_in_dim(stored, trailing_position, 0, keepdims=False)
        given_cot = lax.dynamic_index_in_dim(cot_rows, trailing_position, 0, keepdims=False).astype(
            jnp.float32
        )
        result_gradient = jnp.where(signed, returned.astype(jnp.float32), given_cot)
        input_gradient, added_terms = layer_reverse_pass(
            entry_gradient, result_gradient, trailing_position
        )
        partial_sums = jax.tree.map(
            lambda running_total, added_term: running_total
            + jnp.where(trailing_valid, added_term, 0.0),
            partial_sums,
            added_terms,
        )
        handed = input_gradient.astype(jnp.bfloat16)
        kept_grad = jnp.where(signed, input_gradient, handed.astype(jnp.float32))
        old_grads = lax.dynamic_index_in_dim(grad_rows, trailing_position, 0, keepdims=False)
        grad_rows = lax.dynamic_update_index_in_dim(
            grad_rows, jnp.where(trailing_valid, kept_grad, old_grads), trailing_position, 0
        )
        arrived = shifted(sent, "section", 1)
        returned = shifted(handed, "section", -1)
        return (arrived, returned, stored, acts_rows, grad_rows, partial_sums)

    zero_rows = jnp.zeros((row_count, D), jnp.bfloat16)
    start_sums = (
        jnp.zeros((2, D), jnp.float32),
        jnp.zeros((bias_row.shape[0],), jnp.float32),
        jnp.zeros(qkv_w.shape, jnp.float32),
        jnp.zeros(out_w.shape, jnp.float32),
        jnp.zeros(up_w.shape, jnp.float32),
        jnp.zeros(down_w.shape, jnp.float32),
    )
    start_state = (
        zero_rows,
        zero_rows,
        jnp.zeros((micro_count, row_count, D), jnp.bfloat16),
        jnp.zeros((micro_count, row_count, D), jnp.bfloat16),
        jnp.zeros((micro_count, row_count, D), jnp.float32),
        start_sums,
    )
    final_state = lax.fori_loop(0, micro_count + 2, tick, start_state)
    acts_rows = final_state[3]
    grad_rows = final_state[4]
    partial_sums = final_state[5]
    totals = (
        lax.psum_scatter(partial_sums[0], ("dp", "ctx"), scatter_dimension=1, tiled=True),
        lax.psum_scatter(partial_sums[1], ("dp", "ctx"), scatter_dimension=0, tiled=True),
        lax.psum_scatter(partial_sums[2], ("dp", "ctx"), scatter_dimension=0, tiled=True),
        lax.psum_scatter(partial_sums[3], ("dp", "ctx"), scatter_dimension=0, tiled=True),
        lax.psum_scatter(partial_sums[4], ("dp", "ctx"), scatter_dimension=0, tiled=True),
        lax.psum_scatter(partial_sums[5], ("dp", "ctx"), scatter_dimension=0, tiled=True),
    )
    return (
        acts_rows[None, :, None],
        grad_rows[None, :, None],
        totals[0][None],
        totals[1][None],
        totals[2][None],
        totals[3][None],
        totals[4][None],
        totals[5][None],
    )


def swap_halves(value):
    count = lax.axis_size("ctx")
    return lax.ppermute(value, "ctx", [(at, (at + count // 2) % count) for at in range(count)])


def swap_cores(value):
    return lax.ppermute(value, "ctx", [(at, at ^ 1) for at in range(lax.axis_size("ctx"))])


def swap_z(value, step):
    return lax.ppermute(value, "dp", [(at, at ^ step) for at in range(lax.axis_size("dp"))])


def wide_sum(kept, arrived):
    return kept.astype(jnp.float32) + arrived.astype(jnp.float32)


def fast_body(inputs, slot_order, cotangent, gains, biases, w_qkv, w_out, w_up, w_down):
    rows = inputs.shape[2]
    count = lax.axis_size("ctx")
    z_count = lax.axis_size("dp")
    half = count // 2
    ctx_at = lax.axis_index("ctx")
    mine = ctx_at // half
    y_at, core_at = ctx_at // 2, ctx_at % 2
    signed = lax.axis_index("section") == 0
    which = signed.astype(jnp.int32)[None]
    place = core_at[None].astype(jnp.int32)
    y_place = y_at[None].astype(jnp.int32)
    z_at = lax.axis_index("dp")
    gain_pair = gains[0]
    wide, narrow, barrier = jnp.float32, jnp.bfloat16, lax.optimization_barrier

    def gathered(value):
        kept = lax.dynamic_index_in_dim(value, mine, 0, keepdims=False)
        sent = lax.dynamic_index_in_dim(value, 1 - mine, 0, keepdims=False)
        return jnp.concatenate([kept, swap_halves(sent)], axis=0)

    def returned(kept, arrived):
        arrived = arrived.astype(kept.dtype)
        first = jnp.where(mine == 0, kept, arrived)
        second = jnp.where(mine == 0, arrived, kept)
        return jnp.stack([first, second])

    order = lax.dynamic_index_in_dim(slot_order[:, 0], mine, 0, keepdims=False)
    pairs = order.reshape(count, 2)

    def slots_of(device):
        return jnp.concatenate([pairs[device], pairs[(device + half) % count]])

    meta = slot_meta(slots_of(ctx_at), slots_of(ctx_at ^ 1), signed)

    inputs, meta = barrier((inputs, meta))
    first = gathered(inputs[:, 0])
    qkv_t, out_t = flip(w_qkv, pltpu.HBM), flip(w_out, pltpu.HBM)
    first, qkv_t, out_t = barrier((first, qkv_t, out_t))
    _, queries, kv = front(first, gain_pair, biases, w_qkv)
    attended, _ = sorted_attend(meta, queries, kv, swap_cores(kv))
    sent = rest(first, attended, gain_pair, biases, w_out, w_up, w_down)
    sent, later = barrier((sent, (cotangent, w_up, w_down)))
    arrived = shifted(sent, "section", 1)
    given = gathered(later[0][:, 0])
    up_t, down_t = [flip(weight, pltpu.HBM) for weight in later[1:]]
    arrived, given, up_t, down_t = barrier((arrived, given, up_t, down_t))
    entry, normed, queries, kv = chosen_front(which, first, arrived, gain_pair, biases, w_qkv)
    kv_there = swap_cores(kv)
    normed_t = flip(normed, pltpu.HBM)
    kv_there, normed_t = barrier((kv_there, normed_t))
    attended, lse = sorted_attend(meta, queries, kv, kv_there)
    middle, normed_two, active, slope, grad_middle, grad_att = turn(
        entry, attended, given, gain_pair, biases, w_out, w_up, out_t, up_t, down_t
    )

    waiting = meta.at[-1].set(jnp.where(signed, IDLE, 0))
    grad_q, own, sent = sorted_attend_back(waiting, queries, kv, kv_there, attended, grad_att, lse)
    own, sent, attended, normed_two = barrier((own, sent, attended, normed_two))
    there = swap_cores(sent)
    attended_t, normed_two_t = flip(attended, pltpu.HBM), flip(normed_two, pltpu.HBM)
    there, attended_t, normed_two_t = barrier((there, attended_t, normed_two_t))
    handed, _ = front_back(grad_q, own, there, entry, grad_middle, gain_pair, qkv_t, narrow)
    handed, active, middle, weights = barrier((handed, active, middle, (w_up, w_down)))
    back = shifted(handed, "section", -1)
    result = middle + dot(active, w_down[0], NN) + biases[0, 5 * D : 6 * D]
    result = result.astype(narrow)
    acts_there = swap_halves(result[rows:])
    middle, acts_there, active = barrier((middle, acts_there, active))
    up_t, down_t = [flip(in_hbm(weight), pltpu.VMEM) for weight in weights]
    active_t = flip(active, pltpu.VMEM)
    back, up_t, down_t, active_t = barrier((back, up_t, down_t, active_t))

    z_steps = [1 << at for at in range(z_count.bit_length() - 1)]
    split = [2] * len(z_steps)
    by_z = [((z_at >> at) & 1)[None].astype(jnp.int32) for at in range(len(z_steps))]

    def bits(value, before):
        return value.reshape(value.shape[:before] + tuple(split) + value.shape[before + 1 :])

    places = jnp.concatenate([place, y_place, by_z[0]])
    back, grad_hidden, grad_middle, grad_att, sums_two, up_sum = down_back(
        which, back, given, slope, middle, gain_pair, out_t, up_t, down_t
    )
    back, grad_hidden = barrier((back, grad_hidden))
    down_there = down_sent(places, active_t, back, z_count)
    grad_hidden, down_there = barrier((grad_hidden, down_there))
    down_there = swap_cores(down_there)
    up_there = up_sent(places, normed_two_t, grad_hidden, z_count)
    down_there, up_there = barrier((down_there, up_there))
    up_there = swap_cores(up_there)
    down_keep, down_send = down_kept(places, active_t, back, down_there, z_count)
    up_there, down_send = barrier((up_there, down_send))
    up_keep, up_send = up_kept(places, normed_two_t, grad_hidden, up_there, z_count)
    grad_att, down_send, up_send = barrier((grad_att, down_send, up_send))
    down_there, up_there = swap_halves(down_send), swap_z(up_send, z_steps[0])
    grad_q, own, sent = sorted_attend_back(meta, queries, kv, kv_there, attended, grad_att, lse)

    grad_q, own, sent, down_there, up_there = barrier((grad_q, own, sent, down_there, up_there))
    there = swap_cores(sent)
    outer_there = outer_sent(places, attended_t, normed_t, grad_middle, grad_q, z_count)
    there, outer_there = barrier((there, outer_there))
    outer_there = swap_cores(outer_there)
    inner_there = inner_sent(places, normed_t, own, there, z_count)
    inner_there, down_there, up_there = barrier((inner_there, down_there, up_there))
    inner_there = swap_cores(inner_there)
    down_keep, down_send = stream_fold(bits(down_keep, 0), bits(down_there, 0), by_z[0], len(split) - 1)
    up_keep, up_send = stream_fold(up_keep, up_there, by_z[1], 1)
    outer_there, inner_there, down_send, up_send = barrier((outer_there, inner_there, down_send, up_send))
    rest_keep, rest_send = rest_kept(
        places, attended_t, normed_t, grad_middle, grad_q, own, there, outer_there, inner_there, z_count
    )
    rest_send, down_send, up_send, grad_q, own, there = barrier((rest_send, down_send, up_send, grad_q, own, there))
    rest_there, down_there, up_there = swap_halves(rest_send), swap_z(down_send, z_steps[0]), swap_z(up_send, z_steps[1])
    input_gradient, sums_one = front_back(grad_q, own, there, entry, grad_middle, gain_pair, qkv_t, wide)
    small = jnp.concatenate([sums_one, sums_two, up_sum], axis=0)
    small = small + swap_cores(small)
    rounded = input_gradient.astype(narrow)
    small_there = swap_halves(small)
    down_there, rounded = barrier((down_there, rounded))
    down_keep, down_send = fold(down_keep, down_there, by_z[1], 0)
    down_send, rest_there, small_there = barrier((down_send, rest_there, small_there))
    down_there = swap_z(down_send, z_steps[1])

    rest_keep, rest_send = fold(bits(rest_keep, 0), bits(rest_there, 0), by_z[0], len(split) - 1)
    small = small + small_there
    rest_send, up_there, small = barrier((rest_send, up_there, small))
    rest_there, small_there = swap_z(rest_send, z_steps[0]), swap_z(small, z_steps[0])
    up_keep, up_send = fold(up_keep, up_there, y_place, 0)
    up_there = swap_halves(up_send)
    rounded, up_send = barrier((rounded, up_send))
    grads_there = swap_halves(rounded[rows:])
    rest_there, up_there, small_there, down_there, grads_there = barrier(
        (rest_there, up_there, small_there, down_there, grads_there)
    )
    rest_keep, rest_send = fold(rest_keep, rest_there, by_z[1], 0)
    rest_send, small_there, grads_there, result, acts_there = barrier(
        (rest_send, small_there, grads_there, result, acts_there)
    )
    rest_there = swap_z(rest_send, z_steps[1])
    small = small + small_there
    small = small + swap_z(small, z_steps[1])
    wdown = wide_sum(down_keep, down_there)
    wup = wide_sum(up_keep, up_there)
    grads_kept = jnp.where(signed, input_gradient[:rows], rounded[:rows].astype(wide))
    grad_rows = returned(grads_kept, grads_there)
    grad_rows, rest_there = barrier((grad_rows, rest_there))
    wout = wide_sum(rest_keep[:, :D], rest_there[:, :D])
    wqkv = wide_sum(rest_keep[:, D:], rest_there[:, D:])
    blocks = count * z_count
    block_at = lax.axis_index("dp") * count + ctx_at
    gain_piece = lax.dynamic_slice_in_dim(small[0:5:4], block_at * (D // blocks), D // blocks, 1)
    bias_row = jnp.concatenate([small[1:2], small[5:6], small[2:4], small[6:]], axis=0).reshape(-1)
    width = bias_row.shape[0] // blocks
    bias_piece = lax.dynamic_slice_in_dim(bias_row, block_at * width, width, 0)
    return (
        returned(result[:rows], acts_there)[None, :, None],
        grad_rows[None, :, None],
        gain_piece[None],
        bias_piece[None],
        wqkv[None],
        wout[None],
        wup[None],
        wdown[None],
    )


def body_for(mesh):
    sizes = dict(mesh.shape)
    return fast_body if (sizes["ctx"], sizes["dp"]) == (4, 4) else general_body


def solution(mesh):
    in_specs = (
        P(None, "dp", "ctx", None),
        P(None, "dp", None),
        P(None, "dp", "ctx", None),
        P("section", None, None),
        P("section", None),
        P("section", None, None),
        P("section", None, None),
        P("section", None, None),
        P("section", None, None),
    )
    out_specs = (
        P("section", None, "dp", "ctx", None),
        P("section", None, "dp", "ctx", None),
        P("section", None, ("dp", "ctx")),
        P("section", ("dp", "ctx")),
        P("section", ("dp", "ctx"), None),
        P("section", ("dp", "ctx"), None),
        P("section", ("dp", "ctx"), None),
        P("section", ("dp", "ctx"), None),
    )
    return jax.shard_map(
        body_for(mesh), mesh=mesh, in_specs=in_specs, out_specs=out_specs, check_vma=False
    )
```

```python
import functools
import math
import jax
import jax.numpy as jnp
from jax import lax
from jax.experimental import pallas as pl
from jax.experimental.pallas import tpu as pltpu
from jax.sharding import PartitionSpec as P

D = 768
HEADS = 12
HDIM = 64
PAIR = 2 * HDIM
PAIRS = HEADS // 2
OWN = 4
CHUNK = 128
SAFE = 60.0
NT = (((1,), (1,)), ((), ()))
TN = (((0,), (0,)), ((), ()))
NN = (((1,), (0,)), ((), ()))


def dot(left, right, dims):
    return lax.dot_general(left, right, dims, preferred_element_type=jnp.float32)


def slot_meta(own_pos, other_pos, signed):
    rank = jnp.sum((own_pos[None, :] < own_pos[:, None]).astype(jnp.int32), axis=1)
    chosen = rank[None, :] == jnp.arange(OWN, dtype=jnp.int32)[:, None]
    ranked = jnp.sum(jnp.where(chosen, jnp.arange(OWN, dtype=jnp.int32)[None, :], 0), axis=1)
    ranked_pos = jnp.sum(jnp.where(chosen, own_pos[None, :], 0), axis=1)
    return jnp.concatenate([own_pos, other_pos, ranked, ranked_pos, signed.astype(jnp.int32)[None]])


def sort_rows(meta, own, other, target, span, first):
    columns = slice(first, first + D)
    for slot in range(OWN):
        for base, source in ((0, own), (OWN, other)):
            start = pl.multiple_of(meta[base + slot] * span, span)
            target[pl.ds(start, span), :] = source[slot * span : (slot + 1) * span, columns]


def reach(rank, slots):
    return ((0, slots // 2 - 2), (1, slots // 2 - 1), (slots // 2, slots - 2), (slots // 2 + 1, slots - 1))[rank]


def stacked_heads(rows):
    second = lax.broadcasted_iota(jnp.int32, rows.shape, 1) >= HDIM
    zero = jnp.zeros_like(rows)
    return jnp.concatenate([jnp.where(second, zero, rows), jnp.where(second, rows, zero)], axis=0)


def visible(values, start, least, span, position, fill):
    if start + values.shape[0] <= least * span:
        return values
    key_at = lax.broadcasted_iota(jnp.int32, values.shape, 0) + start
    lane = lax.broadcasted_iota(jnp.int32, values.shape, 1)
    query_at = position * span + jnp.where(lane >= span, lane - span, lane)
    return jnp.where(key_at <= query_at, values, fill)


def unstack(pair, span):
    row = lax.broadcasted_iota(jnp.int32, (PAIR, span), 0)
    return jnp.where(row < HDIM, pair[:, :span], pair[:, span:]).T


def chunks_of(count, chunk):
    return [slice(start, min(start + chunk, count)) for start in range(0, count, chunk)]


def eight(values):
    return values.reshape(-1, 8, values.shape[-1])


def pair_columns(at):
    return pl.ds(pl.multiple_of(at * PAIR, PAIR), PAIR)


def largest_norm(rows_ref):
    feature = lax.broadcasted_iota(jnp.int32, (D, PAIR), 0) // HDIM
    head = lax.broadcasted_iota(jnp.int32, (D, PAIR), 1)
    chosen = jnp.where(feature == head, 1.0, 0.0).astype(jnp.bfloat16)
    rows = rows_ref[...]
    return jnp.max(dot(rows * rows, chosen, NN))


def forward_kernel(meta, q_ref, kv_ref, kv2_ref, o_ref, lse_ref, keys, values, *, span):
    slots = keys.shape[0] // span
    sort_rows(meta, kv_ref, kv2_ref, keys, span, 0)
    sort_rows(meta, kv_ref, kv2_ref, values, span, D)
    bound = largest_norm(q_ref) * largest_norm(keys) * (1.1 / HDIM)
    near = bound < SAFE * SAFE

    def run(signed, safe):
        def one_pair(pair, _):
            columns = pair_columns(pair)
            values_t = values[:, columns].T
            for rank in reversed(range(OWN)):
                least, most = reach(rank, slots)
                count = (most + 1) * span
                row_at = pl.multiple_of(meta[2 * OWN + rank] * span, span)
                position = meta[3 * OWN + rank]
                queries = stacked_heads(q_ref[pl.ds(row_at, span), columns] * 0.125)
                largest = None
                if not safe:
                    most_seen = jnp.full((8, 2 * span), -1e30, jnp.float32)
                    for part in chunks_of(count, CHUNK):
                        scores = dot(keys[part, columns], queries, NT)
                        scores = jnp.abs(scores) if signed else scores
                        scores = visible(scores, part.start, least, span, position, -1e30)
                        most_seen = jnp.maximum(most_seen, jnp.max(eight(scores), axis=0))
                    largest = jnp.max(most_seen, axis=0, keepdims=True)
                    if signed:
                        square = largest * largest + 1.0
                        largest = square * lax.rsqrt(square)
                total = jnp.zeros((8, 2 * span), jnp.float32)
                gathered = jnp.zeros((PAIR, 2 * span), jnp.float32)
                for part in chunks_of(count, CHUNK):
                    scores = dot(keys[part, columns], queries, NT)
                    argument = scores
                    if signed:
                        square = scores * scores + 1.0
                        inverse = lax.rsqrt(square)
                        argument = square * inverse
                    if not safe:
                        argument = argument - largest
                    weights = jnp.exp(visible(argument, part.start, least, span, position, -1e30))
                    total += jnp.sum(eight(weights), axis=0)
                    if signed:
                        weights = weights * (scores * inverse)
                    gathered += dot(values_t[:, part], weights.astype(jnp.bfloat16), NN)
                total = jnp.sum(total, axis=0, keepdims=True)
                lse = jnp.log(total)
                lse_ref[pair, rank : rank + 1, :] = lse if safe else lse + largest
                gathered = gathered * (1.0 / total)
                o_ref[pl.ds(row_at, span), columns] = unstack(gathered, span).astype(jnp.bfloat16)
            return 0

        lax.fori_loop(0, PAIRS, one_pair, 0)

    for signed in (True, False):
        for safe in (True, False):
            chosen = (meta[4 * OWN] == int(signed)) & (near == safe)
            pl.when(chosen)(functools.partial(run, signed, safe))


def in_vmem(*values):
    return [pltpu.with_memory_space_constraint(value, pltpu.VMEM) for value in values]


SMEM_SPEC = pl.BlockSpec(memory_space=pltpu.SMEM)
VMEM_SPEC = pl.BlockSpec(memory_space=pltpu.VMEM)


def sorted_attend(meta, queries, kv, kv_other):
    rows = kv.shape[0]
    span = rows // OWN
    return pl.pallas_call(
        functools.partial(forward_kernel, span=span),
        in_specs=[SMEM_SPEC] + [VMEM_SPEC] * 3,
        out_specs=[VMEM_SPEC] * 2,
        scratch_shapes=[pltpu.VMEM((2 * rows, D), jnp.bfloat16)] * 2,
        out_shape=[
            jax.ShapeDtypeStruct((rows, D), jnp.bfloat16),
            jax.ShapeDtypeStruct((PAIRS, OWN, 2 * span), jnp.float32),
        ],
        compiler_params=pltpu.CompilerParams(vmem_limit_bytes=10 * 1024 * 1024),
        cost_estimate=pl.CostEstimate(flops=4_000_000_000, bytes_accessed=0, transcendentals=0),
        name="attend",
    )(meta, *in_vmem(queries, kv, kv_other))


def reaches(slots, span):
    found, at = [], 0
    for rank in range(OWN):
        least, most = reach(rank, slots)
        found.append((least, (most + 1) * span, at))
        at += (most + 1) * span
    return found, at


def kept_copies(pair, side, factor_buf, weight_buf, factors, weights, done, out):
    copies = []
    for part, (buffer, far) in enumerate(((factor_buf, factors), (weight_buf, weights))):
        near, there = buffer.at[side], far.at[pair]
        source, target = (near, there) if out else (there, near)
        copies.append(pltpu.make_async_copy(source, target, done.at[side, part]))
    return copies


def backward_kernel(
    meta, q_ref, kv_ref, kv2_ref, o_ref, do_ref, lse_ref, *refs, span, prepare
):
    if prepare:
        dq_ref, own_ref, other_ref, factors, weight_rows, *scratch = refs
    else:
        factors, weight_rows, dq_ref, own_ref, other_ref, *scratch = refs
    keys, values, grad_k, grad_v, factor_buf, weight_buf, done = scratch
    slots = keys.shape[0] // span
    ranks, _ = reaches(slots, span)
    sort_rows(meta, kv_ref, kv2_ref, keys, span, 0)
    sort_rows(meta, kv_ref, kv2_ref, values, span, D)

    def copies(pair, side):
        return kept_copies(pair, side, factor_buf, weight_buf, factors, weight_rows, done, prepare)

    def queries_at(rank, columns):
        row_at = pl.multiple_of(meta[2 * OWN + rank] * span, span)
        return row_at, stacked_heads(q_ref[pl.ds(row_at, span), columns] * 0.125)

    def make_ahead():
        def one_pair(pair, _):
            side = lax.rem(pair, 2)
            columns = pair_columns(pair)

            @pl.when(pair >= 2)
            def _():
                for copy in copies(pair, side):
                    copy.wait()

            for rank, (least, count, start) in enumerate(ranks):
                _, queries = queries_at(rank, columns)
                scores = dot(keys[:count, columns], queries, NT)
                square = scores * scores + 1.0
                inverse = lax.rsqrt(square)
                argument = square * inverse - lse_ref[pair, rank : rank + 1, :]
                prob = jnp.exp(visible(argument, 0, least, span, meta[3 * OWN + rank], -1e30))
                sign_pattern = scores * inverse
                factor = prob * (sign_pattern * sign_pattern + inverse * inverse * inverse)
                factor_buf[side, start : start + count, :] = factor.astype(jnp.bfloat16)
                weight_buf[side, start : start + count, :] = (prob * sign_pattern).astype(jnp.bfloat16)
            for copy in copies(pair, side):
                copy.start()
            return 0

        lax.fori_loop(0, PAIRS, one_pair, 0)
        for pair in range(PAIRS - 2, PAIRS):
            for copy in copies(pair, pair % 2):
                copy.wait()
        for out_ref in (dq_ref, own_ref, other_ref):
            out_ref[...] = jnp.zeros_like(out_ref)

    def run(made):
        if made:
            for copy in copies(0, 0):
                copy.start()

        def one_pair(pair, _):
            side = lax.rem(pair, 2)
            columns = pair_columns(pair)
            keys_t = keys[:, columns].T
            if made:

                @pl.when(pair + 1 < PAIRS)
                def _():
                    for copy in copies(pair + 1, 1 - side):
                        copy.start()

                for copy in copies(pair, side):
                    copy.wait()
            for rank in reversed(range(OWN)):
                least, count, start = ranks[rank]
                row_at, queries = queries_at(rank, columns)
                grad_rows = do_ref[pl.ds(row_at, span), columns]
                grads = stacked_heads(grad_rows)
                product = grad_rows.astype(jnp.float32) * o_ref[pl.ds(row_at, span), columns].astype(jnp.float32)
                delta = jnp.sum(stacked_heads(product).T, axis=0, keepdims=True)
                along = dot(values[:count, columns], grads, NT)
                if made:
                    weights = weight_buf[side, start : start + count, :]
                    factor = factor_buf[side, start : start + count, :].astype(jnp.float32)
                    dscore = factor * along - weights.astype(jnp.float32) * delta
                else:
                    scores = dot(keys[:count, columns], queries, NT)
                    argument = scores - lse_ref[pair, rank : rank + 1, :]
                    weights = jnp.exp(visible(argument, 0, least, span, meta[3 * OWN + rank], -1e30))
                    dscore = weights * (along - delta)
                    weights = weights.astype(jnp.bfloat16)
                dscore = dscore.astype(jnp.bfloat16)
                added_v = dot(weights, grads, NN)
                added_k = dot(dscore, queries, NN)
                if rank == OWN - 1:
                    grad_v[...] = added_v
                    grad_k[...] = added_k
                else:
                    grad_v[:count, :] += added_v
                    grad_k[:count, :] += added_k
                gathered = dot(keys_t[:, :count], dscore, NN)
                dq_ref[pl.ds(row_at, span), columns] = (unstack(gathered, span) * 0.125).astype(jnp.bfloat16)
            for slot in range(OWN):
                there = slice(slot * span, (slot + 1) * span)
                own_at = pl.multiple_of(meta[slot] * span, span)
                other_at = pl.multiple_of(meta[OWN + slot] * span, span)
                for part, total in enumerate((grad_k, grad_v)):
                    own_ref[part, there, columns] = total[pl.ds(own_at, span), :].astype(jnp.bfloat16)
                    other_ref[part, there, columns] = total[pl.ds(other_at, span), :].astype(jnp.bfloat16)
            return 0

        lax.fori_loop(0, PAIRS, one_pair, 0)

    pl.when(meta[4 * OWN] == 0)(functools.partial(run, False))
    pl.when(meta[4 * OWN] == 1)(make_ahead if prepare else functools.partial(run, True))


def sorted_attend_back(meta, queries, kv, kv_other, attended, grad_att, lse, made=None):
    rows = kv.shape[0]
    span = rows // OWN
    narrow = jnp.bfloat16
    _, reached = reaches(2 * OWN, span)
    far_spec = pl.BlockSpec(memory_space=pltpu.HBM)
    ahead = [pltpu.HBM((PAIRS, reached, 2 * span), narrow)] * 2
    shapes = [jax.ShapeDtypeStruct((rows, D), narrow)] + [jax.ShapeDtypeStruct((2, rows, D), narrow)] * 2
    prepare = made is None
    given = () if prepare else tuple(pltpu.with_memory_space_constraint(value, pltpu.HBM) for value in made)
    return pl.pallas_call(
        functools.partial(backward_kernel, span=span, prepare=prepare),
        in_specs=[SMEM_SPEC] + [VMEM_SPEC] * 6 + [far_spec] * len(given),
        out_specs=[VMEM_SPEC] * 3 + [far_spec] * (2 if prepare else 0),
        scratch_shapes=[pltpu.VMEM((2 * rows, D), narrow)] * 2
        + [pltpu.VMEM((2 * rows, PAIR), jnp.float32)] * 2
        + [pltpu.VMEM((2, reached, 2 * span), narrow)] * 2
        + [pltpu.SemaphoreType.DMA((2, 2))],
        out_shape=shapes + (ahead if prepare else []),
        compiler_params=pltpu.CompilerParams(vmem_limit_bytes=18 * 1024 * 1024),
        cost_estimate=pl.CostEstimate(flops=8_000_000_000, bytes_accessed=0, transcendentals=0),
        name="attend_back",
    )(meta, *in_vmem(queries, kv, kv_other, attended, grad_att), lse, *given)


TURN_TANH = 0.7978845608028654
CUBE = 0.044715
CHUNKS = 1


def normalised(rows):
    center = rows - jnp.mean(rows, axis=-1, keepdims=True)
    inverse = lax.rsqrt(jnp.mean(center * center, axis=-1, keepdims=True) + 1e-05)
    return center * inverse, inverse


def norm_back(unit, inverse, gain_row, grad):
    scaled = grad * gain_row
    along = jnp.mean(scaled * unit, axis=-1, keepdims=True)
    return inverse * (scaled - jnp.mean(scaled, axis=-1, keepdims=True) - unit * along)


def row_chunks(rows, chunks=CHUNKS):
    return [slice(at * rows // chunks, (at + 1) * rows // chunks) for at in range(chunks)]


def column_sum(values):
    return jnp.sum(values, axis=0, keepdims=True)


def gelu_parts(hidden):
    square = hidden * hidden
    curve = jnp.tanh(hidden * (TURN_TANH + TURN_TANH * CUBE * square))
    half = 0.5 + 0.5 * curve
    inner = hidden * (TURN_TANH + 3.0 * TURN_TANH * CUBE * square)
    return hidden * half, half + 0.5 * (1.0 - curve * curve) * inner


def gelu_only(hidden):
    square = hidden * hidden
    curve = jnp.tanh(hidden * (TURN_TANH + TURN_TANH * CUBE * square))
    return hidden * (0.5 + 0.5 * curve)


def cost(flops):
    return pl.CostEstimate(flops=int(flops) // 8, bytes_accessed=0, transcendentals=0)


def in_hbm(value):
    return pltpu.with_memory_space_constraint(value, pltpu.HBM)


def placed(shape, dtype, space=None):
    return jax.ShapeDtypeStruct(shape, dtype) if space is None else space(shape, dtype)


def call(kernel, name, megabytes, flops, outs, scratch, *operands, smem=0):
    return pl.pallas_call(
        kernel,
        in_specs=[SMEM_SPEC] * smem + [VMEM_SPEC] * (len(operands) - smem),
        out_specs=[VMEM_SPEC] * len(outs),
        out_shape=[placed(*out) for out in outs],
        scratch_shapes=scratch,
        compiler_params=pltpu.CompilerParams(vmem_limit_bytes=megabytes * 1024 * 1024),
        cost_estimate=cost(flops),
        name=name,
    )(*operands)


def bias_part(biases, at):
    return biases[0:1, at * D : (at + 1) * D]


def tile(at):
    return slice(at * D, (at + 1) * D)


def whole(*shape):
    return pl.BlockSpec(shape, lambda *_: (0,) * len(shape))


def flip_kernel(in_ref, out_ref):
    out_ref[...] = in_ref[...].T


def copy_kernel(in_ref, out_ref):
    out_ref[...] = in_ref[...]


def fetched(value):
    height, width = value.shape
    block = pl.BlockSpec((height // 4, width), lambda i: (i, 0))
    return pl.pallas_call(
        copy_kernel,
        grid=(4,),
        in_specs=[block],
        out_specs=block,
        out_shape=placed(value.shape, value.dtype, pltpu.VMEM),
        compiler_params=pltpu.CompilerParams(vmem_limit_bytes=7 * 1024 * 1024),
        cost_estimate=cost(0),
        name="fetched",
    )(in_hbm(value))


def flip(value, space=None):
    height, width = value.shape[-2:]
    lead = (None,) * (value.ndim - 2)
    zeros = (0,) * (value.ndim - 2)
    if height > D:
        grid = height // D
        in_spec = pl.BlockSpec(lead + (D, width), lambda i: zeros + (i, 0))
        out_spec = pl.BlockSpec((width, D), lambda i: (0, i))
    else:
        step = min(width, D)
        grid = width // step
        in_spec = pl.BlockSpec(lead + (height, step), lambda i: zeros + (0, i))
        out_spec = pl.BlockSpec((step, height), lambda i: (i, 0))
    return pl.pallas_call(
        flip_kernel,
        grid=(grid,),
        in_specs=[in_spec],
        out_specs=out_spec,
        out_shape=placed((width, height), value.dtype, space),
        compiler_params=pltpu.CompilerParams(vmem_limit_bytes=7 * 1024 * 1024),
        cost_estimate=cost(0),
        name="flip",
    )(value)


def front_rows(x_ref, gains, biases, w_ref, normed_ref, q_ref, kv_ref):
    for part in row_chunks(x_ref.shape[0]):
        unit, _ = normalised(x_ref[part, :].astype(jnp.float32))
        normed = (unit * gains[0:1, :] + bias_part(biases, 0)).astype(jnp.bfloat16)
        normed_ref[part, :] = normed
        kv_ref[part, :D] = dot(normed, w_ref[0, :, tile(1)], NN).astype(jnp.bfloat16)
        kv_ref[part, D:] = (dot(normed, w_ref[0, :, tile(2)], NN) + bias_part(biases, 3)).astype(jnp.bfloat16)
        q_ref[part, :] = (dot(normed, w_ref[0, :, tile(0)], NN) + bias_part(biases, 2)).astype(jnp.bfloat16)


def choose(which, first_ref, second_ref, chosen_ref):
    for index, source in ((1, first_ref), (0, second_ref)):

        @pl.when(which[0] == index)
        def _():
            chosen_ref[...] = source[...]


def chosen_front_kernel(which, first_ref, second_ref, gains, biases, w_ref, chosen_ref, normed_ref, q_ref, kv_ref):
    choose(which, first_ref, second_ref, chosen_ref)
    front_rows(chosen_ref, gains, biases, w_ref, normed_ref, q_ref, kv_ref)


def front_outs(rows):
    narrow = jnp.bfloat16
    return [((rows, D), narrow), ((rows, D), narrow), ((rows, 2 * D), narrow)]


def front(entry, gains, biases, w_qkv):
    rows = entry.shape[0]
    return call(front_rows, "front", 8, 6 * rows * D * D, front_outs(rows), [], entry, gains, biases, w_qkv)


def chosen_front(which, first, second, gains, biases, w_qkv):
    rows = first.shape[0]
    outs = [((rows, D), jnp.bfloat16)] + front_outs(rows)
    return call(
        chosen_front_kernel, "chosen_front", 8, 6 * rows * D * D, outs, [],
        which, first, second, gains, biases, w_qkv, smem=1,
    )


def middle_rows(x_ref, o_ref, w_out, biases, part):
    return x_ref[part, :].astype(jnp.float32) + dot(o_ref[part, :], w_out[0], NN) + bias_part(biases, 4)


def rest_kernel(x_ref, o_ref, gains, biases, w_out, w_up, w_down, result_ref):
    for part in row_chunks(x_ref.shape[0]):
        middle = middle_rows(x_ref, o_ref, w_out, biases, part)
        unit, _ = normalised(middle)
        normed = (unit * gains[1:2, :] + bias_part(biases, 1)).astype(jnp.bfloat16)
        total = middle + bias_part(biases, 5)
        for at in range(w_up.shape[2] // D):
            hidden = dot(normed, w_up[0, :, tile(at)], NN) + bias_part(biases, 6 + at)
            total += dot(gelu_only(hidden).astype(jnp.bfloat16), w_down[0, tile(at), :], NN)
        result_ref[part, :] = total.astype(jnp.bfloat16)


def rest(entry, attended, gains, biases, w_out, w_up, w_down):
    rows = entry.shape[0]
    flops = 2 * rows * (D * D + 2 * w_up.size)
    return call(
        rest_kernel, "rest", 7, flops, [((rows, D), jnp.bfloat16)], [],
        entry, attended, gains, biases, w_out, w_up, w_down,
    )[0]


def turn_kernel(
    x_ref, o_ref, d_ref, gains, biases, w_out, w_up, out_t, up_t, down_t,
    middle_ref, normed_ref, active_ref, slope_ref, grad_ref, grad_att_ref,
    middle, normed, actives, slopes, done,
):
    copies = []

    def leave(source, target):
        copies.append(pltpu.make_async_copy(source, target, done.at[len(copies)]))
        copies[-1].start()

    rows = x_ref[...].astype(jnp.float32) + dot(o_ref[...], w_out[0], NN) + bias_part(biases, 4)
    middle[...] = rows
    leave(middle, middle_ref)
    unit, _ = normalised(rows)
    normed[...] = (unit * gains[1:2, :] + bias_part(biases, 1)).astype(jnp.bfloat16)
    leave(normed, normed_ref)
    total = jnp.zeros_like(rows)
    for at in range(w_up.shape[2] // D):
        hidden = dot(normed[...], w_up[0, :, tile(at)], NN) + bias_part(biases, 6 + at)
        active, slope = gelu_parts(hidden)
        actives[at] = active.astype(jnp.bfloat16)
        slopes[at] = slope.astype(jnp.bfloat16)
        leave(actives.at[at], active_ref.at[:, tile(at)])
        leave(slopes.at[at], slope_ref.at[:, tile(at)])
        grad_hidden = dot(d_ref[...], down_t[:, tile(at)], NN) * slope
        total += dot(grad_hidden.astype(jnp.bfloat16), up_t[tile(at), :], NN)
    unit, inverse = normalised(middle[...])
    grad = d_ref[...].astype(jnp.float32) + norm_back(unit, inverse, gains[1:2, :], total)
    grad = grad.astype(jnp.bfloat16)
    grad_ref[...] = grad
    grad_att_ref[...] = dot(grad, out_t[...], NN).astype(jnp.bfloat16)
    for copy in copies:
        copy.wait()


def turn(entry, attended, result_gradient, gains, biases, w_out, w_up, out_t, up_t, down_t):
    rows = entry.shape[0]
    wide, narrow = jnp.float32, jnp.bfloat16
    inner = w_up.shape[2]
    steps = inner // D
    far = [((rows, D), wide), ((rows, D), narrow), ((rows, inner), narrow), ((rows, inner), narrow)]
    return pl.pallas_call(
        turn_kernel,
        in_specs=[VMEM_SPEC] * 10,
        out_specs=[pl.BlockSpec(memory_space=pltpu.HBM)] * len(far) + [VMEM_SPEC] * 2,
        out_shape=[placed(*out, pltpu.HBM) for out in far] + [placed((rows, D), narrow)] * 2,
        scratch_shapes=[
            pltpu.VMEM((rows, D), wide),
            pltpu.VMEM((rows, D), narrow),
            pltpu.VMEM((steps, rows, D), narrow),
            pltpu.VMEM((steps, rows, D), narrow),
            pltpu.SemaphoreType.DMA((2 + 2 * steps,)),
        ],
        compiler_params=pltpu.CompilerParams(vmem_limit_bytes=18 * 1024 * 1024),
        cost_estimate=cost(2 * rows * (2 * D * D + 3 * w_up.size)),
        name="turn",
    )(entry, attended, result_gradient, gains, biases, w_out, w_up, out_t, up_t, down_t)


def down_back_kernel(
    which, first_ref, second_ref, slope_ref, middle_ref, gains, out_t, up_t, down_t,
    d_ref, hidden_ref, grad_ref, grad_att_ref, sums_ref, up_ref,
):
    choose(which, first_ref, second_ref, d_ref)
    sums = [jnp.zeros((1, D), jnp.float32)] * 4
    steps = up_t.shape[0] // D
    up_sums = [jnp.zeros((1, D), jnp.float32)] * steps
    for part in row_chunks(d_ref.shape[0]):
        given = d_ref[part, :]
        through = jnp.zeros(given.shape, jnp.float32)
        for at in range(steps):
            grad_hidden = dot(given, down_t[:, tile(at)], NN) * slope_ref[part, tile(at)].astype(jnp.float32)
            up_sums[at] = up_sums[at] + column_sum(grad_hidden)
            grad_hidden = grad_hidden.astype(jnp.bfloat16)
            hidden_ref[part, tile(at)] = grad_hidden
            through += dot(grad_hidden, up_t[tile(at), :], NN)
        unit, inverse = normalised(middle_ref[part, :])
        given = given.astype(jnp.float32)
        grad = given + norm_back(unit, inverse, gains[1:2, :], through)
        grad_b = grad.astype(jnp.bfloat16)
        grad_ref[part, :] = grad_b
        grad_att_ref[part, :] = dot(grad_b, out_t[...], NN).astype(jnp.bfloat16)
        for at, term in enumerate((through * unit, through, grad, given)):
            sums[at] = sums[at] + column_sum(term)
    sums_ref[...] = jnp.concatenate(sums, axis=0)
    up_ref[...] = jnp.concatenate(up_sums, axis=0)


def down_back(which, first, second, slope, middle, gains, out_t, up_t, down_t):
    rows = first.shape[0]
    wide, narrow = jnp.float32, jnp.bfloat16
    inner = up_t.shape[0]
    outs = [
        ((rows, D), narrow), ((rows, inner), narrow), ((rows, D), narrow), ((rows, D), narrow),
        ((4, D), wide), ((inner // D, D), wide),
    ]
    return call(
        down_back_kernel, "down_back", 8, 2 * rows * (D * D + 2 * up_t.size), outs, [],
        which, first, second, slope, middle, gains, out_t, up_t, down_t, smem=1,
    )


def qkv_tiles(part, q_ref, own_ref, there_ref):
    tiles = [q_ref[part, :]]
    for at in range(2):
        total = own_ref[at, part, :].astype(jnp.float32) + there_ref[at, part, :].astype(jnp.float32)
        tiles.append(total.astype(jnp.bfloat16))
    return tiles


def front_back_kernel(q_ref, own_ref, there_ref, x_ref, grad_ref, gains, qkv_t, out_ref, sums_ref):
    sums = [jnp.zeros((1, D), jnp.float32)] * 4
    for part in row_chunks(x_ref.shape[0]):
        tiles = qkv_tiles(part, q_ref, own_ref, there_ref)
        through = sum(dot(value, qkv_t[tile(at), :], NN) for at, value in enumerate(tiles))
        unit, inverse = normalised(x_ref[part, :].astype(jnp.float32))
        out = grad_ref[part, :].astype(jnp.float32) + norm_back(unit, inverse, gains[0:1, :], through)
        out_ref[part, :] = out.astype(out_ref.dtype)
        terms = (through * unit, through, tiles[0].astype(jnp.float32), tiles[2].astype(jnp.float32))
        for at, term in enumerate(terms):
            sums[at] = sums[at] + column_sum(term)
    sums_ref[...] = jnp.concatenate(sums, axis=0)


def front_back(grad_q, own, there, entry, grad_middle, gains, qkv_t, dtype):
    rows = entry.shape[0]
    outs = [((rows, D), dtype, pltpu.VMEM), ((4, D), jnp.float32)]
    return call(
        front_back_kernel, "front_back", 8, 6 * rows * D * D, outs, [],
        grad_q, own, there, entry, grad_middle, gains, qkv_t,
    )


def added(kept, arrived, dtype=jnp.bfloat16):
    return (kept.astype(jnp.float32) + arrived.astype(jnp.float32)).astype(dtype)


def core_rows(left_ref, core, order):
    block = left_ref.shape[0] // (2 * len(order))
    picked = [
        left_ref[pl.ds(pl.multiple_of((2 * (2 * z_at + y_at) + core) * block, block), block), :] for z_at, y_at in order
    ]
    return jnp.concatenate(picked, axis=0)


def by_y_then_z(z_count):
    return [(z_at, y_at) for y_at in range(2) for z_at in range(z_count)]


def down_sent_kernel(place, left_ref, right_ref, sent_ref):
    block = sent_ref.shape[2]
    rows = core_rows(left_ref, 1 - place[0], by_y_then_z(1))
    total = dot(rows, right_ref[...], NN).astype(jnp.bfloat16)
    for y_at in range(2):
        sent_ref[y_at, 0] = total[y_at * block : (y_at + 1) * block]


def down_kept_kernel(place, left_ref, right_ref, there_ref, keep_ref, first_ref, second_ref, *, z_count):
    block = keep_ref.shape[1]
    total = dot(core_rows(left_ref, place[0], by_y_then_z(1)), right_ref[...], NN)
    parts = [added(total[y_at * block : (y_at + 1) * block], there_ref[y_at, 0]) for y_at in range(2)]

    def store(mine, send_ref):
        keep_ref[0] = parts[mine]
        send_ref[0] = parts[1 - mine]

    early = pl.program_id(0) < z_count // 2
    for mine in range(2):
        for now, send_ref in ((early, first_ref), (~early, second_ref)):
            pl.when((place[1] == mine) & now)(functools.partial(store, mine, send_ref))


def grid_call(kernel, name, grid, in_specs, out_specs, shapes, scratch, flops, place, *operands, far=0):
    return pl.pallas_call(
        kernel,
        grid_spec=pltpu.PrefetchScalarGridSpec(
            num_scalar_prefetch=1, grid=(grid,), in_specs=in_specs, out_specs=out_specs, scratch_shapes=scratch
        ),
        out_shape=[
            placed(shape, jnp.bfloat16, pltpu.HBM if at < far else None) for at, shape in enumerate(shapes)
        ],
        compiler_params=pltpu.CompilerParams(vmem_limit_bytes=9 * 1024 * 1024),
        cost_estimate=cost(flops),
        name=name,
    )(place, *operands)


def down_specs(active_t, z_count):
    height, rows = active_t.shape
    block = height // (4 * z_count)
    in_specs = [pl.BlockSpec((height // z_count, rows), lambda i, _: (i, 0)), whole(rows, D)]
    return block, in_specs, pl.BlockSpec((2, 1, block, D), lambda i, _: (0, i, 0, 0))


def down_sent(place, active_t, back, z_count):
    block, in_specs, sent_spec = down_specs(active_t, z_count)
    return grid_call(
        down_sent_kernel, "down_sent", z_count, in_specs, [sent_spec], [(2, z_count, block, D)], [],
        active_t.size * D, place, active_t, back,
    )[0]


def down_kept(place, active_t, back, there, z_count):
    block, in_specs, sent_spec = down_specs(active_t, z_count)
    half = z_count // 2
    out_specs = [
        pl.BlockSpec((1, block, D), lambda i, _: (i, 0, 0)),
        pl.BlockSpec((1, block, D), lambda i, _: (jnp.minimum(i, half - 1), 0, 0)),
        pl.BlockSpec((1, block, D), lambda i, _: (jnp.maximum(i - half, 0), 0, 0)),
    ]
    return grid_call(
        functools.partial(down_kept_kernel, z_count=z_count), "down_kept", z_count, in_specs + [sent_spec], out_specs,
        [(z_count, block, D)] + [(half, block, D)] * 2, [],
        active_t.size * D, place, active_t, back, there, far=1,
    )


def up_sent_kernel(place, left_ref, right_ref, sent_ref, rows):
    z_count, block = sent_ref.shape[1:3]
    order = by_y_then_z(z_count)

    @pl.when(pl.program_id(0) == 0)
    def _():
        rows[...] = core_rows(left_ref, 1 - place[0], order)

    total = dot(rows[...], right_ref[...], NN).astype(jnp.bfloat16)
    for at, (z_at, y_at) in enumerate(order):
        sent_ref[y_at, z_at] = total[at * block : (at + 1) * block]


def up_kept_kernel(place, left_ref, right_ref, there_ref, keep_ref, first_ref, second_ref, rows):
    z_count, block = there_ref.shape[1:3]
    order = by_y_then_z(z_count)

    @pl.when(pl.program_id(0) == 0)
    def _():
        rows[...] = core_rows(left_ref, place[0], order)

    total = dot(rows[...], right_ref[...], NN)
    parts = [added(total[at * block : (at + 1) * block], there_ref[y_at, z_at]) for at, (z_at, y_at) in enumerate(order)]

    def store(mine):
        for part, (z_at, y_at) in zip(parts, order):
            if z_at % 2 == mine:
                keep_ref[y_at, z_at // 2] = part
            else:
                (first_ref, second_ref)[y_at][z_at // 2] = part

    for mine in range(2):
        pl.when(place[2] == mine)(functools.partial(store, mine))


def half_rows(rows):
    return pltpu.VMEM((D // 2, rows), jnp.bfloat16)


def column_spec(z_count):
    return pl.BlockSpec((2, z_count, D // (4 * z_count), D), lambda i, _: (0, 0, 0, i))


def up_sent(place, normed_t, grad_hidden, z_count):
    rows, width = grad_hidden.shape
    in_specs = [whole(D, rows), pl.BlockSpec((rows, D), lambda i, _: (0, i))]
    return grid_call(
        up_sent_kernel, "up_sent", width // D, in_specs, [column_spec(z_count)],
        [(2, z_count, D // (4 * z_count), width)], [half_rows(rows)], grad_hidden.size * D, place, normed_t, grad_hidden,
    )[0]


def up_kept(place, normed_t, grad_hidden, there, z_count):
    rows, width = grad_hidden.shape
    in_specs = [whole(D, rows), pl.BlockSpec((rows, D), lambda i, _: (0, i)), column_spec(z_count)]
    shape = (2, z_count // 2, D // (4 * z_count), width)
    out_spec = pl.BlockSpec(shape[:3] + (D,), lambda i, _: (0, 0, 0, i))
    half_spec = pl.BlockSpec(shape[1:3] + (D,), lambda i, _: (0, 0, i))
    return grid_call(
        up_kept_kernel, "up_kept", width // D, in_specs, [out_spec] + [half_spec] * 2, [shape] + [shape[1:]] * 2,
        [half_rows(rows)],
        grad_hidden.size * D, place, normed_t, grad_hidden, there, far=1,
    )


def store_sent(sent_ref, at, total):
    z_count, block = sent_ref.shape[1:3]
    for row, (z_at, y_at) in enumerate(by_y_then_z(z_count)):
        sent_ref[y_at, z_at, :, tile(at)] = total[row * block : (row + 1) * block].astype(jnp.bfloat16)


def outer_sent_kernel(place, o_ref, normed_ref, d_ref, q_ref, sent_ref):
    order = by_y_then_z(sent_ref.shape[1])
    for at, (left, right) in enumerate(((o_ref, d_ref), (normed_ref, q_ref))):
        store_sent(sent_ref, at, dot(core_rows(left, 1 - place[0], order), right[...], NN))


def outer_sent(place, attended_t, normed_t, grad_middle, grad_q, z_count):
    outs = [((2, z_count, D // (4 * z_count), 2 * D), jnp.bfloat16)]
    return call(
        outer_sent_kernel, "outer_sent", 6, 2 * D * grad_q.size, outs, [],
        place, attended_t, normed_t, grad_middle, grad_q, smem=1,
    )[0]


def inner_sent_kernel(place, normed_ref, own_ref, there_ref, sent_ref):
    rows = core_rows(normed_ref, 1 - place[0], by_y_then_z(sent_ref.shape[1]))
    for at in range(2):
        store_sent(sent_ref, at, dot(rows, added(own_ref[at], there_ref[at]), NN))


def inner_sent(place, normed_t, own, there, z_count):
    outs = [((2, z_count, D // (4 * z_count), 2 * D), jnp.bfloat16)]
    return call(
        inner_sent_kernel, "inner_sent", 6, D * own.size, outs, [], place, normed_t, own, there, smem=1
    )[0]


def rest_kept_kernel(
    place, o_ref, normed_ref, d_ref, q_ref, own_ref, there_ref, outer_ref, inner_ref, keep_ref, send_ref
):
    z_count, block = keep_ref.shape[:2]
    order = by_y_then_z(z_count)
    attended, normed = [core_rows(left, place[0], order) for left in (o_ref, normed_ref)]

    def run(mine):
        for at in range(4):
            left = normed if at else attended
            right = (d_ref[...], q_ref[...])[at] if at < 2 else added(own_ref[at - 2], there_ref[at - 2])
            total = dot(left, right, NN)
            arrived = inner_ref if at > 1 else outer_ref
            for row, (z_at, y_at) in enumerate(order):
                target = keep_ref if y_at == mine else send_ref
                part = total[row * block : (row + 1) * block]
                target[z_at, :, tile(at)] = added(part, arrived[y_at, z_at, :, tile(at % 2)])

    for mine in range(2):
        pl.when(place[1] == mine)(functools.partial(run, mine))


def rest_kept(place, attended_t, normed_t, grad_middle, grad_q, own, there, outer_there, inner_there, z_count):
    outs = [((z_count, D // (4 * z_count), 4 * D), jnp.bfloat16)] * 2
    return call(
        rest_kept_kernel, "rest_kept", 10, 4 * D * grad_q.size, outs, [],
        place, attended_t, normed_t, grad_middle, grad_q, own, there, outer_there, inner_there, smem=1,
    )


def fold_kernel(place, kept_ref, arrived_ref, keep_ref, send_ref):
    for target, chosen in ((send_ref, 1 - place[0]), (keep_ref, place[0])):
        for at in range(target.shape[0]):
            target[at] = added(kept_ref[at, chosen], arrived_ref[at, chosen])


def fold(kept, arrived, place, outer):
    width = kept.shape[-1]
    lead = math.prod(kept.shape[:outer])
    inner = math.prod(kept.shape[outer + 1 : -1])
    shape = (lead, 2, inner, width)
    outs = [((lead, inner, width), kept.dtype)] * 2
    keep, send = call(
        fold_kernel, "fold", 4, 0, outs, [], place, kept.reshape(shape), arrived.reshape(shape), smem=1
    )
    left = kept.shape[:outer] + kept.shape[outer + 1 :]
    return keep.reshape(left), send.reshape(left)


def stream_fold_kernel(place, kept_keep, kept_send, first_keep, first_send, second_keep, second_send, keep_ref, send_ref):
    for step, arrived_keep, arrived_send in ((0, first_keep, first_send), (1, second_keep, second_send)):

        @pl.when(pl.program_id(0) == step)
        def _():
            send_ref[...] = added(kept_send[...], arrived_send[...])
            keep_ref[...] = added(kept_keep[...], arrived_keep[...])


def stream_fold(kept, first, second, place):
    inner, width = kept.shape[-2:]
    half = (None, inner, width)
    kept_specs = [
        pl.BlockSpec((None,) + half, lambda i, place: (i, place[0], 0, 0)),
        pl.BlockSpec((None,) + half, lambda i, place: (i, 1 - place[0], 0, 0)),
    ]
    arrived_specs = [
        pl.BlockSpec(half, lambda i, place: (place[0], 0, 0)),
        pl.BlockSpec(half, lambda i, place: (1 - place[0], 0, 0)),
    ]
    out_spec = pl.BlockSpec(half, lambda i, place: (i, 0, 0))
    return pl.pallas_call(
        stream_fold_kernel,
        grid_spec=pltpu.PrefetchScalarGridSpec(
            num_scalar_prefetch=1,
            grid=(2,),
            in_specs=kept_specs + arrived_specs * 2,
            out_specs=[out_spec, out_spec],
        ),
        out_shape=[jax.ShapeDtypeStruct((2, inner, width), jnp.bfloat16)] * 2,
        compiler_params=pltpu.CompilerParams(vmem_limit_bytes=8 * 1024 * 1024),
        cost_estimate=cost(0),
        name="stream_fold",
    )(place, in_hbm(kept), in_hbm(kept), first, first, second, second)


def shifted(value, axis, steps):
    count = lax.axis_size(axis)
    initial, last = (max(0, -steps), min(count, count - steps))
    return lax.ppermute(value, axis, [(source, source + steps) for source in range(initial, last)])


def layer_norm(inputs_row, gain_row, offset):
    center = inputs_row - jnp.mean(inputs_row, axis=-1, keepdims=True)
    spread = jnp.mean(center * center, axis=-1, keepdims=True)
    return center * lax.rsqrt(spread + 1e-05) * gain_row + offset


def gelu_tanh(hidden):
    return jax.nn.gelu(hidden, approximate=True)


def score_terms(queries, key_rows, query_pos, key_pos, signed):
    key_count = key_rows.shape[0]
    scores = (
        jnp.einsum(
            "rhe,khe->hrk",
            queries,
            key_rows.reshape(key_count, HEADS, HDIM),
            preferred_element_type=jnp.float32,
        )
        * 0.125
    )
    curved = jnp.sqrt(scores * scores + 1.0)
    argument = jnp.where(signed, curved, scores)
    sign_pattern = jnp.where(signed, scores / curved, 1.0)
    slope = jnp.where(signed, sign_pattern, 1.0)
    bend = jnp.where(signed, 1.0 / (curved * curved * curved), 0.0)
    permitted_mask = key_pos[None, None, :] <= query_pos[None, :, None]
    return (argument, sign_pattern, slope, bend, permitted_mask)


def score_grads(
    queries, key_rows, value_rows, query_pos, key_pos, log_total, delta, grad_att, signed
):
    argument, sign_pattern, slope, bend, permitted_mask = score_terms(
        queries, key_rows, query_pos, key_pos, signed
    )
    prob = jnp.where(permitted_mask, jnp.exp(argument - log_total[..., None]), 0.0)
    along = jnp.einsum("rhe,khe->hrk", grad_att, value_rows, preferred_element_type=jnp.float32)
    dscore = (prob * ((sign_pattern * along - delta[..., None]) * slope + along * bend)).astype(
        jnp.bfloat16
    )
    return ((sign_pattern * prob).astype(jnp.bfloat16), dscore)


def key_blocks_of(key_all, value_all, key_pos, key_block):
    blocks = key_all.shape[0] // key_block
    return (
        key_all.reshape(blocks, key_block, D),
        value_all.reshape(blocks, key_block, HEADS, HDIM),
        key_pos.reshape(blocks, key_block),
    )


def attend(queries, query_pos, key_all, value_all, key_pos, signed, key_block):
    row_count = queries.shape[0]
    key_split, value_split, pos_split = key_blocks_of(key_all, value_all, key_pos, key_block)

    def running_total(state_in, element):
        largest, row_total_sum, gathered = state_in
        key_rows, value_rows, block_pos = element
        argument, sign_pattern, _, _, permitted_mask = score_terms(
            queries, key_rows, query_pos, block_pos, signed
        )
        masked_scores = jnp.where(permitted_mask, argument, -1e30)
        exponent_values = jnp.maximum(largest, jnp.max(masked_scores, axis=-1))
        multiplier = jnp.exp(largest - exponent_values)
        added_terms = jnp.where(
            permitted_mask, jnp.exp(masked_scores - exponent_values[..., None]), 0.0
        )
        row_total_sum = row_total_sum * multiplier + jnp.sum(added_terms, axis=-1)
        attention_weights = (sign_pattern * added_terms).astype(jnp.bfloat16)
        added = jnp.einsum(
            "hrk,khe->rhe", attention_weights, value_rows, preferred_element_type=jnp.float32
        )
        gathered = gathered * multiplier.T[:, :, None] + added
        return ((exponent_values, row_total_sum, gathered), None)

    start_max = jnp.full((HEADS, row_count), -1e30, jnp.float32)
    start_sum = jnp.zeros((HEADS, row_count), jnp.float32)
    start_out = jnp.zeros((row_count, HEADS, HDIM), jnp.float32)
    (largest, row_total_sum, gathered), _ = lax.scan(
        running_total, (start_max, start_sum, start_out), (key_split, value_split, pos_split)
    )
    log_total = largest + jnp.log(row_total_sum)
    attended = gathered / row_total_sum.T[:, :, None]
    return (attended, log_total)


def backward_summed(
    queries, query_pos, key_all, value_all, key_pos, log_total, delta, grad_att, signed, key_block
):
    key_split, value_split, pos_split = key_blocks_of(key_all, value_all, key_pos, key_block)

    def step_back(grad_q, element):
        key_rows, value_rows, block_pos = element
        attention_weights, dscore = score_grads(
            queries, key_rows, value_rows, query_pos, block_pos, log_total, delta, grad_att, signed
        )
        grad_q = (
            grad_q
            + jnp.einsum(
                "hrk,khe->rhe",
                dscore,
                key_rows.reshape(-1, HEADS, HDIM),
                preferred_element_type=jnp.float32,
            )
            * 0.125
        )
        grad_k = (
            jnp.einsum("hrk,rhe->khe", dscore, queries, preferred_element_type=jnp.float32) * 0.125
        )
        grad_v = jnp.einsum(
            "hrk,rhe->khe", attention_weights, grad_att, preferred_element_type=jnp.float32
        )
        return (grad_q, (grad_k.reshape(key_block, D), grad_v.reshape(key_block, D)))

    start_q = jnp.zeros(queries.shape, jnp.float32)
    grad_q, (grad_k, grad_v) = lax.scan(step_back, start_q, (key_split, value_split, pos_split))
    grad_k, grad_v = (
        lax.psum_scatter(
            grad_k.reshape(-1, D).astype(jnp.bfloat16), "ctx", scatter_dimension=0, tiled=True
        ).astype(jnp.float32),
        lax.psum_scatter(
            grad_v.reshape(-1, D).astype(jnp.bfloat16), "ctx", scatter_dimension=0, tiled=True
        ).astype(jnp.float32),
    )
    return (grad_q.reshape(-1, D), grad_k, grad_v)


def layer_front(inputs_row, gain_pair, bias_row, qkv_w):
    normed = layer_norm(inputs_row, gain_pair[0], bias_row[0:D]).astype(jnp.bfloat16)
    qkv_bias = jnp.concatenate(
        [bias_row[2 * D : 3 * D], jnp.zeros((D,), jnp.float32), bias_row[3 * D : 4 * D]]
    )
    projected = (jnp.dot(normed, qkv_w, preferred_element_type=jnp.float32) + qkv_bias).astype(
        jnp.bfloat16
    )
    return (normed, projected)


def layer_rest(inputs_row, attended_b, gain_pair, bias_row, out_w, up_w, down_w):
    middle = (
        inputs_row
        + jnp.dot(attended_b, out_w, preferred_element_type=jnp.float32)
        + bias_row[4 * D : 5 * D]
    )
    normed_two = layer_norm(middle, gain_pair[1], bias_row[D : 2 * D]).astype(jnp.bfloat16)
    hidden = jnp.dot(normed_two, up_w, preferred_element_type=jnp.float32) + bias_row[6 * D :]
    active = gelu_tanh(hidden).astype(jnp.bfloat16)
    result = (
        middle
        + jnp.dot(active, down_w, preferred_element_type=jnp.float32)
        + bias_row[5 * D : 6 * D]
    )
    return (middle, normed_two, hidden, active, result)


def general_body(inputs, slot_order, cotangent, gains, biases, w_qkv, w_out, w_up, w_down):
    micro_count = inputs.shape[0]
    row_count = inputs.shape[2]
    section_at = lax.axis_index("section")
    ctx_at = lax.axis_index("ctx")
    signed = section_at == 0
    gain_pair = gains[0]
    bias_row = biases[0]
    qkv_w = w_qkv[0]
    out_w = w_out[0]
    up_w = w_up[0]
    down_w = w_down[0]
    span_len = row_count // 2
    seq_pos = (
        slot_order[:, 0, :, None] * span_len + jnp.arange(span_len, dtype=jnp.int32)
    ).reshape(micro_count, -1)
    key_block = min(seq_pos.shape[1], 512)
    first_inputs = inputs[:, 0]
    cot_rows = cotangent[:, 0]

    def sequence_pos(index):
        whole_pos = lax.dynamic_index_in_dim(seq_pos, index, 0, keepdims=False)
        own_pos = lax.dynamic_slice_in_dim(whole_pos, ctx_at * row_count, row_count, 0)
        return (whole_pos, own_pos)

    def layer_forward(entry, index):
        whole_pos, own_pos = sequence_pos(index)
        inputs_row = entry.astype(jnp.float32)
        normed, projected = layer_front(inputs_row, gain_pair, bias_row, qkv_w)
        key_all, value_all = (
            lax.all_gather(projected[:, D : 2 * D], "ctx", axis=0, tiled=True),
            lax.all_gather(projected[:, 2 * D :], "ctx", axis=0, tiled=True),
        )
        queries = projected[:, :D].reshape(row_count, HEADS, HDIM)
        attended, _ = attend(queries, own_pos, key_all, value_all, whole_pos, signed, key_block)
        attended_b = attended.reshape(row_count, D).astype(jnp.bfloat16)
        result = layer_rest(inputs_row, attended_b, gain_pair, bias_row, out_w, up_w, down_w)[4]
        return result.astype(jnp.bfloat16)

    def layer_reverse_pass(entry, result_gradient, index):
        whole_pos, own_pos = sequence_pos(index)
        inputs_row = entry.astype(jnp.float32)
        normed, projected = layer_front(inputs_row, gain_pair, bias_row, qkv_w)
        queries = projected[:, :D].reshape(row_count, HEADS, HDIM)
        key_all, value_all = (
            lax.all_gather(projected[:, D : 2 * D], "ctx", axis=0, tiled=True),
            lax.all_gather(projected[:, 2 * D :], "ctx", axis=0, tiled=True),
        )
        attended, log_total = attend(
            queries, own_pos, key_all, value_all, whole_pos, signed, key_block
        )
        attended_b = attended.reshape(row_count, D).astype(jnp.bfloat16)
        middle, normed_two, hidden, active, _ = layer_rest(
            inputs_row, attended_b, gain_pair, bias_row, out_w, up_w, down_w
        )
        grad_down_b = result_gradient.astype(jnp.bfloat16)
        grad_wdown = jnp.dot(active.T, grad_down_b, preferred_element_type=jnp.float32)
        grad_active = jnp.dot(grad_down_b, down_w.T, preferred_element_type=jnp.float32)
        _, gelu_back = jax.vjp(gelu_tanh, hidden)
        grad_hidden = gelu_back(grad_active)[0]
        grad_hidden_b = grad_hidden.astype(jnp.bfloat16)
        grad_wup = jnp.dot(normed_two.T, grad_hidden_b, preferred_element_type=jnp.float32)
        grad_normed_two = jnp.dot(grad_hidden_b, up_w.T, preferred_element_type=jnp.float32)
        _, norm_back_two = jax.vjp(layer_norm, middle, gain_pair[1], bias_row[D : 2 * D])
        grad_middle_part, grad_gain_two, grad_offset_two = norm_back_two(grad_normed_two)
        grad_middle = result_gradient + grad_middle_part
        grad_proj_b = grad_middle.astype(jnp.bfloat16)
        grad_wout = jnp.dot(attended_b.T, grad_proj_b, preferred_element_type=jnp.float32)
        grad_att_flat = jnp.dot(grad_proj_b, out_w.T, preferred_element_type=jnp.float32).astype(
            jnp.bfloat16
        )
        grad_att = grad_att_flat.reshape(row_count, HEADS, HDIM)
        delta = jnp.einsum("rhe,rhe->hr", grad_att.astype(jnp.float32), attended)
        grad_q, grad_k, grad_v = backward_summed(
            queries,
            own_pos,
            key_all,
            value_all,
            whole_pos,
            log_total,
            delta,
            grad_att,
            signed,
            key_block,
        )
        grad_qkv_b = jnp.concatenate([grad_q, grad_k, grad_v], axis=1).astype(jnp.bfloat16)
        grad_wqkv = jnp.dot(normed.T, grad_qkv_b, preferred_element_type=jnp.float32)
        grad_normed = jnp.dot(grad_qkv_b, qkv_w.T, preferred_element_type=jnp.float32)
        _, norm_back_one = jax.vjp(layer_norm, inputs_row, gain_pair[0], bias_row[0:D])
        grad_in_part, grad_gain_one, grad_offset_one = norm_back_one(grad_normed)
        input_gradient = grad_middle + grad_in_part
        grad_gain_rows = jnp.stack([grad_gain_one, grad_gain_two])
        grad_bias_row = jnp.concatenate(
            [
                grad_offset_one,
                grad_offset_two,
                jnp.sum(grad_q, axis=0),
                jnp.sum(grad_v, axis=0),
                jnp.sum(grad_middle, axis=0),
                jnp.sum(result_gradient, axis=0),
                jnp.sum(grad_hidden, axis=0),
            ]
        )
        return (
            input_gradient,
            (grad_gain_rows, grad_bias_row, grad_wqkv, grad_wout, grad_wup, grad_wdown),
        )

    def tick(tick_at, state_in):
        arrived, returned, stored, acts_rows, grad_rows, partial_sums = state_in
        ahead = tick_at - section_at
        ahead_ok = (ahead >= 0) & (ahead < micro_count)
        ahead_at = jnp.clip(ahead, 0, micro_count - 1)
        fresh = jnp.where(
            signed, lax.dynamic_index_in_dim(first_inputs, ahead_at, 0, keepdims=False), arrived
        )
        previous = lax.dynamic_index_in_dim(stored, ahead_at, 0, keepdims=False)
        entry = jnp.where(ahead_ok, fresh, previous)
        stored = lax.dynamic_update_index_in_dim(stored, entry, ahead_at, 0)
        sent = layer_forward(entry, ahead_at)
        old_acts = lax.dynamic_index_in_dim(acts_rows, ahead_at, 0, keepdims=False)
        acts_rows = lax.dynamic_update_index_in_dim(
            acts_rows, jnp.where(ahead_ok, sent, old_acts), ahead_at, 0
        )
        behind = tick_at - 2 + section_at
        trailing_valid = (behind >= 0) & (behind < micro_count)
        trailing_position = jnp.clip(behind, 0, micro_count - 1)
        entry_gradient = lax.dynamic_index_in_dim(stored, trailing_position, 0, keepdims=False)
        given_cot = lax.dynamic_index_in_dim(cot_rows, trailing_position, 0, keepdims=False).astype(
            jnp.float32
        )
        result_gradient = jnp.where(signed, returned.astype(jnp.float32), given_cot)
        input_gradient, added_terms = layer_reverse_pass(
            entry_gradient, result_gradient, trailing_position
        )
        partial_sums = jax.tree.map(
            lambda running_total, added_term: running_total
            + jnp.where(trailing_valid, added_term, 0.0),
            partial_sums,
            added_terms,
        )
        handed = input_gradient.astype(jnp.bfloat16)
        kept_grad = jnp.where(signed, input_gradient, handed.astype(jnp.float32))
        old_grads = lax.dynamic_index_in_dim(grad_rows, trailing_position, 0, keepdims=False)
        grad_rows = lax.dynamic_update_index_in_dim(
            grad_rows, jnp.where(trailing_valid, kept_grad, old_grads), trailing_position, 0
        )
        arrived = shifted(sent, "section", 1)
        returned = shifted(handed, "section", -1)
        return (arrived, returned, stored, acts_rows, grad_rows, partial_sums)

    zero_rows = jnp.zeros((row_count, D), jnp.bfloat16)
    start_sums = (
        jnp.zeros((2, D), jnp.float32),
        jnp.zeros((bias_row.shape[0],), jnp.float32),
        jnp.zeros(qkv_w.shape, jnp.float32),
        jnp.zeros(out_w.shape, jnp.float32),
        jnp.zeros(up_w.shape, jnp.float32),
        jnp.zeros(down_w.shape, jnp.float32),
    )
    start_state = (
        zero_rows,
        zero_rows,
        jnp.zeros((micro_count, row_count, D), jnp.bfloat16),
        jnp.zeros((micro_count, row_count, D), jnp.bfloat16),
        jnp.zeros((micro_count, row_count, D), jnp.float32),
        start_sums,
    )
    final_state = lax.fori_loop(0, micro_count + 2, tick, start_state)
    acts_rows = final_state[3]
    grad_rows = final_state[4]
    partial_sums = final_state[5]
    totals = (
        lax.psum_scatter(partial_sums[0], ("dp", "ctx"), scatter_dimension=1, tiled=True),
        lax.psum_scatter(partial_sums[1], ("dp", "ctx"), scatter_dimension=0, tiled=True),
        lax.psum_scatter(partial_sums[2], ("dp", "ctx"), scatter_dimension=0, tiled=True),
        lax.psum_scatter(partial_sums[3], ("dp", "ctx"), scatter_dimension=0, tiled=True),
        lax.psum_scatter(partial_sums[4], ("dp", "ctx"), scatter_dimension=0, tiled=True),
        lax.psum_scatter(partial_sums[5], ("dp", "ctx"), scatter_dimension=0, tiled=True),
    )
    return (
        acts_rows[None, :, None],
        grad_rows[None, :, None],
        totals[0][None],
        totals[1][None],
        totals[2][None],
        totals[3][None],
        totals[4][None],
        totals[5][None],
    )


def swap_halves(value):
    count = lax.axis_size("ctx")
    return lax.ppermute(value, "ctx", [(at, (at + count // 2) % count) for at in range(count)])


def swap_cores(value):
    return lax.ppermute(value, "ctx", [(at, at ^ 1) for at in range(lax.axis_size("ctx"))])


def swap_z(value, step):
    return lax.ppermute(value, "dp", [(at, at ^ step) for at in range(lax.axis_size("dp"))])


def wide_sum(kept, arrived):
    return kept.astype(jnp.float32) + arrived.astype(jnp.float32)


def fast_body(inputs, slot_order, cotangent, gains, biases, w_qkv, w_out, w_up, w_down):
    rows = inputs.shape[2]
    count = lax.axis_size("ctx")
    z_count = lax.axis_size("dp")
    half = count // 2
    ctx_at = lax.axis_index("ctx")
    mine = ctx_at // half
    y_at, core_at = ctx_at // 2, ctx_at % 2
    signed = lax.axis_index("section") == 0
    which = signed.astype(jnp.int32)[None]
    place = core_at[None].astype(jnp.int32)
    y_place = y_at[None].astype(jnp.int32)
    z_at = lax.axis_index("dp")
    gain_pair = gains[0]
    wide, narrow, barrier = jnp.float32, jnp.bfloat16, lax.optimization_barrier

    def gathered(value):
        kept = lax.dynamic_index_in_dim(value, mine, 0, keepdims=False)
        sent = lax.dynamic_index_in_dim(value, 1 - mine, 0, keepdims=False)
        return jnp.concatenate([kept, swap_halves(sent)], axis=0)

    def returned(kept, arrived):
        arrived = arrived.astype(kept.dtype)
        first = jnp.where(mine == 0, kept, arrived)
        second = jnp.where(mine == 0, arrived, kept)
        return jnp.stack([first, second])

    order = lax.dynamic_index_in_dim(slot_order[:, 0], mine, 0, keepdims=False)
    pairs = order.reshape(count, 2)

    def slots_of(device):
        return jnp.concatenate([pairs[device], pairs[(device + half) % count]])

    meta = slot_meta(slots_of(ctx_at), slots_of(ctx_at ^ 1), signed)

    inputs, meta = barrier((inputs, meta))
    first = gathered(inputs[:, 0])
    qkv_t, out_t = flip(w_qkv, pltpu.HBM), flip(w_out, pltpu.HBM)
    first, qkv_t, out_t = barrier((first, qkv_t, out_t))
    _, queries, kv = front(first, gain_pair, biases, w_qkv)
    attended, _ = sorted_attend(meta, queries, kv, swap_cores(kv))
    sent = rest(first, attended, gain_pair, biases, w_out, w_up, w_down)
    sent, later = barrier((sent, (cotangent, w_up, w_down)))
    arrived = shifted(sent, "section", 1)
    given = gathered(later[0][:, 0])
    up_t, down_t = [flip(weight, pltpu.HBM) for weight in later[1:]]
    arrived, given, up_t, down_t = barrier((arrived, given, up_t, down_t))
    entry, normed, queries, kv = chosen_front(which, first, arrived, gain_pair, biases, w_qkv)
    kv_there = swap_cores(kv)
    normed_t = flip(normed, pltpu.HBM)
    kv_there, normed_t = barrier((kv_there, normed_t))
    attended, lse = sorted_attend(meta, queries, kv, kv_there)
    middle, normed_two, active, slope, grad_middle, grad_att = turn(
        entry, attended, given, gain_pair, biases, w_out, w_up, out_t, up_t, down_t
    )

    grad_q, own, sent, *ahead = sorted_attend_back(meta, queries, kv, kv_there, attended, grad_att, lse)
    own, sent, attended, normed_two = barrier((own, sent, attended, normed_two))
    there = swap_cores(sent)
    attended_t, normed_two_t = flip(attended, pltpu.HBM), flip(normed_two, pltpu.HBM)
    there, attended_t, normed_two_t = barrier((there, attended_t, normed_two_t))
    handed, _ = front_back(grad_q, own, there, entry, grad_middle, gain_pair, qkv_t, narrow)
    handed, active, middle, weights = barrier((handed, active, middle, (w_up, w_down)))
    back = shifted(handed, "section", -1)
    result = middle + dot(active, w_down[0], NN) + biases[0, 5 * D : 6 * D]
    result = result.astype(narrow)
    acts_there = swap_halves(result[rows:])
    middle, acts_there, active = barrier((middle, acts_there, active))
    up_t, down_t = [flip(in_hbm(weight), pltpu.VMEM) for weight in weights]
    active_t = flip(active, pltpu.VMEM)
    back, up_t, down_t, active_t = barrier((back, up_t, down_t, active_t))

    z_steps = [1 << at for at in range(z_count.bit_length() - 1)]
    split = [2] * len(z_steps)
    by_z = [((z_at >> at) & 1)[None].astype(jnp.int32) for at in range(len(z_steps))]

    def bits(value, before):
        return value.reshape(value.shape[:before] + tuple(split) + value.shape[before + 1 :])

    places = jnp.concatenate([place, y_place, by_z[0]])
    back, grad_hidden, grad_middle, grad_att, sums_two, up_sum = down_back(
        which, back, given, slope, middle, gain_pair, out_t, up_t, down_t
    )
    back, grad_hidden = barrier((back, grad_hidden))
    down_there = down_sent(places, active_t, back, z_count)
    grad_hidden, down_there = barrier((grad_hidden, down_there))
    down_there = swap_cores(down_there)
    up_there = up_sent(places, normed_two_t, grad_hidden, z_count)
    down_there, up_there = barrier((down_there, up_there))
    up_there = swap_cores(up_there)
    down_keep, down_send, down_later = down_kept(places, active_t, back, down_there, z_count)
    up_there, down_send, down_later = barrier((up_there, down_send, down_later))
    up_keep, up_send, up_later = up_kept(places, normed_two_t, grad_hidden, up_there, z_count)
    grad_att, down_send, up_send = barrier((grad_att, down_send, up_send))
    down_first, up_first = swap_halves(down_send), swap_z(up_send, z_steps[0])
    grad_q, own, sent = sorted_attend_back(meta, queries, kv, kv_there, attended, grad_att, lse, ahead)

    grad_q, own, sent, down_first, up_first, down_later, up_later = barrier(
        (grad_q, own, sent, down_first, up_first, down_later, up_later)
    )
    there = swap_cores(sent)
    down_second, up_second = swap_halves(down_later), swap_z(up_later, z_steps[0])
    outer_there = outer_sent(places, attended_t, normed_t, grad_middle, grad_q, z_count)
    there, outer_there = barrier((there, outer_there))
    outer_there = swap_cores(outer_there)
    inner_there = inner_sent(places, normed_t, own, there, z_count)
    inner_there, down_second, up_second = barrier((inner_there, down_second, up_second))
    inner_there = swap_cores(inner_there)
    down_keep, down_send = stream_fold(bits(down_keep, 0), down_first, down_second, by_z[0])
    up_keep, up_send = stream_fold(up_keep, up_first, up_second, by_z[1])
    outer_there, inner_there, down_send, up_send = barrier((outer_there, inner_there, down_send, up_send))
    rest_keep, rest_send = rest_kept(
        places, attended_t, normed_t, grad_middle, grad_q, own, there, outer_there, inner_there, z_count
    )
    rest_send, down_send, up_send, grad_q, own, there = barrier((rest_send, down_send, up_send, grad_q, own, there))
    rest_there, down_there, up_there = swap_halves(rest_send), swap_z(down_send, z_steps[0]), swap_z(up_send, z_steps[1])
    input_gradient, sums_one = front_back(grad_q, own, there, entry, grad_middle, gain_pair, qkv_t, wide)
    small = jnp.concatenate([sums_one, sums_two, up_sum], axis=0)
    small = small + swap_cores(small)
    rounded = input_gradient.astype(narrow)
    small_there = swap_halves(small)
    down_there, rounded = barrier((down_there, rounded))
    down_keep, down_send = fold(down_keep, down_there, by_z[1], 0)
    down_send, rest_there, small_there = barrier((down_send, rest_there, small_there))
    down_there = swap_z(down_send, z_steps[1])

    rest_keep, rest_send = fold(bits(rest_keep, 0), bits(rest_there, 0), by_z[0], len(split) - 1)
    small = small + small_there
    rest_send, up_there, small = barrier((rest_send, up_there, small))
    rest_there, small_there = swap_z(rest_send, z_steps[0]), swap_z(small, z_steps[0])
    up_keep, up_send = fold(up_keep, up_there, y_place, 0)
    up_there = swap_halves(up_send)
    rounded, up_send = barrier((rounded, up_send))
    grads_there = swap_halves(rounded[rows:])
    rest_there, up_there, small_there, down_there, grads_there = barrier(
        (rest_there, up_there, small_there, down_there, grads_there)
    )
    rest_keep, rest_send = fold(rest_keep, rest_there, by_z[1], 0)
    rest_send, small_there, grads_there, result, acts_there = barrier(
        (rest_send, small_there, grads_there, result, acts_there)
    )
    rest_there = swap_z(rest_send, z_steps[1])
    small = small + small_there
    small = small + swap_z(small, z_steps[1])
    wdown = wide_sum(down_keep, down_there)
    wup = wide_sum(up_keep, up_there)
    grads_kept = jnp.where(signed, input_gradient[:rows], rounded[:rows].astype(wide))
    grad_rows = returned(grads_kept, grads_there)
    grad_rows, rest_there = barrier((grad_rows, rest_there))
    wout = wide_sum(rest_keep[:, :D], rest_there[:, :D])
    wqkv = wide_sum(rest_keep[:, D:], rest_there[:, D:])
    blocks = count * z_count
    block_at = lax.axis_index("dp") * count + ctx_at
    gain_piece = lax.dynamic_slice_in_dim(small[0:5:4], block_at * (D // blocks), D // blocks, 1)
    bias_row = jnp.concatenate([small[1:2], small[5:6], small[2:4], small[6:]], axis=0).reshape(-1)
    width = bias_row.shape[0] // blocks
    bias_piece = lax.dynamic_slice_in_dim(bias_row, block_at * width, width, 0)
    return (
        returned(result[:rows], acts_there)[None, :, None],
        grad_rows[None, :, None],
        gain_piece[None],
        bias_piece[None],
        wqkv[None],
        wout[None],
        wup[None],
        wdown[None],
    )


def body_for(mesh):
    sizes = dict(mesh.shape)
    return fast_body if (sizes["ctx"], sizes["dp"]) == (4, 4) else general_body


def solution(mesh):
    in_specs = (
        P(None, "dp", "ctx", None),
        P(None, "dp", None),
        P(None, "dp", "ctx", None),
        P("section", None, None),
        P("section", None),
        P("section", None, None),
        P("section", None, None),
        P("section", None, None),
        P("section", None, None),
    )
    out_specs = (
        P("section", None, "dp", "ctx", None),
        P("section", None, "dp", "ctx", None),
        P("section", None, ("dp", "ctx")),
        P("section", ("dp", "ctx")),
        P("section", ("dp", "ctx"), None),
        P("section", ("dp", "ctx"), None),
        P("section", ("dp", "ctx"), None),
        P("section", ("dp", "ctx"), None),
    )
    return jax.shard_map(
        body_for(mesh), mesh=mesh, in_specs=in_specs, out_specs=out_specs, check_vma=False
    )
```

```python
import functools
import math
import jax
import jax.numpy as jnp
from jax import lax
from jax.experimental import pallas as pl
from jax.experimental.pallas import tpu as pltpu
from jax.sharding import PartitionSpec as P

D = 768
HEADS = 12
HDIM = 64
PAIR = 2 * HDIM
PAIRS = HEADS // 2
OWN = 4
CHUNK = 128
SAFE = 60.0
NT = (((1,), (1,)), ((), ()))
TN = (((0,), (0,)), ((), ()))
NN = (((1,), (0,)), ((), ()))


def dot(left, right, dims):
    return lax.dot_general(left, right, dims, preferred_element_type=jnp.float32)


def slot_meta(own_pos, other_pos, signed):
    rank = jnp.sum((own_pos[None, :] < own_pos[:, None]).astype(jnp.int32), axis=1)
    chosen = rank[None, :] == jnp.arange(OWN, dtype=jnp.int32)[:, None]
    ranked = jnp.sum(jnp.where(chosen, jnp.arange(OWN, dtype=jnp.int32)[None, :], 0), axis=1)
    ranked_pos = jnp.sum(jnp.where(chosen, own_pos[None, :], 0), axis=1)
    return jnp.concatenate([own_pos, other_pos, ranked, ranked_pos, signed.astype(jnp.int32)[None]])


def sort_rows(meta, own, other, target, span, first):
    columns = slice(first, first + D)
    for slot in range(OWN):
        for base, source in ((0, own), (OWN, other)):
            start = pl.multiple_of(meta[base + slot] * span, span)
            target[pl.ds(start, span), :] = source[slot * span : (slot + 1) * span, columns]


def reach(rank, slots):
    return ((0, slots // 2 - 2), (1, slots // 2 - 1), (slots // 2, slots - 2), (slots // 2 + 1, slots - 1))[rank]


def stacked_heads(rows):
    second = lax.broadcasted_iota(jnp.int32, rows.shape, 1) >= HDIM
    zero = jnp.zeros_like(rows)
    return jnp.concatenate([jnp.where(second, zero, rows), jnp.where(second, rows, zero)], axis=0)


def visible(values, start, least, span, position, fill):
    if start + values.shape[0] <= least * span:
        return values
    key_at = lax.broadcasted_iota(jnp.int32, values.shape, 0) + start
    lane = lax.broadcasted_iota(jnp.int32, values.shape, 1)
    query_at = position * span + jnp.where(lane >= span, lane - span, lane)
    return jnp.where(key_at <= query_at, values, fill)


def unstack(pair, span):
    row = lax.broadcasted_iota(jnp.int32, (PAIR, span), 0)
    return jnp.where(row < HDIM, pair[:, :span], pair[:, span:]).T


def chunks_of(count, chunk):
    return [slice(start, min(start + chunk, count)) for start in range(0, count, chunk)]


def eight(values):
    return values.reshape(-1, 8, values.shape[-1])


def pair_columns(at):
    return pl.ds(pl.multiple_of(at * PAIR, PAIR), PAIR)


def largest_norm(rows_ref):
    feature = lax.broadcasted_iota(jnp.int32, (D, PAIR), 0) // HDIM
    head = lax.broadcasted_iota(jnp.int32, (D, PAIR), 1)
    chosen = jnp.where(feature == head, 1.0, 0.0).astype(jnp.bfloat16)
    rows = rows_ref[...]
    return jnp.max(dot(rows * rows, chosen, NN))


def forward_kernel(meta, q_ref, kv_ref, kv2_ref, o_ref, lse_ref, keys, values, *, span):
    slots = keys.shape[0] // span
    sort_rows(meta, kv_ref, kv2_ref, keys, span, 0)
    sort_rows(meta, kv_ref, kv2_ref, values, span, D)
    bound = largest_norm(q_ref) * largest_norm(keys) * (1.1 / HDIM)
    near = bound < SAFE * SAFE

    def run(signed, safe):
        def one_pair(pair, _):
            columns = pair_columns(pair)
            values_t = values[:, columns].T
            for rank in reversed(range(OWN)):
                least, most = reach(rank, slots)
                count = (most + 1) * span
                row_at = pl.multiple_of(meta[2 * OWN + rank] * span, span)
                position = meta[3 * OWN + rank]
                queries = stacked_heads(q_ref[pl.ds(row_at, span), columns] * 0.125)
                largest = None
                if not safe:
                    most_seen = jnp.full((8, 2 * span), -1e30, jnp.float32)
                    for part in chunks_of(count, CHUNK):
                        scores = dot(keys[part, columns], queries, NT)
                        scores = jnp.abs(scores) if signed else scores
                        scores = visible(scores, part.start, least, span, position, -1e30)
                        most_seen = jnp.maximum(most_seen, jnp.max(eight(scores), axis=0))
                    largest = jnp.max(most_seen, axis=0, keepdims=True)
                    if signed:
                        square = largest * largest + 1.0
                        largest = square * lax.rsqrt(square)
                total = jnp.zeros((8, 2 * span), jnp.float32)
                gathered = jnp.zeros((PAIR, 2 * span), jnp.float32)
                for part in chunks_of(count, CHUNK):
                    scores = dot(keys[part, columns], queries, NT)
                    argument = scores
                    if signed:
                        square = scores * scores + 1.0
                        inverse = lax.rsqrt(square)
                        argument = square * inverse
                    if not safe:
                        argument = argument - largest
                    weights = jnp.exp(visible(argument, part.start, least, span, position, -1e30))
                    total += jnp.sum(eight(weights), axis=0)
                    if signed:
                        weights = weights * (scores * inverse)
                    gathered += dot(values_t[:, part], weights.astype(jnp.bfloat16), NN)
                total = jnp.sum(total, axis=0, keepdims=True)
                lse = jnp.log(total)
                lse_ref[pair, rank : rank + 1, :] = lse if safe else lse + largest
                gathered = gathered * (1.0 / total)
                o_ref[pl.ds(row_at, span), columns] = unstack(gathered, span).astype(jnp.bfloat16)
            return 0

        lax.fori_loop(0, PAIRS, one_pair, 0)

    for signed in (True, False):
        for safe in (True, False):
            chosen = (meta[4 * OWN] == int(signed)) & (near == safe)
            pl.when(chosen)(functools.partial(run, signed, safe))


def in_vmem(*values):
    return [pltpu.with_memory_space_constraint(value, pltpu.VMEM) for value in values]


SMEM_SPEC = pl.BlockSpec(memory_space=pltpu.SMEM)
VMEM_SPEC = pl.BlockSpec(memory_space=pltpu.VMEM)


def sorted_attend(meta, queries, kv, kv_other):
    rows = kv.shape[0]
    span = rows // OWN
    return pl.pallas_call(
        functools.partial(forward_kernel, span=span),
        in_specs=[SMEM_SPEC] + [VMEM_SPEC] * 3,
        out_specs=[VMEM_SPEC] * 2,
        scratch_shapes=[pltpu.VMEM((2 * rows, D), jnp.bfloat16)] * 2,
        out_shape=[
            jax.ShapeDtypeStruct((rows, D), jnp.bfloat16),
            jax.ShapeDtypeStruct((PAIRS, OWN, 2 * span), jnp.float32),
        ],
        compiler_params=pltpu.CompilerParams(vmem_limit_bytes=10 * 1024 * 1024),
        cost_estimate=pl.CostEstimate(flops=4_000_000_000, bytes_accessed=0, transcendentals=0),
        name="attend",
    )(meta, *in_vmem(queries, kv, kv_other))


def reaches(slots, span):
    found, at = [], 0
    for rank in range(OWN):
        least, most = reach(rank, slots)
        found.append((least, (most + 1) * span, at))
        at += (most + 1) * span
    return found, at


def kept_copies(pair, side, factor_buf, weight_buf, factors, weights, done, out):
    copies = []
    for part, (buffer, far) in enumerate(((factor_buf, factors), (weight_buf, weights))):
        near, there = buffer.at[side], far.at[pair]
        source, target = (near, there) if out else (there, near)
        copies.append(pltpu.make_async_copy(source, target, done.at[side, part]))
    return copies


def backward_kernel(
    meta, q_ref, kv_ref, kv2_ref, o_ref, do_ref, lse_ref, *refs, span, prepare
):
    if prepare:
        dq_ref, own_ref, other_ref, factors, weight_rows, *scratch = refs
    else:
        factors, weight_rows, dq_ref, own_ref, other_ref, *scratch = refs
    keys, values, grad_k, grad_v, factor_buf, weight_buf, done = scratch
    slots = keys.shape[0] // span
    ranks, _ = reaches(slots, span)
    sort_rows(meta, kv_ref, kv2_ref, keys, span, 0)
    sort_rows(meta, kv_ref, kv2_ref, values, span, D)

    def copies(pair, side):
        return kept_copies(pair, side, factor_buf, weight_buf, factors, weight_rows, done, prepare)

    def queries_at(rank, columns):
        row_at = pl.multiple_of(meta[2 * OWN + rank] * span, span)
        return row_at, stacked_heads(q_ref[pl.ds(row_at, span), columns] * 0.125)

    def make_ahead():
        def one_pair(pair, _):
            side = lax.rem(pair, 2)
            columns = pair_columns(pair)

            @pl.when(pair >= 2)
            def _():
                for copy in copies(pair, side):
                    copy.wait()

            for rank, (least, count, start) in enumerate(ranks):
                _, queries = queries_at(rank, columns)
                scores = dot(keys[:count, columns], queries, NT)
                square = scores * scores + 1.0
                inverse = lax.rsqrt(square)
                argument = square * inverse - lse_ref[pair, rank : rank + 1, :]
                prob = jnp.exp(visible(argument, 0, least, span, meta[3 * OWN + rank], -1e30))
                sign_pattern = scores * inverse
                factor = prob * (sign_pattern * sign_pattern + inverse * inverse * inverse)
                factor_buf[side, start : start + count, :] = factor.astype(jnp.bfloat16)
                weight_buf[side, start : start + count, :] = (prob * sign_pattern).astype(jnp.bfloat16)
            for copy in copies(pair, side):
                copy.start()
            return 0

        lax.fori_loop(0, PAIRS, one_pair, 0)
        for pair in range(PAIRS - 2, PAIRS):
            for copy in copies(pair, pair % 2):
                copy.wait()
        for out_ref in (dq_ref, own_ref, other_ref):
            out_ref[...] = jnp.zeros_like(out_ref)

    def run(made):
        if made:
            for copy in copies(0, 0):
                copy.start()

        def one_pair(pair, _):
            side = lax.rem(pair, 2)
            columns = pair_columns(pair)
            keys_t = keys[:, columns].T
            if made:

                @pl.when(pair + 1 < PAIRS)
                def _():
                    for copy in copies(pair + 1, 1 - side):
                        copy.start()

                for copy in copies(pair, side):
                    copy.wait()
            for rank in reversed(range(OWN)):
                least, count, start = ranks[rank]
                row_at, queries = queries_at(rank, columns)
                grad_rows = do_ref[pl.ds(row_at, span), columns]
                grads = stacked_heads(grad_rows)
                product = grad_rows.astype(jnp.float32) * o_ref[pl.ds(row_at, span), columns].astype(jnp.float32)
                delta = jnp.sum(stacked_heads(product).T, axis=0, keepdims=True)
                along = dot(values[:count, columns], grads, NT)
                if made:
                    weights = weight_buf[side, start : start + count, :]
                    factor = factor_buf[side, start : start + count, :].astype(jnp.float32)
                    dscore = factor * along - weights.astype(jnp.float32) * delta
                else:
                    scores = dot(keys[:count, columns], queries, NT)
                    argument = scores - lse_ref[pair, rank : rank + 1, :]
                    weights = jnp.exp(visible(argument, 0, least, span, meta[3 * OWN + rank], -1e30))
                    dscore = weights * (along - delta)
                    weights = weights.astype(jnp.bfloat16)
                dscore = dscore.astype(jnp.bfloat16)
                added_v = dot(weights, grads, NN)
                added_k = dot(dscore, queries, NN)
                if rank == OWN - 1:
                    grad_v[...] = added_v
                    grad_k[...] = added_k
                else:
                    grad_v[:count, :] += added_v
                    grad_k[:count, :] += added_k
                gathered = dot(keys_t[:, :count], dscore, NN)
                dq_ref[pl.ds(row_at, span), columns] = (unstack(gathered, span) * 0.125).astype(jnp.bfloat16)
            for slot in range(OWN):
                there = slice(slot * span, (slot + 1) * span)
                own_at = pl.multiple_of(meta[slot] * span, span)
                other_at = pl.multiple_of(meta[OWN + slot] * span, span)
                for part, total in enumerate((grad_k, grad_v)):
                    own_ref[part, there, columns] = total[pl.ds(own_at, span), :].astype(jnp.bfloat16)
                    other_ref[part, there, columns] = total[pl.ds(other_at, span), :].astype(jnp.bfloat16)
            return 0

        lax.fori_loop(0, PAIRS, one_pair, 0)

    pl.when(meta[4 * OWN] == 0)(functools.partial(run, False))
    pl.when(meta[4 * OWN] == 1)(make_ahead if prepare else functools.partial(run, True))


def sorted_attend_back(meta, queries, kv, kv_other, attended, grad_att, lse, made=None):
    rows = kv.shape[0]
    span = rows // OWN
    narrow = jnp.bfloat16
    _, reached = reaches(2 * OWN, span)
    far_spec = pl.BlockSpec(memory_space=pltpu.HBM)
    ahead = [pltpu.HBM((PAIRS, reached, 2 * span), narrow)] * 2
    shapes = [jax.ShapeDtypeStruct((rows, D), narrow)] + [jax.ShapeDtypeStruct((2, rows, D), narrow)] * 2
    prepare = made is None
    given = () if prepare else tuple(pltpu.with_memory_space_constraint(value, pltpu.HBM) for value in made)
    return pl.pallas_call(
        functools.partial(backward_kernel, span=span, prepare=prepare),
        in_specs=[SMEM_SPEC] + [VMEM_SPEC] * 6 + [far_spec] * len(given),
        out_specs=[VMEM_SPEC] * 3 + [far_spec] * (2 if prepare else 0),
        scratch_shapes=[pltpu.VMEM((2 * rows, D), narrow)] * 2
        + [pltpu.VMEM((2 * rows, PAIR), jnp.float32)] * 2
        + [pltpu.VMEM((2, reached, 2 * span), narrow)] * 2
        + [pltpu.SemaphoreType.DMA((2, 2))],
        out_shape=shapes + (ahead if prepare else []),
        compiler_params=pltpu.CompilerParams(vmem_limit_bytes=18 * 1024 * 1024),
        cost_estimate=pl.CostEstimate(flops=8_000_000_000, bytes_accessed=0, transcendentals=0),
        name="attend_back",
    )(meta, *in_vmem(queries, kv, kv_other, attended, grad_att), lse, *given)


TURN_TANH = 0.7978845608028654
CUBE = 0.044715
CHUNKS = 1


def normalised(rows):
    center = rows - jnp.mean(rows, axis=-1, keepdims=True)
    inverse = lax.rsqrt(jnp.mean(center * center, axis=-1, keepdims=True) + 1e-05)
    return center * inverse, inverse


def norm_back(unit, inverse, gain_row, grad):
    scaled = grad * gain_row
    along = jnp.mean(scaled * unit, axis=-1, keepdims=True)
    return inverse * (scaled - jnp.mean(scaled, axis=-1, keepdims=True) - unit * along)


def row_chunks(rows, chunks=CHUNKS):
    return [slice(at * rows // chunks, (at + 1) * rows // chunks) for at in range(chunks)]


def column_sum(values):
    return jnp.sum(values, axis=0, keepdims=True)


def gelu_parts(hidden):
    square = hidden * hidden
    curve = jnp.tanh(hidden * (TURN_TANH + TURN_TANH * CUBE * square))
    half = 0.5 + 0.5 * curve
    inner = hidden * (TURN_TANH + 3.0 * TURN_TANH * CUBE * square)
    return hidden * half, half + 0.5 * (1.0 - curve * curve) * inner


def gelu_only(hidden):
    square = hidden * hidden
    curve = jnp.tanh(hidden * (TURN_TANH + TURN_TANH * CUBE * square))
    return hidden * (0.5 + 0.5 * curve)


def cost(flops):
    return pl.CostEstimate(flops=int(flops) // 8, bytes_accessed=0, transcendentals=0)


def in_hbm(value):
    return pltpu.with_memory_space_constraint(value, pltpu.HBM)


def placed(shape, dtype, space=None):
    return jax.ShapeDtypeStruct(shape, dtype) if space is None else space(shape, dtype)


def call(kernel, name, megabytes, flops, outs, scratch, *operands, smem=0):
    return pl.pallas_call(
        kernel,
        in_specs=[SMEM_SPEC] * smem + [VMEM_SPEC] * (len(operands) - smem),
        out_specs=[VMEM_SPEC] * len(outs),
        out_shape=[placed(*out) for out in outs],
        scratch_shapes=scratch,
        compiler_params=pltpu.CompilerParams(vmem_limit_bytes=megabytes * 1024 * 1024),
        cost_estimate=cost(flops),
        name=name,
    )(*operands)


def bias_part(biases, at):
    return biases[0:1, at * D : (at + 1) * D]


def tile(at):
    return slice(at * D, (at + 1) * D)


def whole(*shape):
    return pl.BlockSpec(shape, lambda *_: (0,) * len(shape))


def flip_kernel(in_ref, out_ref):
    out_ref[...] = in_ref[...].T


def copy_kernel(in_ref, out_ref):
    out_ref[...] = in_ref[...]


def fetched(value):
    height, width = value.shape
    block = pl.BlockSpec((height // 4, width), lambda i: (i, 0))
    return pl.pallas_call(
        copy_kernel,
        grid=(4,),
        in_specs=[block],
        out_specs=block,
        out_shape=placed(value.shape, value.dtype, pltpu.VMEM),
        compiler_params=pltpu.CompilerParams(vmem_limit_bytes=7 * 1024 * 1024),
        cost_estimate=cost(0),
        name="fetched",
    )(in_hbm(value))


def flip(value, space=None):
    height, width = value.shape[-2:]
    lead = (None,) * (value.ndim - 2)
    zeros = (0,) * (value.ndim - 2)
    if height > D:
        grid = height // D
        in_spec = pl.BlockSpec(lead + (D, width), lambda i: zeros + (i, 0))
        out_spec = pl.BlockSpec((width, D), lambda i: (0, i))
    else:
        step = min(width, D)
        grid = width // step
        in_spec = pl.BlockSpec(lead + (height, step), lambda i: zeros + (0, i))
        out_spec = pl.BlockSpec((step, height), lambda i: (i, 0))
    return pl.pallas_call(
        flip_kernel,
        grid=(grid,),
        in_specs=[in_spec],
        out_specs=out_spec,
        out_shape=placed((width, height), value.dtype, space),
        compiler_params=pltpu.CompilerParams(vmem_limit_bytes=7 * 1024 * 1024),
        cost_estimate=cost(0),
        name="flip",
    )(value)


def front_rows(x_ref, gains, biases, w_ref, normed_ref, q_ref, kv_ref):
    for part in row_chunks(x_ref.shape[0]):
        unit, _ = normalised(x_ref[part, :].astype(jnp.float32))
        normed = (unit * gains[0:1, :] + bias_part(biases, 0)).astype(jnp.bfloat16)
        normed_ref[part, :] = normed
        kv_ref[part, :D] = dot(normed, w_ref[0, :, tile(1)], NN).astype(jnp.bfloat16)
        kv_ref[part, D:] = (dot(normed, w_ref[0, :, tile(2)], NN) + bias_part(biases, 3)).astype(jnp.bfloat16)
        q_ref[part, :] = (dot(normed, w_ref[0, :, tile(0)], NN) + bias_part(biases, 2)).astype(jnp.bfloat16)


def choose(which, first_ref, second_ref, chosen_ref):
    for index, source in ((1, first_ref), (0, second_ref)):

        @pl.when(which[0] == index)
        def _():
            chosen_ref[...] = source[...]


def chosen_front_kernel(which, first_ref, second_ref, gains, biases, w_ref, chosen_ref, normed_ref, q_ref, kv_ref):
    choose(which, first_ref, second_ref, chosen_ref)
    front_rows(chosen_ref, gains, biases, w_ref, normed_ref, q_ref, kv_ref)


def front_outs(rows):
    narrow = jnp.bfloat16
    return [((rows, D), narrow), ((rows, D), narrow), ((rows, 2 * D), narrow)]


def front(entry, gains, biases, w_qkv):
    rows = entry.shape[0]
    return call(front_rows, "front", 8, 6 * rows * D * D, front_outs(rows), [], entry, gains, biases, w_qkv)


def chosen_front(which, first, second, gains, biases, w_qkv):
    rows = first.shape[0]
    outs = [((rows, D), jnp.bfloat16)] + front_outs(rows)
    return call(
        chosen_front_kernel, "chosen_front", 8, 6 * rows * D * D, outs, [],
        which, first, second, gains, biases, w_qkv, smem=1,
    )


def middle_rows(x_ref, o_ref, w_out, biases, part):
    return x_ref[part, :].astype(jnp.float32) + dot(o_ref[part, :], w_out[0], NN) + bias_part(biases, 4)


def rest_kernel(x_ref, o_ref, gains, biases, w_out, w_up, w_down, result_ref):
    for part in row_chunks(x_ref.shape[0]):
        middle = middle_rows(x_ref, o_ref, w_out, biases, part)
        unit, _ = normalised(middle)
        normed = (unit * gains[1:2, :] + bias_part(biases, 1)).astype(jnp.bfloat16)
        total = middle + bias_part(biases, 5)
        for at in range(w_up.shape[2] // D):
            hidden = dot(normed, w_up[0, :, tile(at)], NN) + bias_part(biases, 6 + at)
            total += dot(gelu_only(hidden).astype(jnp.bfloat16), w_down[0, tile(at), :], NN)
        result_ref[part, :] = total.astype(jnp.bfloat16)


def rest(entry, attended, gains, biases, w_out, w_up, w_down):
    rows = entry.shape[0]
    flops = 2 * rows * (D * D + 2 * w_up.size)
    return call(
        rest_kernel, "rest", 7, flops, [((rows, D), jnp.bfloat16)], [],
        entry, attended, gains, biases, w_out, w_up, w_down,
    )[0]


def turn_kernel(
    x_ref, o_ref, d_ref, gains, biases, w_out, w_up, out_t, up_t, down_t,
    middle_ref, normed_ref, active_ref, slope_ref, grad_ref, grad_att_ref,
    middle, normed, actives, slopes, done,
):
    copies = []

    def leave(source, target):
        copies.append(pltpu.make_async_copy(source, target, done.at[len(copies)]))
        copies[-1].start()

    rows = x_ref[...].astype(jnp.float32) + dot(o_ref[...], w_out[0], NN) + bias_part(biases, 4)
    middle[...] = rows
    leave(middle, middle_ref)
    unit, _ = normalised(rows)
    normed[...] = (unit * gains[1:2, :] + bias_part(biases, 1)).astype(jnp.bfloat16)
    leave(normed, normed_ref)
    total = jnp.zeros_like(rows)
    for at in range(w_up.shape[2] // D):
        hidden = dot(normed[...], w_up[0, :, tile(at)], NN) + bias_part(biases, 6 + at)
        active, slope = gelu_parts(hidden)
        actives[at] = active.astype(jnp.bfloat16)
        slopes[at] = slope.astype(jnp.bfloat16)
        leave(actives.at[at], active_ref.at[:, tile(at)])
        leave(slopes.at[at], slope_ref.at[:, tile(at)])
        grad_hidden = dot(d_ref[...], down_t[:, tile(at)], NN) * slope
        total += dot(grad_hidden.astype(jnp.bfloat16), up_t[tile(at), :], NN)
    unit, inverse = normalised(middle[...])
    grad = d_ref[...].astype(jnp.float32) + norm_back(unit, inverse, gains[1:2, :], total)
    grad = grad.astype(jnp.bfloat16)
    grad_ref[...] = grad
    grad_att_ref[...] = dot(grad, out_t[...], NN).astype(jnp.bfloat16)
    for copy in copies:
        copy.wait()


def turn(entry, attended, result_gradient, gains, biases, w_out, w_up, out_t, up_t, down_t):
    rows = entry.shape[0]
    wide, narrow = jnp.float32, jnp.bfloat16
    inner = w_up.shape[2]
    steps = inner // D
    far = [((rows, D), wide), ((rows, D), narrow), ((rows, inner), narrow), ((rows, inner), narrow)]
    return pl.pallas_call(
        turn_kernel,
        in_specs=[VMEM_SPEC] * 10,
        out_specs=[pl.BlockSpec(memory_space=pltpu.HBM)] * len(far) + [VMEM_SPEC] * 2,
        out_shape=[placed(*out, pltpu.HBM) for out in far] + [placed((rows, D), narrow)] * 2,
        scratch_shapes=[
            pltpu.VMEM((rows, D), wide),
            pltpu.VMEM((rows, D), narrow),
            pltpu.VMEM((steps, rows, D), narrow),
            pltpu.VMEM((steps, rows, D), narrow),
            pltpu.SemaphoreType.DMA((2 + 2 * steps,)),
        ],
        compiler_params=pltpu.CompilerParams(vmem_limit_bytes=18 * 1024 * 1024),
        cost_estimate=cost(2 * rows * (2 * D * D + 3 * w_up.size)),
        name="turn",
    )(entry, attended, result_gradient, gains, biases, w_out, w_up, out_t, up_t, down_t)


def down_back_kernel(
    which, first_ref, second_ref, slope_ref, middle_ref, gains, out_t, up_t, down_t,
    d_ref, hidden_ref, grad_ref, grad_att_ref, sums_ref, up_ref,
):
    choose(which, first_ref, second_ref, d_ref)
    sums = [jnp.zeros((1, D), jnp.float32)] * 4
    steps = up_t.shape[0] // D
    up_sums = [jnp.zeros((1, D), jnp.float32)] * steps
    for part in row_chunks(d_ref.shape[0]):
        given = d_ref[part, :]
        through = jnp.zeros(given.shape, jnp.float32)
        for at in range(steps):
            grad_hidden = dot(given, down_t[:, tile(at)], NN) * slope_ref[part, tile(at)].astype(jnp.float32)
            up_sums[at] = up_sums[at] + column_sum(grad_hidden)
            grad_hidden = grad_hidden.astype(jnp.bfloat16)
            hidden_ref[part, tile(at)] = grad_hidden
            through += dot(grad_hidden, up_t[tile(at), :], NN)
        unit, inverse = normalised(middle_ref[part, :])
        given = given.astype(jnp.float32)
        grad = given + norm_back(unit, inverse, gains[1:2, :], through)
        grad_b = grad.astype(jnp.bfloat16)
        grad_ref[part, :] = grad_b
        grad_att_ref[part, :] = dot(grad_b, out_t[...], NN).astype(jnp.bfloat16)
        for at, term in enumerate((through * unit, through, grad, given)):
            sums[at] = sums[at] + column_sum(term)
    sums_ref[...] = jnp.concatenate(sums, axis=0)
    up_ref[...] = jnp.concatenate(up_sums, axis=0)


def down_back(which, first, second, slope, middle, gains, out_t, up_t, down_t):
    rows = first.shape[0]
    wide, narrow = jnp.float32, jnp.bfloat16
    inner = up_t.shape[0]
    outs = [
        ((rows, D), narrow), ((rows, inner), narrow), ((rows, D), narrow), ((rows, D), narrow),
        ((4, D), wide), ((inner // D, D), wide),
    ]
    return call(
        down_back_kernel, "down_back", 8, 2 * rows * (D * D + 2 * up_t.size), outs, [],
        which, first, second, slope, middle, gains, out_t, up_t, down_t, smem=1,
    )


def qkv_tiles(part, q_ref, own_ref, there_ref):
    tiles = [q_ref[part, :]]
    for at in range(2):
        total = own_ref[at, part, :].astype(jnp.float32) + there_ref[at, part, :].astype(jnp.float32)
        tiles.append(total.astype(jnp.bfloat16))
    return tiles


def front_back_kernel(q_ref, own_ref, there_ref, x_ref, grad_ref, gains, qkv_t, out_ref, sums_ref):
    sums = [jnp.zeros((1, D), jnp.float32)] * 4
    for part in row_chunks(x_ref.shape[0]):
        tiles = qkv_tiles(part, q_ref, own_ref, there_ref)
        through = sum(dot(value, qkv_t[tile(at), :], NN) for at, value in enumerate(tiles))
        unit, inverse = normalised(x_ref[part, :].astype(jnp.float32))
        out = grad_ref[part, :].astype(jnp.float32) + norm_back(unit, inverse, gains[0:1, :], through)
        out_ref[part, :] = out.astype(out_ref.dtype)
        terms = (through * unit, through, tiles[0].astype(jnp.float32), tiles[2].astype(jnp.float32))
        for at, term in enumerate(terms):
            sums[at] = sums[at] + column_sum(term)
    sums_ref[...] = jnp.concatenate(sums, axis=0)


def front_back(grad_q, own, there, entry, grad_middle, gains, qkv_t, dtype):
    rows = entry.shape[0]
    outs = [((rows, D), dtype, pltpu.VMEM), ((4, D), jnp.float32)]
    return call(
        front_back_kernel, "front_back", 8, 6 * rows * D * D, outs, [],
        grad_q, own, there, entry, grad_middle, gains, qkv_t,
    )


def added(kept, arrived, dtype=jnp.bfloat16):
    return (kept.astype(jnp.float32) + arrived.astype(jnp.float32)).astype(dtype)


def core_rows(left_ref, core, order):
    block = left_ref.shape[0] // (2 * len(order))
    picked = [
        left_ref[pl.ds(pl.multiple_of((2 * (2 * z_at + y_at) + core) * block, block), block), :] for z_at, y_at in order
    ]
    return jnp.concatenate(picked, axis=0)


def by_y_then_z(z_count):
    return [(z_at, y_at) for y_at in range(2) for z_at in range(z_count)]


def down_sent_kernel(place, left_ref, right_ref, sent_ref):
    block = sent_ref.shape[2]
    rows = core_rows(left_ref, 1 - place[0], by_y_then_z(1))
    total = dot(rows, right_ref[...], NN).astype(jnp.bfloat16)
    for y_at in range(2):
        sent_ref[y_at, 0] = total[y_at * block : (y_at + 1) * block]


def down_kept_kernel(place, left_ref, right_ref, there_ref, keep_ref, first_ref, second_ref, *, z_count):
    block = keep_ref.shape[1]
    total = dot(core_rows(left_ref, place[0], by_y_then_z(1)), right_ref[...], NN)
    parts = [added(total[y_at * block : (y_at + 1) * block], there_ref[y_at, 0]) for y_at in range(2)]

    def store(mine, send_ref):
        keep_ref[0] = parts[mine]
        send_ref[0] = parts[1 - mine]

    early = pl.program_id(0) < z_count // 2
    for mine in range(2):
        for now, send_ref in ((early, first_ref), (~early, second_ref)):
            pl.when((place[1] == mine) & now)(functools.partial(store, mine, send_ref))


def grid_call(kernel, name, grid, in_specs, out_specs, shapes, scratch, flops, place, *operands, far=0):
    return pl.pallas_call(
        kernel,
        grid_spec=pltpu.PrefetchScalarGridSpec(
            num_scalar_prefetch=1, grid=(grid,), in_specs=in_specs, out_specs=out_specs, scratch_shapes=scratch
        ),
        out_shape=[
            placed(shape, jnp.bfloat16, pltpu.HBM if at < far else None) for at, shape in enumerate(shapes)
        ],
        compiler_params=pltpu.CompilerParams(vmem_limit_bytes=9 * 1024 * 1024),
        cost_estimate=cost(flops),
        name=name,
    )(place, *operands)


def down_specs(active_t, z_count):
    height, rows = active_t.shape
    block = height // (4 * z_count)
    in_specs = [pl.BlockSpec((height // z_count, rows), lambda i, _: (i, 0)), whole(rows, D)]
    return block, in_specs, pl.BlockSpec((2, 1, block, D), lambda i, _: (0, i, 0, 0))


def down_sent(place, active_t, back, z_count):
    block, in_specs, sent_spec = down_specs(active_t, z_count)
    return grid_call(
        down_sent_kernel, "down_sent", z_count, in_specs, [sent_spec], [(2, z_count, block, D)], [],
        active_t.size * D, place, active_t, back,
    )[0]


def down_kept(place, active_t, back, there, z_count):
    block, in_specs, sent_spec = down_specs(active_t, z_count)
    half = z_count // 2
    out_specs = [
        pl.BlockSpec((1, block, D), lambda i, _: (i, 0, 0)),
        pl.BlockSpec((1, block, D), lambda i, _: (jnp.minimum(i, half - 1), 0, 0)),
        pl.BlockSpec((1, block, D), lambda i, _: (jnp.maximum(i - half, 0), 0, 0)),
    ]
    return grid_call(
        functools.partial(down_kept_kernel, z_count=z_count), "down_kept", z_count, in_specs + [sent_spec], out_specs,
        [(z_count, block, D)] + [(half, block, D)] * 2, [],
        active_t.size * D, place, active_t, back, there, far=1,
    )


def up_sent_kernel(place, left_ref, right_ref, sent_ref, rows):
    z_count, block = sent_ref.shape[1:3]
    order = by_y_then_z(z_count)

    @pl.when(pl.program_id(0) == 0)
    def _():
        rows[...] = core_rows(left_ref, 1 - place[0], order)

    total = dot(rows[...], right_ref[...], NN).astype(jnp.bfloat16)
    for at, (z_at, y_at) in enumerate(order):
        sent_ref[y_at, z_at] = total[at * block : (at + 1) * block]


def up_kept_kernel(place, left_ref, right_ref, there_ref, keep_ref, first_ref, second_ref, rows):
    z_count, block = there_ref.shape[1:3]
    order = by_y_then_z(z_count)

    @pl.when(pl.program_id(0) == 0)
    def _():
        rows[...] = core_rows(left_ref, place[0], order)

    total = dot(rows[...], right_ref[...], NN)
    parts = [added(total[at * block : (at + 1) * block], there_ref[y_at, z_at]) for at, (z_at, y_at) in enumerate(order)]

    def store(mine):
        for part, (z_at, y_at) in zip(parts, order):
            if z_at % 2 == mine:
                keep_ref[y_at, z_at // 2] = part
            else:
                (first_ref, second_ref)[y_at][z_at // 2] = part

    for mine in range(2):
        pl.when(place[2] == mine)(functools.partial(store, mine))


def half_rows(rows):
    return pltpu.VMEM((D // 2, rows), jnp.bfloat16)


def column_spec(z_count):
    return pl.BlockSpec((2, z_count, D // (4 * z_count), D), lambda i, _: (0, 0, 0, i))


def up_sent(place, normed_t, grad_hidden, z_count):
    rows, width = grad_hidden.shape
    in_specs = [whole(D, rows), pl.BlockSpec((rows, D), lambda i, _: (0, i))]
    return grid_call(
        up_sent_kernel, "up_sent", width // D, in_specs, [column_spec(z_count)],
        [(2, z_count, D // (4 * z_count), width)], [half_rows(rows)], grad_hidden.size * D, place, normed_t, grad_hidden,
    )[0]


def up_kept(place, normed_t, grad_hidden, there, z_count):
    rows, width = grad_hidden.shape
    in_specs = [whole(D, rows), pl.BlockSpec((rows, D), lambda i, _: (0, i)), column_spec(z_count)]
    shape = (2, z_count // 2, D // (4 * z_count), width)
    out_spec = pl.BlockSpec(shape[:3] + (D,), lambda i, _: (0, 0, 0, i))
    half_spec = pl.BlockSpec(shape[1:3] + (D,), lambda i, _: (0, 0, i))
    return grid_call(
        up_kept_kernel, "up_kept", width // D, in_specs, [out_spec] + [half_spec] * 2, [shape] + [shape[1:]] * 2,
        [half_rows(rows)],
        grad_hidden.size * D, place, normed_t, grad_hidden, there, far=1,
    )


def store_sent(sent_ref, at, total):
    z_count, block = sent_ref.shape[1:3]
    for row, (z_at, y_at) in enumerate(by_y_then_z(z_count)):
        sent_ref[y_at, z_at, :, tile(at)] = total[row * block : (row + 1) * block].astype(jnp.bfloat16)


def outer_sent_kernel(place, o_ref, normed_ref, d_ref, q_ref, sent_ref):
    order = by_y_then_z(sent_ref.shape[1])
    for at, (left, right) in enumerate(((o_ref, d_ref), (normed_ref, q_ref))):
        store_sent(sent_ref, at, dot(core_rows(left, 1 - place[0], order), right[...], NN))


def outer_sent(place, attended_t, normed_t, grad_middle, grad_q, z_count):
    outs = [((2, z_count, D // (4 * z_count), 2 * D), jnp.bfloat16)]
    return call(
        outer_sent_kernel, "outer_sent", 6, 2 * D * grad_q.size, outs, [],
        place, attended_t, normed_t, grad_middle, grad_q, smem=1,
    )[0]


def inner_sent_kernel(place, normed_ref, own_ref, there_ref, sent_ref):
    rows = core_rows(normed_ref, 1 - place[0], by_y_then_z(sent_ref.shape[1]))
    for at in range(2):
        store_sent(sent_ref, at, dot(rows, added(own_ref[at], there_ref[at]), NN))


def inner_sent(place, normed_t, own, there, z_count):
    outs = [((2, z_count, D // (4 * z_count), 2 * D), jnp.bfloat16)]
    return call(
        inner_sent_kernel, "inner_sent", 6, D * own.size, outs, [], place, normed_t, own, there, smem=1
    )[0]


def rest_kept_kernel(
    place, o_ref, normed_ref, d_ref, q_ref, own_ref, there_ref, outer_ref, inner_ref, keep_ref, send_ref
):
    z_count, block = keep_ref.shape[:2]
    order = by_y_then_z(z_count)
    attended, normed = [core_rows(left, place[0], order) for left in (o_ref, normed_ref)]

    def run(mine):
        for at in range(4):
            left = normed if at else attended
            right = (d_ref[...], q_ref[...])[at] if at < 2 else added(own_ref[at - 2], there_ref[at - 2])
            total = dot(left, right, NN)
            arrived = inner_ref if at > 1 else outer_ref
            for row, (z_at, y_at) in enumerate(order):
                target = keep_ref if y_at == mine else send_ref
                part = total[row * block : (row + 1) * block]
                target[z_at, :, tile(at)] = added(part, arrived[y_at, z_at, :, tile(at % 2)])

    for mine in range(2):
        pl.when(place[1] == mine)(functools.partial(run, mine))


def rest_kept(place, attended_t, normed_t, grad_middle, grad_q, own, there, outer_there, inner_there, z_count):
    outs = [((z_count, D // (4 * z_count), 4 * D), jnp.bfloat16)] * 2
    return call(
        rest_kept_kernel, "rest_kept", 10, 4 * D * grad_q.size, outs, [],
        place, attended_t, normed_t, grad_middle, grad_q, own, there, outer_there, inner_there, smem=1,
    )


def fold_kernel(place, kept_ref, arrived_ref, keep_ref, send_ref):
    for target, chosen in ((send_ref, 1 - place[0]), (keep_ref, place[0])):
        for at in range(target.shape[0]):
            target[at] = added(kept_ref[at, chosen], arrived_ref[at, chosen])


def fold(kept, arrived, place, outer):
    width = kept.shape[-1]
    lead = math.prod(kept.shape[:outer])
    inner = math.prod(kept.shape[outer + 1 : -1])
    shape = (lead, 2, inner, width)
    outs = [((lead, inner, width), kept.dtype)] * 2
    keep, send = call(
        fold_kernel, "fold", 4, 0, outs, [], place, kept.reshape(shape), arrived.reshape(shape), smem=1
    )
    left = kept.shape[:outer] + kept.shape[outer + 1 :]
    return keep.reshape(left), send.reshape(left)


def stream_fold_kernel(place, kept_keep, kept_send, first_keep, first_send, second_keep, second_send, keep_ref, send_ref):
    for step, arrived_keep, arrived_send in ((0, first_keep, first_send), (1, second_keep, second_send)):

        @pl.when(pl.program_id(0) == step)
        def _():
            send_ref[...] = added(kept_send[...], arrived_send[...])
            keep_ref[...] = added(kept_keep[...], arrived_keep[...])


def stream_fold(kept, first, second, place):
    inner, width = kept.shape[-2:]
    half = (None, inner, width)
    kept_specs = [
        pl.BlockSpec((None,) + half, lambda i, place: (i, place[0], 0, 0)),
        pl.BlockSpec((None,) + half, lambda i, place: (i, 1 - place[0], 0, 0)),
    ]
    arrived_specs = [
        pl.BlockSpec(half, lambda i, place: (place[0], 0, 0)),
        pl.BlockSpec(half, lambda i, place: (1 - place[0], 0, 0)),
    ]
    out_spec = pl.BlockSpec(half, lambda i, place: (i, 0, 0))
    return pl.pallas_call(
        stream_fold_kernel,
        grid_spec=pltpu.PrefetchScalarGridSpec(
            num_scalar_prefetch=1,
            grid=(2,),
            in_specs=kept_specs + arrived_specs * 2,
            out_specs=[out_spec, out_spec],
        ),
        out_shape=[jax.ShapeDtypeStruct((2, inner, width), jnp.bfloat16)] * 2,
        compiler_params=pltpu.CompilerParams(vmem_limit_bytes=8 * 1024 * 1024),
        cost_estimate=cost(0),
        name="stream_fold",
    )(place, *(in_hbm(value) for value in (kept, kept, first, first, second, second)))


def shifted(value, axis, steps):
    count = lax.axis_size(axis)
    initial, last = (max(0, -steps), min(count, count - steps))
    return lax.ppermute(value, axis, [(source, source + steps) for source in range(initial, last)])


def layer_norm(inputs_row, gain_row, offset):
    center = inputs_row - jnp.mean(inputs_row, axis=-1, keepdims=True)
    spread = jnp.mean(center * center, axis=-1, keepdims=True)
    return center * lax.rsqrt(spread + 1e-05) * gain_row + offset


def gelu_tanh(hidden):
    return jax.nn.gelu(hidden, approximate=True)


def score_terms(queries, key_rows, query_pos, key_pos, signed):
    key_count = key_rows.shape[0]
    scores = (
        jnp.einsum(
            "rhe,khe->hrk",
            queries,
            key_rows.reshape(key_count, HEADS, HDIM),
            preferred_element_type=jnp.float32,
        )
        * 0.125
    )
    curved = jnp.sqrt(scores * scores + 1.0)
    argument = jnp.where(signed, curved, scores)
    sign_pattern = jnp.where(signed, scores / curved, 1.0)
    slope = jnp.where(signed, sign_pattern, 1.0)
    bend = jnp.where(signed, 1.0 / (curved * curved * curved), 0.0)
    permitted_mask = key_pos[None, None, :] <= query_pos[None, :, None]
    return (argument, sign_pattern, slope, bend, permitted_mask)


def score_grads(
    queries, key_rows, value_rows, query_pos, key_pos, log_total, delta, grad_att, signed
):
    argument, sign_pattern, slope, bend, permitted_mask = score_terms(
        queries, key_rows, query_pos, key_pos, signed
    )
    prob = jnp.where(permitted_mask, jnp.exp(argument - log_total[..., None]), 0.0)
    along = jnp.einsum("rhe,khe->hrk", grad_att, value_rows, preferred_element_type=jnp.float32)
    dscore = (prob * ((sign_pattern * along - delta[..., None]) * slope + along * bend)).astype(
        jnp.bfloat16
    )
    return ((sign_pattern * prob).astype(jnp.bfloat16), dscore)


def key_blocks_of(key_all, value_all, key_pos, key_block):
    blocks = key_all.shape[0] // key_block
    return (
        key_all.reshape(blocks, key_block, D),
        value_all.reshape(blocks, key_block, HEADS, HDIM),
        key_pos.reshape(blocks, key_block),
    )


def attend(queries, query_pos, key_all, value_all, key_pos, signed, key_block):
    row_count = queries.shape[0]
    key_split, value_split, pos_split = key_blocks_of(key_all, value_all, key_pos, key_block)

    def running_total(state_in, element):
        largest, row_total_sum, gathered = state_in
        key_rows, value_rows, block_pos = element
        argument, sign_pattern, _, _, permitted_mask = score_terms(
            queries, key_rows, query_pos, block_pos, signed
        )
        masked_scores = jnp.where(permitted_mask, argument, -1e30)
        exponent_values = jnp.maximum(largest, jnp.max(masked_scores, axis=-1))
        multiplier = jnp.exp(largest - exponent_values)
        added_terms = jnp.where(
            permitted_mask, jnp.exp(masked_scores - exponent_values[..., None]), 0.0
        )
        row_total_sum = row_total_sum * multiplier + jnp.sum(added_terms, axis=-1)
        attention_weights = (sign_pattern * added_terms).astype(jnp.bfloat16)
        added = jnp.einsum(
            "hrk,khe->rhe", attention_weights, value_rows, preferred_element_type=jnp.float32
        )
        gathered = gathered * multiplier.T[:, :, None] + added
        return ((exponent_values, row_total_sum, gathered), None)

    start_max = jnp.full((HEADS, row_count), -1e30, jnp.float32)
    start_sum = jnp.zeros((HEADS, row_count), jnp.float32)
    start_out = jnp.zeros((row_count, HEADS, HDIM), jnp.float32)
    (largest, row_total_sum, gathered), _ = lax.scan(
        running_total, (start_max, start_sum, start_out), (key_split, value_split, pos_split)
    )
    log_total = largest + jnp.log(row_total_sum)
    attended = gathered / row_total_sum.T[:, :, None]
    return (attended, log_total)


def backward_summed(
    queries, query_pos, key_all, value_all, key_pos, log_total, delta, grad_att, signed, key_block
):
    key_split, value_split, pos_split = key_blocks_of(key_all, value_all, key_pos, key_block)

    def step_back(grad_q, element):
        key_rows, value_rows, block_pos = element
        attention_weights, dscore = score_grads(
            queries, key_rows, value_rows, query_pos, block_pos, log_total, delta, grad_att, signed
        )
        grad_q = (
            grad_q
            + jnp.einsum(
                "hrk,khe->rhe",
                dscore,
                key_rows.reshape(-1, HEADS, HDIM),
                preferred_element_type=jnp.float32,
            )
            * 0.125
        )
        grad_k = (
            jnp.einsum("hrk,rhe->khe", dscore, queries, preferred_element_type=jnp.float32) * 0.125
        )
        grad_v = jnp.einsum(
            "hrk,rhe->khe", attention_weights, grad_att, preferred_element_type=jnp.float32
        )
        return (grad_q, (grad_k.reshape(key_block, D), grad_v.reshape(key_block, D)))

    start_q = jnp.zeros(queries.shape, jnp.float32)
    grad_q, (grad_k, grad_v) = lax.scan(step_back, start_q, (key_split, value_split, pos_split))
    grad_k, grad_v = (
        lax.psum_scatter(
            grad_k.reshape(-1, D).astype(jnp.bfloat16), "ctx", scatter_dimension=0, tiled=True
        ).astype(jnp.float32),
        lax.psum_scatter(
            grad_v.reshape(-1, D).astype(jnp.bfloat16), "ctx", scatter_dimension=0, tiled=True
        ).astype(jnp.float32),
    )
    return (grad_q.reshape(-1, D), grad_k, grad_v)


def layer_front(inputs_row, gain_pair, bias_row, qkv_w):
    normed = layer_norm(inputs_row, gain_pair[0], bias_row[0:D]).astype(jnp.bfloat16)
    qkv_bias = jnp.concatenate(
        [bias_row[2 * D : 3 * D], jnp.zeros((D,), jnp.float32), bias_row[3 * D : 4 * D]]
    )
    projected = (jnp.dot(normed, qkv_w, preferred_element_type=jnp.float32) + qkv_bias).astype(
        jnp.bfloat16
    )
    return (normed, projected)


def layer_rest(inputs_row, attended_b, gain_pair, bias_row, out_w, up_w, down_w):
    middle = (
        inputs_row
        + jnp.dot(attended_b, out_w, preferred_element_type=jnp.float32)
        + bias_row[4 * D : 5 * D]
    )
    normed_two = layer_norm(middle, gain_pair[1], bias_row[D : 2 * D]).astype(jnp.bfloat16)
    hidden = jnp.dot(normed_two, up_w, preferred_element_type=jnp.float32) + bias_row[6 * D :]
    active = gelu_tanh(hidden).astype(jnp.bfloat16)
    result = (
        middle
        + jnp.dot(active, down_w, preferred_element_type=jnp.float32)
        + bias_row[5 * D : 6 * D]
    )
    return (middle, normed_two, hidden, active, result)


def general_body(inputs, slot_order, cotangent, gains, biases, w_qkv, w_out, w_up, w_down):
    micro_count = inputs.shape[0]
    row_count = inputs.shape[2]
    section_at = lax.axis_index("section")
    ctx_at = lax.axis_index("ctx")
    signed = section_at == 0
    gain_pair = gains[0]
    bias_row = biases[0]
    qkv_w = w_qkv[0]
    out_w = w_out[0]
    up_w = w_up[0]
    down_w = w_down[0]
    span_len = row_count // 2
    seq_pos = (
        slot_order[:, 0, :, None] * span_len + jnp.arange(span_len, dtype=jnp.int32)
    ).reshape(micro_count, -1)
    key_block = min(seq_pos.shape[1], 512)
    first_inputs = inputs[:, 0]
    cot_rows = cotangent[:, 0]

    def sequence_pos(index):
        whole_pos = lax.dynamic_index_in_dim(seq_pos, index, 0, keepdims=False)
        own_pos = lax.dynamic_slice_in_dim(whole_pos, ctx_at * row_count, row_count, 0)
        return (whole_pos, own_pos)

    def layer_forward(entry, index):
        whole_pos, own_pos = sequence_pos(index)
        inputs_row = entry.astype(jnp.float32)
        normed, projected = layer_front(inputs_row, gain_pair, bias_row, qkv_w)
        key_all, value_all = (
            lax.all_gather(projected[:, D : 2 * D], "ctx", axis=0, tiled=True),
            lax.all_gather(projected[:, 2 * D :], "ctx", axis=0, tiled=True),
        )
        queries = projected[:, :D].reshape(row_count, HEADS, HDIM)
        attended, _ = attend(queries, own_pos, key_all, value_all, whole_pos, signed, key_block)
        attended_b = attended.reshape(row_count, D).astype(jnp.bfloat16)
        result = layer_rest(inputs_row, attended_b, gain_pair, bias_row, out_w, up_w, down_w)[4]
        return result.astype(jnp.bfloat16)

    def layer_reverse_pass(entry, result_gradient, index):
        whole_pos, own_pos = sequence_pos(index)
        inputs_row = entry.astype(jnp.float32)
        normed, projected = layer_front(inputs_row, gain_pair, bias_row, qkv_w)
        queries = projected[:, :D].reshape(row_count, HEADS, HDIM)
        key_all, value_all = (
            lax.all_gather(projected[:, D : 2 * D], "ctx", axis=0, tiled=True),
            lax.all_gather(projected[:, 2 * D :], "ctx", axis=0, tiled=True),
        )
        attended, log_total = attend(
            queries, own_pos, key_all, value_all, whole_pos, signed, key_block
        )
        attended_b = attended.reshape(row_count, D).astype(jnp.bfloat16)
        middle, normed_two, hidden, active, _ = layer_rest(
            inputs_row, attended_b, gain_pair, bias_row, out_w, up_w, down_w
        )
        grad_down_b = result_gradient.astype(jnp.bfloat16)
        grad_wdown = jnp.dot(active.T, grad_down_b, preferred_element_type=jnp.float32)
        grad_active = jnp.dot(grad_down_b, down_w.T, preferred_element_type=jnp.float32)
        _, gelu_back = jax.vjp(gelu_tanh, hidden)
        grad_hidden = gelu_back(grad_active)[0]
        grad_hidden_b = grad_hidden.astype(jnp.bfloat16)
        grad_wup = jnp.dot(normed_two.T, grad_hidden_b, preferred_element_type=jnp.float32)
        grad_normed_two = jnp.dot(grad_hidden_b, up_w.T, preferred_element_type=jnp.float32)
        _, norm_back_two = jax.vjp(layer_norm, middle, gain_pair[1], bias_row[D : 2 * D])
        grad_middle_part, grad_gain_two, grad_offset_two = norm_back_two(grad_normed_two)
        grad_middle = result_gradient + grad_middle_part
        grad_proj_b = grad_middle.astype(jnp.bfloat16)
        grad_wout = jnp.dot(attended_b.T, grad_proj_b, preferred_element_type=jnp.float32)
        grad_att_flat = jnp.dot(grad_proj_b, out_w.T, preferred_element_type=jnp.float32).astype(
            jnp.bfloat16
        )
        grad_att = grad_att_flat.reshape(row_count, HEADS, HDIM)
        delta = jnp.einsum("rhe,rhe->hr", grad_att.astype(jnp.float32), attended)
        grad_q, grad_k, grad_v = backward_summed(
            queries,
            own_pos,
            key_all,
            value_all,
            whole_pos,
            log_total,
            delta,
            grad_att,
            signed,
            key_block,
        )
        grad_qkv_b = jnp.concatenate([grad_q, grad_k, grad_v], axis=1).astype(jnp.bfloat16)
        grad_wqkv = jnp.dot(normed.T, grad_qkv_b, preferred_element_type=jnp.float32)
        grad_normed = jnp.dot(grad_qkv_b, qkv_w.T, preferred_element_type=jnp.float32)
        _, norm_back_one = jax.vjp(layer_norm, inputs_row, gain_pair[0], bias_row[0:D])
        grad_in_part, grad_gain_one, grad_offset_one = norm_back_one(grad_normed)
        input_gradient = grad_middle + grad_in_part
        grad_gain_rows = jnp.stack([grad_gain_one, grad_gain_two])
        grad_bias_row = jnp.concatenate(
            [
                grad_offset_one,
                grad_offset_two,
                jnp.sum(grad_q, axis=0),
                jnp.sum(grad_v, axis=0),
                jnp.sum(grad_middle, axis=0),
                jnp.sum(result_gradient, axis=0),
                jnp.sum(grad_hidden, axis=0),
            ]
        )
        return (
            input_gradient,
            (grad_gain_rows, grad_bias_row, grad_wqkv, grad_wout, grad_wup, grad_wdown),
        )

    def tick(tick_at, state_in):
        arrived, returned, stored, acts_rows, grad_rows, partial_sums = state_in
        ahead = tick_at - section_at
        ahead_ok = (ahead >= 0) & (ahead < micro_count)
        ahead_at = jnp.clip(ahead, 0, micro_count - 1)
        fresh = jnp.where(
            signed, lax.dynamic_index_in_dim(first_inputs, ahead_at, 0, keepdims=False), arrived
        )
        previous = lax.dynamic_index_in_dim(stored, ahead_at, 0, keepdims=False)
        entry = jnp.where(ahead_ok, fresh, previous)
        stored = lax.dynamic_update_index_in_dim(stored, entry, ahead_at, 0)
        sent = layer_forward(entry, ahead_at)
        old_acts = lax.dynamic_index_in_dim(acts_rows, ahead_at, 0, keepdims=False)
        acts_rows = lax.dynamic_update_index_in_dim(
            acts_rows, jnp.where(ahead_ok, sent, old_acts), ahead_at, 0
        )
        behind = tick_at - 2 + section_at
        trailing_valid = (behind >= 0) & (behind < micro_count)
        trailing_position = jnp.clip(behind, 0, micro_count - 1)
        entry_gradient = lax.dynamic_index_in_dim(stored, trailing_position, 0, keepdims=False)
        given_cot = lax.dynamic_index_in_dim(cot_rows, trailing_position, 0, keepdims=False).astype(
            jnp.float32
        )
        result_gradient = jnp.where(signed, returned.astype(jnp.float32), given_cot)
        input_gradient, added_terms = layer_reverse_pass(
            entry_gradient, result_gradient, trailing_position
        )
        partial_sums = jax.tree.map(
            lambda running_total, added_term: running_total
            + jnp.where(trailing_valid, added_term, 0.0),
            partial_sums,
            added_terms,
        )
        handed = input_gradient.astype(jnp.bfloat16)
        kept_grad = jnp.where(signed, input_gradient, handed.astype(jnp.float32))
        old_grads = lax.dynamic_index_in_dim(grad_rows, trailing_position, 0, keepdims=False)
        grad_rows = lax.dynamic_update_index_in_dim(
            grad_rows, jnp.where(trailing_valid, kept_grad, old_grads), trailing_position, 0
        )
        arrived = shifted(sent, "section", 1)
        returned = shifted(handed, "section", -1)
        return (arrived, returned, stored, acts_rows, grad_rows, partial_sums)

    zero_rows = jnp.zeros((row_count, D), jnp.bfloat16)
    start_sums = (
        jnp.zeros((2, D), jnp.float32),
        jnp.zeros((bias_row.shape[0],), jnp.float32),
        jnp.zeros(qkv_w.shape, jnp.float32),
        jnp.zeros(out_w.shape, jnp.float32),
        jnp.zeros(up_w.shape, jnp.float32),
        jnp.zeros(down_w.shape, jnp.float32),
    )
    start_state = (
        zero_rows,
        zero_rows,
        jnp.zeros((micro_count, row_count, D), jnp.bfloat16),
        jnp.zeros((micro_count, row_count, D), jnp.bfloat16),
        jnp.zeros((micro_count, row_count, D), jnp.float32),
        start_sums,
    )
    final_state = lax.fori_loop(0, micro_count + 2, tick, start_state)
    acts_rows = final_state[3]
    grad_rows = final_state[4]
    partial_sums = final_state[5]
    totals = (
        lax.psum_scatter(partial_sums[0], ("dp", "ctx"), scatter_dimension=1, tiled=True),
        lax.psum_scatter(partial_sums[1], ("dp", "ctx"), scatter_dimension=0, tiled=True),
        lax.psum_scatter(partial_sums[2], ("dp", "ctx"), scatter_dimension=0, tiled=True),
        lax.psum_scatter(partial_sums[3], ("dp", "ctx"), scatter_dimension=0, tiled=True),
        lax.psum_scatter(partial_sums[4], ("dp", "ctx"), scatter_dimension=0, tiled=True),
        lax.psum_scatter(partial_sums[5], ("dp", "ctx"), scatter_dimension=0, tiled=True),
    )
    return (
        acts_rows[None, :, None],
        grad_rows[None, :, None],
        totals[0][None],
        totals[1][None],
        totals[2][None],
        totals[3][None],
        totals[4][None],
        totals[5][None],
    )


def swap_halves(value):
    count = lax.axis_size("ctx")
    return lax.ppermute(value, "ctx", [(at, (at + count // 2) % count) for at in range(count)])


def swap_cores(value):
    return lax.ppermute(value, "ctx", [(at, at ^ 1) for at in range(lax.axis_size("ctx"))])


def swap_z(value, step):
    return lax.ppermute(value, "dp", [(at, at ^ step) for at in range(lax.axis_size("dp"))])


def wide_sum(kept, arrived):
    return kept.astype(jnp.float32) + arrived.astype(jnp.float32)


def fast_body(inputs, slot_order, cotangent, gains, biases, w_qkv, w_out, w_up, w_down):
    rows = inputs.shape[2]
    count = lax.axis_size("ctx")
    z_count = lax.axis_size("dp")
    half = count // 2
    ctx_at = lax.axis_index("ctx")
    mine = ctx_at // half
    y_at, core_at = ctx_at // 2, ctx_at % 2
    signed = lax.axis_index("section") == 0
    which = signed.astype(jnp.int32)[None]
    place = core_at[None].astype(jnp.int32)
    y_place = y_at[None].astype(jnp.int32)
    z_at = lax.axis_index("dp")
    gain_pair = gains[0]
    wide, narrow, barrier = jnp.float32, jnp.bfloat16, lax.optimization_barrier

    def gathered(value):
        kept = lax.dynamic_index_in_dim(value, mine, 0, keepdims=False)
        sent = lax.dynamic_index_in_dim(value, 1 - mine, 0, keepdims=False)
        return jnp.concatenate([kept, swap_halves(sent)], axis=0)

    def returned(kept, arrived):
        arrived = arrived.astype(kept.dtype)
        first = jnp.where(mine == 0, kept, arrived)
        second = jnp.where(mine == 0, arrived, kept)
        return jnp.stack([first, second])

    order = lax.dynamic_index_in_dim(slot_order[:, 0], mine, 0, keepdims=False)
    pairs = order.reshape(count, 2)

    def slots_of(device):
        return jnp.concatenate([pairs[device], pairs[(device + half) % count]])

    meta = slot_meta(slots_of(ctx_at), slots_of(ctx_at ^ 1), signed)

    inputs, meta = barrier((inputs, meta))
    first = gathered(inputs[:, 0])
    qkv_t, out_t = flip(w_qkv, pltpu.HBM), flip(w_out, pltpu.HBM)
    first, qkv_t, out_t = barrier((first, qkv_t, out_t))
    _, queries, kv = front(first, gain_pair, biases, w_qkv)
    attended, _ = sorted_attend(meta, queries, kv, swap_cores(kv))
    sent = rest(first, attended, gain_pair, biases, w_out, w_up, w_down)
    sent, later = barrier((sent, (cotangent, w_up, w_down)))
    arrived = shifted(sent, "section", 1)
    given = gathered(later[0][:, 0])
    up_t, down_t = [flip(weight, pltpu.HBM) for weight in later[1:]]
    arrived, given, up_t, down_t = barrier((arrived, given, up_t, down_t))
    entry, normed, queries, kv = chosen_front(which, first, arrived, gain_pair, biases, w_qkv)
    kv_there = swap_cores(kv)
    normed_t = flip(normed, pltpu.HBM)
    kv_there, normed_t = barrier((kv_there, normed_t))
    attended, lse = sorted_attend(meta, queries, kv, kv_there)
    middle, normed_two, active, slope, grad_middle, grad_att = turn(
        entry, attended, given, gain_pair, biases, w_out, w_up, out_t, up_t, down_t
    )

    grad_q, own, sent, *ahead = sorted_attend_back(meta, queries, kv, kv_there, attended, grad_att, lse)
    own, sent, attended, normed_two = barrier((own, sent, attended, normed_two))
    there = swap_cores(sent)
    attended_t, normed_two_t = flip(attended, pltpu.HBM), flip(normed_two, pltpu.HBM)
    there, attended_t, normed_two_t = barrier((there, attended_t, normed_two_t))
    handed, _ = front_back(grad_q, own, there, entry, grad_middle, gain_pair, qkv_t, narrow)
    handed, active, middle, weights = barrier((handed, active, middle, (w_up, w_down)))
    back = shifted(handed, "section", -1)
    result = middle + dot(active, w_down[0], NN) + biases[0, 5 * D : 6 * D]
    result = result.astype(narrow)
    acts_there = swap_halves(result[rows:])
    middle, acts_there, active = barrier((middle, acts_there, active))
    up_t, down_t = [flip(in_hbm(weight), pltpu.VMEM) for weight in weights]
    active_t = flip(active, pltpu.VMEM)
    back, up_t, down_t, active_t = barrier((back, up_t, down_t, active_t))

    z_steps = [1 << at for at in range(z_count.bit_length() - 1)]
    split = [2] * len(z_steps)
    by_z = [((z_at >> at) & 1)[None].astype(jnp.int32) for at in range(len(z_steps))]

    def bits(value, before):
        return value.reshape(value.shape[:before] + tuple(split) + value.shape[before + 1 :])

    places = jnp.concatenate([place, y_place, by_z[0]])
    back, grad_hidden, grad_middle, grad_att, sums_two, up_sum = down_back(
        which, back, given, slope, middle, gain_pair, out_t, up_t, down_t
    )
    back, grad_hidden = barrier((back, grad_hidden))
    down_there = down_sent(places, active_t, back, z_count)
    grad_hidden, down_there = barrier((grad_hidden, down_there))
    down_there = swap_cores(down_there)
    up_there = up_sent(places, normed_two_t, grad_hidden, z_count)
    down_there, up_there = barrier((down_there, up_there))
    up_there = swap_cores(up_there)
    down_keep, down_send, down_later = down_kept(places, active_t, back, down_there, z_count)
    up_there, down_send, down_later = barrier((up_there, down_send, down_later))
    up_keep, up_send, up_later = up_kept(places, normed_two_t, grad_hidden, up_there, z_count)
    grad_att, down_send, up_send = barrier((grad_att, down_send, up_send))
    down_first, up_first = swap_halves(down_send), swap_z(up_send, z_steps[0])
    grad_q, own, sent = sorted_attend_back(meta, queries, kv, kv_there, attended, grad_att, lse, ahead)

    grad_q, own, sent, down_first, up_first, down_later, up_later = barrier(
        (grad_q, own, sent, down_first, up_first, down_later, up_later)
    )
    there = swap_cores(sent)
    down_second, up_second = swap_halves(down_later), swap_z(up_later, z_steps[0])
    outer_there = outer_sent(places, attended_t, normed_t, grad_middle, grad_q, z_count)
    there, outer_there = barrier((there, outer_there))
    outer_there = swap_cores(outer_there)
    inner_there = inner_sent(places, normed_t, own, there, z_count)
    inner_there, down_second, up_second = barrier((inner_there, down_second, up_second))
    inner_there = swap_cores(inner_there)
    down_keep, down_send = stream_fold(bits(down_keep, 0), down_first, down_second, by_z[0])
    up_keep, up_send = stream_fold(up_keep, up_first, up_second, by_z[1])
    outer_there, inner_there, down_send, up_send = barrier((outer_there, inner_there, down_send, up_send))
    rest_keep, rest_send = rest_kept(
        places, attended_t, normed_t, grad_middle, grad_q, own, there, outer_there, inner_there, z_count
    )
    rest_send, down_send, up_send, grad_q, own, there = barrier((rest_send, down_send, up_send, grad_q, own, there))
    rest_there, down_there, up_there = swap_halves(rest_send), swap_z(down_send, z_steps[0]), swap_z(up_send, z_steps[1])
    input_gradient, sums_one = front_back(grad_q, own, there, entry, grad_middle, gain_pair, qkv_t, wide)
    small = jnp.concatenate([sums_one, sums_two, up_sum], axis=0)
    small = small + swap_cores(small)
    rounded = input_gradient.astype(narrow)
    small_there = swap_halves(small)
    down_there, rounded = barrier((down_there, rounded))
    down_keep, down_send = fold(down_keep, down_there, by_z[1], 0)
    down_send, rest_there, small_there = barrier((down_send, rest_there, small_there))
    down_there = swap_z(down_send, z_steps[1])

    rest_keep, rest_send = fold(bits(rest_keep, 0), bits(rest_there, 0), by_z[0], len(split) - 1)
    small = small + small_there
    rest_send, up_there, small = barrier((rest_send, up_there, small))
    rest_there, small_there = swap_z(rest_send, z_steps[0]), swap_z(small, z_steps[0])
    up_keep, up_send = fold(up_keep, up_there, y_place, 0)
    up_there = swap_halves(up_send)
    rounded, up_send = barrier((rounded, up_send))
    grads_there = swap_halves(rounded[rows:])
    rest_there, up_there, small_there, down_there, grads_there = barrier(
        (rest_there, up_there, small_there, down_there, grads_there)
    )
    rest_keep, rest_send = fold(rest_keep, rest_there, by_z[1], 0)
    rest_send, small_there, grads_there, result, acts_there = barrier(
        (rest_send, small_there, grads_there, result, acts_there)
    )
    rest_there = swap_z(rest_send, z_steps[1])
    small = small + small_there
    small = small + swap_z(small, z_steps[1])
    wdown = wide_sum(down_keep, down_there)
    wup = wide_sum(up_keep, up_there)
    grads_kept = jnp.where(signed, input_gradient[:rows], rounded[:rows].astype(wide))
    grad_rows = returned(grads_kept, grads_there)
    grad_rows, rest_there = barrier((grad_rows, rest_there))
    wout = wide_sum(rest_keep[:, :D], rest_there[:, :D])
    wqkv = wide_sum(rest_keep[:, D:], rest_there[:, D:])
    blocks = count * z_count
    block_at = lax.axis_index("dp") * count + ctx_at
    gain_piece = lax.dynamic_slice_in_dim(small[0:5:4], block_at * (D // blocks), D // blocks, 1)
    bias_row = jnp.concatenate([small[1:2], small[5:6], small[2:4], small[6:]], axis=0).reshape(-1)
    width = bias_row.shape[0] // blocks
    bias_piece = lax.dynamic_slice_in_dim(bias_row, block_at * width, width, 0)
    return (
        returned(result[:rows], acts_there)[None, :, None],
        grad_rows[None, :, None],
        gain_piece[None],
        bias_piece[None],
        wqkv[None],
        wout[None],
        wup[None],
        wdown[None],
    )


def body_for(mesh):
    sizes = dict(mesh.shape)
    return fast_body if (sizes["ctx"], sizes["dp"]) == (4, 4) else general_body


def solution(mesh):
    in_specs = (
        P(None, "dp", "ctx", None),
        P(None, "dp", None),
        P(None, "dp", "ctx", None),
        P("section", None, None),
        P("section", None),
        P("section", None, None),
        P("section", None, None),
        P("section", None, None),
        P("section", None, None),
    )
    out_specs = (
        P("section", None, "dp", "ctx", None),
        P("section", None, "dp", "ctx", None),
        P("section", None, ("dp", "ctx")),
        P("section", ("dp", "ctx")),
        P("section", ("dp", "ctx"), None),
        P("section", ("dp", "ctx"), None),
        P("section", ("dp", "ctx"), None),
        P("section", ("dp", "ctx"), None),
    )
    return jax.shard_map(
        body_for(mesh), mesh=mesh, in_specs=in_specs, out_specs=out_specs, check_vma=False
    )
```

```python
import functools
import math
import jax
import jax.numpy as jnp
from jax import lax
from jax.experimental import pallas as pl
from jax.experimental.pallas import tpu as pltpu
from jax.sharding import PartitionSpec as P

D = 768
HEADS = 12
HDIM = 64
PAIR = 2 * HDIM
PAIRS = HEADS // 2
OWN = 4
CHUNK = 128
SAFE = 60.0
NT = (((1,), (1,)), ((), ()))
TN = (((0,), (0,)), ((), ()))
NN = (((1,), (0,)), ((), ()))


def dot(left, right, dims):
    return lax.dot_general(left, right, dims, preferred_element_type=jnp.float32)


def slot_meta(own_pos, other_pos, signed):
    rank = jnp.sum((own_pos[None, :] < own_pos[:, None]).astype(jnp.int32), axis=1)
    chosen = rank[None, :] == jnp.arange(OWN, dtype=jnp.int32)[:, None]
    ranked = jnp.sum(jnp.where(chosen, jnp.arange(OWN, dtype=jnp.int32)[None, :], 0), axis=1)
    ranked_pos = jnp.sum(jnp.where(chosen, own_pos[None, :], 0), axis=1)
    return jnp.concatenate([own_pos, other_pos, ranked, ranked_pos, signed.astype(jnp.int32)[None]])


def sort_rows(meta, own, other, target, span, first):
    columns = slice(first, first + D)
    for slot in range(OWN):
        for base, source in ((0, own), (OWN, other)):
            start = pl.multiple_of(meta[base + slot] * span, span)
            target[pl.ds(start, span), :] = source[slot * span : (slot + 1) * span, columns]


def reach(rank, slots):
    return ((0, slots // 2 - 2), (1, slots // 2 - 1), (slots // 2, slots - 2), (slots // 2 + 1, slots - 1))[rank]


def stacked_heads(rows):
    second = lax.broadcasted_iota(jnp.int32, rows.shape, 1) >= HDIM
    zero = jnp.zeros_like(rows)
    return jnp.concatenate([jnp.where(second, zero, rows), jnp.where(second, rows, zero)], axis=0)


def visible(values, start, least, span, position, fill):
    if start + values.shape[0] <= least * span:
        return values
    key_at = lax.broadcasted_iota(jnp.int32, values.shape, 0) + start
    lane = lax.broadcasted_iota(jnp.int32, values.shape, 1)
    query_at = position * span + jnp.where(lane >= span, lane - span, lane)
    return jnp.where(key_at <= query_at, values, fill)


def unstack(pair, span):
    row = lax.broadcasted_iota(jnp.int32, (PAIR, span), 0)
    return jnp.where(row < HDIM, pair[:, :span], pair[:, span:]).T


def chunks_of(count, chunk):
    return [slice(start, min(start + chunk, count)) for start in range(0, count, chunk)]


def eight(values):
    return values.reshape(-1, 8, values.shape[-1])


def pair_columns(at):
    return pl.ds(pl.multiple_of(at * PAIR, PAIR), PAIR)


def largest_norm(rows_ref):
    feature = lax.broadcasted_iota(jnp.int32, (D, PAIR), 0) // HDIM
    head = lax.broadcasted_iota(jnp.int32, (D, PAIR), 1)
    chosen = jnp.where(feature == head, 1.0, 0.0).astype(jnp.bfloat16)
    rows = rows_ref[...]
    return jnp.max(dot(rows * rows, chosen, NN))


def forward_kernel(meta, q_ref, kv_ref, kv2_ref, o_ref, lse_ref, keys, values, *, span):
    slots = keys.shape[0] // span
    sort_rows(meta, kv_ref, kv2_ref, keys, span, 0)
    sort_rows(meta, kv_ref, kv2_ref, values, span, D)
    bound = largest_norm(q_ref) * largest_norm(keys) * (1.1 / HDIM)
    near = bound < SAFE * SAFE

    def run(signed, safe):
        def one_pair(pair, _):
            columns = pair_columns(pair)
            values_t = values[:, columns].T
            for rank in reversed(range(OWN)):
                least, most = reach(rank, slots)
                count = (most + 1) * span
                row_at = pl.multiple_of(meta[2 * OWN + rank] * span, span)
                position = meta[3 * OWN + rank]
                queries = stacked_heads(q_ref[pl.ds(row_at, span), columns] * 0.125)
                largest = None
                if not safe:
                    most_seen = jnp.full((8, 2 * span), -1e30, jnp.float32)
                    for part in chunks_of(count, CHUNK):
                        scores = dot(keys[part, columns], queries, NT)
                        scores = jnp.abs(scores) if signed else scores
                        scores = visible(scores, part.start, least, span, position, -1e30)
                        most_seen = jnp.maximum(most_seen, jnp.max(eight(scores), axis=0))
                    largest = jnp.max(most_seen, axis=0, keepdims=True)
                    if signed:
                        square = largest * largest + 1.0
                        largest = square * lax.rsqrt(square)
                total = jnp.zeros((8, 2 * span), jnp.float32)
                gathered = jnp.zeros((PAIR, 2 * span), jnp.float32)
                for part in chunks_of(count, CHUNK):
                    scores = dot(keys[part, columns], queries, NT)
                    argument = scores
                    if signed:
                        square = scores * scores + 1.0
                        inverse = lax.rsqrt(square)
                        argument = square * inverse
                    if not safe:
                        argument = argument - largest
                    weights = jnp.exp(visible(argument, part.start, least, span, position, -1e30))
                    total += jnp.sum(eight(weights), axis=0)
                    if signed:
                        weights = weights * (scores * inverse)
                    gathered += dot(values_t[:, part], weights.astype(jnp.bfloat16), NN)
                total = jnp.sum(total, axis=0, keepdims=True)
                lse = jnp.log(total)
                lse_ref[pair, rank : rank + 1, :] = lse if safe else lse + largest
                gathered = gathered * (1.0 / total)
                o_ref[pl.ds(row_at, span), columns] = unstack(gathered, span).astype(jnp.bfloat16)
            return 0

        lax.fori_loop(0, PAIRS, one_pair, 0)

    for signed in (True, False):
        for safe in (True, False):
            chosen = (meta[4 * OWN] == int(signed)) & (near == safe)
            pl.when(chosen)(functools.partial(run, signed, safe))


def in_vmem(*values):
    return [pltpu.with_memory_space_constraint(value, pltpu.VMEM) for value in values]


SMEM_SPEC = pl.BlockSpec(memory_space=pltpu.SMEM)
VMEM_SPEC = pl.BlockSpec(memory_space=pltpu.VMEM)


def sorted_attend(meta, queries, kv, kv_other):
    rows = kv.shape[0]
    span = rows // OWN
    return pl.pallas_call(
        functools.partial(forward_kernel, span=span),
        in_specs=[SMEM_SPEC] + [VMEM_SPEC] * 3,
        out_specs=[VMEM_SPEC] * 2,
        scratch_shapes=[pltpu.VMEM((2 * rows, D), jnp.bfloat16)] * 2,
        out_shape=[
            jax.ShapeDtypeStruct((rows, D), jnp.bfloat16),
            jax.ShapeDtypeStruct((PAIRS, OWN, 2 * span), jnp.float32),
        ],
        compiler_params=pltpu.CompilerParams(vmem_limit_bytes=10 * 1024 * 1024),
        cost_estimate=pl.CostEstimate(flops=4_000_000_000, bytes_accessed=0, transcendentals=0),
        name="attend",
    )(meta, *in_vmem(queries, kv, kv_other))


def reaches(slots, span):
    found, at = [], 0
    for rank in range(OWN):
        least, most = reach(rank, slots)
        found.append((least, (most + 1) * span, at))
        at += (most + 1) * span
    return found, at


def kept_copies(pair, side, factor_buf, weight_buf, factors, weights, done, out):
    copies = []
    for part, (buffer, far) in enumerate(((factor_buf, factors), (weight_buf, weights))):
        near, there = buffer.at[side], far.at[pair]
        source, target = (near, there) if out else (there, near)
        copies.append(pltpu.make_async_copy(source, target, done.at[side, part]))
    return copies


def backward_kernel(
    meta, q_ref, kv_ref, kv2_ref, o_ref, do_ref, lse_ref, *refs, span, prepare
):
    if prepare:
        dq_ref, own_ref, other_ref, factors, weight_rows, *scratch = refs
    else:
        factors, weight_rows, dq_ref, own_ref, other_ref, *scratch = refs
    keys, values, grad_k, grad_v, factor_buf, weight_buf, done = scratch
    slots = keys.shape[0] // span
    ranks, _ = reaches(slots, span)
    sort_rows(meta, kv_ref, kv2_ref, keys, span, 0)
    sort_rows(meta, kv_ref, kv2_ref, values, span, D)

    def copies(pair, side):
        return kept_copies(pair, side, factor_buf, weight_buf, factors, weight_rows, done, prepare)

    def queries_at(rank, columns):
        row_at = pl.multiple_of(meta[2 * OWN + rank] * span, span)
        return row_at, stacked_heads(q_ref[pl.ds(row_at, span), columns] * 0.125)

    def make_ahead():
        def one_pair(pair, _):
            side = lax.rem(pair, 2)
            columns = pair_columns(pair)

            @pl.when(pair >= 2)
            def _():
                for copy in copies(pair, side):
                    copy.wait()

            for rank, (least, count, start) in enumerate(ranks):
                _, queries = queries_at(rank, columns)
                scores = dot(keys[:count, columns], queries, NT)
                square = scores * scores + 1.0
                inverse = lax.rsqrt(square)
                argument = square * inverse - lse_ref[pair, rank : rank + 1, :]
                prob = jnp.exp(visible(argument, 0, least, span, meta[3 * OWN + rank], -1e30))
                sign_pattern = scores * inverse
                factor = prob * (sign_pattern * sign_pattern + inverse * inverse * inverse)
                factor_buf[side, start : start + count, :] = factor.astype(jnp.bfloat16)
                weight_buf[side, start : start + count, :] = (prob * sign_pattern).astype(jnp.bfloat16)
            for copy in copies(pair, side):
                copy.start()
            return 0

        lax.fori_loop(0, PAIRS, one_pair, 0)
        for pair in range(PAIRS - 2, PAIRS):
            for copy in copies(pair, pair % 2):
                copy.wait()
        for out_ref in (dq_ref, own_ref, other_ref):
            out_ref[...] = jnp.zeros_like(out_ref)

    def run(made):
        if made:
            for copy in copies(0, 0):
                copy.start()

        def one_pair(pair, _):
            side = lax.rem(pair, 2)
            columns = pair_columns(pair)
            keys_t = keys[:, columns].T
            if made:

                @pl.when(pair + 1 < PAIRS)
                def _():
                    for copy in copies(pair + 1, 1 - side):
                        copy.start()

                for copy in copies(pair, side):
                    copy.wait()
            for rank in reversed(range(OWN)):
                least, count, start = ranks[rank]
                row_at, queries = queries_at(rank, columns)
                grad_rows = do_ref[pl.ds(row_at, span), columns]
                grads = stacked_heads(grad_rows)
                product = grad_rows.astype(jnp.float32) * o_ref[pl.ds(row_at, span), columns].astype(jnp.float32)
                delta = jnp.sum(stacked_heads(product).T, axis=0, keepdims=True)
                along = dot(values[:count, columns], grads, NT)
                if made:
                    weights = weight_buf[side, start : start + count, :]
                    factor = factor_buf[side, start : start + count, :].astype(jnp.float32)
                    dscore = factor * along - weights.astype(jnp.float32) * delta
                else:
                    scores = dot(keys[:count, columns], queries, NT)
                    argument = scores - lse_ref[pair, rank : rank + 1, :]
                    weights = jnp.exp(visible(argument, 0, least, span, meta[3 * OWN + rank], -1e30))
                    dscore = weights * (along - delta)
                    weights = weights.astype(jnp.bfloat16)
                dscore = dscore.astype(jnp.bfloat16)
                added_v = dot(weights, grads, NN)
                added_k = dot(dscore, queries, NN)
                if rank == OWN - 1:
                    grad_v[...] = added_v
                    grad_k[...] = added_k
                else:
                    grad_v[:count, :] += added_v
                    grad_k[:count, :] += added_k
                gathered = dot(keys_t[:, :count], dscore, NN)
                dq_ref[pl.ds(row_at, span), columns] = (unstack(gathered, span) * 0.125).astype(jnp.bfloat16)
            for slot in range(OWN):
                there = slice(slot * span, (slot + 1) * span)
                own_at = pl.multiple_of(meta[slot] * span, span)
                other_at = pl.multiple_of(meta[OWN + slot] * span, span)
                for part, total in enumerate((grad_k, grad_v)):
                    own_ref[part, there, columns] = total[pl.ds(own_at, span), :].astype(jnp.bfloat16)
                    other_ref[part, there, columns] = total[pl.ds(other_at, span), :].astype(jnp.bfloat16)
            return 0

        lax.fori_loop(0, PAIRS, one_pair, 0)

    pl.when(meta[4 * OWN] == 0)(functools.partial(run, False))
    pl.when(meta[4 * OWN] == 1)(make_ahead if prepare else functools.partial(run, True))


def sorted_attend_back(meta, queries, kv, kv_other, attended, grad_att, lse, made=None):
    rows = kv.shape[0]
    span = rows // OWN
    narrow = jnp.bfloat16
    _, reached = reaches(2 * OWN, span)
    far_spec = pl.BlockSpec(memory_space=pltpu.HBM)
    ahead = [pltpu.HBM((PAIRS, reached, 2 * span), narrow)] * 2
    shapes = [jax.ShapeDtypeStruct((rows, D), narrow)] + [jax.ShapeDtypeStruct((2, rows, D), narrow)] * 2
    prepare = made is None
    given = () if prepare else tuple(pltpu.with_memory_space_constraint(value, pltpu.HBM) for value in made)
    return pl.pallas_call(
        functools.partial(backward_kernel, span=span, prepare=prepare),
        in_specs=[SMEM_SPEC] + [VMEM_SPEC] * 6 + [far_spec] * len(given),
        out_specs=[VMEM_SPEC] * 3 + [far_spec] * (2 if prepare else 0),
        scratch_shapes=[pltpu.VMEM((2 * rows, D), narrow)] * 2
        + [pltpu.VMEM((2 * rows, PAIR), jnp.float32)] * 2
        + [pltpu.VMEM((2, reached, 2 * span), narrow)] * 2
        + [pltpu.SemaphoreType.DMA((2, 2))],
        out_shape=shapes + (ahead if prepare else []),
        compiler_params=pltpu.CompilerParams(vmem_limit_bytes=18 * 1024 * 1024),
        cost_estimate=pl.CostEstimate(flops=8_000_000_000, bytes_accessed=0, transcendentals=0),
        name="attend_back",
    )(meta, *in_vmem(queries, kv, kv_other, attended, grad_att), lse, *given)


TURN_TANH = 0.7978845608028654
CUBE = 0.044715
CHUNKS = 1


def normalised(rows):
    center = rows - jnp.mean(rows, axis=-1, keepdims=True)
    inverse = lax.rsqrt(jnp.mean(center * center, axis=-1, keepdims=True) + 1e-05)
    return center * inverse, inverse


def norm_back(unit, inverse, gain_row, grad):
    scaled = grad * gain_row
    along = jnp.mean(scaled * unit, axis=-1, keepdims=True)
    return inverse * (scaled - jnp.mean(scaled, axis=-1, keepdims=True) - unit * along)


def row_chunks(rows, chunks=CHUNKS):
    return [slice(at * rows // chunks, (at + 1) * rows // chunks) for at in range(chunks)]


def column_sum(values):
    return jnp.sum(values, axis=0, keepdims=True)


def gelu_parts(hidden):
    square = hidden * hidden
    curve = jnp.tanh(hidden * (TURN_TANH + TURN_TANH * CUBE * square))
    half = 0.5 + 0.5 * curve
    inner = hidden * (TURN_TANH + 3.0 * TURN_TANH * CUBE * square)
    return hidden * half, half + 0.5 * (1.0 - curve * curve) * inner


def gelu_only(hidden):
    square = hidden * hidden
    curve = jnp.tanh(hidden * (TURN_TANH + TURN_TANH * CUBE * square))
    return hidden * (0.5 + 0.5 * curve)


def cost(flops):
    return pl.CostEstimate(flops=int(flops) // 8, bytes_accessed=0, transcendentals=0)


def in_hbm(value):
    return pltpu.with_memory_space_constraint(value, pltpu.HBM)


def placed(shape, dtype, space=None):
    return jax.ShapeDtypeStruct(shape, dtype) if space is None else space(shape, dtype)


def call(kernel, name, megabytes, flops, outs, scratch, *operands, smem=0):
    return pl.pallas_call(
        kernel,
        in_specs=[SMEM_SPEC] * smem + [VMEM_SPEC] * (len(operands) - smem),
        out_specs=[VMEM_SPEC] * len(outs),
        out_shape=[placed(*out) for out in outs],
        scratch_shapes=scratch,
        compiler_params=pltpu.CompilerParams(vmem_limit_bytes=megabytes * 1024 * 1024),
        cost_estimate=cost(flops),
        name=name,
    )(*operands)


def bias_part(biases, at):
    return biases[0:1, at * D : (at + 1) * D]


def tile(at):
    return slice(at * D, (at + 1) * D)


def whole(*shape):
    return pl.BlockSpec(shape, lambda *_: (0,) * len(shape))


def flip_kernel(in_ref, out_ref):
    out_ref[...] = in_ref[...].T


def copy_kernel(in_ref, out_ref):
    out_ref[...] = in_ref[...]


def fetched(value):
    height, width = value.shape
    block = pl.BlockSpec((height // 4, width), lambda i: (i, 0))
    return pl.pallas_call(
        copy_kernel,
        grid=(4,),
        in_specs=[block],
        out_specs=block,
        out_shape=placed(value.shape, value.dtype, pltpu.VMEM),
        compiler_params=pltpu.CompilerParams(vmem_limit_bytes=7 * 1024 * 1024),
        cost_estimate=cost(0),
        name="fetched",
    )(in_hbm(value))


def flip(value, space=None):
    height, width = value.shape[-2:]
    lead = (None,) * (value.ndim - 2)
    zeros = (0,) * (value.ndim - 2)
    if height > D:
        grid = height // D
        in_spec = pl.BlockSpec(lead + (D, width), lambda i: zeros + (i, 0))
        out_spec = pl.BlockSpec((width, D), lambda i: (0, i))
    else:
        step = min(width, D)
        grid = width // step
        in_spec = pl.BlockSpec(lead + (height, step), lambda i: zeros + (0, i))
        out_spec = pl.BlockSpec((step, height), lambda i: (i, 0))
    return pl.pallas_call(
        flip_kernel,
        grid=(grid,),
        in_specs=[in_spec],
        out_specs=out_spec,
        out_shape=placed((width, height), value.dtype, space),
        compiler_params=pltpu.CompilerParams(vmem_limit_bytes=7 * 1024 * 1024),
        cost_estimate=cost(0),
        name="flip",
    )(value)


def front_rows(x_ref, gains, biases, w_ref, normed_ref, kv_ref):
    unit, _ = normalised(x_ref[...].astype(jnp.float32))
    normed = (unit * gains[0:1, :] + bias_part(biases, 0)).astype(jnp.bfloat16)
    normed_ref[...] = normed
    kv_ref[:, :D] = dot(normed, w_ref[0, :, tile(1)], NN).astype(jnp.bfloat16)
    kv_ref[:, D:] = (dot(normed, w_ref[0, :, tile(2)], NN) + bias_part(biases, 3)).astype(jnp.bfloat16)


def choose(which, first_ref, second_ref, chosen_ref):
    for index, source in ((1, first_ref), (0, second_ref)):

        @pl.when(which[0] == index)
        def _():
            chosen_ref[...] = source[...]


def chosen_front_kernel(which, first_ref, second_ref, gains, biases, w_ref, chosen_ref, normed_ref, q_ref, kv_ref):
    choose(which, first_ref, second_ref, chosen_ref)
    front_rows(chosen_ref, gains, biases, w_ref, normed_ref, kv_ref)
    queries_kernel(normed_ref, biases, w_ref, q_ref)


def front_outs(rows):
    narrow = jnp.bfloat16
    return [((rows, D), narrow), ((rows, 2 * D), narrow)]


def front(entry, gains, biases, w_qkv):
    rows = entry.shape[0]
    return call(front_rows, "front", 8, 4 * rows * D * D, front_outs(rows), [], entry, gains, biases, w_qkv)


def chosen_front(which, first, second, gains, biases, w_qkv):
    rows = first.shape[0]
    narrow = jnp.bfloat16
    outs = [((rows, D), narrow)] * 3 + [((rows, 2 * D), narrow)]
    return call(
        chosen_front_kernel, "chosen_front", 8, 6 * rows * D * D, outs, [],
        which, first, second, gains, biases, w_qkv, smem=1,
    )


def queries_kernel(normed_ref, biases, w_ref, q_ref):
    q_ref[...] = (dot(normed_ref[...], w_ref[0, :, tile(0)], NN) + bias_part(biases, 2)).astype(jnp.bfloat16)


def queries_of(normed, biases, w_qkv):
    rows = normed.shape[0]
    outs = [((rows, D), jnp.bfloat16)]
    return call(queries_kernel, "queries", 8, 2 * rows * D * D, outs, [], normed, biases, w_qkv)[0]


def middle_rows(x_ref, o_ref, w_out, biases, part):
    return x_ref[part, :].astype(jnp.float32) + dot(o_ref[part, :], w_out[0], NN) + bias_part(biases, 4)


def rest_kernel(x_ref, o_ref, gains, biases, w_out, w_up, w_down, result_ref):
    for part in row_chunks(x_ref.shape[0]):
        middle = middle_rows(x_ref, o_ref, w_out, biases, part)
        unit, _ = normalised(middle)
        normed = (unit * gains[1:2, :] + bias_part(biases, 1)).astype(jnp.bfloat16)
        total = middle + bias_part(biases, 5)
        for at in range(w_up.shape[2] // D):
            hidden = dot(normed, w_up[0, :, tile(at)], NN) + bias_part(biases, 6 + at)
            total += dot(gelu_only(hidden).astype(jnp.bfloat16), w_down[0, tile(at), :], NN)
        result_ref[part, :] = total.astype(jnp.bfloat16)


def rest(entry, attended, gains, biases, w_out, w_up, w_down):
    rows = entry.shape[0]
    flops = 2 * rows * (D * D + 2 * w_up.size)
    return call(
        rest_kernel, "rest", 7, flops, [((rows, D), jnp.bfloat16)], [],
        entry, attended, gains, biases, w_out, w_up, w_down,
    )[0]


def turn_kernel(
    x_ref, o_ref, d_ref, gains, biases, w_out, w_up, out_t, up_t, down_t,
    middle_ref, normed_ref, active_ref, slope_ref, grad_ref, grad_att_ref,
    middle, normed, actives, slopes, done,
):
    copies = []

    def leave(source, target):
        copies.append(pltpu.make_async_copy(source, target, done.at[len(copies)]))
        copies[-1].start()

    rows = x_ref[...].astype(jnp.float32) + dot(o_ref[...], w_out[0], NN) + bias_part(biases, 4)
    middle[...] = rows
    leave(middle, middle_ref)
    unit, _ = normalised(rows)
    normed[...] = (unit * gains[1:2, :] + bias_part(biases, 1)).astype(jnp.bfloat16)
    leave(normed, normed_ref)
    total = jnp.zeros_like(rows)
    for at in range(w_up.shape[2] // D):
        hidden = dot(normed[...], w_up[0, :, tile(at)], NN) + bias_part(biases, 6 + at)
        active, slope = gelu_parts(hidden)
        actives[at] = active.astype(jnp.bfloat16)
        slopes[at] = slope.astype(jnp.bfloat16)
        leave(actives.at[at], active_ref.at[:, tile(at)])
        leave(slopes.at[at], slope_ref.at[:, tile(at)])
        grad_hidden = dot(d_ref[...], down_t[:, tile(at)], NN) * slope
        total += dot(grad_hidden.astype(jnp.bfloat16), up_t[tile(at), :], NN)
    unit, inverse = normalised(middle[...])
    grad = d_ref[...].astype(jnp.float32) + norm_back(unit, inverse, gains[1:2, :], total)
    grad = grad.astype(jnp.bfloat16)
    grad_ref[...] = grad
    grad_att_ref[...] = dot(grad, out_t[...], NN).astype(jnp.bfloat16)
    for copy in copies:
        copy.wait()


def turn(entry, attended, result_gradient, gains, biases, w_out, w_up, out_t, up_t, down_t):
    rows = entry.shape[0]
    wide, narrow = jnp.float32, jnp.bfloat16
    inner = w_up.shape[2]
    steps = inner // D
    far = [((rows, D), wide), ((rows, D), narrow), ((rows, inner), narrow), ((rows, inner), narrow)]
    return pl.pallas_call(
        turn_kernel,
        in_specs=[VMEM_SPEC] * 10,
        out_specs=[pl.BlockSpec(memory_space=pltpu.HBM)] * len(far) + [VMEM_SPEC] * 2,
        out_shape=[placed(*out, pltpu.HBM) for out in far] + [placed((rows, D), narrow)] * 2,
        scratch_shapes=[
            pltpu.VMEM((rows, D), wide),
            pltpu.VMEM((rows, D), narrow),
            pltpu.VMEM((steps, rows, D), narrow),
            pltpu.VMEM((steps, rows, D), narrow),
            pltpu.SemaphoreType.DMA((2 + 2 * steps,)),
        ],
        compiler_params=pltpu.CompilerParams(vmem_limit_bytes=18 * 1024 * 1024),
        cost_estimate=cost(2 * rows * (2 * D * D + 3 * w_up.size)),
        name="turn",
    )(entry, attended, result_gradient, gains, biases, w_out, w_up, out_t, up_t, down_t)


def down_back_kernel(
    which, first_ref, second_ref, slope_ref, middle_ref, gains, out_t, up_t, down_t,
    d_ref, hidden_ref, grad_ref, grad_att_ref, sums_ref, up_ref,
):
    choose(which, first_ref, second_ref, d_ref)
    sums = [jnp.zeros((1, D), jnp.float32)] * 4
    steps = up_t.shape[0] // D
    up_sums = [jnp.zeros((1, D), jnp.float32)] * steps
    for part in row_chunks(d_ref.shape[0]):
        given = d_ref[part, :]
        through = jnp.zeros(given.shape, jnp.float32)
        for at in range(steps):
            grad_hidden = dot(given, down_t[:, tile(at)], NN) * slope_ref[part, tile(at)].astype(jnp.float32)
            up_sums[at] = up_sums[at] + column_sum(grad_hidden)
            grad_hidden = grad_hidden.astype(jnp.bfloat16)
            hidden_ref[part, tile(at)] = grad_hidden
            through += dot(grad_hidden, up_t[tile(at), :], NN)
        unit, inverse = normalised(middle_ref[part, :])
        given = given.astype(jnp.float32)
        grad = given + norm_back(unit, inverse, gains[1:2, :], through)
        grad_b = grad.astype(jnp.bfloat16)
        grad_ref[part, :] = grad_b
        grad_att_ref[part, :] = dot(grad_b, out_t[...], NN).astype(jnp.bfloat16)
        for at, term in enumerate((through * unit, through, grad, given)):
            sums[at] = sums[at] + column_sum(term)
    sums_ref[...] = jnp.concatenate(sums, axis=0)
    up_ref[...] = jnp.concatenate(up_sums, axis=0)


def down_back(which, first, second, slope, middle, gains, out_t, up_t, down_t):
    rows = first.shape[0]
    wide, narrow = jnp.float32, jnp.bfloat16
    inner = up_t.shape[0]
    outs = [
        ((rows, D), narrow), ((rows, inner), narrow), ((rows, D), narrow), ((rows, D), narrow),
        ((4, D), wide), ((inner // D, D), wide),
    ]
    return call(
        down_back_kernel, "down_back", 8, 2 * rows * (D * D + 2 * up_t.size), outs, [],
        which, first, second, slope, middle, gains, out_t, up_t, down_t, smem=1,
    )


def qkv_tiles(part, q_ref, own_ref, there_ref):
    tiles = [q_ref[part, :]]
    for at in range(2):
        total = own_ref[at, part, :].astype(jnp.float32) + there_ref[at, part, :].astype(jnp.float32)
        tiles.append(total.astype(jnp.bfloat16))
    return tiles


def front_back_kernel(q_ref, own_ref, there_ref, x_ref, grad_ref, gains, qkv_t, out_ref, sums_ref):
    sums = [jnp.zeros((1, D), jnp.float32)] * 4
    for part in row_chunks(x_ref.shape[0]):
        tiles = qkv_tiles(part, q_ref, own_ref, there_ref)
        through = sum(dot(value, qkv_t[tile(at), :], NN) for at, value in enumerate(tiles))
        unit, inverse = normalised(x_ref[part, :].astype(jnp.float32))
        out = grad_ref[part, :].astype(jnp.float32) + norm_back(unit, inverse, gains[0:1, :], through)
        out_ref[part, :] = out.astype(out_ref.dtype)
        terms = (through * unit, through, tiles[0].astype(jnp.float32), tiles[2].astype(jnp.float32))
        for at, term in enumerate(terms):
            sums[at] = sums[at] + column_sum(term)
    sums_ref[...] = jnp.concatenate(sums, axis=0)


def front_back(grad_q, own, there, entry, grad_middle, gains, qkv_t, dtype):
    rows = entry.shape[0]
    outs = [((rows, D), dtype, pltpu.VMEM), ((4, D), jnp.float32)]
    return call(
        front_back_kernel, "front_back", 8, 6 * rows * D * D, outs, [],
        grad_q, own, there, entry, grad_middle, gains, qkv_t,
    )


def begin_back_kernel(q_ref, qkv_t, out_ref):
    out_ref[...] = dot(q_ref[...], qkv_t[tile(0), :], NN)


def begin_back(grad_q, qkv_t):
    rows = grad_q.shape[0]
    return call(begin_back_kernel, "begin_back", 6, 2 * rows * D * D, [((rows, D), jnp.float32)], [], grad_q, qkv_t)[0]


def finish_back_kernel(begun_ref, own_ref, there_ref, x_ref, grad_ref, gains, qkv_t, out_ref):
    through = begun_ref[...]
    for at in range(2):
        total = own_ref[at].astype(jnp.float32) + there_ref[at].astype(jnp.float32)
        through += dot(total.astype(jnp.bfloat16), qkv_t[tile(at + 1), :], NN)
    unit, inverse = normalised(x_ref[...].astype(jnp.float32))
    out = grad_ref[...].astype(jnp.float32) + norm_back(unit, inverse, gains[0:1, :], through)
    out_ref[...] = out.astype(out_ref.dtype)


def finish_back(begun, own, there, entry, grad_middle, gains, qkv_t):
    rows = entry.shape[0]
    outs = [((rows, D), jnp.bfloat16)]
    return call(
        finish_back_kernel, "finish_back", 8, 4 * rows * D * D, outs, [],
        begun, own, there, entry, grad_middle, gains, qkv_t,
    )[0]


def added(kept, arrived, dtype=jnp.bfloat16):
    return (kept.astype(jnp.float32) + arrived.astype(jnp.float32)).astype(dtype)


def core_rows(left_ref, core, order):
    block = left_ref.shape[0] // (2 * len(order))
    picked = [
        left_ref[pl.ds(pl.multiple_of((2 * (2 * z_at + y_at) + core) * block, block), block), :] for z_at, y_at in order
    ]
    return jnp.concatenate(picked, axis=0)


def by_y_then_z(z_count):
    return [(z_at, y_at) for y_at in range(2) for z_at in range(z_count)]


def down_sent_kernel(place, left_ref, right_ref, sent_ref):
    block = sent_ref.shape[2]
    rows = core_rows(left_ref, 1 - place[0], by_y_then_z(1))
    total = dot(rows, right_ref[...], NN).astype(jnp.bfloat16)
    for y_at in range(2):
        sent_ref[y_at, 0] = total[y_at * block : (y_at + 1) * block]


def down_kept_kernel(place, left_ref, right_ref, there_ref, keep_ref, first_ref, second_ref, *, z_count):
    block = keep_ref.shape[1]
    total = dot(core_rows(left_ref, place[0], by_y_then_z(1)), right_ref[...], NN)
    parts = [added(total[y_at * block : (y_at + 1) * block], there_ref[y_at, 0]) for y_at in range(2)]

    def store(mine, send_ref):
        keep_ref[0] = parts[mine]
        send_ref[0] = parts[1 - mine]

    early = pl.program_id(0) < z_count // 2
    for mine in range(2):
        for now, send_ref in ((early, first_ref), (~early, second_ref)):
            pl.when((place[1] == mine) & now)(functools.partial(store, mine, send_ref))


def grid_call(kernel, name, grid, in_specs, out_specs, shapes, scratch, flops, place, *operands, far=0):
    return pl.pallas_call(
        kernel,
        grid_spec=pltpu.PrefetchScalarGridSpec(
            num_scalar_prefetch=1, grid=(grid,), in_specs=in_specs, out_specs=out_specs, scratch_shapes=scratch
        ),
        out_shape=[
            placed(shape, jnp.bfloat16, pltpu.HBM if at < far else None) for at, shape in enumerate(shapes)
        ],
        compiler_params=pltpu.CompilerParams(vmem_limit_bytes=9 * 1024 * 1024),
        cost_estimate=cost(flops),
        name=name,
    )(place, *operands)


def down_specs(active_t, z_count):
    height, rows = active_t.shape
    block = height // (4 * z_count)
    in_specs = [pl.BlockSpec((height // z_count, rows), lambda i, _: (i, 0)), whole(rows, D)]
    return block, in_specs, pl.BlockSpec((2, 1, block, D), lambda i, _: (0, i, 0, 0))


def down_sent(place, active_t, back, z_count):
    block, in_specs, sent_spec = down_specs(active_t, z_count)
    return grid_call(
        down_sent_kernel, "down_sent", z_count, in_specs, [sent_spec], [(2, z_count, block, D)], [],
        active_t.size * D, place, active_t, back,
    )[0]


def down_kept(place, active_t, back, there, z_count):
    block, in_specs, sent_spec = down_specs(active_t, z_count)
    half = z_count // 2
    out_specs = [
        pl.BlockSpec((1, block, D), lambda i, _: (i, 0, 0)),
        pl.BlockSpec((1, block, D), lambda i, _: (jnp.minimum(i, half - 1), 0, 0)),
        pl.BlockSpec((1, block, D), lambda i, _: (jnp.maximum(i - half, 0), 0, 0)),
    ]
    return grid_call(
        functools.partial(down_kept_kernel, z_count=z_count), "down_kept", z_count, in_specs + [sent_spec], out_specs,
        [(z_count, block, D)] + [(half, block, D)] * 2, [],
        active_t.size * D, place, active_t, back, there, far=1,
    )


def up_sent_kernel(place, left_ref, right_ref, sent_ref, rows):
    z_count, block = sent_ref.shape[1:3]
    order = by_y_then_z(z_count)

    @pl.when(pl.program_id(0) == 0)
    def _():
        rows[...] = core_rows(left_ref, 1 - place[0], order)

    total = dot(rows[...], right_ref[...], NN).astype(jnp.bfloat16)
    for at, (z_at, y_at) in enumerate(order):
        sent_ref[y_at, z_at] = total[at * block : (at + 1) * block]


def up_kept_kernel(place, left_ref, right_ref, there_ref, keep_ref, first_ref, second_ref, rows):
    z_count, block = there_ref.shape[1:3]
    order = by_y_then_z(z_count)

    @pl.when(pl.program_id(0) == 0)
    def _():
        rows[...] = core_rows(left_ref, place[0], order)

    total = dot(rows[...], right_ref[...], NN)
    parts = [added(total[at * block : (at + 1) * block], there_ref[y_at, z_at]) for at, (z_at, y_at) in enumerate(order)]

    def store(mine):
        for part, (z_at, y_at) in zip(parts, order):
            if z_at % 2 == mine:
                keep_ref[y_at, z_at // 2] = part
            else:
                (first_ref, second_ref)[y_at][z_at // 2] = part

    for mine in range(2):
        pl.when(place[2] == mine)(functools.partial(store, mine))


def half_rows(rows):
    return pltpu.VMEM((D // 2, rows), jnp.bfloat16)


def column_spec(z_count):
    return pl.BlockSpec((2, z_count, D // (4 * z_count), D), lambda i, _: (0, 0, 0, i))


def up_sent(place, normed_t, grad_hidden, z_count):
    rows, width = grad_hidden.shape
    in_specs = [whole(D, rows), pl.BlockSpec((rows, D), lambda i, _: (0, i))]
    return grid_call(
        up_sent_kernel, "up_sent", width // D, in_specs, [column_spec(z_count)],
        [(2, z_count, D // (4 * z_count), width)], [half_rows(rows)], grad_hidden.size * D, place, normed_t, grad_hidden,
    )[0]


def up_kept(place, normed_t, grad_hidden, there, z_count):
    rows, width = grad_hidden.shape
    in_specs = [whole(D, rows), pl.BlockSpec((rows, D), lambda i, _: (0, i)), column_spec(z_count)]
    shape = (2, z_count // 2, D // (4 * z_count), width)
    out_spec = pl.BlockSpec(shape[:3] + (D,), lambda i, _: (0, 0, 0, i))
    half_spec = pl.BlockSpec(shape[1:3] + (D,), lambda i, _: (0, 0, i))
    return grid_call(
        up_kept_kernel, "up_kept", width // D, in_specs, [out_spec] + [half_spec] * 2, [shape] + [shape[1:]] * 2,
        [half_rows(rows)],
        grad_hidden.size * D, place, normed_t, grad_hidden, there, far=1,
    )


def store_sent(sent_ref, at, total):
    z_count, block = sent_ref.shape[1:3]
    for row, (z_at, y_at) in enumerate(by_y_then_z(z_count)):
        sent_ref[y_at, z_at, :, tile(at)] = total[row * block : (row + 1) * block].astype(jnp.bfloat16)


def outer_sent_kernel(place, o_ref, normed_ref, d_ref, q_ref, sent_ref):
    order = by_y_then_z(sent_ref.shape[1])
    for at, (left, right) in enumerate(((o_ref, d_ref), (normed_ref, q_ref))):
        store_sent(sent_ref, at, dot(core_rows(left, 1 - place[0], order), right[...], NN))


def outer_sent(place, attended_t, normed_t, grad_middle, grad_q, z_count):
    outs = [((2, z_count, D // (4 * z_count), 2 * D), jnp.bfloat16)]
    return call(
        outer_sent_kernel, "outer_sent", 6, 2 * D * grad_q.size, outs, [],
        place, attended_t, normed_t, grad_middle, grad_q, smem=1,
    )[0]


def inner_sent_kernel(place, normed_ref, own_ref, there_ref, sent_ref):
    rows = core_rows(normed_ref, 1 - place[0], by_y_then_z(sent_ref.shape[1]))
    for at in range(2):
        store_sent(sent_ref, at, dot(rows, added(own_ref[at], there_ref[at]), NN))


def inner_sent(place, normed_t, own, there, z_count):
    outs = [((2, z_count, D // (4 * z_count), 2 * D), jnp.bfloat16)]
    return call(
        inner_sent_kernel, "inner_sent", 6, D * own.size, outs, [], place, normed_t, own, there, smem=1
    )[0]


def rest_kept_kernel(
    place, o_ref, normed_ref, d_ref, q_ref, own_ref, there_ref, outer_ref, inner_ref, keep_ref, send_ref
):
    z_count, block = keep_ref.shape[:2]
    order = by_y_then_z(z_count)
    attended, normed = [core_rows(left, place[0], order) for left in (o_ref, normed_ref)]

    def run(mine):
        for at in range(4):
            left = normed if at else attended
            right = (d_ref[...], q_ref[...])[at] if at < 2 else added(own_ref[at - 2], there_ref[at - 2])
            total = dot(left, right, NN)
            arrived = inner_ref if at > 1 else outer_ref
            for row, (z_at, y_at) in enumerate(order):
                target = keep_ref if y_at == mine else send_ref
                part = total[row * block : (row + 1) * block]
                target[z_at, :, tile(at)] = added(part, arrived[y_at, z_at, :, tile(at % 2)])

    for mine in range(2):
        pl.when(place[1] == mine)(functools.partial(run, mine))


def rest_kept(place, attended_t, normed_t, grad_middle, grad_q, own, there, outer_there, inner_there, z_count):
    outs = [((z_count, D // (4 * z_count), 4 * D), jnp.bfloat16)] * 2
    return call(
        rest_kept_kernel, "rest_kept", 10, 4 * D * grad_q.size, outs, [],
        place, attended_t, normed_t, grad_middle, grad_q, own, there, outer_there, inner_there, smem=1,
    )


def fold_kernel(place, kept_ref, arrived_ref, keep_ref, send_ref):
    for target, chosen in ((send_ref, 1 - place[0]), (keep_ref, place[0])):
        for at in range(target.shape[0]):
            target[at] = added(kept_ref[at, chosen], arrived_ref[at, chosen])


def fold(kept, arrived, place, outer):
    width = kept.shape[-1]
    lead = math.prod(kept.shape[:outer])
    inner = math.prod(kept.shape[outer + 1 : -1])
    shape = (lead, 2, inner, width)
    outs = [((lead, inner, width), kept.dtype)] * 2
    keep, send = call(
        fold_kernel, "fold", 4, 0, outs, [], place, kept.reshape(shape), arrived.reshape(shape), smem=1
    )
    left = kept.shape[:outer] + kept.shape[outer + 1 :]
    return keep.reshape(left), send.reshape(left)


def stream_fold_kernel(place, kept_keep, kept_send, first_keep, first_send, second_keep, second_send, keep_ref, send_ref):
    for step, arrived_keep, arrived_send in ((0, first_keep, first_send), (1, second_keep, second_send)):

        @pl.when(pl.program_id(0) == step)
        def _():
            send_ref[...] = added(kept_send[...], arrived_send[...])
            keep_ref[...] = added(kept_keep[...], arrived_keep[...])


def stream_fold(kept, first, second, place):
    inner, width = kept.shape[-2:]
    half = (None, inner, width)
    kept_specs = [
        pl.BlockSpec((None,) + half, lambda i, place: (i, place[0], 0, 0)),
        pl.BlockSpec((None,) + half, lambda i, place: (i, 1 - place[0], 0, 0)),
    ]
    arrived_specs = [
        pl.BlockSpec(half, lambda i, place: (place[0], 0, 0)),
        pl.BlockSpec(half, lambda i, place: (1 - place[0], 0, 0)),
    ]
    out_spec = pl.BlockSpec(half, lambda i, place: (i, 0, 0))
    return pl.pallas_call(
        stream_fold_kernel,
        grid_spec=pltpu.PrefetchScalarGridSpec(
            num_scalar_prefetch=1,
            grid=(2,),
            in_specs=kept_specs + arrived_specs * 2,
            out_specs=[out_spec, out_spec],
        ),
        out_shape=[jax.ShapeDtypeStruct((2, inner, width), jnp.bfloat16)] * 2,
        compiler_params=pltpu.CompilerParams(vmem_limit_bytes=8 * 1024 * 1024),
        cost_estimate=cost(0),
        name="stream_fold",
    )(place, *(in_hbm(value) for value in (kept, kept, first, first, second, second)))


def shifted(value, axis, steps):
    count = lax.axis_size(axis)
    initial, last = (max(0, -steps), min(count, count - steps))
    return lax.ppermute(value, axis, [(source, source + steps) for source in range(initial, last)])


def layer_norm(inputs_row, gain_row, offset):
    center = inputs_row - jnp.mean(inputs_row, axis=-1, keepdims=True)
    spread = jnp.mean(center * center, axis=-1, keepdims=True)
    return center * lax.rsqrt(spread + 1e-05) * gain_row + offset


def gelu_tanh(hidden):
    return jax.nn.gelu(hidden, approximate=True)


def score_terms(queries, key_rows, query_pos, key_pos, signed):
    key_count = key_rows.shape[0]
    scores = (
        jnp.einsum(
            "rhe,khe->hrk",
            queries,
            key_rows.reshape(key_count, HEADS, HDIM),
            preferred_element_type=jnp.float32,
        )
        * 0.125
    )
    curved = jnp.sqrt(scores * scores + 1.0)
    argument = jnp.where(signed, curved, scores)
    sign_pattern = jnp.where(signed, scores / curved, 1.0)
    slope = jnp.where(signed, sign_pattern, 1.0)
    bend = jnp.where(signed, 1.0 / (curved * curved * curved), 0.0)
    permitted_mask = key_pos[None, None, :] <= query_pos[None, :, None]
    return (argument, sign_pattern, slope, bend, permitted_mask)


def score_grads(
    queries, key_rows, value_rows, query_pos, key_pos, log_total, delta, grad_att, signed
):
    argument, sign_pattern, slope, bend, permitted_mask = score_terms(
        queries, key_rows, query_pos, key_pos, signed
    )
    prob = jnp.where(permitted_mask, jnp.exp(argument - log_total[..., None]), 0.0)
    along = jnp.einsum("rhe,khe->hrk", grad_att, value_rows, preferred_element_type=jnp.float32)
    dscore = (prob * ((sign_pattern * along - delta[..., None]) * slope + along * bend)).astype(
        jnp.bfloat16
    )
    return ((sign_pattern * prob).astype(jnp.bfloat16), dscore)


def key_blocks_of(key_all, value_all, key_pos, key_block):
    blocks = key_all.shape[0] // key_block
    return (
        key_all.reshape(blocks, key_block, D),
        value_all.reshape(blocks, key_block, HEADS, HDIM),
        key_pos.reshape(blocks, key_block),
    )


def attend(queries, query_pos, key_all, value_all, key_pos, signed, key_block):
    row_count = queries.shape[0]
    key_split, value_split, pos_split = key_blocks_of(key_all, value_all, key_pos, key_block)

    def running_total(state_in, element):
        largest, row_total_sum, gathered = state_in
        key_rows, value_rows, block_pos = element
        argument, sign_pattern, _, _, permitted_mask = score_terms(
            queries, key_rows, query_pos, block_pos, signed
        )
        masked_scores = jnp.where(permitted_mask, argument, -1e30)
        exponent_values = jnp.maximum(largest, jnp.max(masked_scores, axis=-1))
        multiplier = jnp.exp(largest - exponent_values)
        added_terms = jnp.where(
            permitted_mask, jnp.exp(masked_scores - exponent_values[..., None]), 0.0
        )
        row_total_sum = row_total_sum * multiplier + jnp.sum(added_terms, axis=-1)
        attention_weights = (sign_pattern * added_terms).astype(jnp.bfloat16)
        added = jnp.einsum(
            "hrk,khe->rhe", attention_weights, value_rows, preferred_element_type=jnp.float32
        )
        gathered = gathered * multiplier.T[:, :, None] + added
        return ((exponent_values, row_total_sum, gathered), None)

    start_max = jnp.full((HEADS, row_count), -1e30, jnp.float32)
    start_sum = jnp.zeros((HEADS, row_count), jnp.float32)
    start_out = jnp.zeros((row_count, HEADS, HDIM), jnp.float32)
    (largest, row_total_sum, gathered), _ = lax.scan(
        running_total, (start_max, start_sum, start_out), (key_split, value_split, pos_split)
    )
    log_total = largest + jnp.log(row_total_sum)
    attended = gathered / row_total_sum.T[:, :, None]
    return (attended, log_total)


def backward_summed(
    queries, query_pos, key_all, value_all, key_pos, log_total, delta, grad_att, signed, key_block
):
    key_split, value_split, pos_split = key_blocks_of(key_all, value_all, key_pos, key_block)

    def step_back(grad_q, element):
        key_rows, value_rows, block_pos = element
        attention_weights, dscore = score_grads(
            queries, key_rows, value_rows, query_pos, block_pos, log_total, delta, grad_att, signed
        )
        grad_q = (
            grad_q
            + jnp.einsum(
                "hrk,khe->rhe",
                dscore,
                key_rows.reshape(-1, HEADS, HDIM),
                preferred_element_type=jnp.float32,
            )
            * 0.125
        )
        grad_k = (
            jnp.einsum("hrk,rhe->khe", dscore, queries, preferred_element_type=jnp.float32) * 0.125
        )
        grad_v = jnp.einsum(
            "hrk,rhe->khe", attention_weights, grad_att, preferred_element_type=jnp.float32
        )
        return (grad_q, (grad_k.reshape(key_block, D), grad_v.reshape(key_block, D)))

    start_q = jnp.zeros(queries.shape, jnp.float32)
    grad_q, (grad_k, grad_v) = lax.scan(step_back, start_q, (key_split, value_split, pos_split))
    grad_k, grad_v = (
        lax.psum_scatter(
            grad_k.reshape(-1, D).astype(jnp.bfloat16), "ctx", scatter_dimension=0, tiled=True
        ).astype(jnp.float32),
        lax.psum_scatter(
            grad_v.reshape(-1, D).astype(jnp.bfloat16), "ctx", scatter_dimension=0, tiled=True
        ).astype(jnp.float32),
    )
    return (grad_q.reshape(-1, D), grad_k, grad_v)


def layer_front(inputs_row, gain_pair, bias_row, qkv_w):
    normed = layer_norm(inputs_row, gain_pair[0], bias_row[0:D]).astype(jnp.bfloat16)
    qkv_bias = jnp.concatenate(
        [bias_row[2 * D : 3 * D], jnp.zeros((D,), jnp.float32), bias_row[3 * D : 4 * D]]
    )
    projected = (jnp.dot(normed, qkv_w, preferred_element_type=jnp.float32) + qkv_bias).astype(
        jnp.bfloat16
    )
    return (normed, projected)


def layer_rest(inputs_row, attended_b, gain_pair, bias_row, out_w, up_w, down_w):
    middle = (
        inputs_row
        + jnp.dot(attended_b, out_w, preferred_element_type=jnp.float32)
        + bias_row[4 * D : 5 * D]
    )
    normed_two = layer_norm(middle, gain_pair[1], bias_row[D : 2 * D]).astype(jnp.bfloat16)
    hidden = jnp.dot(normed_two, up_w, preferred_element_type=jnp.float32) + bias_row[6 * D :]
    active = gelu_tanh(hidden).astype(jnp.bfloat16)
    result = (
        middle
        + jnp.dot(active, down_w, preferred_element_type=jnp.float32)
        + bias_row[5 * D : 6 * D]
    )
    return (middle, normed_two, hidden, active, result)


def general_body(inputs, slot_order, cotangent, gains, biases, w_qkv, w_out, w_up, w_down):
    micro_count = inputs.shape[0]
    row_count = inputs.shape[2]
    section_at = lax.axis_index("section")
    ctx_at = lax.axis_index("ctx")
    signed = section_at == 0
    gain_pair = gains[0]
    bias_row = biases[0]
    qkv_w = w_qkv[0]
    out_w = w_out[0]
    up_w = w_up[0]
    down_w = w_down[0]
    span_len = row_count // 2
    seq_pos = (
        slot_order[:, 0, :, None] * span_len + jnp.arange(span_len, dtype=jnp.int32)
    ).reshape(micro_count, -1)
    key_block = min(seq_pos.shape[1], 512)
    first_inputs = inputs[:, 0]
    cot_rows = cotangent[:, 0]

    def sequence_pos(index):
        whole_pos = lax.dynamic_index_in_dim(seq_pos, index, 0, keepdims=False)
        own_pos = lax.dynamic_slice_in_dim(whole_pos, ctx_at * row_count, row_count, 0)
        return (whole_pos, own_pos)

    def layer_forward(entry, index):
        whole_pos, own_pos = sequence_pos(index)
        inputs_row = entry.astype(jnp.float32)
        normed, projected = layer_front(inputs_row, gain_pair, bias_row, qkv_w)
        key_all, value_all = (
            lax.all_gather(projected[:, D : 2 * D], "ctx", axis=0, tiled=True),
            lax.all_gather(projected[:, 2 * D :], "ctx", axis=0, tiled=True),
        )
        queries = projected[:, :D].reshape(row_count, HEADS, HDIM)
        attended, _ = attend(queries, own_pos, key_all, value_all, whole_pos, signed, key_block)
        attended_b = attended.reshape(row_count, D).astype(jnp.bfloat16)
        result = layer_rest(inputs_row, attended_b, gain_pair, bias_row, out_w, up_w, down_w)[4]
        return result.astype(jnp.bfloat16)

    def layer_reverse_pass(entry, result_gradient, index):
        whole_pos, own_pos = sequence_pos(index)
        inputs_row = entry.astype(jnp.float32)
        normed, projected = layer_front(inputs_row, gain_pair, bias_row, qkv_w)
        queries = projected[:, :D].reshape(row_count, HEADS, HDIM)
        key_all, value_all = (
            lax.all_gather(projected[:, D : 2 * D], "ctx", axis=0, tiled=True),
            lax.all_gather(projected[:, 2 * D :], "ctx", axis=0, tiled=True),
        )
        attended, log_total = attend(
            queries, own_pos, key_all, value_all, whole_pos, signed, key_block
        )
        attended_b = attended.reshape(row_count, D).astype(jnp.bfloat16)
        middle, normed_two, hidden, active, _ = layer_rest(
            inputs_row, attended_b, gain_pair, bias_row, out_w, up_w, down_w
        )
        grad_down_b = result_gradient.astype(jnp.bfloat16)
        grad_wdown = jnp.dot(active.T, grad_down_b, preferred_element_type=jnp.float32)
        grad_active = jnp.dot(grad_down_b, down_w.T, preferred_element_type=jnp.float32)
        _, gelu_back = jax.vjp(gelu_tanh, hidden)
        grad_hidden = gelu_back(grad_active)[0]
        grad_hidden_b = grad_hidden.astype(jnp.bfloat16)
        grad_wup = jnp.dot(normed_two.T, grad_hidden_b, preferred_element_type=jnp.float32)
        grad_normed_two = jnp.dot(grad_hidden_b, up_w.T, preferred_element_type=jnp.float32)
        _, norm_back_two = jax.vjp(layer_norm, middle, gain_pair[1], bias_row[D : 2 * D])
        grad_middle_part, grad_gain_two, grad_offset_two = norm_back_two(grad_normed_two)
        grad_middle = result_gradient + grad_middle_part
        grad_proj_b = grad_middle.astype(jnp.bfloat16)
        grad_wout = jnp.dot(attended_b.T, grad_proj_b, preferred_element_type=jnp.float32)
        grad_att_flat = jnp.dot(grad_proj_b, out_w.T, preferred_element_type=jnp.float32).astype(
            jnp.bfloat16
        )
        grad_att = grad_att_flat.reshape(row_count, HEADS, HDIM)
        delta = jnp.einsum("rhe,rhe->hr", grad_att.astype(jnp.float32), attended)
        grad_q, grad_k, grad_v = backward_summed(
            queries,
            own_pos,
            key_all,
            value_all,
            whole_pos,
            log_total,
            delta,
            grad_att,
            signed,
            key_block,
        )
        grad_qkv_b = jnp.concatenate([grad_q, grad_k, grad_v], axis=1).astype(jnp.bfloat16)
        grad_wqkv = jnp.dot(normed.T, grad_qkv_b, preferred_element_type=jnp.float32)
        grad_normed = jnp.dot(grad_qkv_b, qkv_w.T, preferred_element_type=jnp.float32)
        _, norm_back_one = jax.vjp(layer_norm, inputs_row, gain_pair[0], bias_row[0:D])
        grad_in_part, grad_gain_one, grad_offset_one = norm_back_one(grad_normed)
        input_gradient = grad_middle + grad_in_part
        grad_gain_rows = jnp.stack([grad_gain_one, grad_gain_two])
        grad_bias_row = jnp.concatenate(
            [
                grad_offset_one,
                grad_offset_two,
                jnp.sum(grad_q, axis=0),
                jnp.sum(grad_v, axis=0),
                jnp.sum(grad_middle, axis=0),
                jnp.sum(result_gradient, axis=0),
                jnp.sum(grad_hidden, axis=0),
            ]
        )
        return (
            input_gradient,
            (grad_gain_rows, grad_bias_row, grad_wqkv, grad_wout, grad_wup, grad_wdown),
        )

    def tick(tick_at, state_in):
        arrived, returned, stored, acts_rows, grad_rows, partial_sums = state_in
        ahead = tick_at - section_at
        ahead_ok = (ahead >= 0) & (ahead < micro_count)
        ahead_at = jnp.clip(ahead, 0, micro_count - 1)
        fresh = jnp.where(
            signed, lax.dynamic_index_in_dim(first_inputs, ahead_at, 0, keepdims=False), arrived
        )
        previous = lax.dynamic_index_in_dim(stored, ahead_at, 0, keepdims=False)
        entry = jnp.where(ahead_ok, fresh, previous)
        stored = lax.dynamic_update_index_in_dim(stored, entry, ahead_at, 0)
        sent = layer_forward(entry, ahead_at)
        old_acts = lax.dynamic_index_in_dim(acts_rows, ahead_at, 0, keepdims=False)
        acts_rows = lax.dynamic_update_index_in_dim(
            acts_rows, jnp.where(ahead_ok, sent, old_acts), ahead_at, 0
        )
        behind = tick_at - 2 + section_at
        trailing_valid = (behind >= 0) & (behind < micro_count)
        trailing_position = jnp.clip(behind, 0, micro_count - 1)
        entry_gradient = lax.dynamic_index_in_dim(stored, trailing_position, 0, keepdims=False)
        given_cot = lax.dynamic_index_in_dim(cot_rows, trailing_position, 0, keepdims=False).astype(
            jnp.float32
        )
        result_gradient = jnp.where(signed, returned.astype(jnp.float32), given_cot)
        input_gradient, added_terms = layer_reverse_pass(
            entry_gradient, result_gradient, trailing_position
        )
        partial_sums = jax.tree.map(
            lambda running_total, added_term: running_total
            + jnp.where(trailing_valid, added_term, 0.0),
            partial_sums,
            added_terms,
        )
        handed = input_gradient.astype(jnp.bfloat16)
        kept_grad = jnp.where(signed, input_gradient, handed.astype(jnp.float32))
        old_grads = lax.dynamic_index_in_dim(grad_rows, trailing_position, 0, keepdims=False)
        grad_rows = lax.dynamic_update_index_in_dim(
            grad_rows, jnp.where(trailing_valid, kept_grad, old_grads), trailing_position, 0
        )
        arrived = shifted(sent, "section", 1)
        returned = shifted(handed, "section", -1)
        return (arrived, returned, stored, acts_rows, grad_rows, partial_sums)

    zero_rows = jnp.zeros((row_count, D), jnp.bfloat16)
    start_sums = (
        jnp.zeros((2, D), jnp.float32),
        jnp.zeros((bias_row.shape[0],), jnp.float32),
        jnp.zeros(qkv_w.shape, jnp.float32),
        jnp.zeros(out_w.shape, jnp.float32),
        jnp.zeros(up_w.shape, jnp.float32),
        jnp.zeros(down_w.shape, jnp.float32),
    )
    start_state = (
        zero_rows,
        zero_rows,
        jnp.zeros((micro_count, row_count, D), jnp.bfloat16),
        jnp.zeros((micro_count, row_count, D), jnp.bfloat16),
        jnp.zeros((micro_count, row_count, D), jnp.float32),
        start_sums,
    )
    final_state = lax.fori_loop(0, micro_count + 2, tick, start_state)
    acts_rows = final_state[3]
    grad_rows = final_state[4]
    partial_sums = final_state[5]
    totals = (
        lax.psum_scatter(partial_sums[0], ("dp", "ctx"), scatter_dimension=1, tiled=True),
        lax.psum_scatter(partial_sums[1], ("dp", "ctx"), scatter_dimension=0, tiled=True),
        lax.psum_scatter(partial_sums[2], ("dp", "ctx"), scatter_dimension=0, tiled=True),
        lax.psum_scatter(partial_sums[3], ("dp", "ctx"), scatter_dimension=0, tiled=True),
        lax.psum_scatter(partial_sums[4], ("dp", "ctx"), scatter_dimension=0, tiled=True),
        lax.psum_scatter(partial_sums[5], ("dp", "ctx"), scatter_dimension=0, tiled=True),
    )
    return (
        acts_rows[None, :, None],
        grad_rows[None, :, None],
        totals[0][None],
        totals[1][None],
        totals[2][None],
        totals[3][None],
        totals[4][None],
        totals[5][None],
    )


def swap_halves(value):
    count = lax.axis_size("ctx")
    return lax.ppermute(value, "ctx", [(at, (at + count // 2) % count) for at in range(count)])


def swap_cores(value):
    return lax.ppermute(value, "ctx", [(at, at ^ 1) for at in range(lax.axis_size("ctx"))])


def swap_z(value, step):
    return lax.ppermute(value, "dp", [(at, at ^ step) for at in range(lax.axis_size("dp"))])


def wide_sum(kept, arrived):
    return kept.astype(jnp.float32) + arrived.astype(jnp.float32)


def fast_body(inputs, slot_order, cotangent, gains, biases, w_qkv, w_out, w_up, w_down):
    rows = inputs.shape[2]
    count = lax.axis_size("ctx")
    z_count = lax.axis_size("dp")
    half = count // 2
    ctx_at = lax.axis_index("ctx")
    mine = ctx_at // half
    y_at, core_at = ctx_at // 2, ctx_at % 2
    signed = lax.axis_index("section") == 0
    which = signed.astype(jnp.int32)[None]
    place = core_at[None].astype(jnp.int32)
    y_place = y_at[None].astype(jnp.int32)
    z_at = lax.axis_index("dp")
    gain_pair = gains[0]
    wide, narrow, barrier = jnp.float32, jnp.bfloat16, lax.optimization_barrier

    def gathered(value):
        kept = lax.dynamic_index_in_dim(value, mine, 0, keepdims=False)
        sent = lax.dynamic_index_in_dim(value, 1 - mine, 0, keepdims=False)
        return jnp.concatenate([kept, swap_halves(sent)], axis=0)

    def returned(kept, arrived):
        arrived = arrived.astype(kept.dtype)
        first = jnp.where(mine == 0, kept, arrived)
        second = jnp.where(mine == 0, arrived, kept)
        return jnp.stack([first, second])

    order = lax.dynamic_index_in_dim(slot_order[:, 0], mine, 0, keepdims=False)
    pairs = order.reshape(count, 2)

    def slots_of(device):
        return jnp.concatenate([pairs[device], pairs[(device + half) % count]])

    meta = slot_meta(slots_of(ctx_at), slots_of(ctx_at ^ 1), signed)

    inputs, meta = barrier((inputs, meta))
    first = gathered(inputs[:, 0])
    qkv_t, out_t = flip(w_qkv, pltpu.HBM), flip(w_out, pltpu.HBM)
    first, qkv_t, out_t = barrier((first, qkv_t, out_t))
    normed, kv = front(first, gain_pair, biases, w_qkv)
    normed, kv = barrier((normed, kv))
    queries, kv_there = barrier((queries_of(normed, biases, w_qkv), swap_cores(kv)))
    attended, _ = sorted_attend(meta, queries, kv, kv_there)
    sent = rest(first, attended, gain_pair, biases, w_out, w_up, w_down)
    sent, later = barrier((sent, (cotangent, w_up, w_down)))
    arrived = shifted(sent, "section", 1)
    given = gathered(later[0][:, 0])
    up_t, down_t = [flip(weight, pltpu.HBM) for weight in later[1:]]
    arrived, given, up_t, down_t = barrier((arrived, given, up_t, down_t))
    entry, normed, queries, kv = chosen_front(which, first, arrived, gain_pair, biases, w_qkv)
    kv_there = swap_cores(kv)
    normed_t = flip(normed, pltpu.HBM)
    kv_there, normed_t = barrier((kv_there, normed_t))
    attended, lse = sorted_attend(meta, queries, kv, kv_there)
    middle, normed_two, active, slope, grad_middle, grad_att = turn(
        entry, attended, given, gain_pair, biases, w_out, w_up, out_t, up_t, down_t
    )

    grad_q, own, sent, *ahead = sorted_attend_back(meta, queries, kv, kv_there, attended, grad_att, lse)
    own, sent, grad_q, attended, normed_two = barrier((own, sent, grad_q, attended, normed_two))
    there = swap_cores(sent)
    begun = begin_back(grad_q, qkv_t)
    attended_t, normed_two_t = flip(attended, pltpu.HBM), flip(normed_two, pltpu.HBM)
    there, begun, attended_t, normed_two_t = barrier((there, begun, attended_t, normed_two_t))
    handed = finish_back(begun, own, there, entry, grad_middle, gain_pair, qkv_t)
    handed, active, middle, weights = barrier((handed, active, middle, (w_up, w_down)))
    back = shifted(handed, "section", -1)
    result = middle + dot(active, w_down[0], NN) + biases[0, 5 * D : 6 * D]
    result = result.astype(narrow)
    acts_there = swap_halves(result[rows:])
    middle, acts_there, active = barrier((middle, acts_there, active))
    up_t, down_t = [flip(in_hbm(weight), pltpu.VMEM) for weight in weights]
    active_t = flip(active, pltpu.VMEM)
    back, up_t, down_t, active_t = barrier((back, up_t, down_t, active_t))

    z_steps = [1 << at for at in range(z_count.bit_length() - 1)]
    split = [2] * len(z_steps)
    by_z = [((z_at >> at) & 1)[None].astype(jnp.int32) for at in range(len(z_steps))]

    def bits(value, before):
        return value.reshape(value.shape[:before] + tuple(split) + value.shape[before + 1 :])

    places = jnp.concatenate([place, y_place, by_z[0]])
    back, grad_hidden, grad_middle, grad_att, sums_two, up_sum = down_back(
        which, back, given, slope, middle, gain_pair, out_t, up_t, down_t
    )
    back, grad_hidden = barrier((back, grad_hidden))
    down_there = down_sent(places, active_t, back, z_count)
    grad_hidden, down_there = barrier((grad_hidden, down_there))
    down_there = swap_cores(down_there)
    up_there = up_sent(places, normed_two_t, grad_hidden, z_count)
    down_there, up_there = barrier((down_there, up_there))
    up_there = swap_cores(up_there)
    down_keep, down_send, down_later = down_kept(places, active_t, back, down_there, z_count)
    up_there, down_send, down_later = barrier((up_there, down_send, down_later))
    up_keep, up_send, up_later = up_kept(places, normed_two_t, grad_hidden, up_there, z_count)
    grad_att, down_send, up_send = barrier((grad_att, down_send, up_send))
    down_first, up_first = swap_halves(down_send), swap_z(up_send, z_steps[0])
    grad_q, own, sent = sorted_attend_back(meta, queries, kv, kv_there, attended, grad_att, lse, ahead)

    grad_q, own, sent, down_first, up_first, down_later, up_later = barrier(
        (grad_q, own, sent, down_first, up_first, down_later, up_later)
    )
    there = swap_cores(sent)
    down_second, up_second = swap_halves(down_later), swap_z(up_later, z_steps[0])
    outer_there = outer_sent(places, attended_t, normed_t, grad_middle, grad_q, z_count)
    there, outer_there = barrier((there, outer_there))
    outer_there = swap_cores(outer_there)
    inner_there = inner_sent(places, normed_t, own, there, z_count)
    inner_there, down_second, up_second = barrier((inner_there, down_second, up_second))
    inner_there = swap_cores(inner_there)
    down_keep, down_send = stream_fold(bits(down_keep, 0), down_first, down_second, by_z[0])
    up_keep, up_send = stream_fold(up_keep, up_first, up_second, by_z[1])
    outer_there, inner_there, down_send, up_send = barrier((outer_there, inner_there, down_send, up_send))
    rest_keep, rest_send = rest_kept(
        places, attended_t, normed_t, grad_middle, grad_q, own, there, outer_there, inner_there, z_count
    )
    rest_send, down_send, up_send, grad_q, own, there = barrier((rest_send, down_send, up_send, grad_q, own, there))
    rest_there, down_there, up_there = swap_halves(rest_send), swap_z(down_send, z_steps[0]), swap_z(up_send, z_steps[1])
    input_gradient, sums_one = front_back(grad_q, own, there, entry, grad_middle, gain_pair, qkv_t, wide)
    small = jnp.concatenate([sums_one, sums_two, up_sum], axis=0)
    small = small + swap_cores(small)
    rounded = input_gradient.astype(narrow)
    small_there = swap_halves(small)
    down_there, rounded = barrier((down_there, rounded))
    down_keep, down_send = fold(down_keep, down_there, by_z[1], 0)
    down_send, rest_there, small_there = barrier((down_send, rest_there, small_there))
    down_there = swap_z(down_send, z_steps[1])

    rest_keep, rest_send = fold(bits(rest_keep, 0), bits(rest_there, 0), by_z[0], len(split) - 1)
    small = small + small_there
    rest_send, up_there, small = barrier((rest_send, up_there, small))
    rest_there, small_there = swap_z(rest_send, z_steps[0]), swap_z(small, z_steps[0])
    up_keep, up_send = fold(up_keep, up_there, y_place, 0)
    up_there = swap_halves(up_send)
    rounded, up_send = barrier((rounded, up_send))
    grads_there = swap_halves(rounded[rows:])
    rest_there, up_there, small_there, down_there, grads_there = barrier(
        (rest_there, up_there, small_there, down_there, grads_there)
    )
    rest_keep, rest_send = fold(rest_keep, rest_there, by_z[1], 0)
    rest_send, small_there, grads_there, result, acts_there = barrier(
        (rest_send, small_there, grads_there, result, acts_there)
    )
    rest_there = swap_z(rest_send, z_steps[1])
    small = small + small_there
    small = small + swap_z(small, z_steps[1])
    wdown = wide_sum(down_keep, down_there)
    wup = wide_sum(up_keep, up_there)
    grads_kept = jnp.where(signed, input_gradient[:rows], rounded[:rows].astype(wide))
    grad_rows = returned(grads_kept, grads_there)
    grad_rows, rest_there = barrier((grad_rows, rest_there))
    wout = wide_sum(rest_keep[:, :D], rest_there[:, :D])
    wqkv = wide_sum(rest_keep[:, D:], rest_there[:, D:])
    blocks = count * z_count
    block_at = lax.axis_index("dp") * count + ctx_at
    gain_piece = lax.dynamic_slice_in_dim(small[0:5:4], block_at * (D // blocks), D // blocks, 1)
    bias_row = jnp.concatenate([small[1:2], small[5:6], small[2:4], small[6:]], axis=0).reshape(-1)
    width = bias_row.shape[0] // blocks
    bias_piece = lax.dynamic_slice_in_dim(bias_row, block_at * width, width, 0)
    return (
        returned(result[:rows], acts_there)[None, :, None],
        grad_rows[None, :, None],
        gain_piece[None],
        bias_piece[None],
        wqkv[None],
        wout[None],
        wup[None],
        wdown[None],
    )


def body_for(mesh):
    sizes = dict(mesh.shape)
    return fast_body if (sizes["ctx"], sizes["dp"]) == (4, 4) else general_body


def solution(mesh):
    in_specs = (
        P(None, "dp", "ctx", None),
        P(None, "dp", None),
        P(None, "dp", "ctx", None),
        P("section", None, None),
        P("section", None),
        P("section", None, None),
        P("section", None, None),
        P("section", None, None),
        P("section", None, None),
    )
    out_specs = (
        P("section", None, "dp", "ctx", None),
        P("section", None, "dp", "ctx", None),
        P("section", None, ("dp", "ctx")),
        P("section", ("dp", "ctx")),
        P("section", ("dp", "ctx"), None),
        P("section", ("dp", "ctx"), None),
        P("section", ("dp", "ctx"), None),
        P("section", ("dp", "ctx"), None),
    )
    return jax.shard_map(
        body_for(mesh), mesh=mesh, in_specs=in_specs, out_specs=out_specs, check_vma=False
    )
```
